32 devices in a mesh: dp: 8 (over y, x, core), tensor: 4 (over z).
Axes of the slice: x: 2, y: 2, z: 4, core: 2. Of those that a mesh axis runs over, the one named last changes fastest.
Arguments:
- block_input: bfloat16 [8192, 1024], P(('dp', 'tensor')), may hold values from -6 to 6
- doc_lengths: int32 [8, 16], P('dp'), may hold values from 1 to 769, 1024 in all within a row
- pad_mask: int32 [8, 1024], P('dp'), may hold values 0 or 1
- norm1_gain: float32 [1024], replicated, may hold values from 0.5 to 1.5
- w_query: bfloat16 [1024, 1024], P(None, 'tensor'), may hold values from -0.1875 to 0.1875
- w_key: bfloat16 [1024, 512], P(None, 'tensor'), may hold values from -0.1875 to 0.1875
- w_value: bfloat16 [1024, 512], P(None, 'tensor'), may hold values from -0.1875 to 0.1875
- query_gain: float32 [64], replicated, may hold values from 0.5 to 1.5
- key_gain: float32 [64], replicated, may hold values from 0.5 to 1.5
- w_out: bfloat16 [1024, 1024], P('tensor'), may hold values from -3 to 3
- norm2_gain: float32 [1024], replicated, may hold values from 0.5 to 1.5
- w_gate: bfloat16 [1024, 4608], P(None, 'tensor'), may hold values from -0.1875 to 0.1875
- w_up: bfloat16 [1024, 4608], P(None, 'tensor'), may hold values from -0.1875 to 0.1875
- w_down: bfloat16 [4608, 1024], P('tensor'), may hold values from -0.09375 to 0.09375
- cotangent: bfloat16 [8192, 1024], P(('dp', 'tensor')), may hold values from -6 to 6
Outputs:
- block_output: float32 [8192, 1024], P(('dp', 'tensor'))
- input_grad: float32 [8192, 1024], P(('dp', 'tensor'))
- grad_norm1: float32 [1024], replicated
- grad_query: float32 [1024, 1024], P(None, 'tensor')
- grad_key: float32 [1024, 512], P(None, 'tensor')
- grad_value: float32 [1024, 512], P(None, 'tensor')
- grad_query_gain: float32 [64], replicated
- grad_key_gain: float32 [64], replicated
- grad_out: float32 [1024, 1024], P('tensor')
- grad_norm2: float32 [1024], replicated
- grad_gate: float32 [1024, 4608], P(None, 'tensor')
- grad_up: float32 [1024, 4608], P(None, 'tensor')
- grad_down: float32 [4608, 1024], P('tensor')
The draws below stay inside these ranges and needn't reach their ends.
Inputs may be any that keep to these rules, and one draw needn't show every extreme that they name: `doc_lengths`: each row's lengths sum to 1024; exactly one document of each row is 769 long.
All inputs are finite; a program needn't handle non-finite values. No bound on the sum of `pad_mask` on one device may be relied on, other than what follows from the above.
Results may differ from the reference program's by a relative error of at most 0.015.
Values may be sent and summed in bfloat16 or wider, within the bound.
No kernel may reach another device: no remote copies, remote signals or barrier semaphores. Data moves between devices by JAX's collectives and lax.ppermute only.
A program may use at most 128 MiB of HBM per device.

```python
import math
import jax
import jax.numpy as jnp
import numpy as np
from jax import lax

D = 1024
HEADS = 16
KV_HEADS = 8
HD = 64
FF = 4608
DOCS = 16
SEQ = 1024
LONGEST = 769
TOKENS = 8192
N_DP = 8


def touch_ends(values, rng, low, high):
    extent = values.shape
    place = [jax.random.randint(jax.random.fold_in(rng, axis), (), 0, extent[axis]) for axis in range(len(extent))]
    values = values.at[tuple(place)].set(low)
    longest = extent.index(max(extent))
    place[longest] = (place[longest] + 1) % extent[longest]
    return values.at[tuple(place)].set(high)


def block_scale(own_key, dims, cuts, least, largest):
    loudness, own = 1.0, jax.random.fold_in(own_key, 6)
    for axis_at, blocks in cuts:
        heights = jnp.exp(jax.random.uniform(jax.random.fold_in(own, axis_at), (blocks,), jnp.float32, least / len(cuts), largest / len(cuts)))
        loudness = loudness * jnp.repeat(heights, dims[axis_at] // blocks).reshape([-1 if axis == axis_at else 1 for axis in range(len(dims))])
    return loudness


def profile(amount, total, bound, lean):
    portions = [(1 << 20) // math.isqrt(grade ** lean) + 1 for grade in range(2, amount + 1)]
    spare, holding = total - bound - (amount - 1), [1] * (amount - 1)
    while spare > 0:
        movable = [i for i in range(amount - 1) if holding[i] < bound]
        whole, budget = sum([portions[i] for i in movable]), spare
        for i in movable:
            addition = min(bound - holding[i], max(1, budget * portions[i] // whole), spare)
            holding[i] = holding[i] + addition
            spare = spare - addition
    return np.array([bound] + holding)


def uneven(rng, count, total, bound, skew):
    if count == 2:
        one = jax.random.randint(rng, (), max(1, total - bound), min(bound, total - 1) + 1)
        return jnp.stack([one, total - one])
    tallies = jnp.asarray(profile(count, total, bound, skew), jnp.int32)
    pairs = (count - 1) // 2
    source_of, sink = tallies[1:1 + 2 * pairs:2], tallies[2:2 + 2 * pairs:2]
    room = jnp.minimum(source_of - 1, bound - sink)
    shifted = jax.random.randint(jax.random.fold_in(rng, 1), (pairs,), 0, 1 << 20) % (room + 1)
    tallies = tallies.at[1:1 + 2 * pairs:2].set(source_of - shifted).at[2:2 + 2 * pairs:2].set(sink + shifted)
    return tallies[jax.random.permutation(jax.random.fold_in(rng, 2), count)]


def gaussian(stream_key, extent, width, reach, cuts=(), held_as=jnp.bfloat16):
    values = width * jax.random.normal(stream_key, extent, jnp.float32)
    if cuts:
        values = values * block_scale(stream_key, extent, cuts, -0.22, 0.18)
    return jnp.clip(values, -reach, reach).astype(held_as)


def setup_inputs(seed: int = 0) -> dict:
    streams_of = jax.random.split(jax.random.key(seed), 16)
    return {
        "block_input": gaussian(streams_of[0], (TOKENS, D), 1.0, 6.0, ((0, 32),)),
        "doc_lengths": jax.vmap(lambda own: uneven(own, DOCS, SEQ, LONGEST, 4))(jax.random.split(streams_of[1], N_DP)).reshape((N_DP, DOCS)).astype(jnp.int32),
        "pad_mask": touch_ends((jax.random.randint(streams_of[2], (N_DP, SEQ), 0, 4) < 3).astype(jnp.int32), jax.random.fold_in(streams_of[2], 1), 0, 1),
        "norm1_gain": jnp.clip(1.0 + 0.1 * jax.random.normal(streams_of[3], (D,), jnp.float32), 0.5, 1.5),
        "w_query": gaussian(streams_of[4], (D, HEADS * HD), D ** -0.5, 0.1875, ((1, 4),)),
        "w_key": gaussian(streams_of[5], (D, KV_HEADS * HD), D ** -0.5, 0.1875, ((1, 4),)),
        "w_value": gaussian(streams_of[6], (D, KV_HEADS * HD), D ** -0.5, 0.1875, ((1, 4),)),
        "query_gain": jnp.clip(1.0 + 0.1 * jax.random.normal(streams_of[7], (HD,), jnp.float32), 0.5, 1.5),
        "key_gain": jnp.clip(1.0 + 0.1 * jax.random.normal(streams_of[8], (HD,), jnp.float32), 0.5, 1.5),
        "w_out": gaussian(streams_of[9], (HEADS * HD, D), (max(HEADS * HD // 256, 2)) ** -0.5, 3.0, ((0, 4),)),
        "norm2_gain": jnp.clip(1.0 + 0.1 * jax.random.normal(streams_of[10], (D,), jnp.float32), 0.5, 1.5),
        "w_gate": gaussian(streams_of[11], (D, FF), D ** -0.5, 0.1875, ((1, 4),)),
        "w_up": gaussian(streams_of[12], (D, FF), D ** -0.5, 0.1875, ((1, 4),)),
        "w_down": gaussian(streams_of[13], (FF, D), FF ** -0.5, 0.09375, ((0, 4),)),
        "cotangent": gaussian(streams_of[14], (TOKENS, D), 1.0, 6.0, ((0, 32),)),
    }


epsilon = 1e-05
rope_base = 1000000.0
masked_value = -1000000000.0

@jax.custom_vjp
def low(v):
    return lax.optimization_barrier(v.astype(jnp.bfloat16)).astype(jnp.float32)

@jax.custom_vjp
def low_back(v):
    return v

def low_keep(v):
    return (low(v), None)

def low_pass(kept, grad):
    return (grad,)

def back_keep(v):
    return (v, None)

def back_low(kept, grad):
    return (low(grad),)
low.defvjp(low_keep, low_pass)
low_back.defvjp(back_keep, back_low)

def rms_norm(values, gain_vec):
    return values * lax.rsqrt(lax.optimization_barrier(jnp.mean(values * values, axis=-1, keepdims=True)) + epsilon) * gain_vec

def rotate(values, cos_table, sine_table):
    half_dim = values.shape[-1] // 2
    first_half = values[..., :half_dim]
    second_half = values[..., half_dim:]
    return jnp.concatenate([first_half * cos_table - second_half * sine_table, second_half * cos_table + first_half * sine_table], axis=-1)

def doc_tables(lengths_row, seq_len, head_dim):
    positions = jnp.arange(seq_len, dtype=jnp.int32)
    doc_ends = jnp.cumsum(lengths_row).astype(jnp.int32)
    passed = positions[:, None] >= doc_ends[None, :]
    doc_ids = lax.optimization_barrier(jnp.sum(passed.astype(jnp.int32), axis=1)).astype(jnp.int32)
    doc_starts = lax.optimization_barrier(jnp.sum(jnp.where(passed, lengths_row[None, :], 0), axis=1)).astype(jnp.int32)
    offsets = (positions - doc_starts).astype(jnp.float32)
    freqs = jnp.exp(jnp.arange(head_dim // 2, dtype=jnp.float32) * (-2.0 * math.log(rope_base) / head_dim))
    angles = offsets[:, None] * freqs[None, :]
    return (doc_ids, jnp.cos(angles), jnp.sin(angles))

def allowed_block(doc_ids, pad_row, row_start, block_rows):
    seq_len = doc_ids.shape[0]
    query_pos = row_start + jnp.arange(block_rows, dtype=jnp.int32)
    key_pos = jnp.arange(seq_len, dtype=jnp.int32)
    query_docs = lax.dynamic_slice_in_dim(doc_ids, row_start, block_rows, 0)
    same_doc = query_docs[:, None] == doc_ids[None, :]
    causal = key_pos[None, :] <= query_pos[:, None]
    live = (pad_row[None, :] == 1) | (key_pos[None, :] == query_pos[:, None])
    return same_doc & causal & live

def project(left, right):
    return jnp.einsum('...d,de->...e', left, right, precision=lax.Precision.HIGHEST)

def reference(block_input, doc_lengths, pad_mask, norm1_gain, w_query, w_key, w_value, query_gain, key_gain, w_out, norm2_gain, w_gate, w_up, w_down, cotangent):
    doc_ids, cos_table, sine_table = jax.vmap(lambda lengths_row: doc_tables(lengths_row, SEQ, HD))(doc_lengths)
    cos_four = cos_table[:, :, None, :]
    sine_four = sine_table[:, :, None, :]
    block_rows = min(512, SEQ)
    block_count = SEQ // block_rows
    group_size = HEADS // KV_HEADS
    score_scale = HD ** (-0.5)

    def attend_row(operands):
        queries, keys, values, row_docs, pad_row = operands
        grouped = queries.reshape(SEQ, KV_HEADS, group_size, HD)

        def attend_block(block_index):
            row_start = (block_index * block_rows).astype(jnp.int32)
            query_block = lax.dynamic_slice_in_dim(grouped, row_start, block_rows, 0)
            scores = low_back(jnp.einsum('qkgd,skd->kgqs', query_block, keys, precision=lax.Precision.HIGHEST))
            allowed = allowed_block(row_docs, pad_row, row_start, block_rows)
            scaled = jnp.where(allowed, scores * score_scale, masked_value)
            probs = low(jax.nn.softmax(scaled, axis=-1))
            return jnp.einsum('kgqs,skd->qkgd', probs, values, precision=lax.Precision.HIGHEST)
        blocks = lax.map(jax.checkpoint(attend_block), jnp.arange(block_count, dtype=jnp.int32))
        return blocks.reshape(SEQ, HEADS * HD)

    def forward(inputs_f, gain_one, query_w, key_w, value_w, qgain_vec, kgain_vec, out_w, gain_two, gate_w, up_w, down_w):
        inputs_three = inputs_f.reshape(N_DP, SEQ, D)
        normed1 = low(rms_norm(inputs_three, gain_one))
        query_pre = low_back(project(normed1, query_w)).reshape(N_DP, SEQ, HEADS, HD)
        key_pre = low_back(project(normed1, key_w)).reshape(N_DP, SEQ, KV_HEADS, HD)
        values = low(low_back(project(normed1, value_w))).reshape(N_DP, SEQ, KV_HEADS, HD)
        queries = low(rotate(rms_norm(query_pre, qgain_vec), cos_four, sine_four))
        keys = low(rotate(rms_norm(key_pre, kgain_vec), cos_four, sine_four))
        attended = low(low_back(lax.map(attend_row, (queries, keys, values, doc_ids, pad_mask))))
        residual = inputs_three + low_back(project(attended, out_w))
        normed2 = low(rms_norm(residual, gain_two))
        gate_act = low_back(project(normed2, gate_w))
        up_act = low_back(project(normed2, up_w))
        hidden = low(jax.nn.silu(gate_act) * up_act)
        result = residual + low_back(project(hidden, down_w))
        return result.reshape(N_DP * SEQ, D)
    primals = (block_input.astype(jnp.float32), norm1_gain.astype(jnp.float32), w_query.astype(jnp.float32), w_key.astype(jnp.float32), w_value.astype(jnp.float32), query_gain.astype(jnp.float32), key_gain.astype(jnp.float32), w_out.astype(jnp.float32), norm2_gain.astype(jnp.float32), w_gate.astype(jnp.float32), w_up.astype(jnp.float32), w_down.astype(jnp.float32))
    block_output, backward = jax.vjp(forward, *primals)
    grads = backward(cotangent.astype(jnp.float32))
    return (block_output, grads[0], grads[1], grads[2], grads[3], grads[4], grads[5], grads[6], grads[7], grads[8], grads[9], grads[10], grads[11])
```

```python
import math

import jax
import jax.numpy as jnp
from jax import lax
from jax.experimental import pallas as pl
from jax.experimental.pallas import tpu as pltpu
from jax.sharding import PartitionSpec as P

HD = 64
AX = ("dp", "tensor")
T4 = 4
VMEM_MB = 1 << 20

epsilon = 1e-05
rope_base = 1000000.0
NEG = -1000000000.0
bf16 = jnp.bfloat16
f32 = jnp.float32


def doc_tables(lengths_row, positions, head_dim):
    doc_ends = jnp.cumsum(lengths_row)
    passed = positions[:, None] >= doc_ends[None, :]
    doc_starts = jnp.sum(jnp.where(passed, lengths_row[None, :], 0), axis=1)
    offsets = (positions - doc_starts).astype(f32)
    freqs = jnp.exp(
        jnp.arange(head_dim // 2, dtype=f32) * (-2.0 * math.log(rope_base) / head_dim)
    )
    angles = offsets[:, None] * freqs[None, :]
    return (doc_starts, jnp.cos(angles), jnp.sin(angles))


def contract(a, b, da, db, precision=None):
    return lax.dot_general(
        a, b, (((da,), (db,)), ((), ())), preferred_element_type=f32, precision=precision
    )


def swap_halves(y):
    width = y.shape[1]
    lane = lax.broadcasted_iota(jnp.int32, y.shape, 1)
    return jnp.where(lane % HD < HD // 2, pltpu.roll(y, width - HD // 2, 1), pltpu.roll(y, HD // 2, 1))


def head_mean(y):
    width = y.shape[1]
    at = lax.broadcasted_iota(jnp.int32, (width, width), 0) // HD
    to = lax.broadcasted_iota(jnp.int32, (width, width), 1) // HD
    ones = jnp.where(at == to, 1.0 / HD, 0.0).astype(f32)
    return contract(y, ones, 1, 0, lax.Precision.HIGHEST)


class Weight:
    def __init__(self, own, parts, to, sems, core, e):
        self.own, self.parts, self.to, self.sems, self.core, self.e = own, parts, to, sems, core, e

    def piece(self, j):
        rows = self.parts[j].shape[0]
        at = pl.multiple_of((self.e ^ j) * rows, rows)
        return pltpu.make_async_copy(self.parts[j], self.to.at[pl.ds(at, rows), :], self.sems.at[j])

    def start(self):
        @pl.when(self.core == 0)
        def _():
            pltpu.make_async_copy(self.own, self.to, self.sems.at[4]).start()

        @pl.when(self.core == 1)
        def _():
            for j in range(4):
                self.piece(j).start()

    def wait(self):
        @pl.when(self.core == 0)
        def _():
            pltpu.make_async_copy(self.own, self.to, self.sems.at[4]).wait()

        @pl.when(self.core == 1)
        def _():
            for j in range(4):
                self.piece(j).wait()


ANY = pl.BlockSpec(memory_space=pl.ANY)


def fixed(*shape):
    return pl.BlockSpec(shape, lambda *_: (0,) * len(shape))


def params(mib):
    return pltpu.CompilerParams(vmem_limit_bytes=mib * VMEM_MB)


def qkv_kernel(s_ref, x0, x1, x2, x3, w_own, w0, w1, w2, w3, g1_ref, gains_ref, cos_ref, sin_ref,
               n1_ref, pre_ref, qk_ref, v_ref, w_ref, xs, xsem, wsem):
    j = pl.program_id(0)
    pieces = (x0, x1, x2, x3)
    weight = Weight(w_own, (w0, w1, w2, w3), w_ref, wsem, s_ref[1], s_ref[2])

    @pl.when(j == 0)
    def _():
        for k in range(4):
            pltpu.make_async_copy(pieces[k], xs.at[k], xsem.at[k]).start()
        weight.start()

    pltpu.make_async_copy(x0, xs.at[j], xsem.at[j]).wait()
    x = xs[j].astype(f32)
    inv = lax.rsqrt(jnp.mean(x * x, axis=-1, keepdims=True) + epsilon)
    n1 = (x * inv * g1_ref[...]).astype(bf16)
    n1_ref[...] = n1

    @pl.when(j == 0)
    def _():
        weight.wait()

    qkv = jnp.dot(n1, w_ref[...], preferred_element_type=f32)
    width = pre_ref.shape[1]
    pre = qkv[:, :width]
    pre_ref[...] = pre
    v_ref[...] = qkv[:, width:].astype(bf16)
    y = pre * lax.rsqrt(head_mean(pre * pre) + epsilon) * gains_ref[...]
    cos = jnp.concatenate([cos_ref[...]] * (width // 128), 1)
    sin = jnp.concatenate([sin_ref[...]] * (width // 128), 1)
    qk = (y * cos + swap_halves(y) * sin).astype(bf16)
    lane = lax.broadcasted_iota(jnp.int32, qk.shape, 1)
    qk_ref[...] = jnp.where(lane < width - 128, qk * 0.125, qk).astype(bf16)


def qkv_call(s, xs, w_own, w_parts, g1, gains, cos, sin):
    b, d = xs[0].shape
    wid = w_own.shape[1]
    qkw = wid - 128
    natural = lambda j, s: (s[0] ^ j, 0)
    return pl.pallas_call(
        qkv_kernel,
        grid_spec=pltpu.PrefetchScalarGridSpec(
            num_scalar_prefetch=1,
            grid=(4,),
            in_specs=[ANY] * 9
            + [fixed(1, d), fixed(1, qkw), pl.BlockSpec((b, 128), natural), pl.BlockSpec((b, 128), natural)],
            out_specs=[
                pl.BlockSpec((b, d), lambda j, s: (j, 0)),
                pl.BlockSpec((b, qkw), natural),
                pl.BlockSpec((b, qkw), natural),
                pl.BlockSpec((b, 128), natural),
                fixed(d, wid),
            ],
            scratch_shapes=[
                pltpu.VMEM((4, b, d), bf16),
                pltpu.SemaphoreType.DMA((4,)),
                pltpu.SemaphoreType.DMA((5,)),
            ],
        ),
        out_shape=[
            jax.ShapeDtypeStruct((4 * b, d), bf16),
            jax.ShapeDtypeStruct((4 * b, qkw), f32),
            jax.ShapeDtypeStruct((4 * b, qkw), bf16),
            jax.ShapeDtypeStruct((4 * b, 128), bf16),
            jax.ShapeDtypeStruct((d, wid), bf16),
        ],
        compiler_params=params(32),
        cost_estimate=pl.CostEstimate(flops=8 * b * d * wid, bytes_accessed=9 * VMEM_MB, transcendentals=0),
        name="qkv",
    )(s, *xs, w_own, *w_parts, g1, gains, cos, sin)


def both_heads(pair):
    lane = lax.broadcasted_iota(jnp.int32, pair.shape, 1)
    zero = jnp.zeros_like(pair)
    return jnp.concatenate([jnp.where(lane < HD, pair, zero), jnp.where(lane < HD, zero, pair)], 0)


def pick_heads(both):
    r = both.shape[0] // 2
    lane = lax.broadcasted_iota(jnp.int32, (r, 128), 1)
    return jnp.where(lane < HD, both[:r], both[r:])


def twice(kv, g):
    lane = lax.broadcasted_iota(jnp.int32, kv.shape, 1)
    turned = pltpu.roll(kv.astype(f32), HD, 1).astype(kv.dtype)
    return jnp.where((lane < HD) == (g == 0), kv, turned)


def attend_kernel(s_ref, q_ref, k_ref, v_ref, start_ref, live_ref, att_ref, out_ref, lse_ref, bias):
    g = pl.program_id(0)
    n = k_ref.shape[0]
    b = n // 4

    @pl.when(g == 0)
    def _():
        for a in range(4):
            keys = (a + 1) * b
            start = start_ref[a * b : (a + 1) * b, :1]
            q_at = lax.broadcasted_iota(jnp.int32, (b, keys), 0) + a * b
            k_at = lax.broadcasted_iota(jnp.int32, (b, keys), 1)
            allowed = ((live_ref[:1, :keys] >= start) & (k_at <= q_at)) | (k_at == q_at)
            bias[a * b : (a + 1) * b, :keys] = jnp.where(allowed, 0.0, NEG)

    kd = twice(k_ref[...], g)
    vd = twice(v_ref[...], g)
    for a in range(4):
        keys = (a + 1) * b
        rows = slice(a * b, (a + 1) * b)
        qm = both_heads(q_ref[rows, :])
        scores = contract(qm, kd[:keys], 1, 1)
        extra = bias[rows, :keys]
        expo = jnp.exp(scores + jnp.concatenate([extra, extra], 0))
        total = jnp.sum(expo, axis=-1, keepdims=True)
        pair = pick_heads(contract(expo.astype(bf16), vd[:keys], 1, 0) / total)
        out_ref[rows, :] = pair
        att_ref[pl.ds(pl.multiple_of((s_ref[0] ^ a) * b, b), b), :] = pair.astype(bf16)
        lse_ref[0, a] = jnp.transpose(jnp.broadcast_to(jnp.log(total), (2 * b, 128)))[:1]


def attend_call(s, qk, v, start, live):
    n = qk.shape[0]
    b = n // 4
    lanes = lambda g, s: (0, g)
    return pl.pallas_call(
        attend_kernel,
        grid_spec=pltpu.PrefetchScalarGridSpec(
            num_scalar_prefetch=1,
            grid=(2,),
            in_specs=[
                pl.BlockSpec((n, 128), lanes),
                pl.BlockSpec((n, 128), lambda g, s: (0, 2)),
                fixed(n, 128),
                fixed(n, 128),
                fixed(8, n),
            ],
            out_specs=[
                pl.BlockSpec((n, 128), lanes),
                pl.BlockSpec((n, 128), lanes),
                pl.BlockSpec((1, 4, 1, 2 * b), lambda g, s: (g, 0, 0, 0)),
            ],
            scratch_shapes=[pltpu.VMEM((n, n), f32)],
        ),
        out_shape=[
            jax.ShapeDtypeStruct((n, 256), bf16),
            jax.ShapeDtypeStruct((n, 256), f32),
            jax.ShapeDtypeStruct((2, 4, 1, 2 * b), f32),
        ],
        compiler_params=params(40),
        cost_estimate=pl.CostEstimate(
            flops=16 * n * n * HD, bytes_accessed=4 * VMEM_MB, transcendentals=4 * n * n
        ),
        name="attend",
    )(s, qk, qk, v, start, live)


def norm_back(grad, pre, gain, cos, sin):
    turned = grad * cos - swap_halves(grad) * sin
    inv = lax.rsqrt(head_mean(pre * pre) + epsilon)
    scaled = turned * gain
    dpre = inv * scaled - pre * (inv * inv * inv) * head_mean(scaled * pre)
    return dpre, jnp.sum(turned * pre * inv, axis=0, keepdims=True)


def attend_back_kernel(s_ref, q_ref, k_ref, v_ref, qpre_ref, kpre_ref, gains_ref, kgain_ref, cos_ref, sin_ref,
                       start_ref, live_ref, out_ref, lse_ref, wout_ref, w_ref, b0, b1, b2, b3,
                       low_ref, gain_ref, lo_ref, hi_ref, bias, dk, dv, dkall, dvall, dos, gb, sems):
    g = pl.program_id(0)
    n = k_ref.shape[0]
    b = n // 4
    pieces = (b0, b1, b2, b3)

    @pl.when(g == 0)
    def _():
        for k in range(4):
            pltpu.make_async_copy(pieces[k], gb.at[k], sems.at[k]).start()
        for a in range(4):
            keys = (a + 1) * b
            start = start_ref[:1, a * b : (a + 1) * b]
            k_at = lax.broadcasted_iota(jnp.int32, (keys, b), 0)
            q_at = lax.broadcasted_iota(jnp.int32, (keys, b), 1) + a * b
            allowed = ((live_ref[:keys, :1] >= start) & (k_at <= q_at)) | (k_at == q_at)
            bias[:keys, a * b : (a + 1) * b] = jnp.where(allowed, 0.0, NEG)
        for k in range(4):
            pltpu.make_async_copy(pieces[k], gb.at[k], sems.at[k]).wait()
            dos[k] = contract(gb[k], wout_ref[...], 1, 1).astype(bf16)

    kd = twice(k_ref[...], g)
    vd = twice(v_ref[...], g)
    gain_sum = jnp.zeros((1, 128), f32)
    ones = jnp.ones((8, 128), f32)
    for a in (3, 2, 1, 0):
        keys = (a + 1) * b
        rows = slice(a * b, (a + 1) * b)
        home = s_ref[0] ^ a
        qm = both_heads(q_ref[rows, :])
        dout = jnp.where(g == 0, dos[home, :, :128], dos[home, :, 128:])
        dom = both_heads(dout)
        delta = contract(ones, both_heads(dout.astype(f32) * out_ref[rows, :]), 1, 1, lax.Precision.HIGHEST)[:1]
        scores = contract(kd[:keys], qm, 1, 1)
        extra = bias[:keys, rows]
        probs = jnp.exp(scores + (jnp.concatenate([extra, extra], 1) - lse_ref[0, a]))
        dprobs = contract(vd[:keys], dom, 1, 1)
        dscores = (probs * (dprobs - delta)).astype(bf16)
        dv_add = contract(probs.astype(bf16), dom, 1, 0)
        dk_add = contract(dscores, qm, 1, 0)
        if a == 3:
            dv[...] = dv_add
            dk[...] = dk_add
        else:
            dv[:keys] += dv_add
            dk[:keys] += dk_add
        dq = pick_heads(contract(dscores, kd[:keys], 0, 0)) * 0.125
        dpre, gain_part = norm_back(dq, qpre_ref[rows, :], gains_ref[...], cos_ref[rows, :], sin_ref[rows, :])
        at = pl.ds(pl.multiple_of(home * b, b), b)
        low_ref[at, pl.ds(pl.multiple_of(g * 128, 128), 128)] = dpre.astype(bf16)
        gain_sum = gain_sum + gain_part
    gain_ref[pl.ds(g, 1), :] = gain_sum
    lane = lax.broadcasted_iota(jnp.int32, (n, 128), 1)
    dk_all = dk[...] + pltpu.roll(dk[...], HD, 1)
    dv_all = dv[...] + pltpu.roll(dv[...], HD, 1)

    @pl.when(g == 0)
    def _():
        dkall[...] = dk_all
        dvall[...] = dv_all

    @pl.when(g == 1)
    def _():
        grad_k = jnp.where(lane < HD, dkall[...], dk_all)
        grad_v = jnp.where(lane < HD, dvall[...], dv_all)
        dpre, gain_part = norm_back(grad_k, kpre_ref[...], kgain_ref[...], cos_ref[...], sin_ref[...])
        gain_ref[2:3, :] = gain_part
        for a in range(4):
            at = pl.ds(pl.multiple_of((s_ref[0] ^ a) * b, b), b)
            low_ref[at, 256:384] = dpre[a * b : (a + 1) * b].astype(bf16)
            low_ref[at, 384:512] = grad_v[a * b : (a + 1) * b].astype(bf16)
        hi_ref[...] = contract(low_ref[2 * b :, :], w_ref[...], 1, 1).astype(bf16)
        lo_ref[...] = contract(low_ref[: 2 * b, :], w_ref[...], 1, 1).astype(bf16)


def attend_back_call(s, qk, v, pre, qgain, kgain, cos, sin, start, live, out, lse, wout, w, blocks):
    n = v.shape[0]
    b = n // 4
    d = blocks[0].shape[1]
    lanes = pl.BlockSpec((n, 128), lambda g, s: (0, g))
    third = pl.BlockSpec((n, 128), lambda g, s: (0, 2))
    return pl.pallas_call(
        attend_back_kernel,
        grid_spec=pltpu.PrefetchScalarGridSpec(
            num_scalar_prefetch=1,
            grid=(2,),
            in_specs=[lanes, third, fixed(n, 128), lanes, third, fixed(1, 128), fixed(1, 128), fixed(n, 128),
                      fixed(n, 128), fixed(8, n), fixed(n, 128), lanes,
                      pl.BlockSpec((1, 4, 1, 2 * b), lambda g, s: (g, 0, 0, 0)),
                      fixed(256, d), fixed(d, 512)] + [ANY] * 4,
            out_specs=[fixed(n, 512), fixed(8, 128), fixed(2 * b, d), fixed(2 * b, d)],
            scratch_shapes=[pltpu.VMEM((n, n), f32)]
            + [pltpu.VMEM((n, 128), f32)] * 4
            + [pltpu.VMEM((4, b, 256), bf16), pltpu.VMEM((4, b, d), bf16), pltpu.SemaphoreType.DMA((4,))],
        ),
        out_shape=[
            jax.ShapeDtypeStruct((n, 512), bf16),
            jax.ShapeDtypeStruct((8, 128), f32),
            jax.ShapeDtypeStruct((2 * b, d), bf16),
            jax.ShapeDtypeStruct((2 * b, d), bf16),
        ],
        compiler_params=params(52),
        cost_estimate=pl.CostEstimate(
            flops=40 * n * n * HD + 2 * n * d * 768, bytes_accessed=10 * VMEM_MB, transcendentals=4 * n * n
        ),
        name="attend_back",
    )(s, qk, qk, v, pre, pre, qgain, kgain, cos, sin, start, live, out, lse, wout, w, *blocks)


def ffn_kernel(s_ref, x0, x1, x2, x3, a0, a1, a2, a3, o0, o1, o2, o3, wg_own, g0, g1, g2, g3, wu_own, u0, u1, u2, u3,
               gain_ref, n2_ref, hid_ref, fg_ref, fu_ref, res_ref, wg, wu, xs, att, wout, asem, xsem, osem, gsem, usem):
    j = pl.program_id(0)
    b = x0.shape[0]
    x_in, a_in, o_in = (x0, x1, x2, x3), (a0, a1, a2, a3), (o0, o1, o2, o3)
    gate_w = Weight(wg_own, (g0, g1, g2, g3), wg, gsem, s_ref[1], s_ref[2])
    up_w = Weight(wu_own, (u0, u1, u2, u3), wu, usem, s_ref[1], s_ref[2])

    def out_copy(i):
        return pltpu.make_async_copy(o_in[i], wout.at[pl.ds(i * b, b), :], osem.at[i])

    def att_copy(k, i):
        return pltpu.make_async_copy(
            a_in[i].at[pl.ds((k ^ i) * b, b), :], att.at[k, :, pl.ds(i * b, b)], asem.at[k, i]
        )

    @pl.when(j == 0)
    def _():
        for k in range(4):
            pltpu.make_async_copy(x_in[k], xs.at[k], xsem.at[k]).start()
            for i in range(4):
                att_copy(k, i).start()
            if k == 0:
                for i in range(4):
                    out_copy(i).start()
                gate_w.start()
        up_w.start()
        for i in range(4):
            out_copy(i).wait()

    pltpu.make_async_copy(x0, xs.at[j], xsem.at[j]).wait()
    for i in range(4):
        pltpu.make_async_copy(a_in[i].at[pl.ds(0, b), :], att.at[j, :, pl.ds(i * b, b)], asem.at[j, i]).wait()
    res = xs[j].astype(f32) + jnp.dot(att[j], wout[...], preferred_element_type=f32)

    @pl.when(j == 0)
    def _():
        res_ref[...] = res
        gate_w.wait()
        up_w.wait()

    inv = lax.rsqrt(jnp.mean(res * res, axis=-1, keepdims=True) + epsilon)
    n2 = (res * inv * gain_ref[...]).astype(bf16)
    n2_ref[...] = n2
    gate = jnp.dot(n2, wg[...], preferred_element_type=f32)
    up = jnp.dot(n2, wu[...], preferred_element_type=f32)
    s = jax.nn.sigmoid(gate)
    silu = gate * s
    hid_ref[...] = (silu * up).astype(bf16)
    fg_ref[...] = (up * (s * (1.0 + gate * (1.0 - s)))).astype(bf16)
    fu_ref[...] = silu.astype(bf16)


def ffn_call(s, xs, atts, wouts, wg, g_parts, wu, u_parts, gain):
    b, d = xs[0].shape
    h = wg.shape[1]
    block = lambda wid: pl.BlockSpec((b, wid), lambda j, s: (j, 0))
    return pl.pallas_call(
        ffn_kernel,
        grid_spec=pltpu.PrefetchScalarGridSpec(
            num_scalar_prefetch=1,
            grid=(4,),
            in_specs=[ANY] * 22 + [fixed(1, d)],
            out_specs=[block(d), block(h), block(h), block(h), fixed(b, d), fixed(d, h), fixed(d, h)],
            scratch_shapes=[
                pltpu.VMEM((4, b, d), bf16),
                pltpu.VMEM((4, b, 4 * b), bf16),
                pltpu.VMEM((4 * b, d), bf16),
                pltpu.SemaphoreType.DMA((4, 4)),
                pltpu.SemaphoreType.DMA((4,)),
                pltpu.SemaphoreType.DMA((4,)),
                pltpu.SemaphoreType.DMA((5,)),
                pltpu.SemaphoreType.DMA((5,)),
            ],
        ),
        out_shape=[jax.ShapeDtypeStruct((4 * b, d), bf16)]
        + [jax.ShapeDtypeStruct((4 * b, h), bf16)] * 3
        + [jax.ShapeDtypeStruct((b, d), f32)]
        + [jax.ShapeDtypeStruct((d, h), bf16)] * 2,
        compiler_params=params(48),
        cost_estimate=pl.CostEstimate(
            flops=8 * b * d * (d + 2 * h), bytes_accessed=25 * VMEM_MB, transcendentals=4 * b * h
        ),
        name="ffn",
    )(s, *xs, *atts, *wouts, wg, *g_parts, wu, *u_parts, gain)


def ffn_back_kernel(s_ref, y0, y1, y2, y3, wd_own, d0, d1, d2, d3, fg_ref, fu_ref, wg_in, wu_in,
                    gg_ref, gu_ref, lo_ref, hi_ref, wd, dy, wg, wu, ysem, dsem, wsem):
    j = pl.program_id(0)
    y_in = (y0, y1, y2, y3)
    down_w = Weight(wd_own, (d0, d1, d2, d3), wd, dsem, s_ref[1], s_ref[2])

    @pl.when(j == 0)
    def _():
        for k in range(4):
            pltpu.make_async_copy(y_in[k], dy.at[k], ysem.at[k]).start()
        down_w.start()
        pltpu.make_async_copy(wg_in, wg, wsem.at[0]).start()
        pltpu.make_async_copy(wu_in, wu, wsem.at[1]).start()
        down_w.wait()

    pltpu.make_async_copy(y0, dy.at[j], ysem.at[j]).wait()
    gh = contract(dy[j], wd[...], 1, 1)
    gg = (gh * fg_ref[...].astype(f32)).astype(bf16)
    gu = (gh * fu_ref[...].astype(f32)).astype(bf16)
    gg_ref[...] = gg
    gu_ref[...] = gu

    @pl.when(j == 0)
    def _():
        pltpu.make_async_copy(wg_in, wg, wsem.at[0]).wait()
        pltpu.make_async_copy(wu_in, wu, wsem.at[1]).wait()

    grad = (contract(gg, wg[...], 1, 1) + contract(gu, wu[...], 1, 1)).astype(bf16)

    @pl.when(j < 2)
    def _():
        lo_ref[...] = grad

    @pl.when(j >= 2)
    def _():
        hi_ref[...] = grad


def ffn_back_call(s, dys, wd, d_parts, fg, fu, wg, wu):
    b, d = dys[0].shape
    h = wg.shape[1]
    block = lambda wid: pl.BlockSpec((b, wid), lambda j, s: (j, 0))
    return pl.pallas_call(
        ffn_back_kernel,
        grid_spec=pltpu.PrefetchScalarGridSpec(
            num_scalar_prefetch=1,
            grid=(4,),
            in_specs=[ANY] * 9 + [block(h), block(h), ANY, ANY],
            out_specs=[
                block(h),
                block(h),
                pl.BlockSpec((b, d), lambda j, s: (jnp.minimum(j, 1), 0)),
                pl.BlockSpec((b, d), lambda j, s: (jnp.maximum(j - 2, 0), 0)),
                fixed(h, d),
            ],
            scratch_shapes=[
                pltpu.VMEM((4, b, d), bf16),
                pltpu.VMEM((d, h), bf16),
                pltpu.VMEM((d, h), bf16),
                pltpu.SemaphoreType.DMA((4,)),
                pltpu.SemaphoreType.DMA((5,)),
                pltpu.SemaphoreType.DMA((2,)),
            ],
        ),
        out_shape=[jax.ShapeDtypeStruct((4 * b, h), bf16)] * 2
        + [jax.ShapeDtypeStruct((2 * b, d), bf16)] * 2
        + [jax.ShapeDtypeStruct((h, d), bf16)],
        compiler_params=params(48),
        cost_estimate=pl.CostEstimate(flops=24 * b * d * h, bytes_accessed=22 * VMEM_MB, transcendentals=0),
        name="ffn_back",
    )(s, *dys, wd, *d_parts, fg, fu, wg, wu)


def store_pieces(j, first, second, sent_a, keep_a, sent_b, keep_b):
    @pl.when(j % 2 == 1)
    def _():
        sent_a[0] = first

    @pl.when(j % 2 == 0)
    def _():
        keep_a[0] = first

    @pl.when(j >= 2)
    def _():
        sent_b[0] = second

    @pl.when(j < 2)
    def _():
        keep_b[0] = second


def piece_outputs(rows, cols):
    maps = [
        lambda j, s: (j // 2, 0, 0),
        lambda j, s: (j // 2, 0, 0),
        lambda j, s: (jnp.maximum(j - 2, 0), 0, 0),
        lambda j, s: (jnp.minimum(j, 1), 0, 0),
    ]
    return dict(
        out_specs=[pl.BlockSpec((1, rows, cols), m) for m in maps],
        out_shape=[jax.ShapeDtypeStruct((2, rows, cols), bf16)] * 4,
    )


def grad_rows_kernel(s_ref, left_ref, a_ref, b_ref, *outs):
    left = left_ref[...]
    first = contract(left, a_ref[...], 0, 0).astype(bf16)
    second = contract(left, b_ref[...], 0, 0).astype(bf16)
    store_pieces(pl.program_id(0), first, second, *outs)


def grad_rows_call(s, left, a, b, a_at, b_at, width, name):
    n, rows = left.shape
    out = piece_outputs(rows // 4, width)
    return pl.pallas_call(
        grad_rows_kernel,
        grid_spec=pltpu.PrefetchScalarGridSpec(
            num_scalar_prefetch=1,
            grid=(4,),
            in_specs=[
                pl.BlockSpec((n, rows // 4), lambda j, s: (0, s[2] ^ j)),
                pl.BlockSpec((n, width), lambda j, s: (0, a_at)),
                pl.BlockSpec((n, width), lambda j, s: (0, b_at)),
            ],
            out_specs=out["out_specs"],
        ),
        out_shape=out["out_shape"],
        compiler_params=params(40),
        cost_estimate=pl.CostEstimate(flops=4 * n * rows * width, bytes_accessed=4 * n * (rows + 2 * width), transcendentals=0),
        name=name,
    )(s, left, a, b)


def grad_cols_kernel(s_ref, left_ref, right_ref, *outs):
    grad = contract(left_ref[...], right_ref[...], 0, 0).astype(bf16)
    half = grad.shape[0] // 2
    store_pieces(pl.program_id(0), grad[:half], grad[half:], *outs)


def grad_cols_call(s, left, right, name):
    n, rows = left.shape
    cols = right.shape[1] // 4
    out = piece_outputs(rows // 2, cols)
    return pl.pallas_call(
        grad_cols_kernel,
        grid_spec=pltpu.PrefetchScalarGridSpec(
            num_scalar_prefetch=1,
            grid=(4,),
            in_specs=[fixed(n, rows), pl.BlockSpec((n, cols), lambda j, s: (0, s[2] ^ j))],
            out_specs=out["out_specs"],
        ),
        out_shape=out["out_shape"],
        compiler_params=params(40),
        cost_estimate=pl.CostEstimate(flops=8 * n * rows * cols, bytes_accessed=4 * n * (rows + 4 * cols), transcendentals=0),
        name=name,
    )(s, left, right)


def permute(x, places, move):
    pairs = []
    for d in range(places):
        for t in range(T4):
            to = move(d, t)
            if to is not None:
                pairs.append((d * T4 + t, to[0] * T4 + to[1]))
    return lax.ppermute(x, AX, pairs)


def after(x, *events):
    return lax.optimization_barrier((x,) + events)[0]


def flip_core(d, t):
    return (d ^ 1, t)


def flip_z(d, t):
    return (d, t ^ 1)


def flip_e(bit):
    return lambda d, t: (d ^ (2 << bit), t)


def settle(d, t):
    return (d, t) if (d & 1) == (t >> 1) else (d ^ 1, t ^ 2)


def gather_row(x, n):
    over = permute(x, n, flip_z)
    near = permute(x, n, flip_core)
    far = permute(over, n, flip_core)
    return [x, over, near, far]


def scatter_row(low, high, n):
    b = low.shape[0] // 2
    got = permute(high, n, flip_core)
    return low[:b] + got[:b] + permute(low[b:] + got[b:], n, flip_z)


def hop(w, n, e):
    rows = w.shape[0] // 4
    mine = lax.dynamic_slice_in_dim(w, e * rows, rows, 0)
    return permute(mine, n, lambda d, t: (d, t ^ 2) if d & 1 else None)


def spread(piece, n, order):
    def only_one(bit):
        return lambda d, t: (d ^ (2 << bit), t) if d & 1 else None

    held = {0: piece}
    for bit in order:
        for k in sorted(held):
            held[k | (1 << bit)] = permute(held[k], n, only_one(bit))
    return [held[k] for k in range(4)]


def assemble(own, parts, c, e):
    rows = parts[0].shape[0]
    whole = own
    for j in range(4):
        whole = lax.dynamic_update_slice_in_dim(whole, parts[j], (e ^ j) * rows, 0)
    return jnp.where(c == 0, own, whole)


def first_sum(sent, keep, n, bit, event=None):
    got = permute(sent, n, flip_e(bit))
    if event is not None:
        got = after(got, event)
    return keep[1] + got[1], keep[0] + got[0]


def second_sum(sent, keep, n, bit, event=None):
    got = permute(sent, n, flip_e(bit))
    if event is not None:
        got = after(got, event)
    total = keep + got
    for extra in range(2, 20):
        if (2 << extra) < n:
            total = total + permute(total, n, flip_e(extra))
    return total


def owner_sum(total_a, total_b, n, c, event=None):
    total = jnp.stack([total_a, total_b])
    half = total.shape[1] // 2
    first, second = total[:, :half], total[:, half:]
    one = permute(
        jnp.where(c == 0, second, first), n, lambda d, t: (d ^ 1, t ^ 2) if d & 1 else (d ^ 1, t)
    )
    two = permute(second, n, lambda d, t: (d, t ^ 2) if d & 1 else None)
    if event is not None:
        one, two = after(one, event), after(two, event)
    return jnp.where(c == 0, first, two) + one


def whole_grad(mine, n):
    groups = None if n == 8 else [list(range(k, k + 8)) for k in range(0, n, 8)]
    got = lax.all_gather(mine, "dp", axis_index_groups=groups)
    return got.reshape((4, 2) + mine.shape)


def sum_all(vec, n):
    bit = 1
    while bit < n:
        vec = vec + permute(vec, n, lambda d, t, bit=bit: (d ^ bit, t))
        bit *= 2
    for bit in (1, 2):
        vec = vec + permute(vec, n, lambda d, t, bit=bit: (d, t ^ bit))
    return vec


def local(
    block_input,
    doc_lengths,
    pad_mask,
    norm1_gain,
    w_query,
    w_key,
    w_value,
    query_gain,
    key_gain,
    w_out,
    norm2_gain,
    w_gate,
    w_up,
    w_down,
    cotangent,
):
    n = lax.axis_size("dp")
    d, t = lax.axis_index("dp"), lax.axis_index("tensor")
    c, p = d & 1, t >> 1
    e = (d >> 1) & 3
    shard = 2 * c + (t & 1)
    b = block_input.shape[0]
    seq_len = b * T4
    home = c == p
    wq = w_query.shape[1]
    wk = w_key.shape[1]
    width = block_input.shape[1]
    s = jnp.stack([shard, c, e]).astype(jnp.int32)

    x_own = permute(block_input, n, settle)
    marks = jnp.concatenate([doc_lengths, pad_mask], 1)
    marks = jnp.where(home, marks, permute(marks, n, flip_core))
    lengths_row, pad_row = marks[0, : doc_lengths.shape[1]], marks[0, doc_lengths.shape[1] :]
    w_qkv_own = jnp.concatenate([w_query, w_key, w_value], 1)
    qkv_hop = hop(w_qkv_own, n, e)
    x_blocks = gather_row(x_own, n)
    qkv_parts = spread(qkv_hop, n, (0, 1))
    out_hop = hop(after(w_out, x_own), n, e)
    gate_hop = hop(after(w_gate, x_own), n, e)
    up_hop = hop(after(w_up, qkv_hop, out_hop), n, e)
    dy_own = permute(after(cotangent, gate_hop), n, settle)
    down_hop = hop(after(w_down, up_hop), n, e)

    positions = jnp.arange(seq_len, dtype=jnp.int32)
    doc_starts, cos_half, sin_half = doc_tables(lengths_row, positions, HD)
    cos = jnp.concatenate([cos_half] * 4, 1)
    sin = jnp.concatenate([-sin_half, sin_half] * 2, 1)
    live = jnp.where(pad_row == 1, positions, -1)
    start_col = jnp.broadcast_to(doc_starts[:, None], (seq_len, 128))
    start_row = jnp.broadcast_to(doc_starts[None], (8, seq_len))
    live_col = jnp.broadcast_to(live[:, None], (seq_len, 128))
    live_row = jnp.broadcast_to(live[None], (8, seq_len))
    gains = jnp.concatenate([query_gain] * (wq // HD) + [key_gain] * (wk // HD))[None]
    qgain_pair = jnp.concatenate([query_gain] * 2)[None]
    kgain_pair = jnp.concatenate([key_gain] * 2)[None]

    rows_one, pre, qk, values, w_qkv = qkv_call(
        s, x_blocks, w_qkv_own, qkv_parts, norm1_gain[None], gains, cos, sin
    )
    out_parts = spread(after(out_hop, x_blocks[3]), n, (1, 0))
    gate_parts = spread(after(gate_hop, x_blocks[3]), n, (0, 1))
    w_out_own = assemble(w_out, out_parts, c, e)
    attended, attended_f, lse = attend_call(s, qk, values, start_col, live_row)
    w_out_pieces = gather_row(w_out_own, n)
    att_pieces = gather_row(attended, n)
    up_parts = spread(after(up_hop, attended), n, (1, 0))
    rows_two, hidden, by_gate, by_up, residual, wg, wu = ffn_call(
        s, x_blocks, att_pieces, w_out_pieces, w_gate, gate_parts, w_up, up_parts, norm2_gain[None]
    )
    dy_blocks = gather_row(after(dy_own, att_pieces[1]), n)
    down_parts = spread(after(down_hop, att_pieces[1]), n, (0, 1))

    dy = jnp.concatenate(dy_blocks, 0)
    down_pieces = grad_cols_call(s, hidden, dy, "grad_down")
    gate_grad, up_grad, low2, high2, wd = ffn_back_call(s, dy_blocks, w_down, down_parts, by_gate, by_up, wg, wu)
    grad_n2 = scatter_row(low2, high2, n).astype(f32)
    gate_pieces = grad_rows_call(s, rows_two, gate_grad, up_grad, 0, 0, gate_grad.shape[1], "grad_gate_up")
    inv = lax.rsqrt(jnp.mean(residual * residual, axis=-1, keepdims=True) + epsilon)
    scaled = norm2_gain * grad_n2
    grad_residual = (
        dy_own.astype(f32)
        + inv * scaled
        - residual * (inv * inv * inv) * jnp.mean(scaled * residual, axis=-1, keepdims=True)
    )
    grad_norm2 = jnp.sum(grad_n2 * residual * inv, axis=0)
    gb_blocks = gather_row(grad_residual.astype(bf16), n)

    down_a = first_sum(down_pieces[0], down_pieces[1], n, 0, grad_residual)
    down_b = first_sum(down_pieces[2], down_pieces[3], n, 1, grad_residual)
    down_a = second_sum(*down_a, n, 1, gb_blocks[3])
    down_b = second_sum(*down_b, n, 0, gb_blocks[3])
    gate_a = first_sum(gate_pieces[0], gate_pieces[1], n, 0, gb_blocks[3])
    gate_b = first_sum(gate_pieces[2], gate_pieces[3], n, 1, gb_blocks[3])

    low, gain_terms, low1, high1 = attend_back_call(
        s, qk, values, pre, qgain_pair, kgain_pair, cos, sin, start_row, live_col, attended_f, lse, w_out_own, w_qkv,
        gb_blocks,
    )
    gate_a = second_sum(*gate_a, n, 1, low)
    gate_b = second_sum(*gate_b, n, 0, low)
    down_mine = owner_sum(down_a, down_b, n, c, low)
    gate_mine = owner_sum(gate_a, gate_b, n, c)

    grad_n1 = scatter_row(low1, high1, n).astype(f32)
    qkv_pieces = grad_rows_call(s, rows_one, low, low, 0, 1, 256, "grad_qkv")
    gb = jnp.concatenate(gb_blocks, 0)
    out_pieces = grad_cols_call(s, attended, gb, "grad_out")
    x_f = x_own.astype(f32)
    inv = lax.rsqrt(jnp.mean(x_f * x_f, axis=-1, keepdims=True) + epsilon)
    scaled = norm1_gain * grad_n1
    input_grad = (
        grad_residual
        + inv * scaled
        - x_f * (inv * inv * inv) * jnp.mean(scaled * x_f, axis=-1, keepdims=True)
    )
    grad_norm1 = jnp.sum(grad_n1 * x_f * inv, axis=0)
    input_grad = jnp.where(home, input_grad, permute(input_grad.astype(bf16), n, settle).astype(f32))

    ffn_part = jnp.dot(hidden, wd, preferred_element_type=f32).astype(bf16)
    ffn_branch = scatter_row(ffn_part[: 2 * b], ffn_part[2 * b :], n)
    block_output = residual + ffn_branch.astype(f32)
    block_output = jnp.where(home, block_output, permute(block_output.astype(bf16), n, settle).astype(f32))

    def sums(pieces):
        first = first_sum(pieces[0], pieces[1], n, 0)
        second = first_sum(pieces[2], pieces[3], n, 1)
        return owner_sum(second_sum(*first, n, 1), second_sum(*second, n, 0), n, c)

    def from_rows(whole):
        return [whole[:, :, k].astype(f32).reshape(width, -1) for k in range(2)]

    def from_cols(whole):
        return whole.astype(f32).transpose(2, 1, 3, 0, 4).reshape(-1, width)

    grad_down = from_cols(whole_grad(down_mine, n))
    grad_gate, grad_up = from_rows(whole_grad(gate_mine, n))
    grad_out = from_cols(whole_grad(sums(out_pieces), n))
    grad_query, grad_kv = from_rows(whole_grad(sums(qkv_pieces), n))
    head_terms = gain_terms[:, :HD] + gain_terms[:, HD:]
    vec = jnp.concatenate([grad_norm1, grad_norm2, head_terms[0] + head_terms[1], head_terms[2]])
    vec = sum_all(vec[None], n)[0]
    return (
        block_output,
        input_grad,
        vec[:width],
        grad_query,
        grad_kv[:, :wk],
        grad_kv[:, wk:],
        vec[2 * width : 2 * width + HD],
        vec[2 * width + HD :],
        grad_out,
        vec[width : 2 * width],
        grad_gate,
        grad_up,
        grad_down,
    )


def solution(mesh):
    placed = (
        P(("dp", "tensor"), None),
        P("dp", None),
        P("dp", None),
        P(),
        P(None, "tensor"),
        P(None, "tensor"),
        P(None, "tensor"),
        P(),
        P(),
        P("tensor", None),
        P(),
        P(None, "tensor"),
        P(None, "tensor"),
        P("tensor", None),
        P(("dp", "tensor"), None),
    )
    return jax.shard_map(
        local,
        mesh=mesh,
        in_specs=placed,
        out_specs=(
            P(("dp", "tensor"), None),
            P(("dp", "tensor"), None),
            P(),
            P(None, "tensor"),
            P(None, "tensor"),
            P(None, "tensor"),
            P(),
            P(),
            P("tensor", None),
            P(),
            P(None, "tensor"),
            P(None, "tensor"),
            P("tensor", None),
        ),
        check_vma=False,
    )
```

```python
import math

import jax
import jax.numpy as jnp
from jax import lax
from jax.experimental import pallas as pl
from jax.experimental.pallas import tpu as pltpu
from jax.sharding import PartitionSpec as P

HD = 64
AX = ("dp", "tensor")
T4 = 4
VMEM_MB = 1 << 20

epsilon = 1e-05
rope_base = 1000000.0
NEG = -1000000000.0
bf16 = jnp.bfloat16
f32 = jnp.float32


def doc_tables(lengths_row, positions, head_dim):
    doc_ends = jnp.cumsum(lengths_row)
    passed = positions[:, None] >= doc_ends[None, :]
    doc_starts = jnp.sum(jnp.where(passed, lengths_row[None, :], 0), axis=1)
    offsets = (positions - doc_starts).astype(f32)
    freqs = jnp.exp(
        jnp.arange(head_dim // 2, dtype=f32) * (-2.0 * math.log(rope_base) / head_dim)
    )
    angles = offsets[:, None] * freqs[None, :]
    return (doc_starts, jnp.cos(angles), jnp.sin(angles))


def contract(a, b, da, db, precision=None):
    return lax.dot_general(
        a, b, (((da,), (db,)), ((), ())), preferred_element_type=f32, precision=precision
    )


def swap_halves(y):
    width = y.shape[1]
    lane = lax.broadcasted_iota(jnp.int32, y.shape, 1)
    return jnp.where(lane % HD < HD // 2, pltpu.roll(y, width - HD // 2, 1), pltpu.roll(y, HD // 2, 1))


def head_mean(y):
    width = y.shape[1]
    at = lax.broadcasted_iota(jnp.int32, (width, width), 0) // HD
    to = lax.broadcasted_iota(jnp.int32, (width, width), 1) // HD
    ones = jnp.where(at == to, 1.0 / HD, 0.0).astype(f32)
    return contract(y, ones, 1, 0, lax.Precision.HIGHEST)


class Weight:
    def __init__(self, own, parts, to, sems, core, e):
        self.own, self.parts, self.to, self.sems, self.core, self.e = own, parts, to, sems, core, e

    def side(self, i):
        if len(self.own) == 1:
            return pltpu.make_async_copy(self.own[0], self.to, self.sems.at[4])
        start = sum(w.shape[1] for w in self.own[:i])
        return pltpu.make_async_copy(
            self.own[i], self.to.at[:, pl.ds(start, self.own[i].shape[1])], self.sems.at[4 + i]
        )

    def piece(self, j):
        rows = self.parts[j].shape[0]
        at = pl.multiple_of((self.e ^ j) * rows, rows)
        return pltpu.make_async_copy(self.parts[j], self.to.at[pl.ds(at, rows), :], self.sems.at[j])

    def start(self):
        @pl.when(self.core == 0)
        def _():
            for i in range(len(self.own)):
                self.side(i).start()

        @pl.when(self.core == 1)
        def _():
            for j in range(4):
                self.piece(j).start()

    def wait(self):
        @pl.when(self.core == 0)
        def _():
            for i in range(len(self.own)):
                self.side(i).wait()

        @pl.when(self.core == 1)
        def _():
            for j in range(4):
                self.piece(j).wait()


ANY = pl.BlockSpec(memory_space=pl.ANY)


def fixed(*shape):
    return pl.BlockSpec(shape, lambda *_: (0,) * len(shape))


def params(mib):
    return pltpu.CompilerParams(vmem_limit_bytes=mib * VMEM_MB)


def qkv_kernel(s_ref, x0, x1, x2, x3, wq_own, wk_own, wv_own, w0, w1, w2, w3, g1_ref, gains_ref, cos_ref, sin_ref,
               n1_ref, pre_ref, qk_ref, v_ref, w_ref, xs, xsem, wsem):
    j = pl.program_id(0)
    pieces = (x0, x1, x2, x3)
    weight = Weight((wq_own, wk_own, wv_own), (w0, w1, w2, w3), w_ref, wsem, s_ref[1], s_ref[2])

    @pl.when(j == 0)
    def _():
        for k in range(4):
            pltpu.make_async_copy(pieces[k], xs.at[k], xsem.at[k]).start()
        weight.start()

    pltpu.make_async_copy(x0, xs.at[j], xsem.at[j]).wait()
    x = xs[j].astype(f32)
    inv = lax.rsqrt(jnp.mean(x * x, axis=-1, keepdims=True) + epsilon)
    n1 = (x * inv * g1_ref[...]).astype(bf16)
    n1_ref[...] = n1

    @pl.when(j == 0)
    def _():
        weight.wait()

    qkv = jnp.dot(n1, w_ref[...], preferred_element_type=f32)
    width = pre_ref.shape[1]
    pre = qkv[:, :width]
    pre_ref[...] = pre
    v_ref[...] = qkv[:, width:].astype(bf16)
    y = pre * lax.rsqrt(head_mean(pre * pre) + epsilon) * gains_ref[...]
    cos = jnp.concatenate([cos_ref[...]] * (width // 128), 1)
    sin = jnp.concatenate([sin_ref[...]] * (width // 128), 1)
    qk = (y * cos + swap_halves(y) * sin).astype(bf16)
    lane = lax.broadcasted_iota(jnp.int32, qk.shape, 1)
    qk_ref[...] = jnp.where(lane < width - 128, qk * 0.125, qk).astype(bf16)


def qkv_call(s, xs, w_own, w_parts, g1, gains, cos, sin):
    b, d = xs[0].shape
    wid = w_parts[0].shape[1]
    qkw = wid - 128
    natural = lambda j, s: (s[0] ^ j, 0)
    return pl.pallas_call(
        qkv_kernel,
        grid_spec=pltpu.PrefetchScalarGridSpec(
            num_scalar_prefetch=1,
            grid=(4,),
            in_specs=[ANY] * 11
            + [fixed(1, d), fixed(1, qkw), pl.BlockSpec((b, 128), natural), pl.BlockSpec((b, 128), natural)],
            out_specs=[
                pl.BlockSpec((b, d), lambda j, s: (j, 0)),
                pl.BlockSpec((b, qkw), natural),
                pl.BlockSpec((b, qkw), natural),
                pl.BlockSpec((b, 128), natural),
                fixed(d, wid),
            ],
            scratch_shapes=[
                pltpu.VMEM((4, b, d), bf16),
                pltpu.SemaphoreType.DMA((4,)),
                pltpu.SemaphoreType.DMA((7,)),
            ],
        ),
        out_shape=[
            jax.ShapeDtypeStruct((4 * b, d), bf16),
            jax.ShapeDtypeStruct((4 * b, qkw), f32),
            jax.ShapeDtypeStruct((4 * b, qkw), bf16),
            jax.ShapeDtypeStruct((4 * b, 128), bf16),
            jax.ShapeDtypeStruct((d, wid), bf16),
        ],
        compiler_params=params(32),
        cost_estimate=pl.CostEstimate(flops=8 * b * d * wid, bytes_accessed=9 * VMEM_MB, transcendentals=0),
        name="qkv",
    )(s, *xs, *w_own, *w_parts, g1, gains, cos, sin)


def both_heads(pair):
    lane = lax.broadcasted_iota(jnp.int32, pair.shape, 1)
    zero = jnp.zeros_like(pair)
    return jnp.concatenate([jnp.where(lane < HD, pair, zero), jnp.where(lane < HD, zero, pair)], 0)


def pick_heads(both):
    r = both.shape[0] // 2
    lane = lax.broadcasted_iota(jnp.int32, (r, 128), 1)
    return jnp.where(lane < HD, both[:r], both[r:])


def twice(kv, g):
    lane = lax.broadcasted_iota(jnp.int32, kv.shape, 1)
    turned = pltpu.roll(kv.astype(f32), HD, 1).astype(kv.dtype)
    return jnp.where((lane < HD) == (g == 0), kv, turned)


def attend_kernel(s_ref, q_ref, k_ref, v_ref, start_ref, live_ref, att_ref, out_ref, lse_ref, bias):
    g = pl.program_id(0)
    n = k_ref.shape[0]
    b = n // 4

    @pl.when(g == 0)
    def _():
        for a in range(4):
            keys = (a + 1) * b
            start = start_ref[a * b : (a + 1) * b, :1]
            q_at = lax.broadcasted_iota(jnp.int32, (b, keys), 0) + a * b
            k_at = lax.broadcasted_iota(jnp.int32, (b, keys), 1)
            allowed = ((live_ref[:1, :keys] >= start) & (k_at <= q_at)) | (k_at == q_at)
            bias[a * b : (a + 1) * b, :keys] = jnp.where(allowed, 0.0, NEG)

    kd = twice(k_ref[...], g)
    vd = twice(v_ref[...], g)
    for a in range(4):
        keys = (a + 1) * b
        rows = slice(a * b, (a + 1) * b)
        qm = both_heads(q_ref[rows, :])
        scores = contract(qm, kd[:keys], 1, 1)
        extra = bias[rows, :keys]
        expo = jnp.exp(scores + jnp.concatenate([extra, extra], 0))
        total = jnp.sum(expo, axis=-1, keepdims=True)
        pair = pick_heads(contract(expo.astype(bf16), vd[:keys], 1, 0) / total)
        out_ref[rows, :] = pair
        att_ref[pl.ds(pl.multiple_of((s_ref[0] ^ a) * b, b), b), :] = pair.astype(bf16)
        lse_ref[0, a] = jnp.transpose(jnp.broadcast_to(jnp.log(total), (2 * b, 128)))[:1]


def attend_call(s, qk, v, start, live):
    n = qk.shape[0]
    b = n // 4
    lanes = lambda g, s: (0, g)
    return pl.pallas_call(
        attend_kernel,
        grid_spec=pltpu.PrefetchScalarGridSpec(
            num_scalar_prefetch=1,
            grid=(2,),
            in_specs=[
                pl.BlockSpec((n, 128), lanes),
                pl.BlockSpec((n, 128), lambda g, s: (0, 2)),
                fixed(n, 128),
                fixed(n, 128),
                fixed(8, n),
            ],
            out_specs=[
                pl.BlockSpec((n, 128), lanes),
                pl.BlockSpec((n, 128), lanes),
                pl.BlockSpec((1, 4, 1, 2 * b), lambda g, s: (g, 0, 0, 0)),
            ],
            scratch_shapes=[pltpu.VMEM((n, n), f32)],
        ),
        out_shape=[
            jax.ShapeDtypeStruct((n, 256), bf16),
            jax.ShapeDtypeStruct((n, 256), f32),
            jax.ShapeDtypeStruct((2, 4, 1, 2 * b), f32),
        ],
        compiler_params=params(40),
        cost_estimate=pl.CostEstimate(
            flops=16 * n * n * HD, bytes_accessed=4 * VMEM_MB, transcendentals=4 * n * n
        ),
        name="attend",
    )(s, qk, qk, v, start, live)


def norm_back(grad, pre, gain, cos, sin):
    turned = grad * cos - swap_halves(grad) * sin
    inv = lax.rsqrt(head_mean(pre * pre) + epsilon)
    scaled = turned * gain
    dpre = inv * scaled - pre * (inv * inv * inv) * head_mean(scaled * pre)
    return dpre, jnp.sum(turned * pre * inv, axis=0, keepdims=True)


def attend_back_kernel(s_ref, q_ref, k_ref, v_ref, qpre_ref, kpre_ref, gains_ref, kgain_ref, cos_ref, sin_ref,
                       start_ref, live_ref, out_ref, lse_ref, wout_ref, w_ref, b0, b1, b2, b3,
                       low_ref, gain_ref, lo_ref, hi_ref, bias, dk, dv, dkall, dvall, dos, gb, sems):
    g = pl.program_id(0)
    n = k_ref.shape[0]
    b = n // 4
    pieces = (b0, b1, b2, b3)

    @pl.when(g == 0)
    def _():
        for k in range(4):
            pltpu.make_async_copy(pieces[k], gb.at[k], sems.at[k]).start()
        for a in range(4):
            keys = (a + 1) * b
            start = start_ref[:1, a * b : (a + 1) * b]
            k_at = lax.broadcasted_iota(jnp.int32, (keys, b), 0)
            q_at = lax.broadcasted_iota(jnp.int32, (keys, b), 1) + a * b
            allowed = ((live_ref[:keys, :1] >= start) & (k_at <= q_at)) | (k_at == q_at)
            bias[:keys, a * b : (a + 1) * b] = jnp.where(allowed, 0.0, NEG)
        for k in range(4):
            pltpu.make_async_copy(pieces[k], gb.at[k], sems.at[k]).wait()
            dos[k] = contract(gb[k], wout_ref[...], 1, 1).astype(bf16)

    kd = twice(k_ref[...], g)
    vd = twice(v_ref[...], g)
    gain_sum = jnp.zeros((1, 128), f32)
    ones = jnp.ones((8, 128), f32)
    for a in (3, 2, 1, 0):
        keys = (a + 1) * b
        rows = slice(a * b, (a + 1) * b)
        home = s_ref[0] ^ a
        qm = both_heads(q_ref[rows, :])
        dout = jnp.where(g == 0, dos[home, :, :128], dos[home, :, 128:])
        dom = both_heads(dout)
        delta = contract(ones, both_heads(dout.astype(f32) * out_ref[rows, :]), 1, 1, lax.Precision.HIGHEST)[:1]
        scores = contract(kd[:keys], qm, 1, 1)
        extra = bias[:keys, rows]
        probs = jnp.exp(scores + (jnp.concatenate([extra, extra], 1) - lse_ref[0, a]))
        dprobs = contract(vd[:keys], dom, 1, 1)
        dscores = (probs * (dprobs - delta)).astype(bf16)
        dv_add = contract(probs.astype(bf16), dom, 1, 0)
        dk_add = contract(dscores, qm, 1, 0)
        if a == 3:
            dv[...] = dv_add
            dk[...] = dk_add
        else:
            dv[:keys] += dv_add
            dk[:keys] += dk_add
        dq = pick_heads(contract(dscores, kd[:keys], 0, 0)) * 0.125
        dpre, gain_part = norm_back(dq, qpre_ref[rows, :], gains_ref[...], cos_ref[rows, :], sin_ref[rows, :])
        at = pl.ds(pl.multiple_of(home * b, b), b)
        low_ref[at, pl.ds(pl.multiple_of(g * 128, 128), 128)] = dpre.astype(bf16)
        gain_sum = gain_sum + gain_part
    gain_ref[pl.ds(g, 1), :] = gain_sum
    lane = lax.broadcasted_iota(jnp.int32, (n, 128), 1)
    dk_all = dk[...] + pltpu.roll(dk[...], HD, 1)
    dv_all = dv[...] + pltpu.roll(dv[...], HD, 1)

    @pl.when(g == 0)
    def _():
        dkall[...] = dk_all
        dvall[...] = dv_all

    @pl.when(g == 1)
    def _():
        grad_k = jnp.where(lane < HD, dkall[...], dk_all)
        grad_v = jnp.where(lane < HD, dvall[...], dv_all)
        dpre, gain_part = norm_back(grad_k, kpre_ref[...], kgain_ref[...], cos_ref[...], sin_ref[...])
        gain_ref[2:3, :] = gain_part
        for a in range(4):
            at = pl.ds(pl.multiple_of((s_ref[0] ^ a) * b, b), b)
            low_ref[at, 256:384] = dpre[a * b : (a + 1) * b].astype(bf16)
            low_ref[at, 384:512] = grad_v[a * b : (a + 1) * b].astype(bf16)
        hi_ref[...] = contract(low_ref[2 * b :, :], w_ref[...], 1, 1).astype(bf16)
        lo_ref[...] = contract(low_ref[: 2 * b, :], w_ref[...], 1, 1).astype(bf16)


def attend_back_call(s, qk, v, pre, qgain, kgain, cos, sin, start, live, out, lse, wout, w, blocks):
    n = v.shape[0]
    b = n // 4
    d = blocks[0].shape[1]
    lanes = pl.BlockSpec((n, 128), lambda g, s: (0, g))
    third = pl.BlockSpec((n, 128), lambda g, s: (0, 2))
    return pl.pallas_call(
        attend_back_kernel,
        grid_spec=pltpu.PrefetchScalarGridSpec(
            num_scalar_prefetch=1,
            grid=(2,),
            in_specs=[lanes, third, fixed(n, 128), lanes, third, fixed(1, 128), fixed(1, 128), fixed(n, 128),
                      fixed(n, 128), fixed(8, n), fixed(n, 128), lanes,
                      pl.BlockSpec((1, 4, 1, 2 * b), lambda g, s: (g, 0, 0, 0)),
                      fixed(256, d), fixed(d, 512)] + [ANY] * 4,
            out_specs=[fixed(n, 512), fixed(8, 128), fixed(2 * b, d), fixed(2 * b, d)],
            scratch_shapes=[pltpu.VMEM((n, n), f32)]
            + [pltpu.VMEM((n, 128), f32)] * 4
            + [pltpu.VMEM((4, b, 256), bf16), pltpu.VMEM((4, b, d), bf16), pltpu.SemaphoreType.DMA((4,))],
        ),
        out_shape=[
            jax.ShapeDtypeStruct((n, 512), bf16),
            jax.ShapeDtypeStruct((8, 128), f32),
            jax.ShapeDtypeStruct((2 * b, d), bf16),
            jax.ShapeDtypeStruct((2 * b, d), bf16),
        ],
        compiler_params=params(52),
        cost_estimate=pl.CostEstimate(
            flops=40 * n * n * HD + 2 * n * d * 768, bytes_accessed=10 * VMEM_MB, transcendentals=4 * n * n
        ),
        name="attend_back",
    )(s, qk, qk, v, pre, pre, qgain, kgain, cos, sin, start, live, out, lse, wout, w, *blocks)


def ffn_kernel(s_ref, x0, x1, x2, x3, a0, a1, a2, a3, o_in, wg_own, g0, g1, g2, g3, wu_own, u0, u1, u2, u3,
               gain_ref, n2_ref, hid_ref, fg_ref, fu_ref, res_ref, wg, wu, wout_ref, xs, att, wout, asem, xsem, osem, gsem, usem):
    j = pl.program_id(0)
    b = x0.shape[0]
    x_in, a_in = (x0, x1, x2, x3), (a0, a1, a2, a3)
    gate_w = Weight((wg_own,), (g0, g1, g2, g3), wg, gsem, s_ref[1], s_ref[2])
    up_w = Weight((wu_own,), (u0, u1, u2, u3), wu, usem, s_ref[1], s_ref[2])

    def out_copy(i):
        return pltpu.make_async_copy(o_in.at[:, i ^ (2 * s_ref[1])], wout.at[i], osem.at[i])

    def att_copy(k, i):
        return pltpu.make_async_copy(
            a_in[i].at[pl.ds((k ^ i) * b, b), :], att.at[k, :, pl.ds(i * b, b)], asem.at[k, i]
        )

    @pl.when(j == 0)
    def _():
        for k in range(4):
            pltpu.make_async_copy(x_in[k], xs.at[k], xsem.at[k]).start()
            for i in range(4):
                att_copy(k, i).start()
            if k == 0:
                for i in range(4):
                    out_copy(i).start()
                gate_w.start()
        up_w.start()
        for i in range(4):
            out_copy(i).wait()

    pltpu.make_async_copy(x0, xs.at[j], xsem.at[j]).wait()
    for i in range(4):
        pltpu.make_async_copy(a_in[i].at[pl.ds(0, b), :], att.at[j, :, pl.ds(i * b, b)], asem.at[j, i]).wait()
    res = xs[j].astype(f32) + jnp.dot(att[j], wout[...].reshape(4 * b, -1), preferred_element_type=f32)

    @pl.when(j == 0)
    def _():
        res_ref[...] = res
        wout_ref[...] = wout[0].reshape(b, -1)
        gate_w.wait()
        up_w.wait()

    inv = lax.rsqrt(jnp.mean(res * res, axis=-1, keepdims=True) + epsilon)
    n2 = (res * inv * gain_ref[...]).astype(bf16)
    n2_ref[...] = n2
    gate = jnp.dot(n2, wg[...], preferred_element_type=f32)
    up = jnp.dot(n2, wu[...], preferred_element_type=f32)
    s = jax.nn.sigmoid(gate)
    silu = gate * s
    hid_ref[...] = (silu * up).astype(bf16)
    fg_ref[...] = (up * (s * (1.0 + gate * (1.0 - s)))).astype(bf16)
    fu_ref[...] = silu.astype(bf16)


def ffn_call(s, xs, atts, wout, wg, g_parts, wu, u_parts, gain):
    b, d = xs[0].shape
    h = wg.shape[1]
    block = lambda wid: pl.BlockSpec((b, wid), lambda j, s: (j, 0))
    return pl.pallas_call(
        ffn_kernel,
        grid_spec=pltpu.PrefetchScalarGridSpec(
            num_scalar_prefetch=1,
            grid=(4,),
            in_specs=[ANY] * 19 + [fixed(1, d)],
            out_specs=[block(d), block(h), block(h), block(h), fixed(b, d), fixed(d, h), fixed(d, h), fixed(b, d)],
            scratch_shapes=[
                pltpu.VMEM((4, b, d), bf16),
                pltpu.VMEM((4, b, 4 * b), bf16),
                pltpu.VMEM((4,) + wout.shape[:1] + wout.shape[2:], bf16),
                pltpu.SemaphoreType.DMA((4, 4)),
                pltpu.SemaphoreType.DMA((4,)),
                pltpu.SemaphoreType.DMA((4,)),
                pltpu.SemaphoreType.DMA((5,)),
                pltpu.SemaphoreType.DMA((5,)),
            ],
        ),
        out_shape=[jax.ShapeDtypeStruct((4 * b, d), bf16)]
        + [jax.ShapeDtypeStruct((4 * b, h), bf16)] * 3
        + [jax.ShapeDtypeStruct((b, d), f32)]
        + [jax.ShapeDtypeStruct((d, h), bf16)] * 2
        + [jax.ShapeDtypeStruct((b, d), bf16)],
        compiler_params=params(48),
        cost_estimate=pl.CostEstimate(
            flops=8 * b * d * (d + 2 * h), bytes_accessed=25 * VMEM_MB, transcendentals=4 * b * h
        ),
        name="ffn",
    )(s, *xs, *atts, wout, wg, *g_parts, wu, *u_parts, gain)


def ffn_back_kernel(s_ref, y0, y1, y2, y3, wd_own, d0, d1, d2, d3, fg_ref, fu_ref, wg_in, wu_in,
                    gg_ref, gu_ref, lo_ref, hi_ref, wd, dy, wg, wu, ysem, dsem, wsem):
    j = pl.program_id(0)
    y_in = (y0, y1, y2, y3)
    down_w = Weight((wd_own,), (d0, d1, d2, d3), wd, dsem, s_ref[1], s_ref[2])

    @pl.when(j == 0)
    def _():
        for k in range(4):
            pltpu.make_async_copy(y_in[k], dy.at[k], ysem.at[k]).start()
        down_w.start()
        pltpu.make_async_copy(wg_in, wg, wsem.at[0]).start()
        pltpu.make_async_copy(wu_in, wu, wsem.at[1]).start()
        down_w.wait()

    pltpu.make_async_copy(y0, dy.at[j], ysem.at[j]).wait()
    gh = contract(dy[j], wd[...], 1, 1)
    gg = (gh * fg_ref[...].astype(f32)).astype(bf16)
    gu = (gh * fu_ref[...].astype(f32)).astype(bf16)
    gg_ref[...] = gg
    gu_ref[...] = gu

    @pl.when(j == 0)
    def _():
        pltpu.make_async_copy(wg_in, wg, wsem.at[0]).wait()
        pltpu.make_async_copy(wu_in, wu, wsem.at[1]).wait()

    grad = (contract(gg, wg[...], 1, 1) + contract(gu, wu[...], 1, 1)).astype(bf16)

    @pl.when(j < 2)
    def _():
        lo_ref[...] = grad

    @pl.when(j >= 2)
    def _():
        hi_ref[...] = grad


def ffn_back_call(s, dys, wd, d_parts, fg, fu, wg, wu):
    b, d = dys[0].shape
    h = wg.shape[1]
    block = lambda wid: pl.BlockSpec((b, wid), lambda j, s: (j, 0))
    return pl.pallas_call(
        ffn_back_kernel,
        grid_spec=pltpu.PrefetchScalarGridSpec(
            num_scalar_prefetch=1,
            grid=(4,),
            in_specs=[ANY] * 9 + [block(h), block(h), ANY, ANY],
            out_specs=[
                block(h),
                block(h),
                pl.BlockSpec((b, d), lambda j, s: (jnp.minimum(j, 1), 0)),
                pl.BlockSpec((b, d), lambda j, s: (jnp.maximum(j - 2, 0), 0)),
                fixed(h, d),
            ],
            scratch_shapes=[
                pltpu.VMEM((4, b, d), bf16),
                pltpu.VMEM((d, h), bf16),
                pltpu.VMEM((d, h), bf16),
                pltpu.SemaphoreType.DMA((4,)),
                pltpu.SemaphoreType.DMA((5,)),
                pltpu.SemaphoreType.DMA((2,)),
            ],
        ),
        out_shape=[jax.ShapeDtypeStruct((4 * b, h), bf16)] * 2
        + [jax.ShapeDtypeStruct((2 * b, d), bf16)] * 2
        + [jax.ShapeDtypeStruct((h, d), bf16)],
        compiler_params=params(48),
        cost_estimate=pl.CostEstimate(flops=24 * b * d * h, bytes_accessed=22 * VMEM_MB, transcendentals=0),
        name="ffn_back",
    )(s, *dys, wd, *d_parts, fg, fu, wg, wu)


def store_pieces(j, first, second, sent_a, keep_a, sent_b, keep_b):
    @pl.when(j % 2 == 1)
    def _():
        sent_a[0] = first

    @pl.when(j % 2 == 0)
    def _():
        keep_a[0] = first

    @pl.when(j >= 2)
    def _():
        sent_b[0] = second

    @pl.when(j < 2)
    def _():
        keep_b[0] = second


def piece_outputs(rows, cols):
    maps = [
        lambda j, s: (j // 2, 0, 0),
        lambda j, s: (j // 2, 0, 0),
        lambda j, s: (jnp.maximum(j - 2, 0), 0, 0),
        lambda j, s: (jnp.minimum(j, 1), 0, 0),
    ]
    return dict(
        out_specs=[pl.BlockSpec((1, rows, cols), m) for m in maps],
        out_shape=[jax.ShapeDtypeStruct((2, rows, cols), bf16)] * 4,
    )


def grad_rows_kernel(s_ref, left_ref, right_ref, *outs):
    grad = contract(left_ref[...], right_ref[...], 0, 0).astype(bf16)
    half = grad.shape[0] // 2
    store_pieces(pl.program_id(0), grad[:half], grad[half:], *outs)


def grad_rows_call(s, left, right, name):
    n, rows = left.shape
    cols = right.shape[1]
    out = piece_outputs(rows // 8, cols)
    return pl.pallas_call(
        grad_rows_kernel,
        grid_spec=pltpu.PrefetchScalarGridSpec(
            num_scalar_prefetch=1,
            grid=(4,),
            in_specs=[pl.BlockSpec((n, rows // 4), lambda j, s: (0, s[2] ^ j)), fixed(n, cols)],
            out_specs=out["out_specs"],
        ),
        out_shape=out["out_shape"],
        compiler_params=params(40),
        cost_estimate=pl.CostEstimate(flops=2 * n * rows * cols, bytes_accessed=4 * n * (rows + cols), transcendentals=0),
        name=name,
    )(s, left, right)


def grad_cols_kernel(s_ref, left_ref, right_ref, *outs):
    grad = contract(left_ref[...], right_ref[...], 0, 0).astype(bf16)
    half = grad.shape[0] // 2
    store_pieces(pl.program_id(0), grad[:half], grad[half:], *outs)


def grad_cols_call(s, left, right, name):
    n, rows = left.shape
    cols = right.shape[1] // 4
    out = piece_outputs(rows // 2, cols)
    return pl.pallas_call(
        grad_cols_kernel,
        grid_spec=pltpu.PrefetchScalarGridSpec(
            num_scalar_prefetch=1,
            grid=(4,),
            in_specs=[fixed(n, rows), pl.BlockSpec((n, cols), lambda j, s: (0, s[2] ^ j))],
            out_specs=out["out_specs"],
        ),
        out_shape=out["out_shape"],
        compiler_params=params(40),
        cost_estimate=pl.CostEstimate(flops=8 * n * rows * cols, bytes_accessed=4 * n * (rows + 4 * cols), transcendentals=0),
        name=name,
    )(s, left, right)


def permute(x, places, move):
    pairs = []
    for d in range(places):
        for t in range(T4):
            to = move(d, t)
            if to is not None:
                pairs.append((d * T4 + t, to[0] * T4 + to[1]))
    return lax.ppermute(x, AX, pairs)


def after(x, *events):
    return lax.optimization_barrier((x, events))[0]


def two_up(d, t):
    return (d, t ^ 2) if d & 1 else None


def flip_core(d, t):
    return (d ^ 1, t)


def flip_z(d, t):
    return (d, t ^ 1)


def flip_e(bit):
    return lambda d, t: (d ^ (2 << bit), t)


def settle(d, t):
    return (d, t) if (d & 1) == (t >> 1) else (d ^ 1, t ^ 2)


def settled_row(own, settled, n, home):
    early = permute(own, n, lambda d, t: (d, t ^ 1) if (d & 1) == (t >> 1) else None)
    late = permute(settled, n, lambda d, t: (d, t ^ 1) if (d & 1) != (t >> 1) else None)
    near = permute(settled, n, flip_core)
    over = jnp.where(home, early, late)
    return [settled, over, near, permute(over, n, flip_core)]


def gather_row(x, n):
    over = permute(x, n, flip_z)
    near = permute(x, n, flip_core)
    far = permute(over, n, flip_core)
    return [x, over, near, far]


def scatter_row(low, high, n, *events):
    b = low.shape[0] // 2
    got = permute(high, n, flip_core)
    over = permute(low[b:] + got[b:], n, flip_z)
    return low[:b] + got[:b] + (after(over, *events) if events else over)


def hop(w, n, e):
    rows = w.shape[0] // 4
    mine = lax.dynamic_slice_in_dim(w, e * rows, rows, 0)
    return permute(mine, n, two_up)


def spread(piece, n):
    def only_one(j):
        return lambda d, t: (d ^ (2 * j), t) if d & 1 else None

    return [piece] + [permute(piece, n, only_one(j)) for j in (1, 2, 3)]


def first_sums(pieces, n):
    sent_a, keep_a, sent_b, keep_b = pieces
    got_a = permute(sent_a, n, flip_e(0))
    got_b = permute(sent_b, n, flip_e(1))
    return got_a, got_b


def first_add(pieces, got):
    got_a, got_b = got
    keep_a, keep_b = pieces[1], pieces[3]
    return keep_a[1] + got_a[1], keep_a[0] + got_a[0], keep_b[1] + got_b[1], keep_b[0] + got_b[0]


def second_sums(halves, n):
    return permute(halves[0], n, flip_e(1)), permute(halves[2], n, flip_e(0))


def second_add(halves, got, n):
    total = jnp.stack([halves[1] + got[0], halves[3] + got[1]])
    for extra in range(2, 20):
        if (2 << extra) < n:
            total = total + permute(total, n, flip_e(extra))
    return total


def owner_sums(total, n, c):
    half = total.shape[1] // 2
    first, second = total[:, :half], total[:, half:]
    one = permute(
        jnp.where(c == 0, second, first), n, lambda d, t: (d ^ 1, t ^ 2) if d & 1 else (d ^ 1, t)
    )
    two = permute(second, n, two_up)
    return one, two


def owner_add(total, got, c):
    half = total.shape[1] // 2
    return jnp.where(c == 0, total[:, :half], got[1]) + got[0]


def neighbours(n):
    return None if n == 8 else [list(range(k, k + 8)) for k in range(0, n, 8)]


def whole_grad(mine, n):
    got = lax.all_gather(mine, "dp", axis_index_groups=neighbours(n))
    return got.reshape((4, 2) + mine.shape)


def whole_out(w, n, c, e):
    rows = w.shape[0] // 8
    mine = lax.dynamic_slice_in_dim(w, (2 * e + c) * rows, rows, 0)
    two = jnp.stack([mine, permute(mine, n, flip_z)])
    four = jnp.concatenate([two, permute(two, n, lambda d, t: (d, t ^ 2))])
    return lax.all_gather(four, "dp", axis_index_groups=neighbours(n))


def sum_all(vec, n):
    bit = 1
    while bit < n:
        vec = vec + permute(vec, n, lambda d, t, bit=bit: (d ^ bit, t))
        bit *= 2
    for bit in (1, 2):
        vec = vec + permute(vec, n, lambda d, t, bit=bit: (d, t ^ bit))
    return vec


def local(
    block_input,
    doc_lengths,
    pad_mask,
    norm1_gain,
    w_query,
    w_key,
    w_value,
    query_gain,
    key_gain,
    w_out,
    norm2_gain,
    w_gate,
    w_up,
    w_down,
    cotangent,
):
    n = lax.axis_size("dp")
    d, t = lax.axis_index("dp"), lax.axis_index("tensor")
    c, p = d & 1, t >> 1
    e = (d >> 1) & 3
    shard = 2 * c + (t & 1)
    b = block_input.shape[0]
    seq_len = b * T4
    home = c == p
    wq = w_query.shape[1]
    wk = w_key.shape[1]
    width = block_input.shape[1]
    s = jnp.stack([shard, c, e]).astype(jnp.int32)

    x_own = permute(block_input, n, settle)
    marks = jnp.concatenate([doc_lengths, pad_mask], 1)
    marks = jnp.where(home, marks, permute(marks, n, flip_core))
    lengths_row, pad_row = marks[0, : doc_lengths.shape[1]], marks[0, doc_lengths.shape[1] :]
    qkv_hop = permute(
        jnp.concatenate([lax.dynamic_slice_in_dim(w, e * b, b, 0) for w in (w_query, w_key, w_value)], 1), n, two_up
    )
    x_blocks = settled_row(block_input, x_own, n, home)
    out_all = whole_out(after(w_out, qkv_hop), n, c, e)
    qkv_parts = spread(qkv_hop, n)
    gate_hop = hop(after(w_gate, x_blocks[2], qkv_hop), n, e)
    up_hop = hop(after(w_up, gate_hop), n, e)
    down_hop = hop(after(w_down, up_hop), n, e)

    positions = jnp.arange(seq_len, dtype=jnp.int32)
    doc_starts, cos_half, sin_half = doc_tables(lengths_row, positions, HD)
    cos = jnp.concatenate([cos_half] * 4, 1)
    sin = jnp.concatenate([-sin_half, sin_half] * 2, 1)
    live = jnp.where(pad_row == 1, positions, -1)
    start_col = jnp.broadcast_to(doc_starts[:, None], (seq_len, 128))
    start_row = jnp.broadcast_to(doc_starts[None], (8, seq_len))
    live_col = jnp.broadcast_to(live[:, None], (seq_len, 128))
    live_row = jnp.broadcast_to(live[None], (8, seq_len))
    gains = jnp.concatenate([query_gain] * (wq // HD) + [key_gain] * (wk // HD))[None]
    qgain_pair = jnp.concatenate([query_gain] * 2)[None]
    kgain_pair = jnp.concatenate([key_gain] * 2)[None]

    rows_one, pre, qk, values, w_qkv = qkv_call(
        s, x_blocks, (w_query, w_key, w_value), qkv_parts, norm1_gain[None], gains, cos, sin
    )
    gate_parts = spread(gate_hop, n)
    attended, attended_f, lse = attend_call(s, qk, values, start_col, live_row)
    att_pieces = gather_row(attended, n)
    up_parts = spread(after(up_hop, attended), n)
    rows_two, hidden, by_gate, by_up, residual, wg, wu, w_out_own = ffn_call(
        s, x_blocks, att_pieces, out_all, w_gate, gate_parts, w_up, up_parts, norm2_gain[None]
    )
    dy_own = permute(after(cotangent, down_hop, att_pieces[2]), n, settle)
    dy_blocks = settled_row(after(cotangent, att_pieces[1]), dy_own, n, home)
    down_parts = spread(after(down_hop, att_pieces[1]), n)

    dy = jnp.concatenate(dy_blocks, 0)
    down = grad_cols_call(s, hidden, dy, "grad_down")
    gate_grad, up_grad, low2, high2, wd = ffn_back_call(
        s, dy_blocks, w_down, down_parts, after(by_gate, *down), by_up, wg, wu
    )
    down_got = first_sums(down, n)
    gate = grad_rows_call(s, rows_two, gate_grad, "grad_gate")
    up = grad_rows_call(s, rows_two, after(up_grad, *gate), "grad_up")
    grad_n2 = scatter_row(low2, high2, n, *up).astype(f32)
    inv = lax.rsqrt(jnp.mean(residual * residual, axis=-1, keepdims=True) + epsilon)
    scaled = norm2_gain * grad_n2
    grad_residual = (
        dy_own.astype(f32)
        + inv * scaled
        - residual * (inv * inv * inv) * jnp.mean(scaled * residual, axis=-1, keepdims=True)
    )
    grad_norm2 = jnp.sum(grad_n2 * residual * inv, axis=0)
    gb_own = grad_residual.astype(bf16)
    gb_blocks = gather_row(gb_own, n)

    down = first_add(down, after(down_got, gb_own))
    down_got = second_sums(down, n)
    gate_got = first_sums(gate, n)
    up_got = first_sums(up, n)
    ffn_part = jnp.dot(after(hidden, *down), wd, preferred_element_type=f32).astype(bf16)
    gate = first_add(gate, after(gate_got, ffn_part))
    gate_got = second_sums(gate, n)
    down = second_add(down, after(down_got, *gate), n)
    down_got = owner_sums(down, n, c)
    up = first_add(up, after(up_got, gb_blocks[1], down))
    up_got = second_sums(up, n)
    gate = second_add(gate, after(gate_got, gb_blocks[3], *up), n)
    gate_got = owner_sums(gate, n, c)

    low, gain_terms, low1, high1 = attend_back_call(
        s, qk, after(values, gate, *up), pre, qgain_pair, kgain_pair, cos, sin, start_row, live_col, attended_f, lse,
        w_out_own, w_qkv, gb_blocks,
    )
    down_mine = owner_add(down, after(down_got, low), c)
    down_all = whole_grad(down_mine, n)
    up = second_add(up, after(up_got, low), n)
    up_got = owner_sums(up, n, c)
    gate_mine = owner_add(gate, after(gate_got, low), c)
    gate_all = whole_grad(gate_mine, n)
    qkv = grad_rows_call(s, rows_one, after(low, gate_mine, up), "grad_qkv")
    qkv_got = first_sums(qkv, n)
    gb = jnp.concatenate(gb_blocks, 0)
    out = grad_cols_call(s, attended, after(gb, *qkv), "grad_out")
    out_got = first_sums(out, n)

    grad_n1 = scatter_row(low1, high1, n, *out).astype(f32)
    x_f = x_own.astype(f32)
    inv = lax.rsqrt(jnp.mean(x_f * x_f, axis=-1, keepdims=True) + epsilon)
    scaled = norm1_gain * grad_n1
    input_grad = (
        grad_residual
        + inv * scaled
        - x_f * (inv * inv * inv) * jnp.mean(scaled * x_f, axis=-1, keepdims=True)
    )
    grad_norm1 = jnp.sum(grad_n1 * x_f * inv, axis=0)
    settled_grad = permute(input_grad.astype(bf16), n, settle)
    ffn_branch = scatter_row(ffn_part[: 2 * b], ffn_part[2 * b :], n)
    block_output = residual + ffn_branch.astype(f32)
    settled_output = permute(block_output.astype(bf16), n, settle)
    block_output = jnp.where(home, block_output, settled_output.astype(f32))
    input_grad = jnp.where(home, input_grad, settled_grad.astype(f32))

    qkv = first_add(qkv, after(qkv_got, grad_n1))
    out = first_add(out, after(out_got, grad_n1))
    qkv_got, out_got = second_sums(qkv, n), second_sums(out, n)
    up_mine = owner_add(up, up_got, c)
    up_all = whole_grad(up_mine, n)
    qkv = second_add(qkv, qkv_got, n)
    out = second_add(out, out_got, n)
    qkv_got, out_got = owner_sums(qkv, n, c), owner_sums(out, n, c)
    qkv_all = whole_grad(owner_add(qkv, qkv_got, c), n)
    out_all = whole_grad(owner_add(out, out_got, c), n)

    def from_rows(whole):
        return whole.astype(f32).transpose(0, 2, 1, 3, 4).reshape(width, -1)

    def from_cols(whole):
        return whole.astype(f32).transpose(2, 1, 3, 0, 4).reshape(-1, width)

    grad_down = from_cols(down_all)
    grad_gate = from_rows(gate_all)
    grad_up = from_rows(up_all)
    grad_out = from_cols(out_all)
    grad_qkv = from_rows(qkv_all)
    head_terms = gain_terms[:, :HD] + gain_terms[:, HD:]
    vec = jnp.concatenate([grad_norm1, grad_norm2, head_terms[0] + head_terms[1], head_terms[2]])
    vec = sum_all(vec[None], n)[0]
    return (
        block_output,
        input_grad,
        vec[:width],
        grad_qkv[:, :wq],
        grad_qkv[:, wq : wq + wk],
        grad_qkv[:, wq + wk :],
        vec[2 * width : 2 * width + HD],
        vec[2 * width + HD :],
        grad_out,
        vec[width : 2 * width],
        grad_gate,
        grad_up,
        grad_down,
    )


def solution(mesh):
    placed = (
        P(("dp", "tensor"), None),
        P("dp", None),
        P("dp", None),
        P(),
        P(None, "tensor"),
        P(None, "tensor"),
        P(None, "tensor"),
        P(),
        P(),
        P("tensor", None),
        P(),
        P(None, "tensor"),
        P(None, "tensor"),
        P("tensor", None),
        P(("dp", "tensor"), None),
    )
    return jax.shard_map(
        local,
        mesh=mesh,
        in_specs=placed,
        out_specs=(
            P(("dp", "tensor"), None),
            P(("dp", "tensor"), None),
            P(),
            P(None, "tensor"),
            P(None, "tensor"),
            P(None, "tensor"),
            P(),
            P(),
            P("tensor", None),
            P(),
            P(None, "tensor"),
            P(None, "tensor"),
            P("tensor", None),
        ),
        check_vma=False,
    )
```

```python
import functools
import math

import jax
import jax.numpy as jnp
from jax import lax
from jax.experimental import pallas as pl
from jax.experimental.pallas import tpu as pltpu
from jax.sharding import PartitionSpec as P

HD = 64
AX = ("dp", "tensor")
T4 = 4
VMEM_MB = 1 << 20

epsilon = 1e-05
rope_base = 1000000.0
NEG = -1000000000.0
bf16 = jnp.bfloat16
f32 = jnp.float32


def doc_tables(lengths_row, positions, head_dim):
    doc_ends = jnp.cumsum(lengths_row)
    passed = positions[:, None] >= doc_ends[None, :]
    doc_starts = jnp.sum(jnp.where(passed, lengths_row[None, :], 0), axis=1)
    offsets = (positions - doc_starts).astype(f32)
    freqs = jnp.exp(
        jnp.arange(head_dim // 2, dtype=f32) * (-2.0 * math.log(rope_base) / head_dim)
    )
    angles = offsets[:, None] * freqs[None, :]
    return (doc_starts, jnp.cos(angles), jnp.sin(angles))


def contract(a, b, da, db, precision=None):
    return lax.dot_general(
        a, b, (((da,), (db,)), ((), ())), preferred_element_type=f32, precision=precision
    )


def swap_halves(y):
    width = y.shape[1]
    lane = lax.broadcasted_iota(jnp.int32, y.shape, 1)
    return jnp.where(lane % HD < HD // 2, pltpu.roll(y, width - HD // 2, 1), pltpu.roll(y, HD // 2, 1))


def head_mean(y):
    width = y.shape[1]
    at = lax.broadcasted_iota(jnp.int32, (width, width), 0) // HD
    to = lax.broadcasted_iota(jnp.int32, (width, width), 1) // HD
    ones = jnp.where(at == to, 1.0 / HD, 0.0).astype(f32)
    return contract(y, ones, 1, 0, lax.Precision.HIGHEST)


class Weight:
    def __init__(self, s_ref, own, parts, to, sems, start=0):
        self.core, self.e = s_ref[1], s_ref[2]
        self.own, self.parts, self.to, self.sems, self.start_col = own, parts, to, sems, start

    def copies(self):
        start = 0
        for i, w in enumerate(self.own):
            wide = w.shape[1]
            to = self.to if len(self.own) == 1 else self.to.at[:, pl.ds(start, wide)]
            yield 0, functools.partial(pltpu.make_async_copy, w, to, self.sems.at[8 + i])
            start += wide
        rows = self.to.shape[0] // 8
        for j in range(4):
            for other in range(2):
                at = pl.multiple_of((2 * (self.e ^ j) + 1 - other) * rows, rows)
                src = self.parts[other].at[pl.ds(j * rows, rows), pl.ds(self.start_col, self.to.shape[1])]
                yield 1, functools.partial(
                    pltpu.make_async_copy, src, self.to.at[pl.ds(at, rows), :], self.sems.at[2 * j + other]
                )

    def each(self, act):
        for core in range(2):

            @pl.when(self.core == core)
            def _():
                for whose, copy in self.copies():
                    if whose == core:
                        act(copy())

    def start(self):
        self.each(lambda copy: copy.start())

    def wait(self):
        self.each(lambda copy: copy.wait())


ANY = pl.BlockSpec(memory_space=pl.ANY)


def fixed(*shape):
    return pl.BlockSpec(shape, lambda *_: (0,) * len(shape))


def params(mib):
    return pltpu.CompilerParams(vmem_limit_bytes=mib * VMEM_MB)


def qkv_kernel(s_ref, x0, x1, x2, x3, wq_own, wk_own, wv_own, w0, w1, g1_ref, gains_ref, cos_ref, sin_ref,
               n1_ref, pre_ref, qk_ref, v_ref, w_ref, xs, xsem, wsem):
    j = pl.program_id(0)
    pieces = (x0, x1, x2, x3)
    weight = Weight(s_ref, (wq_own, wk_own, wv_own), (w0, w1), w_ref, wsem)

    @pl.when(j == 0)
    def _():
        for k in range(4):
            pltpu.make_async_copy(pieces[k], xs.at[k], xsem.at[k]).start()
        weight.start()

    pltpu.make_async_copy(x0, xs.at[j], xsem.at[j]).wait()
    x = xs[j].astype(f32)
    inv = lax.rsqrt(jnp.mean(x * x, axis=-1, keepdims=True) + epsilon)
    n1 = (x * inv * g1_ref[...]).astype(bf16)
    n1_ref[...] = n1

    @pl.when(j == 0)
    def _():
        weight.wait()

    qkv = jnp.dot(n1, w_ref[...], preferred_element_type=f32)
    width = pre_ref.shape[1]
    pre = qkv[:, :width]
    pre_ref[...] = pre
    v_ref[...] = qkv[:, width:].astype(bf16)
    y = pre * lax.rsqrt(head_mean(pre * pre) + epsilon) * gains_ref[...]
    cos = jnp.concatenate([cos_ref[...]] * (width // 128), 1)
    sin = jnp.concatenate([sin_ref[...]] * (width // 128), 1)
    qk = (y * cos + swap_halves(y) * sin).astype(bf16)
    lane = lax.broadcasted_iota(jnp.int32, qk.shape, 1)
    qk_ref[...] = jnp.where(lane < width - 128, qk * 0.125, qk).astype(bf16)


def qkv_call(s, xs, w_own, w_parts, g1, gains, cos, sin):
    b, d = xs[0].shape
    wid = w_parts[0].shape[1]
    qkw = wid - 128
    natural = lambda j, s: (s[0] ^ j, 0)
    return pl.pallas_call(
        qkv_kernel,
        grid_spec=pltpu.PrefetchScalarGridSpec(
            num_scalar_prefetch=1,
            grid=(4,),
            in_specs=[ANY] * 9
            + [fixed(1, d), fixed(1, qkw), pl.BlockSpec((b, 128), natural), pl.BlockSpec((b, 128), natural)],
            out_specs=[
                pl.BlockSpec((b, d), lambda j, s: (j, 0)),
                pl.BlockSpec((b, qkw), natural),
                pl.BlockSpec((b, qkw), natural),
                pl.BlockSpec((b, 128), natural),
                fixed(d, wid),
            ],
            scratch_shapes=[
                pltpu.VMEM((4, b, d), bf16),
                pltpu.SemaphoreType.DMA((4,)),
                pltpu.SemaphoreType.DMA((11,)),
            ],
        ),
        out_shape=[
            jax.ShapeDtypeStruct((4 * b, d), bf16),
            jax.ShapeDtypeStruct((4 * b, qkw), f32),
            jax.ShapeDtypeStruct((4 * b, qkw), bf16),
            jax.ShapeDtypeStruct((4 * b, 128), bf16),
            jax.ShapeDtypeStruct((d, wid), bf16),
        ],
        compiler_params=params(20),
        cost_estimate=pl.CostEstimate(flops=8 * b * d * wid, bytes_accessed=9 * VMEM_MB, transcendentals=0),
        name="qkv",
    )(s, *xs, *w_own, *w_parts, g1, gains, cos, sin)


def both_heads(pair):
    lane = lax.broadcasted_iota(jnp.int32, pair.shape, 1)
    zero = jnp.zeros_like(pair)
    return jnp.concatenate([jnp.where(lane < HD, pair, zero), jnp.where(lane < HD, zero, pair)], 0)


def pick_heads(both):
    r = both.shape[0] // 2
    lane = lax.broadcasted_iota(jnp.int32, (r, 128), 1)
    return jnp.where(lane < HD, both[:r], both[r:])


def twice(kv, g):
    lane = lax.broadcasted_iota(jnp.int32, kv.shape, 1)
    turned = pltpu.roll(kv.astype(f32), HD, 1).astype(kv.dtype)
    return jnp.where((lane < HD) == (g == 0), kv, turned)


def attend_kernel(s_ref, q_ref, k_ref, v_ref, start_ref, live_ref, att_ref, out_ref, lse_ref, bias):
    g = pl.program_id(0)
    n = k_ref.shape[0]
    b = n // 4

    @pl.when(g == 0)
    def _():
        for a in range(4):
            keys = (a + 1) * b
            start = start_ref[a * b : (a + 1) * b, :1]
            q_at = lax.broadcasted_iota(jnp.int32, (b, keys), 0) + a * b
            k_at = lax.broadcasted_iota(jnp.int32, (b, keys), 1)
            allowed = ((live_ref[:1, :keys] >= start) & (k_at <= q_at)) | (k_at == q_at)
            bias[a * b : (a + 1) * b, :keys] = jnp.where(allowed, 0.0, NEG)

    kd = twice(k_ref[...], g)
    vd = twice(v_ref[...], g)
    for a in range(4):
        keys = (a + 1) * b
        rows = slice(a * b, (a + 1) * b)
        qm = both_heads(q_ref[rows, :])
        scores = contract(qm, kd[:keys], 1, 1)
        extra = bias[rows, :keys]
        expo = jnp.exp(scores + jnp.concatenate([extra, extra], 0))
        total = jnp.sum(expo, axis=-1, keepdims=True)
        pair = pick_heads(contract(expo.astype(bf16), vd[:keys], 1, 0) / total)
        out_ref[rows, :] = pair
        att_ref[pl.ds(pl.multiple_of((s_ref[0] ^ a) * b, b), b), :] = pair.astype(bf16)
        lse_ref[0, a] = jnp.transpose(jnp.broadcast_to(jnp.log(total), (2 * b, 128)))[:1]


def attend_call(s, qk, v, start, live):
    n = qk.shape[0]
    b = n // 4
    lanes = lambda g, s: (0, g)
    return pl.pallas_call(
        attend_kernel,
        grid_spec=pltpu.PrefetchScalarGridSpec(
            num_scalar_prefetch=1,
            grid=(2,),
            in_specs=[
                pl.BlockSpec((n, 128), lanes),
                pl.BlockSpec((n, 128), lambda g, s: (0, 2)),
                fixed(n, 128),
                fixed(n, 128),
                fixed(8, n),
            ],
            out_specs=[
                pl.BlockSpec((n, 128), lanes),
                pl.BlockSpec((n, 128), lanes),
                pl.BlockSpec((1, 4, 1, 2 * b), lambda g, s: (g, 0, 0, 0)),
            ],
            scratch_shapes=[pltpu.VMEM((n, n), f32)],
        ),
        out_shape=[
            jax.ShapeDtypeStruct((n, 256), bf16),
            jax.ShapeDtypeStruct((n, 256), f32),
            jax.ShapeDtypeStruct((2, 4, 1, 2 * b), f32),
        ],
        compiler_params=params(26),
        cost_estimate=pl.CostEstimate(
            flops=16 * n * n * HD, bytes_accessed=4 * VMEM_MB, transcendentals=4 * n * n
        ),
        name="attend",
    )(s, qk, qk, v, start, live)


def norm_back(grad, pre, gain, cos, sin):
    turned = grad * cos - swap_halves(grad) * sin
    inv = lax.rsqrt(head_mean(pre * pre) + epsilon)
    scaled = turned * gain
    dpre = inv * scaled - pre * (inv * inv * inv) * head_mean(scaled * pre)
    return dpre, jnp.sum(turned * pre * inv, axis=0, keepdims=True)


def attend_back_kernel(s_ref, q_ref, k_ref, v_ref, qpre_ref, kpre_ref, gains_ref, kgain_ref, cos_ref, sin_ref,
                       start_ref, live_ref, out_ref, lse_ref, wout_ref, w_ref, b0, b1, b2, b3,
                       low_ref, gain_ref, lo_ref, hi_ref, bias, dk, dv, dkall, dvall, dos, gb, sems):
    g = pl.program_id(0)
    n = k_ref.shape[0]
    b = n // 4
    pieces = (b0, b1, b2, b3)

    @pl.when(g == 0)
    def _():
        for k in range(4):
            pltpu.make_async_copy(pieces[k], gb.at[k], sems.at[k]).start()
        for a in range(4):
            keys = (a + 1) * b
            start = start_ref[:1, a * b : (a + 1) * b]
            k_at = lax.broadcasted_iota(jnp.int32, (keys, b), 0)
            q_at = lax.broadcasted_iota(jnp.int32, (keys, b), 1) + a * b
            allowed = ((live_ref[:keys, :1] >= start) & (k_at <= q_at)) | (k_at == q_at)
            bias[:keys, a * b : (a + 1) * b] = jnp.where(allowed, 0.0, NEG)
        for k in range(4):
            pltpu.make_async_copy(pieces[k], gb.at[k], sems.at[k]).wait()
            dos[k] = contract(gb[k], wout_ref[...], 1, 1).astype(bf16)

    kd = twice(k_ref[...], g)
    vd = twice(v_ref[...], g)
    gain_sum = jnp.zeros((1, 128), f32)
    ones = jnp.ones((8, 128), f32)
    for a in (3, 2, 1, 0):
        keys = (a + 1) * b
        rows = slice(a * b, (a + 1) * b)
        home = s_ref[0] ^ a
        qm = both_heads(q_ref[rows, :])
        dout = jnp.where(g == 0, dos[home, :, :128], dos[home, :, 128:])
        dom = both_heads(dout)
        delta = contract(ones, both_heads(dout.astype(f32) * out_ref[rows, :]), 1, 1, lax.Precision.HIGHEST)[:1]
        scores = contract(kd[:keys], qm, 1, 1)
        extra = bias[:keys, rows]
        probs = jnp.exp(scores + (jnp.concatenate([extra, extra], 1) - lse_ref[0, a]))
        dprobs = contract(vd[:keys], dom, 1, 1)
        dscores = (probs * (dprobs - delta)).astype(bf16)
        dv_add = contract(probs.astype(bf16), dom, 1, 0)
        dk_add = contract(dscores, qm, 1, 0)
        if a == 3:
            dv[...] = dv_add
            dk[...] = dk_add
        else:
            dv[:keys] += dv_add
            dk[:keys] += dk_add
        dq = pick_heads(contract(dscores, kd[:keys], 0, 0)) * 0.125
        dpre, gain_part = norm_back(dq, qpre_ref[rows, :], gains_ref[...], cos_ref[rows, :], sin_ref[rows, :])
        at = pl.ds(pl.multiple_of(home * b, b), b)
        low_ref[at, pl.ds(pl.multiple_of(g * 128, 128), 128)] = dpre.astype(bf16)
        gain_sum = gain_sum + gain_part
    gain_ref[pl.ds(g, 1), :] = gain_sum
    lane = lax.broadcasted_iota(jnp.int32, (n, 128), 1)
    dk_all = dk[...] + pltpu.roll(dk[...], HD, 1)
    dv_all = dv[...] + pltpu.roll(dv[...], HD, 1)

    @pl.when(g == 0)
    def _():
        dkall[...] = dk_all
        dvall[...] = dv_all

    @pl.when(g == 1)
    def _():
        grad_k = jnp.where(lane < HD, dkall[...], dk_all)
        grad_v = jnp.where(lane < HD, dvall[...], dv_all)
        dpre, gain_part = norm_back(grad_k, kpre_ref[...], kgain_ref[...], cos_ref[...], sin_ref[...])
        gain_ref[2:3, :] = gain_part
        for a in range(4):
            at = pl.ds(pl.multiple_of((s_ref[0] ^ a) * b, b), b)
            low_ref[at, 256:384] = dpre[a * b : (a + 1) * b].astype(bf16)
            low_ref[at, 384:512] = grad_v[a * b : (a + 1) * b].astype(bf16)
        hi_ref[...] = contract(low_ref[2 * b :, :], w_ref[...], 1, 1).astype(bf16)
        lo_ref[...] = contract(low_ref[: 2 * b, :], w_ref[...], 1, 1).astype(bf16)


def attend_back_call(s, qk, v, pre, qgain, kgain, cos, sin, start, live, out, lse, wout, w, blocks):
    n = v.shape[0]
    b = n // 4
    d = blocks[0].shape[1]
    lanes = pl.BlockSpec((n, 128), lambda g, s: (0, g))
    third = pl.BlockSpec((n, 128), lambda g, s: (0, 2))
    return pl.pallas_call(
        attend_back_kernel,
        grid_spec=pltpu.PrefetchScalarGridSpec(
            num_scalar_prefetch=1,
            grid=(2,),
            in_specs=[lanes, third, fixed(n, 128), lanes, third, fixed(1, 128), fixed(1, 128), fixed(n, 128),
                      fixed(n, 128), fixed(8, n), fixed(n, 128), lanes,
                      pl.BlockSpec((1, 4, 1, 2 * b), lambda g, s: (g, 0, 0, 0)),
                      fixed(256, d), fixed(d, 512)] + [ANY] * 4,
            out_specs=[fixed(n, 512), fixed(8, 128), fixed(2 * b, d), fixed(2 * b, d)],
            scratch_shapes=[pltpu.VMEM((n, n), f32)]
            + [pltpu.VMEM((n, 128), f32)] * 4
            + [pltpu.VMEM((4, b, 256), bf16), pltpu.VMEM((4, b, d), bf16), pltpu.SemaphoreType.DMA((4,))],
        ),
        out_shape=[
            jax.ShapeDtypeStruct((n, 512), bf16),
            jax.ShapeDtypeStruct((8, 128), f32),
            jax.ShapeDtypeStruct((2 * b, d), bf16),
            jax.ShapeDtypeStruct((2 * b, d), bf16),
        ],
        compiler_params=params(40),
        cost_estimate=pl.CostEstimate(
            flops=40 * n * n * HD + 2 * n * d * 768, bytes_accessed=10 * VMEM_MB, transcendentals=4 * n * n
        ),
        name="attend_back",
    )(s, qk, qk, v, pre, pre, qgain, kgain, cos, sin, start, live, out, lse, wout, w, *blocks)


def ffn_kernel(s_ref, x0, x1, x2, x3, a0, a1, a2, a3, o_in, wg_own, wu_own, p0, p1,
               gain_ref, n2_ref, hid_ref, fg_ref, fu_ref, res_ref, wg, wu, wout_ref, xs, att, wout, asem, xsem, osem, gsem, usem):
    j = pl.program_id(0)
    b = x0.shape[0]
    x_in, a_in = (x0, x1, x2, x3), (a0, a1, a2, a3)
    gate_w = Weight(s_ref, (wg_own,), (p0, p1), wg, gsem)
    up_w = Weight(s_ref, (wu_own,), (p0, p1), wu, usem, wg.shape[1])

    def out_copy(i):
        return pltpu.make_async_copy(o_in.at[:, i ^ (2 * s_ref[1])], wout.at[i], osem.at[i])

    def att_copy(k, i):
        return pltpu.make_async_copy(
            a_in[i].at[pl.ds((k ^ i) * b, b), :], att.at[k, :, pl.ds(i * b, b)], asem.at[k, i]
        )

    @pl.when(j == 0)
    def _():
        for k in range(4):
            pltpu.make_async_copy(x_in[k], xs.at[k], xsem.at[k]).start()
            for i in range(4):
                att_copy(k, i).start()
            if k == 0:
                for i in range(4):
                    out_copy(i).start()
                gate_w.start()
        up_w.start()
        for i in range(4):
            out_copy(i).wait()

    pltpu.make_async_copy(x0, xs.at[j], xsem.at[j]).wait()
    for i in range(4):
        pltpu.make_async_copy(a_in[i].at[pl.ds(0, b), :], att.at[j, :, pl.ds(i * b, b)], asem.at[j, i]).wait()
    res = xs[j].astype(f32) + jnp.dot(att[j], wout[...].reshape(4 * b, -1), preferred_element_type=f32)

    @pl.when(j == 0)
    def _():
        res_ref[...] = res
        wout_ref[...] = wout[0].reshape(b, -1)
        gate_w.wait()
        up_w.wait()

    inv = lax.rsqrt(jnp.mean(res * res, axis=-1, keepdims=True) + epsilon)
    n2 = (res * inv * gain_ref[...]).astype(bf16)
    n2_ref[...] = n2
    gate = jnp.dot(n2, wg[...], preferred_element_type=f32)
    up = jnp.dot(n2, wu[...], preferred_element_type=f32)
    s = jax.nn.sigmoid(gate)
    silu = gate * s
    hid_ref[...] = (silu * up).astype(bf16)
    fg_ref[...] = (up * (s * (1.0 + gate * (1.0 - s)))).astype(bf16)
    fu_ref[...] = silu.astype(bf16)


def ffn_call(s, xs, atts, wout, wg, wu, parts, gain):
    b, d = xs[0].shape
    h = wg.shape[1]
    block = lambda wid: pl.BlockSpec((b, wid), lambda j, s: (j, 0))
    return pl.pallas_call(
        ffn_kernel,
        grid_spec=pltpu.PrefetchScalarGridSpec(
            num_scalar_prefetch=1,
            grid=(4,),
            in_specs=[ANY] * 13 + [fixed(1, d)],
            out_specs=[block(d), block(h), block(h), block(h), fixed(b, d), fixed(d, h), fixed(d, h), fixed(b, d)],
            scratch_shapes=[
                pltpu.VMEM((4, b, d), bf16),
                pltpu.VMEM((4, b, 4 * b), bf16),
                pltpu.VMEM((4,) + wout.shape[:1] + wout.shape[2:], bf16),
                pltpu.SemaphoreType.DMA((4, 4)),
                pltpu.SemaphoreType.DMA((4,)),
                pltpu.SemaphoreType.DMA((4,)),
                pltpu.SemaphoreType.DMA((9,)),
                pltpu.SemaphoreType.DMA((9,)),
            ],
        ),
        out_shape=[jax.ShapeDtypeStruct((4 * b, d), bf16)]
        + [jax.ShapeDtypeStruct((4 * b, h), bf16)] * 3
        + [jax.ShapeDtypeStruct((b, d), f32)]
        + [jax.ShapeDtypeStruct((d, h), bf16)] * 2
        + [jax.ShapeDtypeStruct((b, d), bf16)],
        compiler_params=params(34),
        cost_estimate=pl.CostEstimate(
            flops=8 * b * d * (d + 2 * h), bytes_accessed=25 * VMEM_MB, transcendentals=4 * b * h
        ),
        name="ffn",
    )(s, *xs, *atts, wout, wg, wu, *parts, gain)


def ffn_back_kernel(s_ref, y0, y1, y2, y3, wd_own, d0, d1, fg_ref, fu_ref, wg_in, wu_in,
                    gg_ref, gu_ref, lo_ref, hi_ref, wd, dy, wg, wu, ysem, dsem, wsem):
    j = pl.program_id(0)
    y_in = (y0, y1, y2, y3)
    down_w = Weight(s_ref, (wd_own,), (d0, d1), wd, dsem)

    @pl.when(j == 0)
    def _():
        for k in range(4):
            pltpu.make_async_copy(y_in[k], dy.at[k], ysem.at[k]).start()
        down_w.start()
        pltpu.make_async_copy(wg_in, wg, wsem.at[0]).start()
        pltpu.make_async_copy(wu_in, wu, wsem.at[1]).start()
        down_w.wait()

    pltpu.make_async_copy(y0, dy.at[j], ysem.at[j]).wait()
    gh = contract(dy[j], wd[...], 1, 1)
    gg = (gh * fg_ref[...].astype(f32)).astype(bf16)
    gu = (gh * fu_ref[...].astype(f32)).astype(bf16)
    gg_ref[...] = gg
    gu_ref[...] = gu

    @pl.when(j == 0)
    def _():
        pltpu.make_async_copy(wg_in, wg, wsem.at[0]).wait()
        pltpu.make_async_copy(wu_in, wu, wsem.at[1]).wait()

    grad = (contract(gg, wg[...], 1, 1) + contract(gu, wu[...], 1, 1)).astype(bf16)

    @pl.when(j < 2)
    def _():
        lo_ref[...] = grad

    @pl.when(j >= 2)
    def _():
        hi_ref[...] = grad


def ffn_back_call(s, dys, wd, d_parts, fg, fu, wg, wu):
    b, d = dys[0].shape
    h = wg.shape[1]
    block = lambda wid: pl.BlockSpec((b, wid), lambda j, s: (j, 0))
    return pl.pallas_call(
        ffn_back_kernel,
        grid_spec=pltpu.PrefetchScalarGridSpec(
            num_scalar_prefetch=1,
            grid=(4,),
            in_specs=[ANY] * 7 + [block(h), block(h), ANY, ANY],
            out_specs=[
                block(h),
                block(h),
                pl.BlockSpec((b, d), lambda j, s: (jnp.minimum(j, 1), 0)),
                pl.BlockSpec((b, d), lambda j, s: (jnp.maximum(j - 2, 0), 0)),
                fixed(h, d),
            ],
            scratch_shapes=[
                pltpu.VMEM((4, b, d), bf16),
                pltpu.VMEM((d, h), bf16),
                pltpu.VMEM((d, h), bf16),
                pltpu.SemaphoreType.DMA((4,)),
                pltpu.SemaphoreType.DMA((9,)),
                pltpu.SemaphoreType.DMA((2,)),
            ],
        ),
        out_shape=[jax.ShapeDtypeStruct((4 * b, h), bf16)] * 2
        + [jax.ShapeDtypeStruct((2 * b, d), bf16)] * 2
        + [jax.ShapeDtypeStruct((h, d), bf16)],
        compiler_params=params(34),
        cost_estimate=pl.CostEstimate(flops=24 * b * d * h, bytes_accessed=22 * VMEM_MB, transcendentals=0),
        name="ffn_back",
    )(s, *dys, wd, *d_parts, fg, fu, wg, wu)


def grad_rows_kernel(by_cols, s_ref, left_ref, right_ref, sent_a, keep_a, sent_b, keep_b):
    j = pl.program_id(0)
    grad = contract(left_ref[...], right_ref[...], 0, 0).astype(bf16)
    rows, cols = grad.shape
    if by_cols:
        first, second = grad[:, : cols // 2], grad[:, cols // 2 :]
    else:
        r = rows // 4
        first = jnp.concatenate([grad[:r], grad[2 * r : 3 * r]], 0)
        second = jnp.concatenate([grad[r : 2 * r], grad[3 * r :]], 0)

    @pl.when(j % 2 == 1)
    def _():
        sent_a[0] = first

    @pl.when(j % 2 == 0)
    def _():
        keep_a[0] = first

    @pl.when(j >= 2)
    def _():
        sent_b[0] = second

    @pl.when(j < 2)
    def _():
        keep_b[0] = second


def grad_rows_call(s, left, right, by_cols, name):
    n, rows = left.shape
    cols = right.shape[1]
    half = (rows // 4, cols // 2) if by_cols else (rows // 8, cols)
    maps = [
        lambda j, s: (j // 2, 0, 0),
        lambda j, s: (j // 2, 0, 0),
        lambda j, s: (jnp.maximum(j - 2, 0), 0, 0),
        lambda j, s: (jnp.minimum(j, 1), 0, 0),
    ]
    return pl.pallas_call(
        functools.partial(grad_rows_kernel, by_cols),
        grid_spec=pltpu.PrefetchScalarGridSpec(
            num_scalar_prefetch=1,
            grid=(4,),
            in_specs=[pl.BlockSpec((n, rows // 4), lambda j, s: (0, s[2] ^ j)), fixed(n, cols)],
            out_specs=[pl.BlockSpec((1,) + half, m) for m in maps],
        ),
        out_shape=[jax.ShapeDtypeStruct((2,) + half, bf16)] * 4,
        compiler_params=params(24),
        cost_estimate=pl.CostEstimate(flops=2 * n * rows * cols, bytes_accessed=4 * n * (rows + cols), transcendentals=0),
        name=name,
    )(s, left, right)


def grad_cols_kernel(s_ref, left_ref, r0, r1, r2, r3, sent_a, keep_a, sent_b, keep_b):
    k = pl.program_id(0)
    b = r0.shape[0]
    grad = None
    for i, right in enumerate((r0, r1, r2, r3)):
        part = contract(left_ref[i * b : (i + 1) * b, :], right[...], 0, 0)
        grad = part if grad is None else grad + part
    grad = grad.astype(bf16)
    rows = grad.shape[0] // 4
    for a in range(4):
        piece = grad[a * rows : (a + 1) * rows]
        j = s_ref[2] ^ a

        @pl.when((k < 2) & (j % 2 == 1))
        def _():
            sent_a[j // 2] = piece

        @pl.when((k < 2) & (j % 2 == 0))
        def _():
            keep_a[j // 2] = piece

        @pl.when((k >= 2) & (j >= 2))
        def _():
            sent_b[j % 2] = piece

        @pl.when((k >= 2) & (j < 2))
        def _():
            keep_b[j % 2] = piece


def grad_cols_call(s, left, rights, name):
    n, rows = left.shape
    b, cols = rights[0].shape
    first = pl.BlockSpec((2, rows // 4, cols // 4), lambda k, s: (0, 0, jnp.minimum(k, 1)))
    second = pl.BlockSpec((2, rows // 4, cols // 4), lambda k, s: (0, 0, jnp.maximum(k - 2, 0)))
    return pl.pallas_call(
        grad_cols_kernel,
        grid_spec=pltpu.PrefetchScalarGridSpec(
            num_scalar_prefetch=1,
            grid=(4,),
            in_specs=[fixed(n, rows)] + [pl.BlockSpec((b, cols // 4), lambda k, s: (0, k))] * 4,
            out_specs=[first, first, second, second],
        ),
        out_shape=[jax.ShapeDtypeStruct((2, rows // 4, cols // 2), bf16)] * 4,
        compiler_params=params(24),
        cost_estimate=pl.CostEstimate(flops=2 * n * rows * cols, bytes_accessed=4 * n * (rows + cols), transcendentals=0),
        name=name,
    )(s, left, *rights)


def permute(x, places, move):
    pairs = []
    for d in range(places):
        for t in range(T4):
            to = move(d, t)
            if to is not None:
                pairs.append((d * T4 + t, to[0] * T4 + to[1]))
    return lax.ppermute(x, AX, pairs)


def after(x, *events):
    return lax.optimization_barrier((x, events))[0]


def flip_core(d, t):
    return (d ^ 1, t)


def flip_z(d, t):
    return (d, t ^ 1)


def flip_far(d, t):
    return (d, t ^ 2)


def flip_e(bit):
    return lambda d, t: (d ^ (2 << bit), t)


def settle(d, t):
    return (d, t) if (d & 1) == (t >> 1) else (d ^ 1, t ^ 2)


def gather_row(x, n):
    over = permute(x, n, flip_z)
    near = permute(x, n, flip_core)
    far = permute(over, n, flip_core)
    return [x, over, near, far]


def scatter_row(low, high, n, *events):
    b = low.shape[0] // 2
    got = permute(high, n, flip_core)
    over = permute(low[b:] + got[b:], n, flip_z)
    return low[:b] + got[:b] + (after(over, *events) if events else over)


def hop(weights, n, c, e):
    rows = weights[0].shape[0] // 8
    mine = [lax.dynamic_slice_in_dim(w, (2 * e + c) * rows, rows, 0) for w in weights]
    return permute(jnp.concatenate(mine, 1) if len(mine) > 1 else mine[0], n, flip_far)


def spread(piece, n):
    mine = jnp.concatenate([piece] + [permute(piece, n, lambda d, t, j=j: (d ^ (2 * j), t)) for j in (1, 2, 3)])
    return mine, permute(mine, n, flip_core)


def first_sums(pieces, n):
    sent_a, keep_a, sent_b, keep_b = pieces
    got_a = permute(sent_a, n, flip_e(0))
    got_b = permute(sent_b, n, flip_e(1))
    return got_a, got_b


def first_add(pieces, got):
    got_a, got_b = got
    keep_a, keep_b = pieces[1], pieces[3]
    return keep_a[1] + got_a[1], keep_a[0] + got_a[0], keep_b[1] + got_b[1], keep_b[0] + got_b[0]


def second_sums(halves, n):
    return permute(halves[0], n, flip_e(1)), permute(halves[2], n, flip_e(0))


def second_add(halves, got, n):
    total = jnp.stack([halves[1] + got[0], halves[3] + got[1]])
    for extra in range(2, 20):
        if (2 << extra) < n:
            total = total + permute(total, n, flip_e(extra))
    return total


def owner_cross(total, n, c):
    half = total.shape[1] // 2
    first, second = total[:, :half], total[:, half:]
    got = permute(jnp.where(c == 0, second, first), n, flip_core)
    return jnp.where(c == 0, first, got), permute(jnp.where(c == 0, got, second), n, flip_far)


def neighbours(n):
    return None if n == 8 else [list(range(k, k + 8)) for k in range(0, n, 8)]


def whole_grad(mine, n):
    return lax.all_gather(mine, "dp", axis_index_groups=neighbours(n))


def whole_out(w, n, c, e):
    rows = w.shape[0] // 8
    mine = lax.dynamic_slice_in_dim(w, (2 * e + c) * rows, rows, 0)
    two = jnp.stack([mine, permute(mine, n, flip_z)])
    four = jnp.concatenate([two, permute(two, n, flip_far)])
    return lax.all_gather(four, "dp", axis_index_groups=neighbours(n))


def sum_all(vec, n):
    bit = 1
    while bit < n:
        vec = vec + permute(vec, n, lambda d, t, bit=bit: (d ^ bit, t))
        bit *= 2
    for bit in (1, 2):
        vec = vec + permute(vec, n, lambda d, t, bit=bit: (d, t ^ bit))
    return vec


def local(
    block_input,
    doc_lengths,
    pad_mask,
    norm1_gain,
    w_query,
    w_key,
    w_value,
    query_gain,
    key_gain,
    w_out,
    norm2_gain,
    w_gate,
    w_up,
    w_down,
    cotangent,
):
    n = lax.axis_size("dp")
    d, t = lax.axis_index("dp"), lax.axis_index("tensor")
    c, p = d & 1, t >> 1
    e = (d >> 1) & 3
    shard = 2 * c + (t & 1)
    b = block_input.shape[0]
    seq_len = b * T4
    home = c == p
    wq = w_query.shape[1]
    wk = w_key.shape[1]
    width = block_input.shape[1]
    s = jnp.stack([shard, c, e]).astype(jnp.int32)

    x_own = permute(block_input, n, settle)
    marks = jnp.concatenate([doc_lengths, pad_mask], 1)
    marks = jnp.where(home, marks, permute(marks, n, flip_core))
    lengths_row, pad_row = marks[0, : doc_lengths.shape[1]], marks[0, doc_lengths.shape[1] :]
    qkv_hop = hop((w_query, w_key, w_value), n, c, e)
    x_blocks = gather_row(x_own, n)
    qkv_parts = spread(qkv_hop, n)
    gate_up_hop = hop((after(w_gate, x_blocks[2]), w_up), n, c, e)
    out_all = whole_out(after(w_out, x_blocks[2]), n, c, e)

    positions = jnp.arange(seq_len, dtype=jnp.int32)
    doc_starts, cos_half, sin_half = doc_tables(lengths_row, positions, HD)
    cos = jnp.concatenate([cos_half] * 4, 1)
    sin = jnp.concatenate([-sin_half, sin_half] * 2, 1)
    live = jnp.where(pad_row == 1, positions, -1)
    start_col = jnp.broadcast_to(doc_starts[:, None], (seq_len, 128))
    start_row = jnp.broadcast_to(doc_starts[None], (8, seq_len))
    live_col = jnp.broadcast_to(live[:, None], (seq_len, 128))
    live_row = jnp.broadcast_to(live[None], (8, seq_len))
    gains = jnp.concatenate([query_gain] * (wq // HD) + [key_gain] * (wk // HD))[None]
    qgain_pair = jnp.concatenate([query_gain] * 2)[None]
    kgain_pair = jnp.concatenate([key_gain] * 2)[None]

    rows_one, pre, qk, values, w_qkv = qkv_call(
        s, x_blocks, (w_query, w_key, w_value), qkv_parts, norm1_gain[None], gains, cos, sin
    )
    attended, attended_f, lse = attend_call(s, qk, values, start_col, live_row)
    att_pieces = gather_row(attended, n)
    gate_up_parts = spread(after(gate_up_hop, attended), n)
    down_hop = hop((after(w_down, attended),), n, c, e)
    dy_own = permute(after(cotangent, attended), n, settle)
    down_parts = spread(after(down_hop, att_pieces[1]), n)
    dy_blocks = gather_row(after(dy_own, att_pieces[1]), n)
    rows_two, hidden, by_gate, by_up, residual, wg, wu, w_out_own = ffn_call(
        s, x_blocks, att_pieces, out_all, w_gate, w_up, gate_up_parts, after(norm2_gain[None], dy_own)
    )

    down = grad_cols_call(s, hidden, dy_blocks, "grad_down")
    gate_grad, up_grad, low2, high2, wd = ffn_back_call(
        s, dy_blocks, w_down, down_parts, after(by_gate, *down), by_up, wg, wu
    )
    down_got = first_sums(down, n)
    down = first_add(down, after(down_got, low2))
    down_got = second_sums(down, n)
    gate = grad_rows_call(s, rows_two, after(gate_grad, *down), False, "grad_gate")
    gate_got = first_sums(gate, n)
    up = grad_rows_call(s, rows_two, after(up_grad, *gate), False, "grad_up")
    up_got = first_sums(up, n)
    grad_n2 = scatter_row(low2, high2, n, *up).astype(f32)
    inv = lax.rsqrt(jnp.mean(residual * residual, axis=-1, keepdims=True) + epsilon)
    scaled = norm2_gain * grad_n2
    grad_residual = (
        dy_own.astype(f32)
        + inv * scaled
        - residual * (inv * inv * inv) * jnp.mean(scaled * residual, axis=-1, keepdims=True)
    )
    grad_norm2 = jnp.sum(grad_n2 * residual * inv, axis=0)
    gb_own = grad_residual.astype(bf16)
    gb_blocks = gather_row(gb_own, n)

    down = second_add(down, after(down_got, gb_own), n)
    down_kept, down_got = owner_cross(down, n, c)
    ffn_part = jnp.dot(after(hidden, down_kept), wd, preferred_element_type=f32).astype(bf16)
    gate = first_add(gate, after(gate_got, ffn_part))
    gate_got = second_sums(gate, n)
    up = first_add(up, after(up_got, gb_blocks[1], *gate))
    up_got = second_sums(up, n)
    down_mine = down_kept + after(down_got, gb_blocks[3], *up)
    down_all = whole_grad(down_mine, n)
    gate = second_add(gate, after(gate_got, down_mine), n)
    gate_kept, gate_got = owner_cross(gate, n, c)
    ffn_got = permute(ffn_part[2 * b :], n, flip_core)
    ffn_half = ffn_part[: 2 * b] + after(ffn_got, gb_blocks[3])
    ffn_over = permute(ffn_half[b:], n, flip_z)

    low, gain_terms, low1, high1 = attend_back_call(
        s, qk, after(values, gate_kept, ffn_half), pre, qgain_pair, kgain_pair, cos, sin, start_row, live_col, attended_f,
        lse, w_out_own, w_qkv, gb_blocks,
    )
    high_got = permute(high1, n, flip_core)
    gate_mine = gate_kept + after(gate_got, low)
    gate_all = whole_grad(gate_mine, n)
    low_half = low1 + after(high_got, gate_mine)
    low_over = permute(low_half[b:], n, flip_z)
    up = second_add(up, after(up_got, low_half), n)
    up_kept, up_got = owner_cross(up, n, c)
    block_output = residual + (ffn_half[:b] + after(ffn_over, low_half, up)).astype(f32)
    settled_output = permute(block_output.astype(bf16), n, settle)
    qkv = grad_rows_call(s, rows_one, after(low, up_kept, block_output), True, "grad_qkv")
    qkv_got = first_sums(qkv, n)
    out = grad_cols_call(s, after(attended, *qkv), gb_blocks, "grad_out")
    out_got = first_sums(out, n)

    grad_n1 = (low_half[:b] + after(low_over, *out)).astype(f32)
    x_f = x_own.astype(f32)
    inv = lax.rsqrt(jnp.mean(x_f * x_f, axis=-1, keepdims=True) + epsilon)
    scaled = norm1_gain * grad_n1
    input_grad = (
        grad_residual
        + inv * scaled
        - x_f * (inv * inv * inv) * jnp.mean(scaled * x_f, axis=-1, keepdims=True)
    )
    grad_norm1 = jnp.sum(grad_n1 * x_f * inv, axis=0)
    settled_grad = permute(input_grad.astype(bf16), n, settle)
    up_mine = up_kept + after(up_got, input_grad)
    up_all = whole_grad(up_mine, n)
    qkv = first_add(qkv, after(qkv_got, up_mine))
    qkv_got = second_sums(qkv, n)
    out = first_add(out, after(out_got, *qkv))
    out_got = second_sums(out, n)
    head_terms = gain_terms[:, :HD] + gain_terms[:, HD:]
    vec = jnp.concatenate([grad_norm1, grad_norm2, head_terms[0] + head_terms[1], head_terms[2]])
    vec = sum_all(after(vec, *out)[None], n)[0]
    qkv = second_add(qkv, after(qkv_got, vec), n)
    out = second_add(out, after(out_got, vec), n)
    qkv_kept, qkv_got = owner_cross(qkv, n, c)
    out_kept, out_got = owner_cross(out, n, c)
    qkv_all = whole_grad(qkv_kept + qkv_got, n)
    out_all = whole_grad(out_kept + out_got, n)
    block_output = jnp.where(home, block_output, after(settled_output, qkv_kept, out_kept).astype(f32))
    input_grad = jnp.where(home, input_grad, after(settled_grad, qkv_kept, out_kept).astype(f32))

    def rows(whole):
        return whole.astype(f32).reshape(width, -1)

    def side_by_side(whole):
        return whole.astype(f32).transpose(0, 2, 1, 3).reshape(-1, width)

    grad_down = side_by_side(down_all)
    grad_gate = rows(gate_all)
    grad_up = rows(up_all)
    grad_out = side_by_side(out_all)
    grad_query = rows(qkv_all[:, 0])
    grad_kv = rows(qkv_all[:, 1])
    return (
        block_output,
        input_grad,
        vec[:width],
        grad_query,
        grad_kv[:, :wk],
        grad_kv[:, wk:],
        vec[2 * width : 2 * width + HD],
        vec[2 * width + HD :],
        grad_out,
        vec[width : 2 * width],
        grad_gate,
        grad_up,
        grad_down,
    )


def solution(mesh):
    placed = (
        P(("dp", "tensor"), None),
        P("dp", None),
        P("dp", None),
        P(),
        P(None, "tensor"),
        P(None, "tensor"),
        P(None, "tensor"),
        P(),
        P(),
        P("tensor", None),
        P(),
        P(None, "tensor"),
        P(None, "tensor"),
        P("tensor", None),
        P(("dp", "tensor"), None),
    )
    return jax.shard_map(
        local,
        mesh=mesh,
        in_specs=placed,
        out_specs=(
            P(("dp", "tensor"), None),
            P(("dp", "tensor"), None),
            P(),
            P(None, "tensor"),
            P(None, "tensor"),
            P(None, "tensor"),
            P(),
            P(),
            P("tensor", None),
            P(),
            P(None, "tensor"),
            P(None, "tensor"),
            P("tensor", None),
        ),
        check_vma=False,
    )
```

```python
import functools
import math

import jax
import jax.numpy as jnp
from jax import lax
from jax.experimental import pallas as pl
from jax.experimental.pallas import tpu as pltpu
from jax.sharding import PartitionSpec as P

HD = 64
AX = ("dp", "tensor")
T4 = 4
VMEM_MB = 1 << 20

epsilon = 1e-05
rope_base = 1000000.0
NEG = -1000000000.0
bf16 = jnp.bfloat16
f32 = jnp.float32


def doc_tables(lengths_row, positions, head_dim):
    doc_ends = jnp.cumsum(lengths_row)
    passed = positions[:, None] >= doc_ends[None, :]
    doc_starts = jnp.sum(jnp.where(passed, lengths_row[None, :], 0), axis=1)
    offsets = (positions - doc_starts).astype(f32)
    freqs = jnp.exp(
        jnp.arange(head_dim // 2, dtype=f32) * (-2.0 * math.log(rope_base) / head_dim)
    )
    angles = offsets[:, None] * freqs[None, :]
    return (doc_starts, jnp.cos(angles), jnp.sin(angles))


def contract(a, b, da, db, precision=None):
    return lax.dot_general(
        a, b, (((da,), (db,)), ((), ())), preferred_element_type=f32, precision=precision
    )


def swap_halves(y):
    width = y.shape[1]
    lane = lax.broadcasted_iota(jnp.int32, y.shape, 1)
    return jnp.where(lane % HD < HD // 2, pltpu.roll(y, width - HD // 2, 1), pltpu.roll(y, HD // 2, 1))


def head_mean(y):
    width = y.shape[1]
    at = lax.broadcasted_iota(jnp.int32, (width, width), 0) // HD
    to = lax.broadcasted_iota(jnp.int32, (width, width), 1) // HD
    ones = jnp.where(at == to, 1.0 / HD, 0.0).astype(f32)
    return contract(y, ones, 1, 0, lax.Precision.HIGHEST)


class Weight:
    def __init__(self, s_ref, own, parts, to, sems, start=0):
        self.core, self.e = s_ref[1], s_ref[2]
        self.own, self.parts, self.to, self.sems, self.start_col = own, parts, to, sems, start

    def copies(self):
        start = 0
        for i, w in enumerate(self.own):
            wide = w.shape[1]
            to = self.to if len(self.own) == 1 else self.to.at[:, pl.ds(start, wide)]
            yield 0, functools.partial(pltpu.make_async_copy, w, to, self.sems.at[8 + i])
            start += wide
        rows = self.to.shape[0] // 8
        for j in range(4):
            for other in range(2):
                at = pl.multiple_of((2 * (self.e ^ j) + 1 - other) * rows, rows)
                src = self.parts[other].at[pl.ds(j * rows, rows), pl.ds(self.start_col, self.to.shape[1])]
                yield 1, functools.partial(
                    pltpu.make_async_copy, src, self.to.at[pl.ds(at, rows), :], self.sems.at[2 * j + other]
                )

    def each(self, act):
        for core in range(2):

            @pl.when(self.core == core)
            def _():
                for whose, copy in self.copies():
                    if whose == core:
                        act(copy())

    def start(self):
        self.each(lambda copy: copy.start())

    def wait(self):
        self.each(lambda copy: copy.wait())


ANY = pl.BlockSpec(memory_space=pl.ANY)


def fixed(*shape):
    return pl.BlockSpec(shape, lambda *_: (0,) * len(shape))


def cost(flops):
    return pl.CostEstimate(flops=flops, bytes_accessed=1 << 16, transcendentals=0)


def params(mib):
    return pltpu.CompilerParams(vmem_limit_bytes=mib * VMEM_MB)


def qkv_kernel(s_ref, x0, x1, x2, x3, wq_own, wk_own, wv_own, w0, w1, g1_ref, gains_ref, cos_ref, sin_ref,
               n1_ref, pre_ref, qk_ref, v_ref, w_ref, xs, xsem, wsem):
    j = pl.program_id(0)
    pieces = (x0, x1, x2, x3)
    weight = Weight(s_ref, (wq_own, wk_own, wv_own), (w0, w1), w_ref, wsem)

    @pl.when(j == 0)
    def _():
        for k in range(4):
            pltpu.make_async_copy(pieces[k], xs.at[k], xsem.at[k]).start()
        weight.start()

    pltpu.make_async_copy(x0, xs.at[j], xsem.at[j]).wait()
    x = xs[j].astype(f32)
    inv = lax.rsqrt(jnp.mean(x * x, axis=-1, keepdims=True) + epsilon)
    n1 = (x * inv * g1_ref[...]).astype(bf16)
    n1_ref[...] = n1

    @pl.when(j == 0)
    def _():
        weight.wait()

    qkv = jnp.dot(n1, w_ref[...], preferred_element_type=f32)
    width = pre_ref.shape[1]
    pre = qkv[:, :width]
    pre_ref[...] = pre
    v_ref[...] = qkv[:, width:].astype(bf16)
    y = pre * lax.rsqrt(head_mean(pre * pre) + epsilon) * gains_ref[...]
    cos = jnp.concatenate([cos_ref[...]] * (width // 128), 1)
    sin = jnp.concatenate([sin_ref[...]] * (width // 128), 1)
    qk = (y * cos + swap_halves(y) * sin).astype(bf16)
    lane = lax.broadcasted_iota(jnp.int32, qk.shape, 1)
    qk_ref[...] = jnp.where(lane < width - 128, qk * 0.125, qk).astype(bf16)


def qkv_call(s, xs, w_own, w_parts, g1, gains, cos, sin):
    b, d = xs[0].shape
    wid = w_parts[0].shape[1]
    qkw = wid - 128
    natural = lambda j, s: (s[0] ^ j, 0)
    return pl.pallas_call(
        qkv_kernel,
        grid_spec=pltpu.PrefetchScalarGridSpec(
            num_scalar_prefetch=1,
            grid=(4,),
            in_specs=[ANY] * 9
            + [fixed(1, d), fixed(1, qkw), pl.BlockSpec((b, 128), natural), pl.BlockSpec((b, 128), natural)],
            out_specs=[
                pl.BlockSpec((b, d), lambda j, s: (j, 0)),
                pl.BlockSpec((b, qkw), natural),
                pl.BlockSpec((b, qkw), natural),
                pl.BlockSpec((b, 128), natural),
                fixed(d, wid),
            ],
            scratch_shapes=[
                pltpu.VMEM((4, b, d), bf16),
                pltpu.SemaphoreType.DMA((4,)),
                pltpu.SemaphoreType.DMA((11,)),
            ],
        ),
        out_shape=[
            jax.ShapeDtypeStruct((4 * b, d), bf16),
            jax.ShapeDtypeStruct((4 * b, qkw), f32),
            jax.ShapeDtypeStruct((4 * b, qkw), bf16),
            jax.ShapeDtypeStruct((4 * b, 128), bf16),
            jax.ShapeDtypeStruct((d, wid), bf16),
        ],
        compiler_params=params(12),
        cost_estimate=cost(1 << 24),
        name="qkv",
    )(s, *xs, *w_own, *w_parts, g1, gains, cos, sin)


def both_heads(pair):
    lane = lax.broadcasted_iota(jnp.int32, pair.shape, 1)
    zero = jnp.zeros_like(pair)
    return jnp.concatenate([jnp.where(lane < HD, pair, zero), jnp.where(lane < HD, zero, pair)], 0)


def pick_heads(both):
    r = both.shape[0] // 2
    lane = lax.broadcasted_iota(jnp.int32, (r, 128), 1)
    return jnp.where(lane < HD, both[:r], both[r:])


def twice(kv, g):
    lane = lax.broadcasted_iota(jnp.int32, kv.shape, 1)
    turned = pltpu.roll(kv.astype(f32), HD, 1).astype(kv.dtype)
    return jnp.where((lane < HD) == (g == 0), kv, turned)


def attend_kernel(s_ref, q_ref, k_ref, v_ref, start_ref, live_ref, att_ref, out_ref, lse_ref, bias):
    g = pl.program_id(0)
    n = k_ref.shape[0]
    b = n // 4

    @pl.when(g == 0)
    def _():
        for a in range(4):
            keys = (a + 1) * b
            start = start_ref[a * b : (a + 1) * b, :1]
            q_at = lax.broadcasted_iota(jnp.int32, (b, keys), 0) + a * b
            k_at = lax.broadcasted_iota(jnp.int32, (b, keys), 1)
            allowed = ((live_ref[:1, :keys] >= start) & (k_at <= q_at)) | (k_at == q_at)
            bias[a * b : (a + 1) * b, :keys] = jnp.where(allowed, 0.0, NEG)

    kd = twice(k_ref[...], g)
    vd = twice(v_ref[...], g)
    for a in range(4):
        keys = (a + 1) * b
        rows = slice(a * b, (a + 1) * b)
        qm = both_heads(q_ref[rows, :])
        scores = contract(qm, kd[:keys], 1, 1)
        extra = bias[rows, :keys]
        expo = jnp.exp(scores + jnp.concatenate([extra, extra], 0))
        total = jnp.sum(expo, axis=-1, keepdims=True)
        pair = pick_heads(contract(expo.astype(bf16), vd[:keys], 1, 0) / total)
        out_ref[rows, :] = pair
        att_ref[pl.ds(pl.multiple_of((s_ref[0] ^ a) * b, b), b), :] = pair.astype(bf16)
        lse_ref[0, a] = jnp.transpose(jnp.broadcast_to(jnp.log(total), (2 * b, 128)))[:1]


def attend_call(s, qk, v, start, live):
    n = qk.shape[0]
    b = n // 4
    lanes = lambda g, s: (0, g)
    return pl.pallas_call(
        attend_kernel,
        grid_spec=pltpu.PrefetchScalarGridSpec(
            num_scalar_prefetch=1,
            grid=(2,),
            in_specs=[
                pl.BlockSpec((n, 128), lanes),
                pl.BlockSpec((n, 128), lambda g, s: (0, 2)),
                fixed(n, 128),
                fixed(n, 128),
                fixed(8, n),
            ],
            out_specs=[
                pl.BlockSpec((n, 128), lanes),
                pl.BlockSpec((n, 128), lanes),
                pl.BlockSpec((1, 4, 1, 2 * b), lambda g, s: (g, 0, 0, 0)),
            ],
            scratch_shapes=[pltpu.VMEM((n, n), f32)],
        ),
        out_shape=[
            jax.ShapeDtypeStruct((n, 256), bf16),
            jax.ShapeDtypeStruct((n, 256), f32),
            jax.ShapeDtypeStruct((2, 4, 1, 2 * b), f32),
        ],
        compiler_params=params(14),
        cost_estimate=cost(1 << 24),
        name="attend",
    )(s, qk, qk, v, start, live)


def norm_back(grad, pre, gain, cos, sin):
    turned = grad * cos - swap_halves(grad) * sin
    inv = lax.rsqrt(head_mean(pre * pre) + epsilon)
    scaled = turned * gain
    dpre = inv * scaled - pre * (inv * inv * inv) * head_mean(scaled * pre)
    return dpre, jnp.sum(turned * pre * inv, axis=0, keepdims=True)


def attend_back_kernel(s_ref, q_ref, k_ref, v_ref, qpre_ref, kpre_ref, gains_ref, kgain_ref, cos_ref, sin_ref,
                       start_ref, live_ref, out_ref, lse_ref, wout_ref, w_ref, b0, b1, b2, b3,
                       low_ref, gain_ref, lo_ref, hi_ref, bias, dk, dv, dkall, dvall, dos, gb, sems):
    g = pl.program_id(0)
    n = k_ref.shape[0]
    b = n // 4
    pieces = (b0, b1, b2, b3)

    @pl.when(g == 0)
    def _():
        for k in range(4):
            pltpu.make_async_copy(pieces[k], gb.at[k], sems.at[k]).start()
        for a in range(4):
            keys = (a + 1) * b
            start = start_ref[:1, a * b : (a + 1) * b]
            k_at = lax.broadcasted_iota(jnp.int32, (keys, b), 0)
            q_at = lax.broadcasted_iota(jnp.int32, (keys, b), 1) + a * b
            allowed = ((live_ref[:keys, :1] >= start) & (k_at <= q_at)) | (k_at == q_at)
            bias[:keys, a * b : (a + 1) * b] = jnp.where(allowed, 0.0, NEG)
        for k in range(4):
            pltpu.make_async_copy(pieces[k], gb.at[k], sems.at[k]).wait()
            dos[k] = contract(gb[k], wout_ref[...], 1, 1).astype(bf16)

    kd = twice(k_ref[...], g)
    vd = twice(v_ref[...], g)
    gain_sum = jnp.zeros((1, 128), f32)
    ones = jnp.ones((8, 128), f32)
    for a in (3, 2, 1, 0):
        keys = (a + 1) * b
        rows = slice(a * b, (a + 1) * b)
        home = s_ref[0] ^ a
        qm = both_heads(q_ref[rows, :])
        dout = jnp.where(g == 0, dos[home, :, :128], dos[home, :, 128:])
        dom = both_heads(dout)
        delta = contract(ones, both_heads(dout.astype(f32) * out_ref[rows, :]), 1, 1, lax.Precision.HIGHEST)[:1]
        scores = contract(kd[:keys], qm, 1, 1)
        extra = bias[:keys, rows]
        probs = jnp.exp(scores + (jnp.concatenate([extra, extra], 1) - lse_ref[0, a]))
        dprobs = contract(vd[:keys], dom, 1, 1)
        dscores = (probs * (dprobs - delta)).astype(bf16)
        dv_add = contract(probs.astype(bf16), dom, 1, 0)
        dk_add = contract(dscores, qm, 1, 0)
        if a == 3:
            dv[...] = dv_add
            dk[...] = dk_add
        else:
            dv[:keys] += dv_add
            dk[:keys] += dk_add
        dq = pick_heads(contract(dscores, kd[:keys], 0, 0)) * 0.125
        dpre, gain_part = norm_back(dq, qpre_ref[rows, :], gains_ref[...], cos_ref[rows, :], sin_ref[rows, :])
        at = pl.ds(pl.multiple_of(home * b, b), b)
        low_ref[at, pl.ds(pl.multiple_of(g * 128, 128), 128)] = dpre.astype(bf16)
        gain_sum = gain_sum + gain_part
    gain_ref[pl.ds(g, 1), :] = gain_sum
    lane = lax.broadcasted_iota(jnp.int32, (n, 128), 1)
    dk_all = dk[...] + pltpu.roll(dk[...], HD, 1)
    dv_all = dv[...] + pltpu.roll(dv[...], HD, 1)

    @pl.when(g == 0)
    def _():
        dkall[...] = dk_all
        dvall[...] = dv_all

    @pl.when(g == 1)
    def _():
        grad_k = jnp.where(lane < HD, dkall[...], dk_all)
        grad_v = jnp.where(lane < HD, dvall[...], dv_all)
        dpre, gain_part = norm_back(grad_k, kpre_ref[...], kgain_ref[...], cos_ref[...], sin_ref[...])
        gain_ref[2:3, :] = gain_part
        for a in range(4):
            at = pl.ds(pl.multiple_of((s_ref[0] ^ a) * b, b), b)
            low_ref[at, 256:384] = dpre[a * b : (a + 1) * b].astype(bf16)
            low_ref[at, 384:512] = grad_v[a * b : (a + 1) * b].astype(bf16)
        hi_ref[...] = contract(low_ref[2 * b :, :], w_ref[...], 1, 1).astype(bf16)
        lo_ref[...] = contract(low_ref[: 2 * b, :], w_ref[...], 1, 1).astype(bf16)


def attend_back_call(s, qk, v, pre, qgain, kgain, cos, sin, start, live, out, lse, wout, w, blocks):
    n = v.shape[0]
    b = n // 4
    d = blocks[0].shape[1]
    lanes = pl.BlockSpec((n, 128), lambda g, s: (0, g))
    third = pl.BlockSpec((n, 128), lambda g, s: (0, 2))
    return pl.pallas_call(
        attend_back_kernel,
        grid_spec=pltpu.PrefetchScalarGridSpec(
            num_scalar_prefetch=1,
            grid=(2,),
            in_specs=[lanes, third, fixed(n, 128), lanes, third, fixed(1, 128), fixed(1, 128), fixed(n, 128),
                      fixed(n, 128), fixed(8, n), fixed(n, 128), lanes,
                      pl.BlockSpec((1, 4, 1, 2 * b), lambda g, s: (g, 0, 0, 0)),
                      fixed(256, d), fixed(d, 512)] + [ANY] * 4,
            out_specs=[fixed(n, 512), fixed(8, 128), fixed(2 * b, d), fixed(2 * b, d)],
            scratch_shapes=[pltpu.VMEM((n, n), f32)]
            + [pltpu.VMEM((n, 128), f32)] * 4
            + [pltpu.VMEM((4, b, 256), bf16), pltpu.VMEM((4, b, d), bf16), pltpu.SemaphoreType.DMA((4,))],
        ),
        out_shape=[
            jax.ShapeDtypeStruct((n, 512), bf16),
            jax.ShapeDtypeStruct((8, 128), f32),
            jax.ShapeDtypeStruct((2 * b, d), bf16),
            jax.ShapeDtypeStruct((2 * b, d), bf16),
        ],
        compiler_params=params(24),
        cost_estimate=cost(1 << 24),
        name="attend_back",
    )(s, qk, qk, v, pre, pre, qgain, kgain, cos, sin, start, live, out, lse, wout, w, *blocks)


def ffn_kernel(s_ref, x0, x1, x2, x3, a0, a1, a2, a3, o_in, wg_own, wu_own, p0, p1,
               gain_ref, n2_ref, hid_ref, fg_ref, fu_ref, res_ref, wout_ref, wg, wu, xs, att, wout, asem, xsem, osem, gsem, usem):
    j = pl.program_id(0)
    b = x0.shape[0]
    x_in, a_in = (x0, x1, x2, x3), (a0, a1, a2, a3)
    gate_w = Weight(s_ref, (wg_own,), (p0, p1), wg, gsem)
    up_w = Weight(s_ref, (wu_own,), (p0, p1), wu, usem, wg.shape[1])

    def out_copy(i):
        return pltpu.make_async_copy(o_in.at[:, i ^ (2 * s_ref[1])], wout.at[i], osem.at[i])

    def att_copy(k, i):
        return pltpu.make_async_copy(
            a_in[i].at[pl.ds((k ^ i) * b, b), :], att.at[k, :, pl.ds(i * b, b)], asem.at[k, i]
        )

    @pl.when(j == 0)
    def _():
        for k in range(4):
            pltpu.make_async_copy(x_in[k], xs.at[k], xsem.at[k]).start()
            for i in range(4):
                att_copy(k, i).start()
            if k == 0:
                for i in range(4):
                    out_copy(i).start()
                gate_w.start()
        up_w.start()
        for i in range(4):
            out_copy(i).wait()

    pltpu.make_async_copy(x0, xs.at[j], xsem.at[j]).wait()
    for i in range(4):
        pltpu.make_async_copy(a_in[i].at[pl.ds(0, b), :], att.at[j, :, pl.ds(i * b, b)], asem.at[j, i]).wait()
    res = xs[j].astype(f32) + jnp.dot(att[j], wout[...].reshape(4 * b, -1), preferred_element_type=f32)

    @pl.when(j == 0)
    def _():
        res_ref[...] = res
        wout_ref[...] = wout[0].reshape(b, -1)
        gate_w.wait()
        up_w.wait()

    inv = lax.rsqrt(jnp.mean(res * res, axis=-1, keepdims=True) + epsilon)
    n2 = (res * inv * gain_ref[...]).astype(bf16)
    n2_ref[...] = n2
    gate = jnp.dot(n2, wg[...], preferred_element_type=f32)
    up = jnp.dot(n2, wu[...], preferred_element_type=f32)
    s = jax.nn.sigmoid(gate)
    silu = gate * s
    hid_ref[...] = (silu * up).astype(bf16)
    fg_ref[...] = (up * (s * (1.0 + gate * (1.0 - s)))).astype(bf16)
    fu_ref[...] = silu.astype(bf16)


def ffn_call(s, xs, atts, wout, wg, wu, parts, gain):
    b, d = xs[0].shape
    h = wg.shape[1]
    block = lambda wid: pl.BlockSpec((b, wid), lambda j, s: (j, 0))
    return pl.pallas_call(
        ffn_kernel,
        grid_spec=pltpu.PrefetchScalarGridSpec(
            num_scalar_prefetch=1,
            grid=(4,),
            in_specs=[ANY] * 13 + [fixed(1, d)],
            out_specs=[block(d), block(h), block(h), block(h), fixed(b, d), fixed(b, d)],
            scratch_shapes=[
                pltpu.VMEM((d, h), bf16),
                pltpu.VMEM((d, h), bf16),
                pltpu.VMEM((4, b, d), bf16),
                pltpu.VMEM((4, b, 4 * b), bf16),
                pltpu.VMEM((4,) + wout.shape[:1] + wout.shape[2:], bf16),
                pltpu.SemaphoreType.DMA((4, 4)),
                pltpu.SemaphoreType.DMA((4,)),
                pltpu.SemaphoreType.DMA((4,)),
                pltpu.SemaphoreType.DMA((9,)),
                pltpu.SemaphoreType.DMA((9,)),
            ],
        ),
        out_shape=[jax.ShapeDtypeStruct((4 * b, d), bf16)]
        + [jax.ShapeDtypeStruct((4 * b, h), bf16)] * 3
        + [jax.ShapeDtypeStruct((b, d), f32), jax.ShapeDtypeStruct((b, d), bf16)],
        compiler_params=params(23),
        cost_estimate=cost(1 << 24),
        name="ffn",
    )(s, *xs, *atts, wout, wg, wu, *parts, gain)


def ffn_back_kernel(s_ref, y0, y1, y2, y3, wd_own, d0, d1, wg_own, wu_own, p0, p1, fg_ref, fu_ref,
                    gg_ref, gu_ref, lo_ref, hi_ref, wd, wg, wu, dy, ysem, dsem, gsem, usem):
    j = pl.program_id(0)
    y_in = (y0, y1, y2, y3)
    down_w = Weight(s_ref, (wd_own,), (d0, d1), wd, dsem)
    gate_w = Weight(s_ref, (wg_own,), (p0, p1), wg, gsem)
    up_w = Weight(s_ref, (wu_own,), (p0, p1), wu, usem, wg.shape[1])

    @pl.when(j == 0)
    def _():
        pltpu.make_async_copy(y_in[0], dy.at[0], ysem.at[0]).start()
        down_w.start()
        for k in range(1, 4):
            pltpu.make_async_copy(y_in[k], dy.at[k], ysem.at[k]).start()
        gate_w.start()
        up_w.start()
        down_w.wait()

    pltpu.make_async_copy(y0, dy.at[j], ysem.at[j]).wait()
    gh = contract(dy[j], wd[...], 1, 1)
    gg = (gh * fg_ref[...].astype(f32)).astype(bf16)
    gu = (gh * fu_ref[...].astype(f32)).astype(bf16)
    gg_ref[...] = gg
    gu_ref[...] = gu

    @pl.when(j == 0)
    def _():
        gate_w.wait()
        up_w.wait()

    grad = (contract(gg, wg[...], 1, 1) + contract(gu, wu[...], 1, 1)).astype(bf16)

    @pl.when(j < 2)
    def _():
        lo_ref[...] = grad

    @pl.when(j >= 2)
    def _():
        hi_ref[...] = grad


def ffn_back_call(s, dys, wd, d_parts, wg, wu, parts, fg, fu):
    b, d = dys[0].shape
    h = wg.shape[1]
    block = lambda wid: pl.BlockSpec((b, wid), lambda j, s: (j, 0))
    return pl.pallas_call(
        ffn_back_kernel,
        grid_spec=pltpu.PrefetchScalarGridSpec(
            num_scalar_prefetch=1,
            grid=(4,),
            in_specs=[ANY] * 11 + [block(h), block(h)],
            out_specs=[
                block(h),
                block(h),
                pl.BlockSpec((b, d), lambda j, s: (jnp.minimum(j, 1), 0)),
                pl.BlockSpec((b, d), lambda j, s: (jnp.maximum(j - 2, 0), 0)),
            ],
            scratch_shapes=[
                pltpu.VMEM((h, d), bf16),
                pltpu.VMEM((d, h), bf16),
                pltpu.VMEM((d, h), bf16),
                pltpu.VMEM((4, b, d), bf16),
                pltpu.SemaphoreType.DMA((4,)),
                pltpu.SemaphoreType.DMA((9,)),
                pltpu.SemaphoreType.DMA((9,)),
                pltpu.SemaphoreType.DMA((9,)),
            ],
        ),
        out_shape=[jax.ShapeDtypeStruct((4 * b, h), bf16)] * 2 + [jax.ShapeDtypeStruct((2 * b, d), bf16)] * 2,
        compiler_params=params(19),
        cost_estimate=cost(1 << 24),
        name="ffn_back",
    )(s, *dys, wd, *d_parts, wg, wu, *parts, fg, fu)


def ffn_out_kernel(s_ref, wd_own, d0, d1, hid_ref, lo_ref, hi_ref, wd, dsem):
    j = pl.program_id(0)
    down_w = Weight(s_ref, (wd_own,), (d0, d1), wd, dsem)

    @pl.when(j == 0)
    def _():
        down_w.start()
        down_w.wait()

    part = jnp.dot(hid_ref[...], wd[...], preferred_element_type=f32).astype(bf16)

    @pl.when(j < 2)
    def _():
        lo_ref[...] = part

    @pl.when(j >= 2)
    def _():
        hi_ref[...] = part


def ffn_out_call(s, wd, d_parts, hidden):
    n, h = hidden.shape
    b, d = n // 4, wd.shape[1]
    return pl.pallas_call(
        ffn_out_kernel,
        grid_spec=pltpu.PrefetchScalarGridSpec(
            num_scalar_prefetch=1,
            grid=(4,),
            in_specs=[ANY] * 3 + [pl.BlockSpec((b, h), lambda j, s: (j, 0))],
            out_specs=[
                pl.BlockSpec((b, d), lambda j, s: (jnp.minimum(j, 1), 0)),
                pl.BlockSpec((b, d), lambda j, s: (jnp.maximum(j - 2, 0), 0)),
            ],
            scratch_shapes=[pltpu.VMEM((h, d), bf16), pltpu.SemaphoreType.DMA((9,))],
        ),
        out_shape=[jax.ShapeDtypeStruct((2 * b, d), bf16)] * 2,
        compiler_params=params(9),
        cost_estimate=cost(1 << 24),
        name="ffn_out",
    )(s, wd, *d_parts, hidden)


def grad_rows_kernel(by_cols, s_ref, left_ref, right_ref, sent_a, keep_a, sent_b, keep_b):
    j = pl.program_id(0)
    grad = contract(left_ref[...], right_ref[...], 0, 0).astype(bf16)
    rows, cols = grad.shape
    if by_cols:
        first, second = grad[:, : cols // 2], grad[:, cols // 2 :]
    else:
        r = rows // 4
        first = jnp.concatenate([grad[:r], grad[2 * r : 3 * r]], 0)
        second = jnp.concatenate([grad[r : 2 * r], grad[3 * r :]], 0)

    @pl.when(j % 2 == 1)
    def _():
        sent_a[0] = first

    @pl.when(j % 2 == 0)
    def _():
        keep_a[0] = first

    @pl.when(j >= 2)
    def _():
        sent_b[0] = second

    @pl.when(j < 2)
    def _():
        keep_b[0] = second


def grad_rows_call(s, left, right, by_cols, name):
    n, rows = left.shape
    cols = right.shape[1]
    half = (rows // 4, cols // 2) if by_cols else (rows // 8, cols)
    maps = [
        lambda j, s: (j // 2, 0, 0),
        lambda j, s: (j // 2, 0, 0),
        lambda j, s: (jnp.maximum(j - 2, 0), 0, 0),
        lambda j, s: (jnp.minimum(j, 1), 0, 0),
    ]
    return pl.pallas_call(
        functools.partial(grad_rows_kernel, by_cols),
        grid_spec=pltpu.PrefetchScalarGridSpec(
            num_scalar_prefetch=1,
            grid=(4,),
            in_specs=[pl.BlockSpec((n, rows // 4), lambda j, s: (0, s[2] ^ j)), fixed(n, cols)],
            out_specs=[pl.BlockSpec((1,) + half, m) for m in maps],
        ),
        out_shape=[jax.ShapeDtypeStruct((2,) + half, bf16)] * 4,
        compiler_params=params(11),
        cost_estimate=cost(1 << 24),
        name=name,
    )(s, left, right)


def grad_cols_kernel(s_ref, left_ref, r0, r1, r2, r3, sent_a, keep_a, sent_b, keep_b):
    k = pl.program_id(0)
    b = r0.shape[0]
    grad = None
    for i, right in enumerate((r0, r1, r2, r3)):
        part = contract(left_ref[i * b : (i + 1) * b, :], right[...], 0, 0)
        grad = part if grad is None else grad + part
    grad = grad.astype(bf16)
    rows = grad.shape[0] // 4
    for a in range(4):
        piece = grad[a * rows : (a + 1) * rows]
        j = s_ref[2] ^ a

        @pl.when((k < 2) & (j % 2 == 1))
        def _():
            sent_a[j // 2] = piece

        @pl.when((k < 2) & (j % 2 == 0))
        def _():
            keep_a[j // 2] = piece

        @pl.when((k >= 2) & (j >= 2))
        def _():
            sent_b[j % 2] = piece

        @pl.when((k >= 2) & (j < 2))
        def _():
            keep_b[j % 2] = piece


def grad_cols_call(s, left, rights, name):
    n, rows = left.shape
    b, cols = rights[0].shape
    first = pl.BlockSpec((2, rows // 4, cols // 4), lambda k, s: (0, 0, jnp.minimum(k, 1)))
    second = pl.BlockSpec((2, rows // 4, cols // 4), lambda k, s: (0, 0, jnp.maximum(k - 2, 0)))
    return pl.pallas_call(
        grad_cols_kernel,
        grid_spec=pltpu.PrefetchScalarGridSpec(
            num_scalar_prefetch=1,
            grid=(4,),
            in_specs=[fixed(n, rows)] + [pl.BlockSpec((b, cols // 4), lambda k, s: (0, k))] * 4,
            out_specs=[first, first, second, second],
        ),
        out_shape=[jax.ShapeDtypeStruct((2, rows // 4, cols // 2), bf16)] * 4,
        compiler_params=params(11),
        cost_estimate=cost(1 << 24),
        name=name,
    )(s, left, *rights)


def widen_kernel(side, in_ref, out_ref):
    first, second = in_ref[0, 0].astype(f32), in_ref[0, 1].astype(f32)
    out_ref[...] = jnp.concatenate([first, second], 1 if side else 0)


def widen_call(whole, side, name):
    _, _, rows, cols = whole.shape
    block = (rows, 2 * cols) if side else (2 * rows, cols)
    return pl.pallas_call(
        functools.partial(widen_kernel, side),
        grid=(8,),
        in_specs=[pl.BlockSpec((1, 2, rows, cols), lambda j: (j, 0, 0, 0))],
        out_specs=pl.BlockSpec(block, lambda j: (j, 0)),
        out_shape=jax.ShapeDtypeStruct((8 * block[0], block[1]), f32),
        compiler_params=params(8),
        cost_estimate=cost(1 << 20),
        name=name,
    )(whole)


def permute(x, places, move):
    pairs = []
    for d in range(places):
        for t in range(T4):
            to = move(d, t)
            if to is not None:
                pairs.append((d * T4 + t, to[0] * T4 + to[1]))
    return lax.ppermute(x, AX, pairs)


def after(x, *events):
    return lax.optimization_barrier((x, events))[0]


def flip_core(d, t):
    return (d ^ 1, t)


def flip_z(d, t):
    return (d, t ^ 1)


def flip_far(d, t):
    return (d, t ^ 2)


def flip_e(bit):
    return lambda d, t: (d ^ (2 << bit), t)


def settle(d, t):
    return (d, t) if (d & 1) == (t >> 1) else (d ^ 1, t ^ 2)


def gather_row(x, n):
    over = permute(x, n, flip_z)
    near = permute(x, n, flip_core)
    far = permute(over, n, flip_core)
    return [x, over, near, far]


def hop(weights, n, c, e):
    rows = weights[0].shape[0] // 8
    mine = [lax.dynamic_slice_in_dim(w, (2 * e + c) * rows, rows, 0) for w in weights]
    return permute(jnp.concatenate(mine, 1) if len(mine) > 1 else mine[0], n, flip_far)


def spread(piece, n, *events):
    got = [permute(piece, n, lambda d, t, j=j: (d ^ (2 * j), t)) for j in (1, 2, 3)]
    if events:
        got = after(got, *events)
    mine = jnp.concatenate([piece] + got)
    return mine, permute(mine, n, flip_core)


def first_sums(pieces, n):
    sent_a, keep_a, sent_b, keep_b = pieces
    got_a = permute(sent_a, n, flip_e(0))
    got_b = permute(sent_b, n, flip_e(1))
    return got_a, got_b


def first_add(pieces, got):
    got_a, got_b = got
    keep_a, keep_b = pieces[1], pieces[3]
    return keep_a[1] + got_a[1], keep_a[0] + got_a[0], keep_b[1] + got_b[1], keep_b[0] + got_b[0]


def second_sums(halves, n):
    return permute(halves[0], n, flip_e(1)), permute(halves[2], n, flip_e(0))


def second_add(halves, got, n):
    total = jnp.stack([halves[1] + got[0], halves[3] + got[1]])
    for extra in range(2, 20):
        if (2 << extra) < n:
            total = total + permute(total, n, flip_e(extra))
    return total


def owner_cross(total, n, c):
    half = total.shape[1] // 2
    first, second = total[:, :half], total[:, half:]
    got = permute(jnp.where(c == 0, second, first), n, flip_core)
    return jnp.where(c == 0, first, got), permute(jnp.where(c == 0, got, second), n, flip_far)


def neighbours(n):
    return None if n == 8 else [list(range(k, k + 8)) for k in range(0, n, 8)]


def whole_grad(mine, n):
    return lax.all_gather(mine, "dp", axis_index_groups=neighbours(n))


def out_slices(w, n, c, e):
    rows = w.shape[0] // 8
    mine = lax.dynamic_slice_in_dim(w, (2 * e + c) * rows, rows, 0)
    two = jnp.stack([mine, permute(mine, n, flip_z)])
    return jnp.concatenate([two, permute(two, n, flip_far)])


def sum_all(vec, n):
    bit = 1
    while bit < n:
        vec = vec + permute(vec, n, lambda d, t, bit=bit: (d ^ bit, t))
        bit *= 2
    for bit in (1, 2):
        vec = vec + permute(vec, n, lambda d, t, bit=bit: (d, t ^ bit))
    return vec


def join_attention(qkv, out):
    r, k = qkv.shape[1] // 2, qkv.shape[2]
    s = out.shape[1] // 2
    parts = []
    for half in range(2):
        some = out[:, half * s : (half + 1) * s]
        parts += [qkv[:, half * r : (half + 1) * r], some[:, :, :k], some[:, :, k:]]
    return jnp.concatenate(parts, 1)


def widen_out(got):
    s = got.shape[2] // 2
    sides = [got[:, half, at * s : (at + 1) * s].reshape(8 * s, -1) for half in range(2) for at in range(2)]
    return jnp.concatenate(sides, 1).astype(f32)


def local(
    block_input,
    doc_lengths,
    pad_mask,
    norm1_gain,
    w_query,
    w_key,
    w_value,
    query_gain,
    key_gain,
    w_out,
    norm2_gain,
    w_gate,
    w_up,
    w_down,
    cotangent,
):
    n = lax.axis_size("dp")
    d, t = lax.axis_index("dp"), lax.axis_index("tensor")
    c, p = d & 1, t >> 1
    e = (d >> 1) & 3
    shard = 2 * c + (t & 1)
    b = block_input.shape[0]
    seq_len = b * T4
    home = c == p
    wq = w_query.shape[1]
    wk = w_key.shape[1]
    width = block_input.shape[1]
    s = jnp.stack([shard, c, e]).astype(jnp.int32)

    x_own = permute(block_input, n, settle)
    marks = jnp.concatenate([doc_lengths, pad_mask], 1)
    marks = jnp.where(home, marks, permute(marks, n, flip_core))
    lengths_row, pad_row = marks[0, : doc_lengths.shape[1]], marks[0, doc_lengths.shape[1] :]
    out_eighth = out_slices(w_out, n, c, e)
    out_all = lax.all_gather(out_eighth, "dp", axis_index_groups=neighbours(n))
    qkv_hop = hop((w_query, w_key, w_value), n, c, e)
    x_blocks = gather_row(x_own, n)
    qkv_parts = spread(qkv_hop, n, x_blocks[1])
    gate_up_hop = hop((after(w_gate, x_blocks[2]), w_up), n, c, e)

    positions = jnp.arange(seq_len, dtype=jnp.int32)
    doc_starts, cos_half, sin_half = doc_tables(lengths_row, positions, HD)
    cos = jnp.concatenate([cos_half] * 4, 1)
    sin = jnp.concatenate([-sin_half, sin_half] * 2, 1)
    live = jnp.where(pad_row == 1, positions, -1)
    start_col = jnp.broadcast_to(doc_starts[:, None], (seq_len, 128))
    start_row = jnp.broadcast_to(doc_starts[None], (8, seq_len))
    live_col = jnp.broadcast_to(live[:, None], (seq_len, 128))
    live_row = jnp.broadcast_to(live[None], (8, seq_len))
    gains = jnp.concatenate([query_gain] * (wq // HD) + [key_gain] * (wk // HD))[None]
    qgain_pair = jnp.concatenate([query_gain] * 2)[None]
    kgain_pair = jnp.concatenate([key_gain] * 2)[None]

    rows_one, pre, qk, values, w_qkv = qkv_call(
        s, x_blocks, (w_query, w_key, w_value), qkv_parts, norm1_gain[None], after(gains, out_eighth), cos, sin
    )
    attended, attended_f, lse = attend_call(s, qk, values, start_col, live_row)
    att_pieces = gather_row(attended, n)
    gate_up_parts = spread(after(gate_up_hop, attended), n, att_pieces[1])
    down_hop = hop((after(w_down, attended),), n, c, e)
    dy_own = permute(after(cotangent, attended), n, settle)
    down_hop = after(down_hop, att_pieces[3])
    dy_own = after(dy_own, att_pieces[3])
    dy_blocks = gather_row(dy_own, n)
    down_parts = spread(down_hop, n, dy_blocks[1])
    rows_two, hidden, by_gate, by_up, residual, w_out_own = ffn_call(
        s, x_blocks, att_pieces, out_all, w_gate, w_up, gate_up_parts, after(norm2_gain[None], dy_own, down_hop)
    )

    down = grad_cols_call(s, hidden, dy_blocks, "grad_down")
    gate_grad, up_grad, low2, high2 = ffn_back_call(
        s, dy_blocks, w_down, down_parts, w_gate, w_up, gate_up_parts, after(by_gate, *down), by_up
    )
    high_got = permute(high2, n, flip_core)
    down_got = first_sums(down, n)
    low_half = low2 + high_got
    low_over = permute(low_half[b:], n, flip_z)
    down = first_add(down, after(down_got, low_half))
    down_got = second_sums(down, n)
    gate = grad_rows_call(s, rows_two, after(gate_grad, *down), False, "grad_gate")
    gate_got = first_sums(gate, n)
    up = grad_rows_call(s, rows_two, after(up_grad, *gate), False, "grad_up")
    up_got = first_sums(up, n)
    grad_n2 = (low_half[:b] + after(low_over, *up)).astype(f32)
    inv = lax.rsqrt(jnp.mean(residual * residual, axis=-1, keepdims=True) + epsilon)
    scaled = norm2_gain * grad_n2
    grad_residual = (
        dy_own.astype(f32)
        + inv * scaled
        - residual * (inv * inv * inv) * jnp.mean(scaled * residual, axis=-1, keepdims=True)
    )
    grad_norm2 = jnp.sum(grad_n2 * residual * inv, axis=0)
    gb_own = grad_residual.astype(bf16)
    gb_blocks = gather_row(gb_own, n)

    down = second_add(down, after(down_got, gb_own), n)
    down_kept, down_got = owner_cross(down, n, c)
    ffn_low, ffn_high = ffn_out_call(s, w_down, down_parts, after(hidden, down))
    ffn_got = permute(ffn_high, n, flip_core)
    gate = first_add(gate, after(gate_got, ffn_low))
    gate_got = second_sums(gate, n)
    up = first_add(up, after(up_got, gb_blocks[1], *gate))
    up_got = second_sums(up, n)
    ffn_half = ffn_low + after(ffn_got, *up)
    ffn_over = permute(ffn_half[b:], n, flip_z)
    down_mine = down_kept + after(down_got, gb_blocks[3], ffn_half)
    down_all = whole_grad(down_mine, n)
    gate = second_add(gate, after(gate_got, down_mine), n)
    gate_kept, gate_got = owner_cross(gate, n, c)

    low, gain_terms, low1, high1 = attend_back_call(
        s, qk, after(values, gate_kept, ffn_half), pre, qgain_pair, kgain_pair, cos, sin, start_row, live_col, attended_f,
        lse, w_out_own, w_qkv, gb_blocks,
    )
    high_got = permute(high1, n, flip_core)
    gate_mine = gate_kept + after(gate_got, high_got)
    gate_all = whole_grad(gate_mine, n)
    low_half = low1 + after(high_got, gate_mine)
    low_over = permute(low_half[b:], n, flip_z)
    up = second_add(up, after(up_got, low_half), n)
    up_kept, up_got = owner_cross(up, n, c)
    qkv = grad_rows_call(s, rows_one, after(low, up_kept), True, "grad_qkv")
    out = grad_cols_call(s, after(attended, *qkv), gb_blocks, "grad_out")
    att = [join_attention(a, o) for a, o in zip(qkv, out)]
    att_got = first_sums(att, n)
    block_output = residual + (ffn_half[:b] + after(ffn_over, *att)).astype(f32)
    settled_output = permute(block_output.astype(bf16), n, settle)

    grad_n1 = (low_half[:b] + after(low_over, block_output)).astype(f32)
    x_f = x_own.astype(f32)
    inv = lax.rsqrt(jnp.mean(x_f * x_f, axis=-1, keepdims=True) + epsilon)
    scaled = norm1_gain * grad_n1
    input_grad = (
        grad_residual
        + inv * scaled
        - x_f * (inv * inv * inv) * jnp.mean(scaled * x_f, axis=-1, keepdims=True)
    )
    grad_norm1 = jnp.sum(grad_n1 * x_f * inv, axis=0)
    settled_grad = permute(input_grad.astype(bf16), n, settle)
    up_mine = up_kept + after(up_got, input_grad)
    up_all = whole_grad(up_mine, n)
    att = first_add(att, after(att_got, up_mine))
    att_got = second_sums(att, n)
    head_terms = gain_terms[:, :HD] + gain_terms[:, HD:]
    vec = jnp.concatenate([grad_norm1, grad_norm2, head_terms[0] + head_terms[1], head_terms[2]])
    vec = sum_all(after(vec, *att)[None], n)[0]
    att = second_add(att, after(att_got, vec), n)
    att_kept, att_got = owner_cross(att, n, c)
    grad_down = widen_call(after(down_all, att_kept), True, "widen_down")
    grad_gate = widen_call(after(gate_all, grad_down), False, "widen_gate")
    att_mine = att_kept + after(att_got, grad_down)
    att_all = whole_grad(att_mine, n)
    block_output = jnp.where(home, block_output, after(settled_output, grad_gate).astype(f32))
    input_grad = jnp.where(home, input_grad, after(settled_grad, grad_gate).astype(f32))
    grad_up = widen_call(after(up_all, grad_gate), False, "widen_up")
    att_all = after(att_all, grad_up)
    eighth = wq // 2
    grad_query = att_all[:, 0, :eighth].astype(f32).reshape(width, wq)
    grad_kv = att_all[:, 1, :eighth].astype(f32).reshape(width, wq)
    grad_out = widen_out(att_all[:, :, eighth:])
    return (
        block_output,
        input_grad,
        vec[:width],
        grad_query,
        grad_kv[:, :wk],
        grad_kv[:, wk:],
        vec[2 * width : 2 * width + HD],
        vec[2 * width + HD :],
        grad_out,
        vec[width : 2 * width],
        grad_gate,
        grad_up,
        grad_down,
    )


def solution(mesh):
    placed = (
        P(("dp", "tensor"), None),
        P("dp", None),
        P("dp", None),
        P(),
        P(None, "tensor"),
        P(None, "tensor"),
        P(None, "tensor"),
        P(),
        P(),
        P("tensor", None),
        P(),
        P(None, "tensor"),
        P(None, "tensor"),
        P("tensor", None),
        P(("dp", "tensor"), None),
    )
    return jax.shard_map(
        local,
        mesh=mesh,
        in_specs=placed,
        out_specs=(
            P(("dp", "tensor"), None),
            P(("dp", "tensor"), None),
            P(),
            P(None, "tensor"),
            P(None, "tensor"),
            P(None, "tensor"),
            P(),
            P(),
            P("tensor", None),
            P(),
            P(None, "tensor"),
            P(None, "tensor"),
            P("tensor", None),
        ),
        check_vma=False,
    )
```

```python
import functools
import math

import jax
import jax.numpy as jnp
from jax import lax
from jax.experimental import pallas as pl
from jax.experimental.pallas import tpu as pltpu
from jax.sharding import PartitionSpec as P

HD = 64
AX = ("dp", "tensor")
T4 = 4
VMEM_MB = 1 << 20

epsilon = 1e-05
rope_base = 1000000.0
NEG = -1000000000.0
bf16 = jnp.bfloat16
f32 = jnp.float32


def doc_tables(lengths_row, positions, head_dim):
    doc_ends = jnp.cumsum(lengths_row)
    passed = positions[:, None] >= doc_ends[None, :]
    doc_starts = jnp.sum(jnp.where(passed, lengths_row[None, :], 0), axis=1)
    offsets = (positions - doc_starts).astype(f32)
    freqs = jnp.exp(
        jnp.arange(head_dim // 2, dtype=f32) * (-2.0 * math.log(rope_base) / head_dim)
    )
    angles = offsets[:, None] * freqs[None, :]
    return (doc_starts, jnp.cos(angles), jnp.sin(angles))


def contract(a, b, da, db, precision=None):
    return lax.dot_general(
        a, b, (((da,), (db,)), ((), ())), preferred_element_type=f32, precision=precision
    )


def swap_halves(y):
    width = y.shape[1]
    lane = lax.broadcasted_iota(jnp.int32, y.shape, 1)
    return jnp.where(lane % HD < HD // 2, pltpu.roll(y, width - HD // 2, 1), pltpu.roll(y, HD // 2, 1))


def head_mean(y):
    width = y.shape[1]
    at = lax.broadcasted_iota(jnp.int32, (width, width), 0) // HD
    to = lax.broadcasted_iota(jnp.int32, (width, width), 1) // HD
    ones = jnp.where(at == to, 1.0 / HD, 0.0).astype(f32)
    return contract(y, ones, 1, 0, lax.Precision.HIGHEST)


class Weight:
    def __init__(self, s_ref, own, parts, to, sems):
        self.core, self.e = s_ref[1], s_ref[2]
        self.own, self.parts, self.to, self.sems = own, parts, to, sems

    def copies(self):
        start = 0
        for i, w in enumerate(self.own):
            wide = w.shape[1]
            to = self.to if len(self.own) == 1 else self.to.at[:, pl.ds(start, wide)]
            yield 0, functools.partial(pltpu.make_async_copy, w, to, self.sems.at[8 + i])
            start += wide
        rows = self.to.shape[0] // 8
        for j in range(4):
            for other in range(2):
                at = pl.multiple_of((2 * (self.e ^ j) + 1 - other) * rows, rows)
                to = self.to.at[pl.ds(at, rows), :]
                yield 1, functools.partial(
                    pltpu.make_async_copy, self.parts[4 * other + j], to, self.sems.at[2 * j + other]
                )

    def each(self, act):
        for core in range(2):

            @pl.when(self.core == core)
            def _():
                for whose, copy in self.copies():
                    if whose == core:
                        act(copy())

    def start(self):
        self.each(lambda copy: copy.start())

    def wait(self):
        self.each(lambda copy: copy.wait())


ANY = pl.BlockSpec(memory_space=pl.ANY)


def fixed(*shape):
    return pl.BlockSpec(shape, lambda *_: (0,) * len(shape))


def cost(flops):
    return pl.CostEstimate(flops=flops, bytes_accessed=1 << 16, transcendentals=0)


def params(mib):
    return pltpu.CompilerParams(vmem_limit_bytes=mib * VMEM_MB)


def qkv_kernel(s_ref, *refs):
    pieces, own, parts, refs = refs[:4], refs[4:7], refs[7:15], refs[15:]
    g1_ref, gains_ref, cos_ref, sin_ref, n1_ref, pre_ref, qk_ref, v_ref, w_ref, xs, xsem, wsem = refs
    j = pl.program_id(0)
    weight = Weight(s_ref, own, parts, w_ref, wsem)

    @pl.when(j == 0)
    def _():
        for k in range(4):
            pltpu.make_async_copy(pieces[k], xs.at[k], xsem.at[k]).start()
        weight.start()

    pltpu.make_async_copy(pieces[0], xs.at[j], xsem.at[j]).wait()
    x = xs[j].astype(f32)
    inv = lax.rsqrt(jnp.mean(x * x, axis=-1, keepdims=True) + epsilon)
    n1 = (x * inv * g1_ref[...]).astype(bf16)
    n1_ref[...] = n1

    @pl.when(j == 0)
    def _():
        weight.wait()

    qkv = jnp.dot(n1, w_ref[...], preferred_element_type=f32)
    width = pre_ref.shape[1]
    pre = qkv[:, :width]
    pre_ref[...] = pre
    v_ref[...] = qkv[:, width:].astype(bf16)
    y = pre * lax.rsqrt(head_mean(pre * pre) + epsilon) * gains_ref[...]
    cos = jnp.concatenate([cos_ref[...]] * (width // 128), 1)
    sin = jnp.concatenate([sin_ref[...]] * (width // 128), 1)
    qk = (y * cos + swap_halves(y) * sin).astype(bf16)
    lane = lax.broadcasted_iota(jnp.int32, qk.shape, 1)
    qk_ref[...] = jnp.where(lane < width - 128, qk * 0.125, qk).astype(bf16)


def qkv_call(s, xs, w_own, w_parts, g1, gains, cos, sin):
    b, d = xs[0].shape
    wid = w_parts[0].shape[1]
    qkw = wid - 128
    natural = lambda j, s: (s[0] ^ j, 0)
    return pl.pallas_call(
        qkv_kernel,
        grid_spec=pltpu.PrefetchScalarGridSpec(
            num_scalar_prefetch=1,
            grid=(4,),
            in_specs=[ANY] * 15
            + [fixed(1, d), fixed(1, qkw), pl.BlockSpec((b, 128), natural), pl.BlockSpec((b, 128), natural)],
            out_specs=[
                pl.BlockSpec((b, d), lambda j, s: (j, 0)),
                pl.BlockSpec((b, qkw), natural),
                pl.BlockSpec((b, qkw), natural),
                pl.BlockSpec((b, 128), natural),
                fixed(d, wid),
            ],
            scratch_shapes=[
                pltpu.VMEM((4, b, d), bf16),
                pltpu.SemaphoreType.DMA((4,)),
                pltpu.SemaphoreType.DMA((11,)),
            ],
        ),
        out_shape=[
            jax.ShapeDtypeStruct((4 * b, d), bf16),
            jax.ShapeDtypeStruct((4 * b, qkw), f32),
            jax.ShapeDtypeStruct((4 * b, qkw), bf16),
            jax.ShapeDtypeStruct((4 * b, 128), bf16),
            jax.ShapeDtypeStruct((d, wid), bf16),
        ],
        compiler_params=params(12),
        cost_estimate=cost(1 << 24),
        name="qkv",
    )(s, *xs, *w_own, *w_parts, g1, gains, cos, sin)


def both_heads(pair):
    lane = lax.broadcasted_iota(jnp.int32, pair.shape, 1)
    zero = jnp.zeros_like(pair)
    return jnp.concatenate([jnp.where(lane < HD, pair, zero), jnp.where(lane < HD, zero, pair)], 0)


def pick_heads(both):
    r = both.shape[0] // 2
    lane = lax.broadcasted_iota(jnp.int32, (r, 128), 1)
    return jnp.where(lane < HD, both[:r], both[r:])


def twice(kv, g):
    lane = lax.broadcasted_iota(jnp.int32, kv.shape, 1)
    turned = pltpu.roll(kv.astype(f32), HD, 1).astype(kv.dtype)
    return jnp.where((lane < HD) == (g == 0), kv, turned)


def attend_kernel(s_ref, q_ref, k_ref, v_ref, start_ref, live_ref, att_ref, out_ref, lse_ref, bias):
    g = pl.program_id(0)
    n = k_ref.shape[0]
    b = n // 4

    @pl.when(g == 0)
    def _():
        for a in range(4):
            keys = (a + 1) * b
            start = start_ref[a * b : (a + 1) * b, :1]
            q_at = lax.broadcasted_iota(jnp.int32, (b, keys), 0) + a * b
            k_at = lax.broadcasted_iota(jnp.int32, (b, keys), 1)
            allowed = ((live_ref[:1, :keys] >= start) & (k_at <= q_at)) | (k_at == q_at)
            bias[a * b : (a + 1) * b, :keys] = jnp.where(allowed, 0.0, NEG)

    kd = twice(k_ref[...], g)
    vd = twice(v_ref[...], g)
    for a in range(4):
        keys = (a + 1) * b
        rows = slice(a * b, (a + 1) * b)
        qm = both_heads(q_ref[rows, :])
        scores = contract(qm, kd[:keys], 1, 1)
        extra = bias[rows, :keys]
        expo = jnp.exp(scores + jnp.concatenate([extra, extra], 0))
        total = jnp.sum(expo, axis=-1, keepdims=True)
        pair = pick_heads(contract(expo.astype(bf16), vd[:keys], 1, 0) / total)
        out_ref[rows, :] = pair
        att_ref[pl.ds(pl.multiple_of((s_ref[0] ^ a) * b, b), b), :] = pair.astype(bf16)
        lse_ref[0, a] = jnp.transpose(jnp.broadcast_to(jnp.log(total), (2 * b, 128)))[:1]


def attend_call(s, qk, v, start, live):
    n = qk.shape[0]
    b = n // 4
    lanes = lambda g, s: (0, g)
    return pl.pallas_call(
        attend_kernel,
        grid_spec=pltpu.PrefetchScalarGridSpec(
            num_scalar_prefetch=1,
            grid=(2,),
            in_specs=[
                pl.BlockSpec((n, 128), lanes),
                pl.BlockSpec((n, 128), lambda g, s: (0, 2)),
                fixed(n, 128),
                fixed(n, 128),
                fixed(8, n),
            ],
            out_specs=[
                pl.BlockSpec((n, 128), lanes),
                pl.BlockSpec((n, 128), lanes),
                pl.BlockSpec((1, 4, 1, 2 * b), lambda g, s: (g, 0, 0, 0)),
            ],
            scratch_shapes=[pltpu.VMEM((n, n), f32)],
        ),
        out_shape=[
            jax.ShapeDtypeStruct((n, 256), bf16),
            jax.ShapeDtypeStruct((n, 256), f32),
            jax.ShapeDtypeStruct((2, 4, 1, 2 * b), f32),
        ],
        compiler_params=params(14),
        cost_estimate=cost(1 << 24),
        name="attend",
    )(s, qk, qk, v, start, live)


def norm_back(grad, pre, gain, cos, sin):
    turned = grad * cos - swap_halves(grad) * sin
    inv = lax.rsqrt(head_mean(pre * pre) + epsilon)
    scaled = turned * gain
    dpre = inv * scaled - pre * (inv * inv * inv) * head_mean(scaled * pre)
    return dpre, jnp.sum(turned * pre * inv, axis=0, keepdims=True)


def attend_back_kernel(s_ref, q_ref, k_ref, v_ref, qpre_ref, kpre_ref, gains_ref, kgain_ref, cos_ref, sin_ref,
                       start_ref, live_ref, out_ref, lse_ref, wout_ref, w_ref, b0, b1, b2, b3,
                       low_ref, gain_ref, lo_ref, hi_ref, bias, dk, dv, dkall, dvall, dos, gb, sems):
    g = pl.program_id(0)
    n = k_ref.shape[0]
    b = n // 4
    pieces = (b0, b1, b2, b3)

    @pl.when(g == 0)
    def _():
        for k in range(4):
            pltpu.make_async_copy(pieces[k], gb.at[k], sems.at[k]).start()
        for a in range(4):
            keys = (a + 1) * b
            start = start_ref[:1, a * b : (a + 1) * b]
            k_at = lax.broadcasted_iota(jnp.int32, (keys, b), 0)
            q_at = lax.broadcasted_iota(jnp.int32, (keys, b), 1) + a * b
            allowed = ((live_ref[:keys, :1] >= start) & (k_at <= q_at)) | (k_at == q_at)
            bias[:keys, a * b : (a + 1) * b] = jnp.where(allowed, 0.0, NEG)
        for k in range(4):
            pltpu.make_async_copy(pieces[k], gb.at[k], sems.at[k]).wait()
            dos[k] = contract(gb[k], wout_ref[...], 1, 1).astype(bf16)

    kd = twice(k_ref[...], g)
    vd = twice(v_ref[...], g)
    gain_sum = jnp.zeros((1, 128), f32)
    ones = jnp.ones((8, 128), f32)
    for a in (3, 2, 1, 0):
        keys = (a + 1) * b
        rows = slice(a * b, (a + 1) * b)
        home = s_ref[0] ^ a
        qm = both_heads(q_ref[rows, :])
        dout = jnp.where(g == 0, dos[home, :, :128], dos[home, :, 128:])
        dom = both_heads(dout)
        delta = contract(ones, both_heads(dout.astype(f32) * out_ref[rows, :]), 1, 1, lax.Precision.HIGHEST)[:1]
        scores = contract(kd[:keys], qm, 1, 1)
        extra = bias[:keys, rows]
        probs = jnp.exp(scores + (jnp.concatenate([extra, extra], 1) - lse_ref[0, a]))
        dprobs = contract(vd[:keys], dom, 1, 1)
        dscores = (probs * (dprobs - delta)).astype(bf16)
        dv_add = contract(probs.astype(bf16), dom, 1, 0)
        dk_add = contract(dscores, qm, 1, 0)
        if a == 3:
            dv[...] = dv_add
            dk[...] = dk_add
        else:
            dv[:keys] += dv_add
            dk[:keys] += dk_add
        dq = pick_heads(contract(dscores, kd[:keys], 0, 0)) * 0.125
        dpre, gain_part = norm_back(dq, qpre_ref[rows, :], gains_ref[...], cos_ref[rows, :], sin_ref[rows, :])
        at = pl.ds(pl.multiple_of(home * b, b), b)
        low_ref[at, pl.ds(pl.multiple_of(g * 128, 128), 128)] = dpre.astype(bf16)
        gain_sum = gain_sum + gain_part
    gain_ref[pl.ds(g, 1), :] = gain_sum
    lane = lax.broadcasted_iota(jnp.int32, (n, 128), 1)
    dk_all = dk[...] + pltpu.roll(dk[...], HD, 1)
    dv_all = dv[...] + pltpu.roll(dv[...], HD, 1)

    @pl.when(g == 0)
    def _():
        dkall[...] = dk_all
        dvall[...] = dv_all

    @pl.when(g == 1)
    def _():
        grad_k = jnp.where(lane < HD, dkall[...], dk_all)
        grad_v = jnp.where(lane < HD, dvall[...], dv_all)
        dpre, gain_part = norm_back(grad_k, kpre_ref[...], kgain_ref[...], cos_ref[...], sin_ref[...])
        gain_ref[2:3, :] = gain_part
        for a in range(4):
            at = pl.ds(pl.multiple_of((s_ref[0] ^ a) * b, b), b)
            low_ref[at, 256:384] = dpre[a * b : (a + 1) * b].astype(bf16)
            low_ref[at, 384:512] = grad_v[a * b : (a + 1) * b].astype(bf16)
        hi_ref[...] = contract(low_ref[2 * b :, :], w_ref[...], 1, 1).astype(bf16)
        lo_ref[...] = contract(low_ref[: 2 * b, :], w_ref[...], 1, 1).astype(bf16)


def attend_back_call(s, qk, v, pre, qgain, kgain, cos, sin, start, live, out, lse, wout, w, blocks):
    n = v.shape[0]
    b = n // 4
    d = blocks[0].shape[1]
    lanes = pl.BlockSpec((n, 128), lambda g, s: (0, g))
    third = pl.BlockSpec((n, 128), lambda g, s: (0, 2))
    return pl.pallas_call(
        attend_back_kernel,
        grid_spec=pltpu.PrefetchScalarGridSpec(
            num_scalar_prefetch=1,
            grid=(2,),
            in_specs=[lanes, third, fixed(n, 128), lanes, third, fixed(1, 128), fixed(1, 128), fixed(n, 128),
                      fixed(n, 128), fixed(8, n), fixed(n, 128), lanes,
                      pl.BlockSpec((1, 4, 1, 2 * b), lambda g, s: (g, 0, 0, 0)),
                      fixed(256, d), fixed(d, 512)] + [ANY] * 4,
            out_specs=[fixed(n, 512), fixed(8, 128), fixed(2 * b, d), fixed(2 * b, d)],
            scratch_shapes=[pltpu.VMEM((n, n), f32)]
            + [pltpu.VMEM((n, 128), f32)] * 4
            + [pltpu.VMEM((4, b, 256), bf16), pltpu.VMEM((4, b, d), bf16), pltpu.SemaphoreType.DMA((4,))],
        ),
        out_shape=[
            jax.ShapeDtypeStruct((n, 512), bf16),
            jax.ShapeDtypeStruct((8, 128), f32),
            jax.ShapeDtypeStruct((2 * b, d), bf16),
            jax.ShapeDtypeStruct((2 * b, d), bf16),
        ],
        compiler_params=params(24),
        cost_estimate=cost(1 << 24),
        name="attend_back",
    )(s, qk, qk, v, pre, pre, qgain, kgain, cos, sin, start, live, out, lse, wout, w, *blocks)


def ffn_kernel(s_ref, *refs):
    x_in, a_in, o_in, refs = refs[:4], refs[4:8], refs[8], refs[9:]
    wg_own, wg_parts, wu_own, wu_parts, refs = refs[0], refs[1:9], refs[9], refs[10:18], refs[18:]
    gain_ref, n2_ref, hid_ref, fg_ref, fu_ref, res_ref, wout_ref, refs = *refs[:7], refs[7:]
    wg, wu, xs, att, wout, asem, xsem, osem, gsem, usem = refs
    j = pl.program_id(0)
    b = xs.shape[1]
    gate_w = Weight(s_ref, (wg_own,), wg_parts, wg, gsem)
    up_w = Weight(s_ref, (wu_own,), wu_parts, wu, usem)

    def out_copy(i):
        return pltpu.make_async_copy(o_in.at[:, i ^ (2 * s_ref[1])], wout.at[i], osem.at[i])

    def att_copy(k, i):
        return pltpu.make_async_copy(
            a_in[i].at[pl.ds((k ^ i) * b, b), :], att.at[k, :, pl.ds(i * b, b)], asem.at[k, i]
        )

    @pl.when(j == 0)
    def _():
        for k in range(4):
            pltpu.make_async_copy(x_in[k], xs.at[k], xsem.at[k]).start()
            for i in range(4):
                att_copy(k, i).start()
            if k == 0:
                for i in range(4):
                    out_copy(i).start()
                gate_w.start()
        up_w.start()
        for i in range(4):
            out_copy(i).wait()

    pltpu.make_async_copy(x_in[0], xs.at[j], xsem.at[j]).wait()
    for i in range(4):
        pltpu.make_async_copy(a_in[i].at[pl.ds(0, b), :], att.at[j, :, pl.ds(i * b, b)], asem.at[j, i]).wait()
    res = xs[j].astype(f32) + jnp.dot(att[j], wout[...].reshape(4 * b, -1), preferred_element_type=f32)

    @pl.when(j == 0)
    def _():
        res_ref[...] = res
        wout_ref[...] = wout[0].reshape(b, -1)
        gate_w.wait()
        up_w.wait()

    inv = lax.rsqrt(jnp.mean(res * res, axis=-1, keepdims=True) + epsilon)
    n2 = (res * inv * gain_ref[...]).astype(bf16)
    n2_ref[...] = n2
    gate = jnp.dot(n2, wg[...], preferred_element_type=f32)
    up = jnp.dot(n2, wu[...], preferred_element_type=f32)
    s = jax.nn.sigmoid(gate)
    silu = gate * s
    hid_ref[...] = (silu * up).astype(bf16)
    fg_ref[...] = (up * (s * (1.0 + gate * (1.0 - s)))).astype(bf16)
    fu_ref[...] = silu.astype(bf16)


def ffn_call(s, xs, atts, wout, wg, g_parts, wu, u_parts, gain):
    b, d = xs[0].shape
    h = wg.shape[1]
    block = lambda wid: pl.BlockSpec((b, wid), lambda j, s: (j, 0))
    return pl.pallas_call(
        ffn_kernel,
        grid_spec=pltpu.PrefetchScalarGridSpec(
            num_scalar_prefetch=1,
            grid=(4,),
            in_specs=[ANY] * 27 + [fixed(1, d)],
            out_specs=[block(d), block(h), block(h), block(h), fixed(b, d), fixed(b, d)],
            scratch_shapes=[
                pltpu.VMEM((d, h), bf16),
                pltpu.VMEM((d, h), bf16),
                pltpu.VMEM((4, b, d), bf16),
                pltpu.VMEM((4, b, 4 * b), bf16),
                pltpu.VMEM((4,) + wout.shape[:1] + wout.shape[2:], bf16),
                pltpu.SemaphoreType.DMA((4, 4)),
                pltpu.SemaphoreType.DMA((4,)),
                pltpu.SemaphoreType.DMA((4,)),
                pltpu.SemaphoreType.DMA((9,)),
                pltpu.SemaphoreType.DMA((9,)),
            ],
        ),
        out_shape=[jax.ShapeDtypeStruct((4 * b, d), bf16)]
        + [jax.ShapeDtypeStruct((4 * b, h), bf16)] * 3
        + [jax.ShapeDtypeStruct((b, d), f32), jax.ShapeDtypeStruct((b, d), bf16)],
        compiler_params=params(58),
        cost_estimate=cost(1 << 24),
        name="ffn",
    )(s, *xs, *atts, wout, wg, *g_parts, wu, *u_parts, gain)


def ffn_back_kernel(s_ref, *refs):
    y_in, wd_own, wd_parts, refs = refs[:4], refs[4], refs[5:13], refs[13:]
    wg_own, wg_parts, wu_own, wu_parts, refs = refs[0], refs[1:9], refs[9], refs[10:18], refs[18:]
    fg_ref, fu_ref, gg_ref, gu_ref, lo_ref, hi_ref, wd, wg, wu, dy, ysem, dsem, gsem, usem = refs
    j = pl.program_id(0)
    down_w = Weight(s_ref, (wd_own,), wd_parts, wd, dsem)
    gate_w = Weight(s_ref, (wg_own,), wg_parts, wg, gsem)
    up_w = Weight(s_ref, (wu_own,), wu_parts, wu, usem)

    @pl.when(j == 0)
    def _():
        pltpu.make_async_copy(y_in[0], dy.at[0], ysem.at[0]).start()
        down_w.start()
        for k in range(1, 4):
            pltpu.make_async_copy(y_in[k], dy.at[k], ysem.at[k]).start()
        gate_w.start()
        up_w.start()
        down_w.wait()

    pltpu.make_async_copy(y_in[0], dy.at[j], ysem.at[j]).wait()
    gh = contract(dy[j], wd[...], 1, 1)
    gg = (gh * fg_ref[...].astype(f32)).astype(bf16)
    gu = (gh * fu_ref[...].astype(f32)).astype(bf16)
    gg_ref[...] = gg
    gu_ref[...] = gu

    @pl.when(j == 0)
    def _():
        gate_w.wait()
        up_w.wait()

    grad = (contract(gg, wg[...], 1, 1) + contract(gu, wu[...], 1, 1)).astype(bf16)

    @pl.when(j < 2)
    def _():
        lo_ref[...] = grad

    @pl.when(j >= 2)
    def _():
        hi_ref[...] = grad


def ffn_back_call(s, dys, wd, d_parts, wg, g_parts, wu, u_parts, fg, fu):
    b, d = dys[0].shape
    h = wg.shape[1]
    block = lambda wid: pl.BlockSpec((b, wid), lambda j, s: (j, 0))
    return pl.pallas_call(
        ffn_back_kernel,
        grid_spec=pltpu.PrefetchScalarGridSpec(
            num_scalar_prefetch=1,
            grid=(4,),
            in_specs=[ANY] * 31 + [block(h), block(h)],
            out_specs=[
                block(h),
                block(h),
                pl.BlockSpec((b, d), lambda j, s: (jnp.minimum(j, 1), 0)),
                pl.BlockSpec((b, d), lambda j, s: (jnp.maximum(j - 2, 0), 0)),
            ],
            scratch_shapes=[
                pltpu.VMEM((h, d), bf16),
                pltpu.VMEM((d, h), bf16),
                pltpu.VMEM((d, h), bf16),
                pltpu.VMEM((4, b, d), bf16),
                pltpu.SemaphoreType.DMA((4,)),
                pltpu.SemaphoreType.DMA((9,)),
                pltpu.SemaphoreType.DMA((9,)),
                pltpu.SemaphoreType.DMA((9,)),
            ],
        ),
        out_shape=[jax.ShapeDtypeStruct((4 * b, h), bf16)] * 2 + [jax.ShapeDtypeStruct((2 * b, d), bf16)] * 2,
        compiler_params=params(58),
        cost_estimate=cost(1 << 24),
        name="ffn_back",
    )(s, *dys, wd, *d_parts, wg, *g_parts, wu, *u_parts, fg, fu)


def ffn_out_kernel(s_ref, wd_own, *refs):
    wd_parts, (hid_ref, lo_ref, hi_ref, wd, dsem) = refs[:8], refs[8:]
    j = pl.program_id(0)
    down_w = Weight(s_ref, (wd_own,), wd_parts, wd, dsem)

    @pl.when(j == 0)
    def _():
        down_w.start()
        down_w.wait()

    part = jnp.dot(hid_ref[...], wd[...], preferred_element_type=f32).astype(bf16)

    @pl.when(j < 2)
    def _():
        lo_ref[...] = part

    @pl.when(j >= 2)
    def _():
        hi_ref[...] = part


def ffn_out_call(s, wd, d_parts, hidden):
    n, h = hidden.shape
    b, d = n // 4, wd.shape[1]
    return pl.pallas_call(
        ffn_out_kernel,
        grid_spec=pltpu.PrefetchScalarGridSpec(
            num_scalar_prefetch=1,
            grid=(4,),
            in_specs=[ANY] * 9 + [pl.BlockSpec((b, h), lambda j, s: (j, 0))],
            out_specs=[
                pl.BlockSpec((b, d), lambda j, s: (jnp.minimum(j, 1), 0)),
                pl.BlockSpec((b, d), lambda j, s: (jnp.maximum(j - 2, 0), 0)),
            ],
            scratch_shapes=[pltpu.VMEM((h, d), bf16), pltpu.SemaphoreType.DMA((9,))],
        ),
        out_shape=[jax.ShapeDtypeStruct((2 * b, d), bf16)] * 2,
        compiler_params=params(9),
        cost_estimate=cost(1 << 24),
        name="ffn_out",
    )(s, wd, *d_parts, hidden)


def grad_rows_kernel(by_cols, s_ref, left_ref, right_ref, sent_a, keep_a, sent_b, keep_b):
    j = pl.program_id(0)
    grad = contract(left_ref[...], right_ref[...], 0, 0).astype(bf16)
    rows, cols = grad.shape
    if by_cols:
        first, second = grad[:, : cols // 2], grad[:, cols // 2 :]
    else:
        r = rows // 4
        first = jnp.concatenate([grad[:r], grad[2 * r : 3 * r]], 0)
        second = jnp.concatenate([grad[r : 2 * r], grad[3 * r :]], 0)

    @pl.when(j % 2 == 1)
    def _():
        sent_a[0] = first

    @pl.when(j % 2 == 0)
    def _():
        keep_a[0] = first

    @pl.when(j >= 2)
    def _():
        sent_b[0] = second

    @pl.when(j < 2)
    def _():
        keep_b[0] = second


def grad_rows_call(s, left, right, by_cols, name):
    n, rows = left.shape
    cols = right.shape[1]
    half = (rows // 4, cols // 2) if by_cols else (rows // 8, cols)
    maps = [
        lambda j, s: (j // 2, 0, 0),
        lambda j, s: (j // 2, 0, 0),
        lambda j, s: (jnp.maximum(j - 2, 0), 0, 0),
        lambda j, s: (jnp.minimum(j, 1), 0, 0),
    ]
    return pl.pallas_call(
        functools.partial(grad_rows_kernel, by_cols),
        grid_spec=pltpu.PrefetchScalarGridSpec(
            num_scalar_prefetch=1,
            grid=(4,),
            in_specs=[pl.BlockSpec((n, rows // 4), lambda j, s: (0, s[2] ^ j)), fixed(n, cols)],
            out_specs=[pl.BlockSpec((1,) + half, m) for m in maps],
        ),
        out_shape=[jax.ShapeDtypeStruct((2,) + half, bf16)] * 4,
        compiler_params=params(11),
        cost_estimate=cost(1 << 24),
        name=name,
    )(s, left, right)


def grad_cols_kernel(s_ref, left_ref, r0, r1, r2, r3, sent_a, keep_a, sent_b, keep_b, right, sems):
    k = pl.program_id(0)
    b = r0.shape[0]
    cols = left_ref.shape[0] // 4

    def copy(k, i):
        src = (r0, r1, r2, r3)[i].at[:, pl.ds(pl.multiple_of(k * cols, cols), cols)]
        return pltpu.make_async_copy(src, right.at[k, pl.ds(i * b, b), :], sems.at[k, i])

    @pl.when(k == 0)
    def _():
        for block in range(4):
            for i in range(4):
                copy(block, i).start()

    for i in range(4):
        copy(k, i).wait()
    grad = contract(left_ref[...], right[k], 0, 0)
    grad = grad.astype(bf16)
    rows = grad.shape[0] // 4
    for a in range(4):
        piece = grad[a * rows : (a + 1) * rows]
        j = s_ref[2] ^ a

        @pl.when((k < 2) & (j % 2 == 1))
        def _():
            sent_a[j // 2] = piece

        @pl.when((k < 2) & (j % 2 == 0))
        def _():
            keep_a[j // 2] = piece

        @pl.when((k >= 2) & (j >= 2))
        def _():
            sent_b[j % 2] = piece

        @pl.when((k >= 2) & (j < 2))
        def _():
            keep_b[j % 2] = piece


def grad_cols_call(s, left, rights, name):
    n, rows = left.shape
    b, cols = rights[0].shape
    first = pl.BlockSpec((2, rows // 4, cols // 4), lambda k, s: (0, 0, jnp.minimum(k, 1)))
    second = pl.BlockSpec((2, rows // 4, cols // 4), lambda k, s: (0, 0, jnp.maximum(k - 2, 0)))
    return pl.pallas_call(
        grad_cols_kernel,
        grid_spec=pltpu.PrefetchScalarGridSpec(
            num_scalar_prefetch=1,
            grid=(4,),
            in_specs=[fixed(n, rows)] + [ANY] * 4,
            out_specs=[first, first, second, second],
            scratch_shapes=[pltpu.VMEM((4, n, cols // 4), bf16), pltpu.SemaphoreType.DMA((4, 4))],
        ),
        out_shape=[jax.ShapeDtypeStruct((2, rows // 4, cols // 2), bf16)] * 4,
        compiler_params=params(14),
        cost_estimate=cost(1 << 24),
        name=name,
    )(s, left, *rights)


def widen_kernel(side, in_ref, out_ref):
    first, second = in_ref[0, 0].astype(f32), in_ref[0, 1].astype(f32)
    out_ref[...] = jnp.concatenate([first, second], 1 if side else 0)


def widen_call(whole, side, name):
    _, _, rows, cols = whole.shape
    block = (rows, 2 * cols) if side else (2 * rows, cols)
    return pl.pallas_call(
        functools.partial(widen_kernel, side),
        grid=(8,),
        in_specs=[pl.BlockSpec((1, 2, rows, cols), lambda j: (j, 0, 0, 0))],
        out_specs=pl.BlockSpec(block, lambda j: (j, 0)),
        out_shape=jax.ShapeDtypeStruct((8 * block[0], block[1]), f32),
        compiler_params=params(8),
        cost_estimate=cost(1 << 20),
        name=name,
    )(whole)


def place_kernel(write, s_ref, *refs):
    k = pl.program_id(0)
    for i in range(8):

        @pl.when(k == i)
        def _():
            write(refs[i], refs[8:])


def write_rows(piece, outs):
    outs[0][...] = jnp.concatenate([piece[0], piece[1]], 0).astype(f32)


def write_attention(piece, outs):
    query, key, value, out = outs
    r, s = query.shape[0], out.shape[0]
    query[...] = piece[0, :r].astype(f32)
    key[...] = piece[1, :r, :128].astype(f32)
    value[...] = piece[1, :r, 128:].astype(f32)
    sides = [piece[half, r + at * s : r + (at + 1) * s] for half in range(2) for at in range(2)]
    out[...] = jnp.concatenate(sides, 1).astype(f32)


def place_call(s, pieces, write, blocks, name):
    eighth = lambda k, s: (2 * (s[2] ^ (k % 4)) + (s[1] ^ (k // 4)), 0)
    return pl.pallas_call(
        functools.partial(place_kernel, write),
        grid_spec=pltpu.PrefetchScalarGridSpec(
            num_scalar_prefetch=1,
            grid=(8,),
            in_specs=[fixed(*pieces[0].shape)] * 8,
            out_specs=[pl.BlockSpec(block, eighth) for block in blocks],
        ),
        out_shape=[jax.ShapeDtypeStruct((8 * r, cols), f32) for r, cols in blocks],
        compiler_params=params(12),
        cost_estimate=cost(1 << 20),
        name=name,
    )(s, *pieces)


def grad_attention_kernel(s_ref, n1_ref, low_ref, att_ref, b0, b1, b2, b3, sent_a, keep_a, sent_b, keep_b, whole):
    j = pl.program_id(0)
    b = b0.shape[0]

    @pl.when(j == 0)
    def _():
        total = None
        for i, block in enumerate((b0, b1, b2, b3)):
            part = contract(att_ref[i * b : (i + 1) * b, :], block[...], 0, 0)
            total = part if total is None else total + part
        whole[...] = total.astype(bf16)

    qkv = contract(n1_ref[...], low_ref[...], 0, 0).astype(bf16)
    r = qkv.shape[0] // 2
    s = whole.shape[0] // 8
    k = qkv.shape[1] // 2
    out = whole[pl.ds(pl.multiple_of((s_ref[2] ^ j) * 2 * s, 2 * s), 2 * s), :]

    def joined(at):
        parts = []
        for core in range(2):
            some = out[core * s : (core + 1) * s]
            parts += [
                qkv[core * r : (core + 1) * r, at * k : (at + 1) * k],
                some[:, 2 * at * k : (2 * at + 1) * k],
                some[:, (2 * at + 1) * k : (2 * at + 2) * k],
            ]
        return jnp.concatenate(parts, 0)

    @pl.when(j % 2 == 1)
    def _():
        sent_a[0] = joined(0)

    @pl.when(j % 2 == 0)
    def _():
        keep_a[0] = joined(0)

    @pl.when(j >= 2)
    def _():
        sent_b[0] = joined(1)

    @pl.when(j < 2)
    def _():
        keep_b[0] = joined(1)


def grad_attention_call(s, n1, low, att, blocks):
    n, d = n1.shape
    b = n // 4
    half = (d // 4 + att.shape[1] // 2, 256)
    maps = [
        lambda j, s: (j // 2, 0, 0),
        lambda j, s: (j // 2, 0, 0),
        lambda j, s: (jnp.maximum(j - 2, 0), 0, 0),
        lambda j, s: (jnp.minimum(j, 1), 0, 0),
    ]
    return pl.pallas_call(
        grad_attention_kernel,
        grid_spec=pltpu.PrefetchScalarGridSpec(
            num_scalar_prefetch=1,
            grid=(4,),
            in_specs=[pl.BlockSpec((n, d // 4), lambda j, s: (0, s[2] ^ j)), fixed(n, low.shape[1]), fixed(n, att.shape[1])]
            + [fixed(b, d)] * 4,
            out_specs=[pl.BlockSpec((1,) + half, m) for m in maps],
            scratch_shapes=[pltpu.VMEM((att.shape[1], d), bf16)],
        ),
        out_shape=[jax.ShapeDtypeStruct((2,) + half, bf16)] * 4,
        compiler_params=params(18),
        cost_estimate=cost(1 << 24),
        name="grad_attention",
    )(s, n1, low, att, *blocks)


def permute(x, places, move):
    pairs = []
    for d in range(places):
        for t in range(T4):
            to = move(d, t)
            if to is not None:
                pairs.append((d * T4 + t, to[0] * T4 + to[1]))
    return lax.ppermute(x, AX, pairs)


def after(x, *events):
    return lax.optimization_barrier((x, events))[0]


def flip_core(d, t):
    return (d ^ 1, t)


def flip_z(d, t):
    return (d, t ^ 1)


def flip_far(d, t):
    return (d, t ^ 2)


def flip_e(bit):
    return lambda d, t: (d ^ (2 << bit), t)


def settle(d, t):
    return (d, t) if (d & 1) == (t >> 1) else (d ^ 1, t ^ 2)


def step(*values):
    return lax.optimization_barrier(values)


def eighth(w, c, e):
    rows = w.shape[0] // 8
    return lax.dynamic_slice_in_dim(w, (2 * e + c) * rows, rows, 0)


def around(piece, n):
    return [permute(piece, n, lambda d, t, j=j: (d ^ (2 * j), t)) for j in (1, 2, 3)]


def across(pieces, n):
    return [permute(piece, n, flip_core) for piece in pieces]


def first_sums(pieces, n):
    sent_a, keep_a, sent_b, keep_b = pieces
    got_a = permute(sent_a, n, flip_e(0))
    got_b = permute(sent_b, n, flip_e(1))
    return got_a, got_b


def first_add(pieces, got):
    got_a, got_b = got
    keep_a, keep_b = pieces[1], pieces[3]
    return keep_a[1] + got_a[1], keep_a[0] + got_a[0], keep_b[1] + got_b[1], keep_b[0] + got_b[0]


def second_sums(halves, n):
    return permute(halves[0], n, flip_e(1)), permute(halves[2], n, flip_e(0))


def second_add(halves, got, n):
    total = jnp.stack([halves[1] + got[0], halves[3] + got[1]])
    for extra in range(2, 20):
        if (2 << extra) < n:
            total = total + permute(total, n, flip_e(extra))
    return total


def cross_sent(total, c):
    half = total.shape[1] // 2
    return jnp.where(c == 0, total[:, half:], total[:, :half])


def cross_got(total, got, c):
    half = total.shape[1] // 2
    return jnp.where(c == 0, total[:, :half], got), jnp.where(c == 0, got, total[:, half:])


def neighbours(n):
    return None if n == 8 else [list(range(k, k + 8)) for k in range(0, n, 8)]


def whole_grad(mine, n):
    return lax.all_gather(mine, "dp", axis_index_groups=neighbours(n))


def vector_moves(n):
    bits = [1 << k for k in range(20) if 1 << k < n]
    return [lambda d, t, bit=bit: (d ^ bit, t) for bit in bits] + [flip_z, flip_far]


def local(
    block_input,
    doc_lengths,
    pad_mask,
    norm1_gain,
    w_query,
    w_key,
    w_value,
    query_gain,
    key_gain,
    w_out,
    norm2_gain,
    w_gate,
    w_up,
    w_down,
    cotangent,
):
    n = lax.axis_size("dp")
    d, t = lax.axis_index("dp"), lax.axis_index("tensor")
    c, p = d & 1, t >> 1
    e = (d >> 1) & 3
    shard = 2 * c + (t & 1)
    b = block_input.shape[0]
    seq_len = b * T4
    home = c == p
    wq = w_query.shape[1]
    wk = w_key.shape[1]
    width = block_input.shape[1]
    s = jnp.stack([shard, c, e]).astype(jnp.int32)

    marks = jnp.concatenate([doc_lengths, pad_mask], 1)
    mine_out = eighth(w_out, c, e)
    mine_qkv = jnp.concatenate([eighth(w, c, e) for w in (w_query, w_key, w_value)], 1)
    mine_gate, mine_up, mine_down = (eighth(w, c, e) for w in (w_gate, w_up, w_down))
    x_own = permute(block_input, n, settle)
    qkv_hop = permute(mine_qkv, n, flip_far)
    out_z = permute(mine_out, n, flip_z)
    marks = jnp.where(home, marks, permute(marks, n, flip_core))
    lengths_row, pad_row = marks[0, : doc_lengths.shape[1]], marks[0, doc_lengths.shape[1] :]
    x_over, x_near = permute(x_own, n, flip_z), permute(x_own, n, flip_core)
    qkv_hop, out_z, mine_gate, mine_up, mine_down, late_dy = after(
        [qkv_hop, out_z, mine_gate, mine_up, mine_down, cotangent], x_own
    )
    two_out = jnp.stack([mine_out, out_z])
    out_far = permute(two_out, n, flip_far)
    qkv_around = around(qkv_hop, n)
    dy_own = permute(late_dy, n, settle)
    x_over, x_near = step(x_over, x_near)
    x_far = permute(x_over, n, flip_core)
    qkv_around, out_far, mine_gate, mine_up = after([qkv_around, out_far, mine_gate, mine_up], x_over)
    qkv_mine = [qkv_hop] + qkv_around
    qkv_other = across(qkv_mine, n)
    out_all = lax.all_gather(jnp.concatenate([two_out, out_far]), "dp", axis_index_groups=neighbours(n))
    gate_hop, up_hop = permute(mine_gate, n, flip_far), permute(mine_up, n, flip_far)
    x_blocks = [x_own, x_over, x_near, x_far]

    positions = jnp.arange(seq_len, dtype=jnp.int32)
    doc_starts, cos_half, sin_half = doc_tables(lengths_row, positions, HD)
    cos = jnp.concatenate([cos_half] * 4, 1)
    sin = jnp.concatenate([-sin_half, sin_half] * 2, 1)
    live = jnp.where(pad_row == 1, positions, -1)
    start_col = jnp.broadcast_to(doc_starts[:, None], (seq_len, 128))
    start_row = jnp.broadcast_to(doc_starts[None], (8, seq_len))
    live_col = jnp.broadcast_to(live[:, None], (seq_len, 128))
    live_row = jnp.broadcast_to(live[None], (8, seq_len))
    gains = jnp.concatenate([query_gain] * (wq // HD) + [key_gain] * (wk // HD))[None]
    qgain_pair = jnp.concatenate([query_gain] * 2)[None]
    kgain_pair = jnp.concatenate([key_gain] * 2)[None]

    rows_one, pre, qk, values, w_qkv = qkv_call(
        s, x_blocks, (w_query, w_key, w_value), qkv_mine + qkv_other, norm1_gain[None], gains, cos, sin
    )
    gate_hop, dy_own = after([gate_hop, dy_own], qk)
    gate_around = around(gate_hop, n)
    dy_over, dy_near = permute(dy_own, n, flip_z), permute(dy_own, n, flip_core)
    attended, attended_f, lse = attend_call(s, qk, after(values, gate_hop, dy_own), start_col, live_row)

    att_over, att_near = permute(attended, n, flip_z), permute(attended, n, flip_core)
    up_hop, mine_down = after([up_hop, mine_down], attended)
    up_around = around(up_hop, n)
    down_hop = permute(mine_down, n, flip_far)
    att_over, att_near = step(att_over, att_near)
    att_far = permute(att_over, n, flip_core)
    gate_around, dy_over, dy_near = after([gate_around, dy_over, dy_near], att_over)
    gate_mine = [gate_hop] + gate_around
    gate_parts = gate_mine + across(gate_mine, n)
    dy_far = permute(dy_over, n, flip_core)
    up_around, down_hop = after([up_around, down_hop], att_far)
    up_mine = [up_hop] + up_around
    up_parts = up_mine + across(up_mine, n)
    down_around = around(down_hop, n)
    dy_blocks = [dy_own, dy_over, dy_near, dy_far]
    rows_two, hidden, by_gate, by_up, residual, w_out_own = ffn_call(
        s, x_blocks, [attended, att_over, att_near, att_far], out_all, w_gate, gate_parts, w_up, up_parts,
        after(norm2_gain[None], down_hop),
    )

    down = grad_cols_call(s, hidden, dy_blocks, "grad_down")
    down_mine = [down_hop] + after(down_around, hidden)
    down_parts = down_mine + across(down_mine, n)
    down_got = first_sums(down, n)
    gate_grad, up_grad, low2, high2 = ffn_back_call(
        s, dy_blocks, w_down, down_parts, w_gate, gate_parts, w_up, up_parts, after(by_gate, *down), by_up
    )
    (high_got,) = step(permute(high2, n, flip_core))
    low_half = low2 + high_got
    low_over = permute(low_half[b:], n, flip_z)
    gate = grad_rows_call(s, rows_two, after(gate_grad, low_half), False, "grad_gate")
    gate_got = first_sums(gate, n)
    up = grad_rows_call(s, rows_two, after(up_grad, *gate), False, "grad_up")
    up_got = first_sums(up, n)
    down = first_add(down, after(down_got, *up))
    down_got = second_sums(down, n)
    grad_n2 = (low_half[:b] + after(low_over, *down)).astype(f32)
    inv = lax.rsqrt(jnp.mean(residual * residual, axis=-1, keepdims=True) + epsilon)
    scaled = norm2_gain * grad_n2
    grad_residual = (
        dy_own.astype(f32)
        + inv * scaled
        - residual * (inv * inv * inv) * jnp.mean(scaled * residual, axis=-1, keepdims=True)
    )
    grad_norm2 = jnp.sum(grad_n2 * residual * inv, axis=0)
    gb_own = grad_residual.astype(bf16)
    gb_over, gb_near = permute(gb_own, n, flip_z), permute(gb_own, n, flip_core)
    ffn_low, ffn_high = ffn_out_call(s, w_down, down_parts, after(hidden, gb_own))
    gate = first_add(gate, after(gate_got, ffn_low))
    gate_got = second_sums(gate, n)
    ffn_got = permute(ffn_high, n, flip_core)
    gb_over, gb_near = step(*after([gb_over, gb_near], *gate))
    ffn_got = after(ffn_got, gb_over)
    gb_far = permute(gb_over, n, flip_core)
    up = first_add(up, after(up_got, gb_over))
    up_got = second_sums(up, n)
    down = second_add(down, after(down_got, gb_over, *up), n)
    gate = second_add(gate, after(gate_got, down), n)
    ffn_half = ffn_low + ffn_got
    gb_far, down_got, gate_got = step(
        gb_far, permute(cross_sent(down, c), n, flip_core), permute(cross_sent(gate, c), n, flip_core)
    )
    down_kept, down_sent = cross_got(down, down_got, c)
    gate_kept, gate_sent = cross_got(gate, gate_got, c)
    down_got, gate_got = permute(down_sent, n, flip_far), permute(gate_sent, n, flip_far)
    ffn_over = permute(ffn_half[b:], n, flip_z)
    gb_blocks = [gb_own, gb_over, gb_near, gb_far]

    low, gain_terms, low1, high1 = attend_back_call(
        s, qk, after(values, ffn_half, gate_sent, down_sent), pre, qgain_pair, kgain_pair, cos, sin, start_row, live_col,
        attended_f, lse, w_out_own, w_qkv, gb_blocks,
    )
    up = second_add(up, after(up_got, low), n)
    high_got, up_got = step(permute(high1, n, flip_core), permute(cross_sent(up, c), n, flip_core))
    low_half = low1 + high_got
    low_over = permute(low_half[b:], n, flip_z)
    up_kept, up_sent = cross_got(up, up_got, c)
    up_got = permute(up_sent, n, flip_far)
    down_mine = down_kept + after(down_got, low_half)
    down_all = whole_grad(down_mine, n)
    att = grad_attention_call(s, rows_one, after(low, down_mine, up_sent), attended, gb_blocks)
    att_got = first_sums(att, n)
    block_output = residual + (ffn_half[:b] + after(ffn_over, *att)).astype(f32)
    gate_mine = gate_kept + after(gate_got, *att)
    low_over = after(low_over, gate_mine, block_output)
    grad_n1 = (low_half[:b] + low_over).astype(f32)
    gate_around = around(gate_mine, n)
    att = first_add(att, after(att_got, low_over))
    att_got = second_sums(att, n)
    x_f = x_own.astype(f32)
    inv = lax.rsqrt(jnp.mean(x_f * x_f, axis=-1, keepdims=True) + epsilon)
    scaled = norm1_gain * after(grad_n1, *att)
    input_grad = (
        grad_residual
        + inv * scaled
        - x_f * (inv * inv * inv) * jnp.mean(scaled * x_f, axis=-1, keepdims=True)
    )
    grad_norm1 = jnp.sum(grad_n1 * x_f * inv, axis=0)
    head_terms = gain_terms[:, :HD] + gain_terms[:, HD:]
    vec = jnp.concatenate([grad_norm1, grad_norm2, head_terms[0] + head_terms[1], head_terms[2]])[None]
    moves = vector_moves(n)
    vec_got = permute(vec, n, moves[0])
    att = second_add(att, after(att_got, input_grad, vec), n)
    att_got = permute(cross_sent(att, c), n, flip_core)
    up_mine = up_kept + after(up_got, att)
    up_around = around(up_mine, n)
    att_got, vec_got = step(after(att_got, up_mine), vec_got)
    att_kept, att_sent = cross_got(att, att_got, c)
    att_got = permute(att_sent, n, flip_far)
    vec = vec + vec_got
    vec_got = permute(after(vec, att_sent), n, moves[1])
    late_output, late_grad, gate_around = after([block_output, input_grad, gate_around], att_sent)
    settled_output = permute(late_output.astype(bf16), n, settle)
    settled_grad = permute(late_grad.astype(bf16), n, settle)
    gate_across = across([gate_mine] + gate_around, n)
    att_got, vec_got = step(*after([att_got, vec_got], gate_around))
    att_mine = att_kept + att_got
    att_around = around(att_mine, n)
    vec = vec + vec_got
    vec_got = permute(after(vec, att_mine), n, moves[2])
    (grad_gate,) = place_call(
        s, [gate_mine] + gate_around + after(gate_across, att_mine), write_rows, [(width // 8, w_gate.shape[1])], "place_gate"
    )
    up_around = after(up_around, grad_gate)
    up_across = across([up_mine] + up_around, n)
    att_around, vec_got = after([att_around, vec_got], up_around)
    att_across = across([att_mine] + att_around, n)
    vec = vec + vec_got
    vec_got = permute(vec, n, moves[3])
    (grad_up,) = place_call(
        s, [up_mine] + up_around + after(up_across, vec), write_rows, [(width // 8, w_gate.shape[1])], "place_up"
    )
    vec = vec + after(vec_got, grad_up)
    vec_got = permute(vec, n, moves[4])
    grad_query, grad_key, grad_value, grad_out = place_call(
        s,
        [att_mine] + att_around + after(att_across, vec),
        write_attention,
        [(width // 8, wq), (width // 8, wk), (width // 8, wk), (w_out.shape[0] // 8, width)],
        "place_attention",
    )
    vec = vec + after(vec_got, grad_query)
    for move in moves[5:]:
        vec = vec + permute(vec, n, move)
    vec = vec[0]
    grad_down = widen_call(after(down_all, vec), True, "widen_down")
    block_output = jnp.where(home, block_output, after(settled_output, grad_down).astype(f32))
    input_grad = jnp.where(home, input_grad, after(settled_grad, grad_down).astype(f32))
    return (
        block_output,
        input_grad,
        vec[:width],
        grad_query,
        grad_key,
        grad_value,
        vec[2 * width : 2 * width + HD],
        vec[2 * width + HD :],
        grad_out,
        vec[width : 2 * width],
        grad_gate,
        grad_up,
        grad_down,
    )


def solution(mesh):
    placed = (
        P(("dp", "tensor"), None),
        P("dp", None),
        P("dp", None),
        P(),
        P(None, "tensor"),
        P(None, "tensor"),
        P(None, "tensor"),
        P(),
        P(),
        P("tensor", None),
        P(),
        P(None, "tensor"),
        P(None, "tensor"),
        P("tensor", None),
        P(("dp", "tensor"), None),
    )
    return jax.shard_map(
        local,
        mesh=mesh,
        in_specs=placed,
        out_specs=(
            P(("dp", "tensor"), None),
            P(("dp", "tensor"), None),
            P(),
            P(None, "tensor"),
            P(None, "tensor"),
            P(None, "tensor"),
            P(),
            P(),
            P("tensor", None),
            P(),
            P(None, "tensor"),
            P(None, "tensor"),
            P("tensor", None),
        ),
        check_vma=False,
    )
```

```python
import functools
import math

import jax
import jax.numpy as jnp
from jax import lax
from jax.experimental import pallas as pl
from jax.experimental.pallas import tpu as pltpu
from jax.sharding import PartitionSpec as P

HD = 64
AX = ("dp", "tensor")
T4 = 4
VMEM_MB = 1 << 20

epsilon = 1e-05
rope_base = 1000000.0
NEG = -1000000000.0
bf16 = jnp.bfloat16
f32 = jnp.float32


def doc_tables(lengths_row, positions, head_dim):
    doc_ends = jnp.cumsum(lengths_row)
    passed = positions[:, None] >= doc_ends[None, :]
    doc_starts = jnp.sum(jnp.where(passed, lengths_row[None, :], 0), axis=1)
    offsets = (positions - doc_starts).astype(f32)
    freqs = jnp.exp(
        jnp.arange(head_dim // 2, dtype=f32) * (-2.0 * math.log(rope_base) / head_dim)
    )
    angles = offsets[:, None] * freqs[None, :]
    return (doc_starts, jnp.cos(angles), jnp.sin(angles))


def contract(a, b, da, db, precision=None):
    return lax.dot_general(
        a, b, (((da,), (db,)), ((), ())), preferred_element_type=f32, precision=precision
    )


def swap_halves(y):
    width = y.shape[1]
    lane = lax.broadcasted_iota(jnp.int32, y.shape, 1)
    return jnp.where(lane % HD < HD // 2, pltpu.roll(y, width - HD // 2, 1), pltpu.roll(y, HD // 2, 1))


def head_mean(y):
    width = y.shape[1]
    at = lax.broadcasted_iota(jnp.int32, (width, width), 0) // HD
    to = lax.broadcasted_iota(jnp.int32, (width, width), 1) // HD
    ones = jnp.where(at == to, 1.0 / HD, 0.0).astype(f32)
    return contract(y, ones, 1, 0, lax.Precision.HIGHEST)


class Weight:
    def __init__(self, s_ref, own, parts, to, sems, start=0):
        self.core, self.e = s_ref[1], s_ref[2]
        self.own, self.parts, self.to, self.sems, self.start_col = own, parts, to, sems, start

    def copies(self):
        start = 0
        for i, w in enumerate(self.own):
            wide = w.shape[1]
            to = self.to if len(self.own) == 1 else self.to.at[:, pl.ds(start, wide)]
            yield 0, functools.partial(pltpu.make_async_copy, w, to, self.sems.at[8 + i])
            start += wide
        rows = self.to.shape[0] // 8
        for j in range(4):
            for other in range(2):
                at = pl.multiple_of((2 * (self.e ^ j) + 1 - other) * rows, rows)
                src = self.parts[4 * other + j]
                if src.shape[1] != self.to.shape[1]:
                    src = src.at[:, pl.ds(self.start_col, self.to.shape[1])]
                to = self.to.at[pl.ds(at, rows), :]
                yield 1, functools.partial(pltpu.make_async_copy, src, to, self.sems.at[2 * j + other])

    def each(self, act):
        for core in range(2):

            @pl.when(self.core == core)
            def _():
                for whose, copy in self.copies():
                    if whose == core:
                        act(copy())

    def start(self):
        self.each(lambda copy: copy.start())

    def wait(self):
        self.each(lambda copy: copy.wait())


ANY = pl.BlockSpec(memory_space=pl.ANY)


def fixed(*shape):
    return pl.BlockSpec(shape, lambda *_: (0,) * len(shape))


def cost(flops):
    return pl.CostEstimate(flops=flops, bytes_accessed=1 << 16, transcendentals=0)


def params(mib):
    return pltpu.CompilerParams(vmem_limit_bytes=mib * VMEM_MB)


def qkv_kernel(s_ref, *refs):
    pieces, own, parts, refs = refs[:4], refs[4:7], refs[7:15], refs[15:]
    g1_ref, gains_ref, cos_ref, sin_ref, n1_ref, pre_ref, qk_ref, v_ref, w_ref, xs, xsem, wsem = refs
    j = pl.program_id(0)
    weight = Weight(s_ref, own, parts, w_ref, wsem)

    @pl.when(j == 0)
    def _():
        for k in range(4):
            pltpu.make_async_copy(pieces[k], xs.at[k], xsem.at[k]).start()
        weight.start()

    pltpu.make_async_copy(pieces[0], xs.at[j], xsem.at[j]).wait()
    x = xs[j].astype(f32)
    inv = lax.rsqrt(jnp.mean(x * x, axis=-1, keepdims=True) + epsilon)
    n1 = (x * inv * g1_ref[...]).astype(bf16)
    n1_ref[...] = n1

    @pl.when(j == 0)
    def _():
        weight.wait()

    qkv = jnp.dot(n1, w_ref[...], preferred_element_type=f32)
    width = pre_ref.shape[1]
    pre = qkv[:, :width]
    pre_ref[...] = pre
    v_ref[...] = qkv[:, width:].astype(bf16)
    y = pre * lax.rsqrt(head_mean(pre * pre) + epsilon) * gains_ref[...]
    cos = jnp.concatenate([cos_ref[...]] * (width // 128), 1)
    sin = jnp.concatenate([sin_ref[...]] * (width // 128), 1)
    qk = (y * cos + swap_halves(y) * sin).astype(bf16)
    lane = lax.broadcasted_iota(jnp.int32, qk.shape, 1)
    qk_ref[...] = jnp.where(lane < width - 128, qk * 0.125, qk).astype(bf16)


def qkv_call(s, xs, w_own, w_parts, g1, gains, cos, sin):
    b, d = xs[0].shape
    wid = w_parts[0].shape[1]
    qkw = wid - 128
    natural = lambda j, s: (s[0] ^ j, 0)
    return pl.pallas_call(
        qkv_kernel,
        grid_spec=pltpu.PrefetchScalarGridSpec(
            num_scalar_prefetch=1,
            grid=(4,),
            in_specs=[ANY] * 15
            + [fixed(1, d), fixed(1, qkw), pl.BlockSpec((b, 128), natural), pl.BlockSpec((b, 128), natural)],
            out_specs=[
                pl.BlockSpec((b, d), lambda j, s: (j, 0)),
                pl.BlockSpec((b, qkw), natural),
                pl.BlockSpec((b, qkw), natural),
                pl.BlockSpec((b, 128), natural),
                fixed(d, wid),
            ],
            scratch_shapes=[
                pltpu.VMEM((4, b, d), bf16),
                pltpu.SemaphoreType.DMA((4,)),
                pltpu.SemaphoreType.DMA((11,)),
            ],
        ),
        out_shape=[
            jax.ShapeDtypeStruct((4 * b, d), bf16),
            jax.ShapeDtypeStruct((4 * b, qkw), f32),
            jax.ShapeDtypeStruct((4 * b, qkw), bf16),
            jax.ShapeDtypeStruct((4 * b, 128), bf16),
            jax.ShapeDtypeStruct((d, wid), bf16),
        ],
        compiler_params=params(58),
        cost_estimate=cost(1 << 24),
        name="qkv",
    )(s, *xs, *w_own, *w_parts, g1, gains, cos, sin)


def both_heads(pair):
    lane = lax.broadcasted_iota(jnp.int32, pair.shape, 1)
    zero = jnp.zeros_like(pair)
    return jnp.concatenate([jnp.where(lane < HD, pair, zero), jnp.where(lane < HD, zero, pair)], 0)


def pick_heads(both):
    r = both.shape[0] // 2
    lane = lax.broadcasted_iota(jnp.int32, (r, 128), 1)
    return jnp.where(lane < HD, both[:r], both[r:])


def twice(kv, g):
    lane = lax.broadcasted_iota(jnp.int32, kv.shape, 1)
    turned = pltpu.roll(kv.astype(f32), HD, 1).astype(kv.dtype)
    return jnp.where((lane < HD) == (g == 0), kv, turned)


def attend_kernel(s_ref, q_ref, k_ref, v_ref, start_ref, live_ref, att_ref, out_ref, lse_ref, bias):
    g = pl.program_id(0)
    n = k_ref.shape[0]
    b = n // 4

    @pl.when(g == 0)
    def _():
        for a in range(4):
            keys = (a + 1) * b
            start = start_ref[a * b : (a + 1) * b, :1]
            q_at = lax.broadcasted_iota(jnp.int32, (b, keys), 0) + a * b
            k_at = lax.broadcasted_iota(jnp.int32, (b, keys), 1)
            allowed = ((live_ref[:1, :keys] >= start) & (k_at <= q_at)) | (k_at == q_at)
            bias[a * b : (a + 1) * b, :keys] = jnp.where(allowed, 0.0, NEG)

    kd = twice(k_ref[...], g)
    vd = twice(v_ref[...], g)
    for a in range(4):
        keys = (a + 1) * b
        rows = slice(a * b, (a + 1) * b)
        qm = both_heads(q_ref[rows, :])
        scores = contract(qm, kd[:keys], 1, 1)
        extra = bias[rows, :keys]
        expo = jnp.exp(scores + jnp.concatenate([extra, extra], 0))
        total = jnp.sum(expo, axis=-1, keepdims=True)
        pair = pick_heads(contract(expo.astype(bf16), vd[:keys], 1, 0) / total)
        out_ref[rows, :] = pair
        att_ref[pl.ds(pl.multiple_of((s_ref[0] ^ a) * b, b), b), :] = pair.astype(bf16)
        lse_ref[0, a] = jnp.transpose(jnp.broadcast_to(jnp.log(total), (2 * b, 128)))[:1]


def attend_call(s, qk, v, start, live):
    n = qk.shape[0]
    b = n // 4
    lanes = lambda g, s: (0, g)
    return pl.pallas_call(
        attend_kernel,
        grid_spec=pltpu.PrefetchScalarGridSpec(
            num_scalar_prefetch=1,
            grid=(2,),
            in_specs=[
                pl.BlockSpec((n, 128), lanes),
                pl.BlockSpec((n, 128), lambda g, s: (0, 2)),
                fixed(n, 128),
                fixed(n, 128),
                fixed(8, n),
            ],
            out_specs=[
                pl.BlockSpec((n, 128), lanes),
                pl.BlockSpec((n, 128), lanes),
                pl.BlockSpec((1, 4, 1, 2 * b), lambda g, s: (g, 0, 0, 0)),
            ],
            scratch_shapes=[pltpu.VMEM((n, n), f32)],
        ),
        out_shape=[
            jax.ShapeDtypeStruct((n, 256), bf16),
            jax.ShapeDtypeStruct((n, 256), f32),
            jax.ShapeDtypeStruct((2, 4, 1, 2 * b), f32),
        ],
        compiler_params=params(14),
        cost_estimate=cost(1 << 24),
        name="attend",
    )(s, qk, qk, v, start, live)


def norm_back(grad, pre, gain, cos, sin):
    turned = grad * cos - swap_halves(grad) * sin
    inv = lax.rsqrt(head_mean(pre * pre) + epsilon)
    scaled = turned * gain
    dpre = inv * scaled - pre * (inv * inv * inv) * head_mean(scaled * pre)
    return dpre, jnp.sum(turned * pre * inv, axis=0, keepdims=True)


def attend_back_kernel(s_ref, q_ref, k_ref, v_ref, qpre_ref, kpre_ref, gains_ref, kgain_ref, cos_ref, sin_ref,
                       start_ref, live_ref, out_ref, lse_ref, wout_ref, w_ref, b0, b1, b2, b3,
                       low_ref, gain_ref, lo_ref, hi_ref, bias, dk, dv, dkall, dvall, dos, gb, sems):
    g = pl.program_id(0)
    n = k_ref.shape[0]
    b = n // 4
    pieces = (b0, b1, b2, b3)

    @pl.when(g == 0)
    def _():
        for k in range(4):
            pltpu.make_async_copy(pieces[k], gb.at[k], sems.at[k]).start()
        for a in range(4):
            keys = (a + 1) * b
            start = start_ref[:1, a * b : (a + 1) * b]
            k_at = lax.broadcasted_iota(jnp.int32, (keys, b), 0)
            q_at = lax.broadcasted_iota(jnp.int32, (keys, b), 1) + a * b
            allowed = ((live_ref[:keys, :1] >= start) & (k_at <= q_at)) | (k_at == q_at)
            bias[:keys, a * b : (a + 1) * b] = jnp.where(allowed, 0.0, NEG)
        for k in range(4):
            pltpu.make_async_copy(pieces[k], gb.at[k], sems.at[k]).wait()
            dos[k] = contract(gb[k], wout_ref[...], 1, 1).astype(bf16)

    kd = twice(k_ref[...], g)
    vd = twice(v_ref[...], g)
    gain_sum = jnp.zeros((1, 128), f32)
    ones = jnp.ones((8, 128), f32)
    for a in (3, 2, 1, 0):
        keys = (a + 1) * b
        rows = slice(a * b, (a + 1) * b)
        home = s_ref[0] ^ a
        qm = both_heads(q_ref[rows, :])
        dout = jnp.where(g == 0, dos[home, :, :128], dos[home, :, 128:])
        dom = both_heads(dout)
        delta = contract(ones, both_heads(dout.astype(f32) * out_ref[rows, :]), 1, 1, lax.Precision.HIGHEST)[:1]
        scores = contract(kd[:keys], qm, 1, 1)
        extra = bias[:keys, rows]
        probs = jnp.exp(scores + (jnp.concatenate([extra, extra], 1) - lse_ref[0, a]))
        dprobs = contract(vd[:keys], dom, 1, 1)
        dscores = (probs * (dprobs - delta)).astype(bf16)
        dv_add = contract(probs.astype(bf16), dom, 1, 0)
        dk_add = contract(dscores, qm, 1, 0)
        if a == 3:
            dv[...] = dv_add
            dk[...] = dk_add
        else:
            dv[:keys] += dv_add
            dk[:keys] += dk_add
        dq = pick_heads(contract(dscores, kd[:keys], 0, 0)) * 0.125
        dpre, gain_part = norm_back(dq, qpre_ref[rows, :], gains_ref[...], cos_ref[rows, :], sin_ref[rows, :])
        at = pl.ds(pl.multiple_of(home * b, b), b)
        low_ref[at, pl.ds(pl.multiple_of(g * 128, 128), 128)] = dpre.astype(bf16)
        gain_sum = gain_sum + gain_part
    gain_ref[pl.ds(g, 1), :] = gain_sum
    lane = lax.broadcasted_iota(jnp.int32, (n, 128), 1)
    dk_all = dk[...] + pltpu.roll(dk[...], HD, 1)
    dv_all = dv[...] + pltpu.roll(dv[...], HD, 1)

    @pl.when(g == 0)
    def _():
        dkall[...] = dk_all
        dvall[...] = dv_all

    @pl.when(g == 1)
    def _():
        grad_k = jnp.where(lane < HD, dkall[...], dk_all)
        grad_v = jnp.where(lane < HD, dvall[...], dv_all)
        dpre, gain_part = norm_back(grad_k, kpre_ref[...], kgain_ref[...], cos_ref[...], sin_ref[...])
        gain_ref[2:3, :] = gain_part
        for a in range(4):
            at = pl.ds(pl.multiple_of((s_ref[0] ^ a) * b, b), b)
            low_ref[at, 256:384] = dpre[a * b : (a + 1) * b].astype(bf16)
            low_ref[at, 384:512] = grad_v[a * b : (a + 1) * b].astype(bf16)
        hi_ref[...] = contract(low_ref[2 * b :, :], w_ref[...], 1, 1).astype(bf16)
        lo_ref[...] = contract(low_ref[: 2 * b, :], w_ref[...], 1, 1).astype(bf16)


def attend_back_call(s, qk, v, pre, qgain, kgain, cos, sin, start, live, out, lse, wout, w, blocks):
    n = v.shape[0]
    b = n // 4
    d = blocks[0].shape[1]
    lanes = pl.BlockSpec((n, 128), lambda g, s: (0, g))
    third = pl.BlockSpec((n, 128), lambda g, s: (0, 2))
    return pl.pallas_call(
        attend_back_kernel,
        grid_spec=pltpu.PrefetchScalarGridSpec(
            num_scalar_prefetch=1,
            grid=(2,),
            in_specs=[lanes, third, fixed(n, 128), lanes, third, fixed(1, 128), fixed(1, 128), fixed(n, 128),
                      fixed(n, 128), fixed(8, n), fixed(n, 128), lanes,
                      pl.BlockSpec((1, 4, 1, 2 * b), lambda g, s: (g, 0, 0, 0)),
                      fixed(256, d), fixed(d, 512)] + [ANY] * 4,
            out_specs=[fixed(n, 512), fixed(8, 128), fixed(2 * b, d), fixed(2 * b, d)],
            scratch_shapes=[pltpu.VMEM((n, n), f32)]
            + [pltpu.VMEM((n, 128), f32)] * 4
            + [pltpu.VMEM((4, b, 256), bf16), pltpu.VMEM((4, b, d), bf16), pltpu.SemaphoreType.DMA((4,))],
        ),
        out_shape=[
            jax.ShapeDtypeStruct((n, 512), bf16),
            jax.ShapeDtypeStruct((8, 128), f32),
            jax.ShapeDtypeStruct((2 * b, d), bf16),
            jax.ShapeDtypeStruct((2 * b, d), bf16),
        ],
        compiler_params=params(24),
        cost_estimate=cost(1 << 24),
        name="attend_back",
    )(s, qk, qk, v, pre, pre, qgain, kgain, cos, sin, start, live, out, lse, wout, w, *blocks)


def ffn_kernel(s_ref, *refs):
    x_in, a_in, o_in, refs = refs[:4], refs[4:8], refs[8], refs[9:]
    wg_own, wu_own, parts, refs = refs[0], refs[1], refs[2:10], refs[10:]
    gain_ref, n2_ref, hid_ref, fg_ref, fu_ref, res_ref, wout_ref, refs = *refs[:7], refs[7:]
    wg, wu, xs, att, wout, asem, xsem, osem, gsem, usem = refs
    j = pl.program_id(0)
    b = xs.shape[1]
    gate_w = Weight(s_ref, (wg_own,), parts, wg, gsem)
    up_w = Weight(s_ref, (wu_own,), parts, wu, usem, wg.shape[1])

    def out_copy(i):
        return pltpu.make_async_copy(o_in.at[:, i ^ (2 * s_ref[1])], wout.at[i], osem.at[i])

    def att_copy(k, i):
        return pltpu.make_async_copy(
            a_in[i].at[pl.ds((k ^ i) * b, b), :], att.at[k, :, pl.ds(i * b, b)], asem.at[k, i]
        )

    @pl.when(j == 0)
    def _():
        for k in range(4):
            pltpu.make_async_copy(x_in[k], xs.at[k], xsem.at[k]).start()
            for i in range(4):
                att_copy(k, i).start()
            if k == 0:
                for i in range(4):
                    out_copy(i).start()
                gate_w.start()
        up_w.start()
        for i in range(4):
            out_copy(i).wait()

    pltpu.make_async_copy(x_in[0], xs.at[j], xsem.at[j]).wait()
    for i in range(4):
        pltpu.make_async_copy(a_in[i].at[pl.ds(0, b), :], att.at[j, :, pl.ds(i * b, b)], asem.at[j, i]).wait()
    res = xs[j].astype(f32) + jnp.dot(att[j], wout[...].reshape(4 * b, -1), preferred_element_type=f32)

    @pl.when(j == 0)
    def _():
        res_ref[...] = res
        wout_ref[...] = wout[0].reshape(b, -1)
        gate_w.wait()
        up_w.wait()

    inv = lax.rsqrt(jnp.mean(res * res, axis=-1, keepdims=True) + epsilon)
    n2 = (res * inv * gain_ref[...]).astype(bf16)
    n2_ref[...] = n2
    gate = jnp.dot(n2, wg[...], preferred_element_type=f32)
    up = jnp.dot(n2, wu[...], preferred_element_type=f32)
    s = jax.nn.sigmoid(gate)
    silu = gate * s
    hid_ref[...] = (silu * up).astype(bf16)
    fg_ref[...] = (up * (s * (1.0 + gate * (1.0 - s)))).astype(bf16)
    fu_ref[...] = silu.astype(bf16)


def ffn_call(s, xs, atts, wout, wg, wu, parts, gain):
    b, d = xs[0].shape
    h = wg.shape[1]
    block = lambda wid: pl.BlockSpec((b, wid), lambda j, s: (j, 0))
    return pl.pallas_call(
        ffn_kernel,
        grid_spec=pltpu.PrefetchScalarGridSpec(
            num_scalar_prefetch=1,
            grid=(4,),
            in_specs=[ANY] * 19 + [fixed(1, d)],
            out_specs=[block(d), block(h), block(h), block(h), fixed(b, d), fixed(b, d)],
            scratch_shapes=[
                pltpu.VMEM((d, h), bf16),
                pltpu.VMEM((d, h), bf16),
                pltpu.VMEM((4, b, d), bf16),
                pltpu.VMEM((4, b, 4 * b), bf16),
                pltpu.VMEM((4,) + wout.shape[:1] + wout.shape[2:], bf16),
                pltpu.SemaphoreType.DMA((4, 4)),
                pltpu.SemaphoreType.DMA((4,)),
                pltpu.SemaphoreType.DMA((4,)),
                pltpu.SemaphoreType.DMA((9,)),
                pltpu.SemaphoreType.DMA((9,)),
            ],
        ),
        out_shape=[jax.ShapeDtypeStruct((4 * b, d), bf16)]
        + [jax.ShapeDtypeStruct((4 * b, h), bf16)] * 3
        + [jax.ShapeDtypeStruct((b, d), f32), jax.ShapeDtypeStruct((b, d), bf16)],
        compiler_params=params(58),
        cost_estimate=cost(1 << 24),
        name="ffn",
    )(s, *xs, *atts, wout, wg, wu, *parts, gain)


def ffn_back_kernel(s_ref, *refs):
    y_in, wd_own, wd_parts, refs = refs[:4], refs[4], refs[5:13], refs[13:]
    wg_own, wu_own, parts, refs = refs[0], refs[1], refs[2:10], refs[10:]
    fg_ref, fu_ref, gg_ref, gu_ref, lo_ref, hi_ref, wd, wg, wu, dy, ysem, dsem, gsem, usem = refs
    j = pl.program_id(0)
    down_w = Weight(s_ref, (wd_own,), wd_parts, wd, dsem)
    gate_w = Weight(s_ref, (wg_own,), parts, wg, gsem)
    up_w = Weight(s_ref, (wu_own,), parts, wu, usem, wg.shape[1])

    @pl.when(j == 0)
    def _():
        pltpu.make_async_copy(y_in[0], dy.at[0], ysem.at[0]).start()
        down_w.start()
        for k in range(1, 4):
            pltpu.make_async_copy(y_in[k], dy.at[k], ysem.at[k]).start()
        gate_w.start()
        up_w.start()
        down_w.wait()

    pltpu.make_async_copy(y_in[0], dy.at[j], ysem.at[j]).wait()
    gh = contract(dy[j], wd[...], 1, 1)
    gg = (gh * fg_ref[...].astype(f32)).astype(bf16)
    gu = (gh * fu_ref[...].astype(f32)).astype(bf16)
    gg_ref[...] = gg
    gu_ref[...] = gu

    @pl.when(j == 0)
    def _():
        gate_w.wait()
        up_w.wait()

    grad = (contract(gg, wg[...], 1, 1) + contract(gu, wu[...], 1, 1)).astype(bf16)

    @pl.when(j < 2)
    def _():
        lo_ref[...] = grad

    @pl.when(j >= 2)
    def _():
        hi_ref[...] = grad


def ffn_back_call(s, dys, wd, d_parts, wg, wu, parts, fg, fu):
    b, d = dys[0].shape
    h = wg.shape[1]
    block = lambda wid: pl.BlockSpec((b, wid), lambda j, s: (j, 0))
    return pl.pallas_call(
        ffn_back_kernel,
        grid_spec=pltpu.PrefetchScalarGridSpec(
            num_scalar_prefetch=1,
            grid=(4,),
            in_specs=[ANY] * 23 + [block(h), block(h)],
            out_specs=[
                block(h),
                block(h),
                pl.BlockSpec((b, d), lambda j, s: (jnp.minimum(j, 1), 0)),
                pl.BlockSpec((b, d), lambda j, s: (jnp.maximum(j - 2, 0), 0)),
            ],
            scratch_shapes=[
                pltpu.VMEM((h, d), bf16),
                pltpu.VMEM((d, h), bf16),
                pltpu.VMEM((d, h), bf16),
                pltpu.VMEM((4, b, d), bf16),
                pltpu.SemaphoreType.DMA((4,)),
                pltpu.SemaphoreType.DMA((9,)),
                pltpu.SemaphoreType.DMA((9,)),
                pltpu.SemaphoreType.DMA((9,)),
            ],
        ),
        out_shape=[jax.ShapeDtypeStruct((4 * b, h), bf16)] * 2 + [jax.ShapeDtypeStruct((2 * b, d), bf16)] * 2,
        compiler_params=params(58),
        cost_estimate=cost(1 << 24),
        name="ffn_back",
    )(s, *dys, wd, *d_parts, wg, wu, *parts, fg, fu)


def ffn_out_kernel(s_ref, wd_own, *refs):
    wd_parts, (hid_ref, lo_ref, hi_ref, wd, dsem) = refs[:8], refs[8:]
    j = pl.program_id(0)
    down_w = Weight(s_ref, (wd_own,), wd_parts, wd, dsem)

    @pl.when(j == 0)
    def _():
        down_w.start()
        down_w.wait()

    part = jnp.dot(hid_ref[...], wd[...], preferred_element_type=f32).astype(bf16)

    @pl.when(j < 2)
    def _():
        lo_ref[...] = part

    @pl.when(j >= 2)
    def _():
        hi_ref[...] = part


def ffn_out_call(s, wd, d_parts, hidden):
    n, h = hidden.shape
    b, d = n // 4, wd.shape[1]
    return pl.pallas_call(
        ffn_out_kernel,
        grid_spec=pltpu.PrefetchScalarGridSpec(
            num_scalar_prefetch=1,
            grid=(4,),
            in_specs=[ANY] * 9 + [pl.BlockSpec((b, h), lambda j, s: (j, 0))],
            out_specs=[
                pl.BlockSpec((b, d), lambda j, s: (jnp.minimum(j, 1), 0)),
                pl.BlockSpec((b, d), lambda j, s: (jnp.maximum(j - 2, 0), 0)),
            ],
            scratch_shapes=[pltpu.VMEM((h, d), bf16), pltpu.SemaphoreType.DMA((9,))],
        ),
        out_shape=[jax.ShapeDtypeStruct((2 * b, d), bf16)] * 2,
        compiler_params=params(58),
        cost_estimate=cost(1 << 24),
        name="ffn_out",
    )(s, wd, *d_parts, hidden)


def grad_rows_kernel(s_ref, left_ref, a_ref, b_ref, sent_a, keep_a, sent_b, keep_b):
    j = pl.program_id(0)
    left = left_ref[...]
    first = contract(left, a_ref[...], 0, 0).astype(bf16)
    second = contract(left, b_ref[...], 0, 0).astype(bf16)

    @pl.when(j % 2 == 1)
    def _():
        sent_a[0] = first

    @pl.when(j % 2 == 0)
    def _():
        keep_a[0] = first

    @pl.when(j >= 2)
    def _():
        sent_b[0] = second

    @pl.when(j < 2)
    def _():
        keep_b[0] = second


def grad_rows_call(s, left, a, b, name):
    n, rows = left.shape
    cols = a.shape[1]
    maps = [
        lambda j, s: (j // 2, 0, 0),
        lambda j, s: (j // 2, 0, 0),
        lambda j, s: (jnp.maximum(j - 2, 0), 0, 0),
        lambda j, s: (jnp.minimum(j, 1), 0, 0),
    ]
    return pl.pallas_call(
        grad_rows_kernel,
        grid_spec=pltpu.PrefetchScalarGridSpec(
            num_scalar_prefetch=1,
            grid=(4,),
            in_specs=[pl.BlockSpec((n, rows // 4), lambda j, s: (0, s[2] ^ j)), fixed(n, cols), fixed(n, cols)],
            out_specs=[pl.BlockSpec((1, rows // 4, cols), m) for m in maps],
        ),
        out_shape=[jax.ShapeDtypeStruct((2, rows // 4, cols), bf16)] * 4,
        compiler_params=params(58),
        cost_estimate=cost(1 << 24),
        name=name,
    )(s, left, a, b)


def grad_cols_kernel(s_ref, left_ref, r0, r1, r2, r3, sent_a, keep_a, sent_b, keep_b, right, sems):
    k = pl.program_id(0)
    b = r0.shape[0]
    cols = left_ref.shape[0] // 4

    def copy(k, i):
        src = (r0, r1, r2, r3)[i].at[:, pl.ds(pl.multiple_of(k * cols, cols), cols)]
        return pltpu.make_async_copy(src, right.at[k, pl.ds(i * b, b), :], sems.at[k, i])

    @pl.when(k == 0)
    def _():
        for block in range(4):
            for i in range(4):
                copy(block, i).start()

    for i in range(4):
        copy(k, i).wait()
    grad = contract(left_ref[...], right[k], 0, 0)
    grad = grad.astype(bf16)
    rows = grad.shape[0] // 4
    for a in range(4):
        piece = grad[a * rows : (a + 1) * rows]
        j = s_ref[2] ^ a

        @pl.when((k < 2) & (j % 2 == 1))
        def _():
            sent_a[j // 2] = piece

        @pl.when((k < 2) & (j % 2 == 0))
        def _():
            keep_a[j // 2] = piece

        @pl.when((k >= 2) & (j >= 2))
        def _():
            sent_b[j % 2] = piece

        @pl.when((k >= 2) & (j < 2))
        def _():
            keep_b[j % 2] = piece


def grad_cols_call(s, left, rights, name):
    n, rows = left.shape
    b, cols = rights[0].shape
    first = pl.BlockSpec((2, rows // 4, cols // 4), lambda k, s: (0, 0, jnp.minimum(k, 1)))
    second = pl.BlockSpec((2, rows // 4, cols // 4), lambda k, s: (0, 0, jnp.maximum(k - 2, 0)))
    return pl.pallas_call(
        grad_cols_kernel,
        grid_spec=pltpu.PrefetchScalarGridSpec(
            num_scalar_prefetch=1,
            grid=(4,),
            in_specs=[fixed(n, rows)] + [ANY] * 4,
            out_specs=[first, first, second, second],
            scratch_shapes=[pltpu.VMEM((4, n, cols // 4), bf16), pltpu.SemaphoreType.DMA((4, 4))],
        ),
        out_shape=[jax.ShapeDtypeStruct((2, rows // 4, cols // 2), bf16)] * 4,
        compiler_params=params(58),
        cost_estimate=cost(1 << 24),
        name=name,
    )(s, left, *rights)


def widen_kernel(side, in_ref, out_ref):
    first, second = in_ref[0, 0].astype(f32), in_ref[0, 1].astype(f32)
    out_ref[...] = jnp.concatenate([first, second], 1 if side else 0)


def widen_call(whole, side, name):
    _, _, rows, cols = whole.shape
    block = (rows, 2 * cols) if side else (2 * rows, cols)
    return pl.pallas_call(
        functools.partial(widen_kernel, side),
        grid=(8,),
        in_specs=[pl.BlockSpec((1, 2, rows, cols), lambda j: (j, 0, 0, 0))],
        out_specs=pl.BlockSpec(block, lambda j: (j, 0)),
        out_shape=jax.ShapeDtypeStruct((8 * block[0], block[1]), f32),
        compiler_params=params(8),
        cost_estimate=cost(1 << 20),
        name=name,
    )(whole)


def place_kernel(write, s_ref, *refs):
    k = pl.program_id(0)
    for i in range(8):

        @pl.when(k == i)
        def _():
            write(refs[i], refs[8:])


def write_rows(piece, outs):
    outs[0][...] = piece[...].astype(f32)


def write_attention(piece, outs):
    query, key, value, out = outs
    r, s = query.shape[0], out.shape[0]
    query[...] = piece[0, :r].astype(f32)
    key[...] = piece[1, :r, :128].astype(f32)
    value[...] = piece[1, :r, 128:].astype(f32)
    sides = [piece[half, r + at * s : r + (at + 1) * s] for half in range(2) for at in range(2)]
    out[...] = jnp.concatenate(sides, 1).astype(f32)


def place_call(s, pieces, write, blocks, name):
    eighth = lambda k, s: (2 * (s[2] ^ (k % 4)) + (s[1] ^ (k // 4)), 0)
    return pl.pallas_call(
        functools.partial(place_kernel, write),
        grid_spec=pltpu.PrefetchScalarGridSpec(
            num_scalar_prefetch=1,
            grid=(8,),
            in_specs=[fixed(*pieces[0].shape)] * 8,
            out_specs=[pl.BlockSpec(block, eighth) for block in blocks],
        ),
        out_shape=[jax.ShapeDtypeStruct((8 * r, cols), f32) for r, cols in blocks],
        compiler_params=params(12),
        cost_estimate=cost(1 << 20),
        name=name,
    )(s, *pieces)


def grad_attention_kernel(s_ref, n1_ref, low_ref, att_ref, b0, b1, b2, b3, sent_a, keep_a, sent_b, keep_b, whole):
    j = pl.program_id(0)
    b = b0.shape[0]

    @pl.when(j == 0)
    def _():
        total = None
        for i, block in enumerate((b0, b1, b2, b3)):
            part = contract(att_ref[i * b : (i + 1) * b, :], block[...], 0, 0)
            total = part if total is None else total + part
        whole[...] = total.astype(bf16)

    qkv = contract(n1_ref[...], low_ref[...], 0, 0).astype(bf16)
    r = qkv.shape[0] // 2
    s = whole.shape[0] // 8
    k = qkv.shape[1] // 2
    out = whole[pl.ds(pl.multiple_of((s_ref[2] ^ j) * 2 * s, 2 * s), 2 * s), :]

    def joined(at):
        parts = []
        for core in range(2):
            some = out[core * s : (core + 1) * s]
            parts += [
                qkv[core * r : (core + 1) * r, at * k : (at + 1) * k],
                some[:, 2 * at * k : (2 * at + 1) * k],
                some[:, (2 * at + 1) * k : (2 * at + 2) * k],
            ]
        return jnp.concatenate(parts, 0)

    @pl.when(j % 2 == 1)
    def _():
        sent_a[0] = joined(0)

    @pl.when(j % 2 == 0)
    def _():
        keep_a[0] = joined(0)

    @pl.when(j >= 2)
    def _():
        sent_b[0] = joined(1)

    @pl.when(j < 2)
    def _():
        keep_b[0] = joined(1)


def grad_attention_call(s, n1, low, att, blocks):
    n, d = n1.shape
    b = n // 4
    half = (d // 4 + att.shape[1] // 2, 256)
    maps = [
        lambda j, s: (j // 2, 0, 0),
        lambda j, s: (j // 2, 0, 0),
        lambda j, s: (jnp.maximum(j - 2, 0), 0, 0),
        lambda j, s: (jnp.minimum(j, 1), 0, 0),
    ]
    return pl.pallas_call(
        grad_attention_kernel,
        grid_spec=pltpu.PrefetchScalarGridSpec(
            num_scalar_prefetch=1,
            grid=(4,),
            in_specs=[pl.BlockSpec((n, d // 4), lambda j, s: (0, s[2] ^ j)), fixed(n, low.shape[1]), fixed(n, att.shape[1])]
            + [fixed(b, d)] * 4,
            out_specs=[pl.BlockSpec((1,) + half, m) for m in maps],
            scratch_shapes=[pltpu.VMEM((att.shape[1], d), bf16)],
        ),
        out_shape=[jax.ShapeDtypeStruct((2,) + half, bf16)] * 4,
        compiler_params=params(58),
        cost_estimate=cost(1 << 24),
        name="grad_attention",
    )(s, n1, low, att, *blocks)


def permute(x, places, move):
    pairs = []
    for d in range(places):
        for t in range(T4):
            to = move(d, t)
            if to is not None:
                pairs.append((d * T4 + t, to[0] * T4 + to[1]))
    return lax.ppermute(x, AX, pairs)


def after(x, *events):
    return lax.optimization_barrier((x, events))[0]


def flip_core(d, t):
    return (d ^ 1, t)


def flip_z(d, t):
    return (d, t ^ 1)


def flip_far(d, t):
    return (d, t ^ 2)


def flip_e(bit):
    return lambda d, t: (d ^ (2 << bit), t)


def settle(d, t):
    return (d, t) if (d & 1) == (t >> 1) else (d ^ 1, t ^ 2)


def step(*values):
    return lax.optimization_barrier(values)


def eighth(w, c, e):
    rows = w.shape[0] // 8
    return lax.dynamic_slice_in_dim(w, (2 * e + c) * rows, rows, 0)


def around(piece, n):
    return [permute(piece, n, lambda d, t, j=j: (d ^ (2 * j), t)) for j in (1, 2, 3)]


def across(pieces, n):
    return [permute(piece, n, flip_core) for piece in pieces]


def first_sums(pieces, n):
    sent_a, keep_a, sent_b, keep_b = pieces
    got_a = permute(sent_a, n, flip_e(0))
    got_b = permute(sent_b, n, flip_e(1))
    return got_a, got_b


def first_add(pieces, got):
    got_a, got_b = got
    keep_a, keep_b = pieces[1], pieces[3]
    return keep_a[1] + got_a[1], keep_a[0] + got_a[0], keep_b[1] + got_b[1], keep_b[0] + got_b[0]


def second_sums(halves, n):
    return permute(halves[0], n, flip_e(1)), permute(halves[2], n, flip_e(0))


def second_add(halves, got, n):
    total = jnp.stack([halves[1] + got[0], halves[3] + got[1]])
    for extra in range(2, 20):
        if (2 << extra) < n:
            total = total + permute(total, n, flip_e(extra))
    return total


def cross_sent(total, c):
    half = total.shape[1] // 2
    return jnp.where(c == 0, total[:, half:], total[:, :half])


def cross_got(total, got, c):
    half = total.shape[1] // 2
    return jnp.where(c == 0, total[:, :half], got), jnp.where(c == 0, got, total[:, half:])


def neighbours(n):
    return None if n == 8 else [list(range(k, k + 8)) for k in range(0, n, 8)]


def whole_grad(mine, n):
    return lax.all_gather(mine, "dp", axis_index_groups=neighbours(n))


def vector_moves(n):
    bits = [1 << k for k in range(20) if 1 << k < n]
    return [flip_z] + [lambda d, t, bit=bit: (d ^ bit, t) for bit in bits] + [flip_far]


def local(
    block_input,
    doc_lengths,
    pad_mask,
    norm1_gain,
    w_query,
    w_key,
    w_value,
    query_gain,
    key_gain,
    w_out,
    norm2_gain,
    w_gate,
    w_up,
    w_down,
    cotangent,
):
    n = lax.axis_size("dp")
    d, t = lax.axis_index("dp"), lax.axis_index("tensor")
    c, p = d & 1, t >> 1
    e = (d >> 1) & 3
    shard = 2 * c + (t & 1)
    b = block_input.shape[0]
    seq_len = b * T4
    home = c == p
    wq = w_query.shape[1]
    wk = w_key.shape[1]
    width = block_input.shape[1]
    s = jnp.stack([shard, c, e]).astype(jnp.int32)

    marks = jnp.concatenate([doc_lengths, pad_mask], 1)
    mine_out = eighth(w_out, c, e)
    mine_qkv = jnp.concatenate([eighth(w, c, e) for w in (w_query, w_key, w_value)], 1)
    x_own = permute(block_input, n, settle)
    qkv_hop = permute(mine_qkv, n, flip_far)
    out_z = permute(mine_out, n, flip_z)
    marks = jnp.where(home, marks, permute(marks, n, flip_core))
    lengths_row, pad_row = marks[0, : doc_lengths.shape[1]], marks[0, doc_lengths.shape[1] :]
    mine_gate_up = jnp.concatenate([eighth(w, c, e) for w in (w_gate, w_up)], 1)
    mine_down = eighth(w_down, c, e)

    positions = jnp.arange(seq_len, dtype=jnp.int32)
    doc_starts, cos_half, sin_half = doc_tables(lengths_row, positions, HD)
    cos = jnp.concatenate([cos_half] * 4, 1)
    sin = jnp.concatenate([-sin_half, sin_half] * 2, 1)
    live = jnp.where(pad_row == 1, positions, -1)
    start_col = jnp.broadcast_to(doc_starts[:, None], (seq_len, 128))
    start_row = jnp.broadcast_to(doc_starts[None], (8, seq_len))
    live_col = jnp.broadcast_to(live[:, None], (seq_len, 128))
    live_row = jnp.broadcast_to(live[None], (8, seq_len))
    gains = jnp.concatenate([query_gain] * (wq // HD) + [key_gain] * (wk // HD))[None]
    qgain_pair = jnp.concatenate([query_gain] * 2)[None]
    kgain_pair = jnp.concatenate([key_gain] * 2)[None]

    x_own, qkv_hop, out_z, mine_gate_up, mine_down, late_dy, cos, sin, start_col, start_row, live_col, live_row = step(
        x_own, qkv_hop, out_z, mine_gate_up, mine_down, cotangent, cos, sin, start_col, start_row, live_col, live_row
    )
    x_over, x_near = permute(x_own, n, flip_z), permute(x_own, n, flip_core)
    two_out = jnp.stack([mine_out, out_z])
    out_far = permute(two_out, n, flip_far)
    qkv_around = around(qkv_hop, n)
    gate_up_hop = permute(mine_gate_up, n, flip_far)
    x_over, x_near, out_far, late_dy, *qkv_around = step(x_over, x_near, out_far, late_dy, *qkv_around)
    x_far = permute(x_over, n, flip_core)
    qkv_mine = [qkv_hop] + qkv_around
    qkv_other = across(qkv_mine, n)
    out_all = lax.all_gather(jnp.concatenate([two_out, out_far]), "dp", axis_index_groups=neighbours(n))
    dy_own = permute(late_dy, n, settle)
    x_blocks = [x_own, x_over, x_near, x_far]

    rows_one, pre, qk, values, w_qkv = qkv_call(
        s, x_blocks, (w_query, w_key, w_value), qkv_mine + qkv_other, norm1_gain[None], gains, cos, sin
    )
    gate_up_hop = after(gate_up_hop, qk)
    gate_up_around = around(gate_up_hop, n)
    attended, attended_f, lse = attend_call(s, qk, values, start_col, live_row)

    att_over, att_near = permute(attended, n, flip_z), permute(attended, n, flip_core)
    down_hop = permute(after(mine_down, gate_up_hop), n, flip_far)
    att_over, att_near, down_hop = step(att_over, att_near, down_hop)
    att_far = permute(att_over, n, flip_core)
    dy_own = after(dy_own, att_over)
    dy_over, dy_near = permute(dy_own, n, flip_z), permute(dy_own, n, flip_core)
    gate_up_around = after(gate_up_around, att_far)
    gate_up_mine = [gate_up_hop] + gate_up_around
    gate_up_parts = gate_up_mine + across(gate_up_mine, n)
    down_around = around(after(down_hop, *gate_up_around), n)
    rows_two, hidden, by_gate, by_up, residual, w_out_own = ffn_call(
        s, x_blocks, [attended, att_over, att_near, att_far], out_all, w_gate, w_up, gate_up_parts,
        after(norm2_gain[None], dy_own),
    )
    hidden, dy_over, dy_near, *down_around = step(hidden, dy_over, dy_near, *down_around)
    dy_blocks = [dy_own, dy_over, dy_near, permute(dy_over, n, flip_core)]

    down = grad_cols_call(s, hidden, dy_blocks, "grad_down")
    down_mine = [down_hop] + down_around
    down_parts = down_mine + across(down_mine, n)
    down_got = first_sums(down, n)
    gate_grad, up_grad, low2, high2 = ffn_back_call(
        s, dy_blocks, w_down, down_parts, w_gate, w_up, gate_up_parts, after(by_gate, *down), by_up
    )
    low2, high2, *down_got = step(low2, high2, *down_got)
    (high_got,) = step(permute(high2, n, flip_core))
    low_half = low2 + high_got
    low_over = permute(low_half[b:], n, flip_z)
    gate_up = grad_rows_call(s, rows_two, after(gate_grad, low_half), up_grad, "grad_gate_up")
    gate_up_got = first_sums(gate_up, n)
    down = first_add(down, after(down_got, *gate_up))
    down_got = second_sums(down, n)
    grad_n2 = (low_half[:b] + after(low_over, *down)).astype(f32)
    inv = lax.rsqrt(jnp.mean(residual * residual, axis=-1, keepdims=True) + epsilon)
    scaled = norm2_gain * grad_n2
    grad_residual = (
        dy_own.astype(f32)
        + inv * scaled
        - residual * (inv * inv * inv) * jnp.mean(scaled * residual, axis=-1, keepdims=True)
    )
    grad_norm2 = jnp.sum(grad_n2 * residual * inv, axis=0)
    gb_own = grad_residual.astype(bf16)
    gb_over, gb_near = permute(gb_own, n, flip_z), permute(gb_own, n, flip_core)
    ffn_low, ffn_high = ffn_out_call(s, w_down, down_parts, after(hidden, gb_own))
    ffn_got = permute(ffn_high, n, flip_core)
    gb_over, gb_near = step(*after([gb_over, gb_near], ffn_low))
    ffn_got = after(ffn_got, gb_over)
    gb_far = permute(gb_over, n, flip_core)
    gate_up = first_add(gate_up, after(gate_up_got, gb_over))
    gate_up_got = second_sums(gate_up, n)
    down = second_add(down, after(down_got, gb_over, *gate_up), n)
    ffn_half = ffn_low + ffn_got
    gb_far, down_got = step(gb_far, permute(cross_sent(down, c), n, flip_core))
    down_kept, down_sent = cross_got(down, down_got, c)
    down_got = permute(down_sent, n, flip_far)
    ffn_over = permute(ffn_half[b:], n, flip_z)
    gb_blocks = [gb_own, gb_over, gb_near, gb_far]

    low, gain_terms, low1, high1 = attend_back_call(
        s, qk, after(values, ffn_half, down_sent), pre, qgain_pair, kgain_pair, cos, sin, start_row, live_col,
        attended_f, lse, w_out_own, w_qkv, gb_blocks,
    )
    low, low1, high1, down_got, ffn_over, *gate_up_got = step(low, low1, high1, down_got, ffn_over, *gate_up_got)
    gate_up = second_add(gate_up, gate_up_got, n)
    high_got, gate_up_got = step(permute(high1, n, flip_core), permute(cross_sent(gate_up, c), n, flip_core))
    low_half = low1 + high_got
    low_over = permute(low_half[b:], n, flip_z)
    gate_up_kept, gate_up_sent = cross_got(gate_up, gate_up_got, c)
    gate_up_got = permute(gate_up_sent, n, flip_far)
    down_mine = down_kept + after(down_got, low_half)
    down_all = whole_grad(down_mine, n)
    att = grad_attention_call(s, rows_one, after(low, down_mine, gate_up_sent), attended, gb_blocks)
    att_got = first_sums(att, n)
    block_output = residual + (ffn_half[:b] + after(ffn_over, *att)).astype(f32)
    low_over = after(low_over, block_output)
    grad_n1 = (low_half[:b] + low_over).astype(f32)
    att = first_add(att, after(att_got, low_over))
    att_got = second_sums(att, n)
    x_f = x_own.astype(f32)
    inv = lax.rsqrt(jnp.mean(x_f * x_f, axis=-1, keepdims=True) + epsilon)
    scaled = norm1_gain * after(grad_n1, *att)
    input_grad = (
        grad_residual
        + inv * scaled
        - x_f * (inv * inv * inv) * jnp.mean(scaled * x_f, axis=-1, keepdims=True)
    )
    grad_norm1 = jnp.sum(grad_n1 * x_f * inv, axis=0)
    head_terms = gain_terms[:, :HD] + gain_terms[:, HD:]
    vec = jnp.concatenate([grad_norm1, grad_norm2, head_terms[0] + head_terms[1], head_terms[2]])[None]
    moves = vector_moves(n)
    vec_got = permute(vec, n, moves[0])
    att = second_add(att, after(att_got, input_grad, vec), n)
    att_got = permute(cross_sent(att, c), n, flip_core)
    gate_up_mine = gate_up_kept + after(gate_up_got, att)
    gate_mine, up_mine = gate_up_mine[0], gate_up_mine[1]
    gate_around = around(gate_mine, n)
    att_got, vec_got = after([att_got, vec_got], gate_mine)
    att_kept, att_sent = cross_got(att, att_got, c)
    att_got = permute(att_sent, n, flip_far)
    late_output, late_grad = after([block_output, input_grad], att_sent)
    settled_output = permute(late_output.astype(bf16), n, settle)
    settled_grad = permute(late_grad.astype(bf16), n, settle)
    vec = vec + vec_got
    vec_got = permute(vec, n, moves[1])
    att_got, vec_got, *gate_around = step(*after([att_got, vec_got], att_sent), *gate_around)
    att_mine = att_kept + att_got
    att_around = around(att_mine, n)
    gate_across = across([gate_mine] + gate_around, n)
    up_mine = after(up_mine, att_mine)
    up_around = around(up_mine, n)
    vec = vec + vec_got
    vec_got = permute(vec, n, moves[2])
    shape = [(width // 8, w_gate.shape[1])]
    (grad_gate,) = place_call(s, [gate_mine] + gate_around + after(gate_across, up_mine), write_rows, shape, "place_gate")
    att_around, vec_got = after([att_around, vec_got], grad_gate)
    att_across = across([att_mine] + att_around, n)
    vec = vec + vec_got
    vec_got = permute(vec, n, moves[3])
    grad_down = widen_call(after(down_all, vec), True, "widen_down")
    grad_query, grad_key, grad_value, grad_out = place_call(
        s,
        [att_mine] + att_around + after(att_across, grad_down),
        write_attention,
        [(width // 8, wq), (width // 8, wk), (width // 8, wk), (w_out.shape[0] // 8, width)],
        "place_attention",
    )
    vec_got, settled_output, settled_grad, *up_around = after([vec_got, settled_output, settled_grad] + up_around, grad_query)
    up_across = across([up_mine] + up_around, n)
    vec = vec + vec_got
    vec_got = permute(vec, n, moves[4])
    block_output = jnp.where(home, block_output, settled_output.astype(f32))
    input_grad = jnp.where(home, input_grad, settled_grad.astype(f32))
    up_across, vec_got = after([up_across, vec_got], block_output, input_grad)
    (grad_up,) = place_call(s, [up_mine] + up_around + up_across, write_rows, shape, "place_up")
    vec = vec + vec_got
    for move in moves[5:]:
        vec = vec + permute(vec, n, move)
    vec = vec[0]
    return (
        block_output,
        input_grad,
        vec[:width],
        grad_query,
        grad_key,
        grad_value,
        vec[2 * width : 2 * width + HD],
        vec[2 * width + HD :],
        grad_out,
        vec[width : 2 * width],
        grad_gate,
        grad_up,
        grad_down,
    )


def solution(mesh):
    placed = (
        P(("dp", "tensor"), None),
        P("dp", None),
        P("dp", None),
        P(),
        P(None, "tensor"),
        P(None, "tensor"),
        P(None, "tensor"),
        P(),
        P(),
        P("tensor", None),
        P(),
        P(None, "tensor"),
        P(None, "tensor"),
        P("tensor", None),
        P(("dp", "tensor"), None),
    )
    return jax.shard_map(
        local,
        mesh=mesh,
        in_specs=placed,
        out_specs=(
            P(("dp", "tensor"), None),
            P(("dp", "tensor"), None),
            P(),
            P(None, "tensor"),
            P(None, "tensor"),
            P(None, "tensor"),
            P(),
            P(),
            P("tensor", None),
            P(),
            P(None, "tensor"),
            P(None, "tensor"),
            P("tensor", None),
        ),
        check_vma=False,
    )
```

```python
import functools
import math

import jax
import jax.numpy as jnp
from jax import lax
from jax.experimental import pallas as pl
from jax.experimental.pallas import tpu as pltpu
from jax.sharding import PartitionSpec as P

HD = 64
AX = ("dp", "tensor")
T4 = 4
VMEM_MB = 1 << 20

epsilon = 1e-05
rope_base = 1000000.0
NEG = -1000000000.0
bf16 = jnp.bfloat16
f32 = jnp.float32


def doc_tables(lengths_row, positions, head_dim):
    doc_ends = jnp.cumsum(lengths_row)
    passed = positions[:, None] >= doc_ends[None, :]
    doc_starts = jnp.sum(jnp.where(passed, lengths_row[None, :], 0), axis=1)
    offsets = (positions - doc_starts).astype(f32)
    freqs = jnp.exp(
        jnp.arange(head_dim // 2, dtype=f32) * (-2.0 * math.log(rope_base) / head_dim)
    )
    angles = offsets[:, None] * freqs[None, :]
    return (doc_starts, jnp.cos(angles), jnp.sin(angles))


def contract(a, b, da, db):
    return lax.dot_general(a, b, (((da,), (db,)), ((), ())), preferred_element_type=f32)


def swap_halves(y):
    width = y.shape[1]
    lane = lax.broadcasted_iota(jnp.int32, y.shape, 1)
    return jnp.where(lane % HD < HD // 2, pltpu.roll(y, width - HD // 2, 1), pltpu.roll(y, HD // 2, 1))


def split_dot(left, right, da, db):
    high = left.astype(bf16)
    low = (left - high.astype(f32)).astype(bf16)
    return contract(high, right, da, db) + contract(low, right, da, db)


def head_mean(y):
    at = lax.broadcasted_iota(jnp.int32, (128, 128), 0) // HD
    to = lax.broadcasted_iota(jnp.int32, (128, 128), 1) // HD
    ones = jnp.where(at == to, 1.0 / HD, 0.0).astype(bf16)
    sides = [split_dot(y[:, k : k + 128], ones, 1, 0) for k in range(0, y.shape[1], 128)]
    return sides[0] if len(sides) == 1 else jnp.concatenate(sides, 1)


class Weight:
    def __init__(self, s_ref, own, parts, to, sems, start=0):
        self.core, self.e = s_ref[1], s_ref[2]
        self.own, self.parts, self.to, self.sems, self.start_col = own, parts, to, sems, start

    def copies(self):
        start = 0
        for i, w in enumerate(self.own):
            wide = w.shape[1]
            to = self.to if len(self.own) == 1 else self.to.at[:, pl.ds(start, wide)]
            yield 0, functools.partial(pltpu.make_async_copy, w, to, self.sems.at[8 + i])
            start += wide
        rows = self.to.shape[0] // 8
        for j in range(4):
            for other in range(2):
                at = pl.multiple_of((2 * (self.e ^ j) + 1 - other) * rows, rows)
                src = self.parts[4 * other + j]
                if src.shape[1] != self.to.shape[1]:
                    src = src.at[:, pl.ds(self.start_col, self.to.shape[1])]
                to = self.to.at[pl.ds(at, rows), :]
                yield 1, functools.partial(pltpu.make_async_copy, src, to, self.sems.at[2 * j + other])

    def each(self, act):
        for core in range(2):

            @pl.when(self.core == core)
            def _():
                for whose, copy in self.copies():
                    if whose == core:
                        act(copy())

    def start(self):
        self.each(lambda copy: copy.start())

    def wait(self):
        self.each(lambda copy: copy.wait())


ANY = pl.BlockSpec(memory_space=pl.ANY)


def fixed(*shape):
    return pl.BlockSpec(shape, lambda *_: (0,) * len(shape))


def cost(flops):
    return pl.CostEstimate(flops=flops, bytes_accessed=1 << 16, transcendentals=0)


def params(mib):
    return pltpu.CompilerParams(vmem_limit_bytes=mib * VMEM_MB)


def qkv_kernel(s_ref, *refs):
    pieces, own, parts, refs = refs[:4], refs[4:7], refs[7:15], refs[15:]
    g1_ref, gains_ref, cos_ref, sin_ref, n1_ref, pre_ref, qk_ref, v_ref, w_ref, xs, xsem, wsem = refs
    j = pl.program_id(0)
    weight = Weight(s_ref, own, parts, w_ref, wsem)

    @pl.when(j == 0)
    def _():
        for k in range(4):
            pltpu.make_async_copy(pieces[k], xs.at[k], xsem.at[k]).start()
        weight.start()

    pltpu.make_async_copy(pieces[0], xs.at[j], xsem.at[j]).wait()
    x = xs[j].astype(f32)
    inv = lax.rsqrt(jnp.mean(x * x, axis=-1, keepdims=True) + epsilon)
    n1 = (x * inv * g1_ref[...]).astype(bf16)
    n1_ref[...] = n1

    @pl.when(j == 0)
    def _():
        weight.wait()

    qkv = jnp.dot(n1, w_ref[...], preferred_element_type=f32)
    width = pre_ref.shape[1]
    pre = qkv[:, :width]
    pre_ref[...] = pre
    v_ref[...] = qkv[:, width:].astype(bf16)
    y = pre * lax.rsqrt(head_mean(pre * pre) + epsilon) * gains_ref[...]
    cos = jnp.concatenate([cos_ref[...]] * (width // 128), 1)
    sin = jnp.concatenate([sin_ref[...]] * (width // 128), 1)
    qk = (y * cos + swap_halves(y) * sin).astype(bf16)
    lane = lax.broadcasted_iota(jnp.int32, qk.shape, 1)
    qk_ref[...] = jnp.where(lane < width - 128, qk * 0.125, qk).astype(bf16)


def qkv_call(s, xs, w_own, w_parts, g1, gains, cos, sin):
    b, d = xs[0].shape
    wid = w_parts[0].shape[1]
    qkw = wid - 128
    natural = lambda j, s: (s[0] ^ j, 0)
    return pl.pallas_call(
        qkv_kernel,
        grid_spec=pltpu.PrefetchScalarGridSpec(
            num_scalar_prefetch=1,
            grid=(4,),
            in_specs=[ANY] * 15
            + [fixed(1, d), fixed(1, qkw), pl.BlockSpec((b, 128), natural), pl.BlockSpec((b, 128), natural)],
            out_specs=[
                pl.BlockSpec((b, d), lambda j, s: (j, 0)),
                pl.BlockSpec((b, qkw), natural),
                pl.BlockSpec((b, qkw), natural),
                pl.BlockSpec((b, 128), natural),
                fixed(d, wid),
            ],
            scratch_shapes=[
                pltpu.VMEM((4, b, d), bf16),
                pltpu.SemaphoreType.DMA((4,)),
                pltpu.SemaphoreType.DMA((11,)),
            ],
        ),
        out_shape=[
            jax.ShapeDtypeStruct((4 * b, d), bf16),
            jax.ShapeDtypeStruct((4 * b, qkw), f32),
            jax.ShapeDtypeStruct((4 * b, qkw), bf16),
            jax.ShapeDtypeStruct((4 * b, 128), bf16),
            jax.ShapeDtypeStruct((d, wid), bf16),
        ],
        compiler_params=params(58),
        cost_estimate=cost(1 << 24),
        name="qkv",
    )(s, *xs, *w_own, *w_parts, g1, gains, cos, sin)


def both_heads(pair):
    lane = lax.broadcasted_iota(jnp.int32, pair.shape, 1)
    zero = jnp.zeros_like(pair)
    return jnp.concatenate([jnp.where(lane < HD, pair, zero), jnp.where(lane < HD, zero, pair)], 0)


def pick_heads(both):
    r = both.shape[0] // 2
    lane = lax.broadcasted_iota(jnp.int32, (r, 128), 1)
    return jnp.where(lane < HD, both[:r], both[r:])


def twice(kv, g):
    lane = lax.broadcasted_iota(jnp.int32, kv.shape, 1)
    turned = pltpu.roll(kv.astype(f32), HD, 1).astype(kv.dtype)
    return jnp.where((lane < HD) == (g == 0), kv, turned)


def attend_kernel(s_ref, q_ref, k_ref, v_ref, start_ref, live_ref, att_ref, out_ref, lse_ref, bias):
    g = pl.program_id(0)
    n = k_ref.shape[0]
    b = n // 4

    @pl.when(g == 0)
    def _():
        for a in range(4):
            keys = (a + 1) * b
            start = start_ref[a * b : (a + 1) * b, :1]
            q_at = lax.broadcasted_iota(jnp.int32, (b, keys), 0) + a * b
            k_at = lax.broadcasted_iota(jnp.int32, (b, keys), 1)
            allowed = ((live_ref[:1, :keys] >= start) & (k_at <= q_at)) | (k_at == q_at)
            bias[a * b : (a + 1) * b, :keys] = jnp.where(allowed, 0.0, NEG)

    kd = twice(k_ref[...], g)
    vd = twice(v_ref[...], g)
    for a in range(4):
        keys = (a + 1) * b
        rows = slice(a * b, (a + 1) * b)
        qm = both_heads(q_ref[rows, :])
        scores = contract(qm, kd[:keys], 1, 1)
        extra = bias[rows, :keys]
        expo = jnp.exp(scores + jnp.concatenate([extra, extra], 0))
        total = jnp.sum(expo, axis=-1, keepdims=True)
        pair = pick_heads(contract(expo.astype(bf16), vd[:keys], 1, 0) / total)
        out_ref[rows, :] = pair
        att_ref[pl.ds(pl.multiple_of((s_ref[0] ^ a) * b, b), b), :] = pair.astype(bf16)
        lse_ref[0, a] = jnp.transpose(jnp.broadcast_to(jnp.log(total), (2 * b, 128)))[:1]


def attend_call(s, qk, v, start, live):
    n = qk.shape[0]
    b = n // 4
    lanes = lambda g, s: (0, g)
    return pl.pallas_call(
        attend_kernel,
        grid_spec=pltpu.PrefetchScalarGridSpec(
            num_scalar_prefetch=1,
            grid=(2,),
            in_specs=[
                pl.BlockSpec((n, 128), lanes),
                pl.BlockSpec((n, 128), lambda g, s: (0, 2)),
                fixed(n, 128),
                fixed(n, 128),
                fixed(8, n),
            ],
            out_specs=[
                pl.BlockSpec((n, 128), lanes),
                pl.BlockSpec((n, 128), lanes),
                pl.BlockSpec((1, 4, 1, 2 * b), lambda g, s: (g, 0, 0, 0)),
            ],
            scratch_shapes=[pltpu.VMEM((n, n), f32)],
        ),
        out_shape=[
            jax.ShapeDtypeStruct((n, 256), bf16),
            jax.ShapeDtypeStruct((n, 256), f32),
            jax.ShapeDtypeStruct((2, 4, 1, 2 * b), f32),
        ],
        compiler_params=params(14),
        cost_estimate=cost(1 << 24),
        name="attend",
    )(s, qk, qk, v, start, live)


def norm_back(grad, pre, gain, cos, sin):
    turned = grad * cos - swap_halves(grad) * sin
    inv = lax.rsqrt(head_mean(pre * pre) + epsilon)
    scaled = turned * gain
    dpre = inv * scaled - pre * (inv * inv * inv) * head_mean(scaled * pre)
    return dpre, jnp.sum(turned * pre * inv, axis=0, keepdims=True)


def attend_back_kernel(s_ref, q_ref, k_ref, v_ref, qpre_ref, kpre_ref, gains_ref, kgain_ref, cos_ref, sin_ref,
                       start_ref, live_ref, out_ref, lse_ref, wout_ref, w_ref, b0, b1, b2, b3,
                       low_ref, gain_ref, lo_ref, hi_ref, bias, dk, dv, dkall, dvall, dos, gb, sems):
    g = pl.program_id(0)
    n = k_ref.shape[0]
    b = n // 4
    pieces = (b0, b1, b2, b3)

    @pl.when(g == 0)
    def _():
        for k in range(4):
            pltpu.make_async_copy(pieces[k], gb.at[k], sems.at[k]).start()
        for a in range(4):
            keys = (a + 1) * b
            start = start_ref[:1, a * b : (a + 1) * b]
            k_at = lax.broadcasted_iota(jnp.int32, (keys, b), 0)
            q_at = lax.broadcasted_iota(jnp.int32, (keys, b), 1) + a * b
            allowed = ((live_ref[:keys, :1] >= start) & (k_at <= q_at)) | (k_at == q_at)
            bias[:keys, a * b : (a + 1) * b] = jnp.where(allowed, 0.0, NEG)
        for k in range(4):
            pltpu.make_async_copy(pieces[k], gb.at[k], sems.at[k]).wait()
            dos[k] = contract(gb[k], wout_ref[...], 1, 1).astype(bf16)

    kd = twice(k_ref[...], g)
    vd = twice(v_ref[...], g)
    gain_sum = jnp.zeros((1, 128), f32)
    ones = jnp.ones((16, 128), bf16)
    for a in (3, 2, 1, 0):
        keys = (a + 1) * b
        rows = slice(a * b, (a + 1) * b)
        home = s_ref[0] ^ a
        qm = both_heads(q_ref[rows, :])
        dout = jnp.where(g == 0, dos[home, :, :128], dos[home, :, 128:])
        dom = both_heads(dout)
        terms = both_heads(dout.astype(f32) * out_ref[rows, :])
        terms_high = terms.astype(bf16)
        terms_low = (terms - terms_high.astype(f32)).astype(bf16)
        delta = (contract(ones, terms_high, 1, 1) + contract(ones, terms_low, 1, 1))[:1]
        scores = contract(kd[:keys], qm, 1, 1)
        extra = bias[:keys, rows]
        probs = jnp.exp(scores + (jnp.concatenate([extra, extra], 1) - lse_ref[0, a]))
        dprobs = contract(vd[:keys], dom, 1, 1)
        dscores = (probs * (dprobs - delta)).astype(bf16)
        dv_add = contract(probs.astype(bf16), dom, 1, 0)
        dk_add = contract(dscores, qm, 1, 0)
        if a == 3:
            dv[...] = dv_add
            dk[...] = dk_add
        else:
            dv[:keys] += dv_add
            dk[:keys] += dk_add
        dq = pick_heads(contract(dscores, kd[:keys], 0, 0)) * 0.125
        dpre, gain_part = norm_back(dq, qpre_ref[rows, :], gains_ref[...], cos_ref[rows, :], sin_ref[rows, :])
        at = pl.ds(pl.multiple_of(home * b, b), b)
        low_ref[at, pl.ds(pl.multiple_of(g * 128, 128), 128)] = dpre.astype(bf16)
        gain_sum = gain_sum + gain_part
    gain_ref[pl.ds(g, 1), :] = gain_sum
    lane = lax.broadcasted_iota(jnp.int32, (n, 128), 1)
    dk_all = dk[...] + pltpu.roll(dk[...], HD, 1)
    dv_all = dv[...] + pltpu.roll(dv[...], HD, 1)

    @pl.when(g == 0)
    def _():
        dkall[...] = dk_all
        dvall[...] = dv_all

    @pl.when(g == 1)
    def _():
        grad_k = jnp.where(lane < HD, dkall[...], dk_all)
        grad_v = jnp.where(lane < HD, dvall[...], dv_all)
        dpre, gain_part = norm_back(grad_k, kpre_ref[...], kgain_ref[...], cos_ref[...], sin_ref[...])
        gain_ref[2:3, :] = gain_part
        for a in range(4):
            at = pl.ds(pl.multiple_of((s_ref[0] ^ a) * b, b), b)
            low_ref[at, 256:384] = dpre[a * b : (a + 1) * b].astype(bf16)
            low_ref[at, 384:512] = grad_v[a * b : (a + 1) * b].astype(bf16)
        hi_ref[...] = contract(low_ref[2 * b :, :], w_ref[...], 1, 1).astype(bf16)
        lo_ref[...] = contract(low_ref[: 2 * b, :], w_ref[...], 1, 1).astype(bf16)


def attend_back_call(s, qk, v, pre, qgain, kgain, cos, sin, start, live, out, lse, wout, w, blocks):
    n = v.shape[0]
    b = n // 4
    d = blocks[0].shape[1]
    lanes = pl.BlockSpec((n, 128), lambda g, s: (0, g))
    third = pl.BlockSpec((n, 128), lambda g, s: (0, 2))
    return pl.pallas_call(
        attend_back_kernel,
        grid_spec=pltpu.PrefetchScalarGridSpec(
            num_scalar_prefetch=1,
            grid=(2,),
            in_specs=[lanes, third, fixed(n, 128), lanes, third, fixed(1, 128), fixed(1, 128), fixed(n, 128),
                      fixed(n, 128), fixed(8, n), fixed(n, 128), lanes,
                      pl.BlockSpec((1, 4, 1, 2 * b), lambda g, s: (g, 0, 0, 0)),
                      fixed(256, d), fixed(d, 512)] + [ANY] * 4,
            out_specs=[fixed(n, 512), fixed(8, 128), fixed(2 * b, d), fixed(2 * b, d)],
            scratch_shapes=[pltpu.VMEM((n, n), f32)]
            + [pltpu.VMEM((n, 128), f32)] * 4
            + [pltpu.VMEM((4, b, 256), bf16), pltpu.VMEM((4, b, d), bf16), pltpu.SemaphoreType.DMA((4,))],
        ),
        out_shape=[
            jax.ShapeDtypeStruct((n, 512), bf16),
            jax.ShapeDtypeStruct((8, 128), f32),
            jax.ShapeDtypeStruct((2 * b, d), bf16),
            jax.ShapeDtypeStruct((2 * b, d), bf16),
        ],
        compiler_params=params(24),
        cost_estimate=cost(1 << 24),
        name="attend_back",
    )(s, qk, qk, v, pre, pre, qgain, kgain, cos, sin, start, live, out, lse, wout, w, *blocks)


def ffn_kernel(s_ref, *refs):
    x_in, a_in, o_in, refs = refs[:4], refs[4:8], refs[8], refs[9:]
    wg_own, wu_own, parts, refs = refs[0], refs[1], refs[2:10], refs[10:]
    gain_ref, n2_ref, hid_ref, fg_ref, fu_ref, res_ref, wout_ref, refs = *refs[:7], refs[7:]
    wg, wu, xs, att, wout, asem, xsem, osem, gsem, usem = refs
    j = pl.program_id(0)
    b = xs.shape[1]
    gate_w = Weight(s_ref, (wg_own,), parts, wg, gsem)
    up_w = Weight(s_ref, (wu_own,), parts, wu, usem, wg.shape[1])

    def out_copy(i):
        return pltpu.make_async_copy(o_in.at[:, i ^ (2 * s_ref[1])], wout.at[i], osem.at[i])

    def att_copy(k, i):
        return pltpu.make_async_copy(
            a_in[i].at[pl.ds((k ^ i) * b, b), :], att.at[k, :, pl.ds(i * b, b)], asem.at[k, i]
        )

    @pl.when(j == 0)
    def _():
        for k in range(4):
            pltpu.make_async_copy(x_in[k], xs.at[k], xsem.at[k]).start()
            for i in range(4):
                att_copy(k, i).start()
            if k == 0:
                for i in range(4):
                    out_copy(i).start()
                gate_w.start()
        up_w.start()
        for i in range(4):
            out_copy(i).wait()

    pltpu.make_async_copy(x_in[0], xs.at[j], xsem.at[j]).wait()
    for i in range(4):
        pltpu.make_async_copy(a_in[i].at[pl.ds(0, b), :], att.at[j, :, pl.ds(i * b, b)], asem.at[j, i]).wait()
    res = xs[j].astype(f32) + jnp.dot(att[j], wout[...].reshape(4 * b, -1), preferred_element_type=f32)

    @pl.when(j == 0)
    def _():
        res_ref[...] = res
        wout_ref[...] = wout[0].reshape(b, -1)
        gate_w.wait()
        up_w.wait()

    inv = lax.rsqrt(jnp.mean(res * res, axis=-1, keepdims=True) + epsilon)
    n2 = (res * inv * gain_ref[...]).astype(bf16)
    n2_ref[...] = n2
    gate = jnp.dot(n2, wg[...], preferred_element_type=f32)
    up = jnp.dot(n2, wu[...], preferred_element_type=f32)
    s = jax.nn.sigmoid(gate)
    silu = gate * s
    hid_ref[...] = (silu * up).astype(bf16)
    fg_ref[...] = (up * (s * (1.0 + gate * (1.0 - s)))).astype(bf16)
    fu_ref[...] = silu.astype(bf16)


def ffn_call(s, xs, atts, wout, wg, wu, parts, gain):
    b, d = xs[0].shape
    h = wg.shape[1]
    block = lambda wid: pl.BlockSpec((b, wid), lambda j, s: (j, 0))
    return pl.pallas_call(
        ffn_kernel,
        grid_spec=pltpu.PrefetchScalarGridSpec(
            num_scalar_prefetch=1,
            grid=(4,),
            in_specs=[ANY] * 19 + [fixed(1, d)],
            out_specs=[block(d), block(h), block(h), block(h), fixed(b, d), fixed(b, d)],
            scratch_shapes=[
                pltpu.VMEM((d, h), bf16),
                pltpu.VMEM((d, h), bf16),
                pltpu.VMEM((4, b, d), bf16),
                pltpu.VMEM((4, b, 4 * b), bf16),
                pltpu.VMEM((4,) + wout.shape[:1] + wout.shape[2:], bf16),
                pltpu.SemaphoreType.DMA((4, 4)),
                pltpu.SemaphoreType.DMA((4,)),
                pltpu.SemaphoreType.DMA((4,)),
                pltpu.SemaphoreType.DMA((9,)),
                pltpu.SemaphoreType.DMA((9,)),
            ],
        ),
        out_shape=[jax.ShapeDtypeStruct((4 * b, d), bf16)]
        + [jax.ShapeDtypeStruct((4 * b, h), bf16)] * 3
        + [jax.ShapeDtypeStruct((b, d), f32), jax.ShapeDtypeStruct((b, d), bf16)],
        compiler_params=params(58),
        cost_estimate=cost(1 << 24),
        name="ffn",
    )(s, *xs, *atts, wout, wg, wu, *parts, gain)


def ffn_back_kernel(s_ref, *refs):
    y_in, wd_own, wd_parts, refs = refs[:4], refs[4], refs[5:13], refs[13:]
    wg_own, wu_own, parts, refs = refs[0], refs[1], refs[2:10], refs[10:]
    fg_ref, fu_ref, gg_ref, gu_ref, lo_ref, hi_ref, wd, wg, wu, dy, ysem, dsem, gsem, usem = refs
    j = pl.program_id(0)
    down_w = Weight(s_ref, (wd_own,), wd_parts, wd, dsem)
    gate_w = Weight(s_ref, (wg_own,), parts, wg, gsem)
    up_w = Weight(s_ref, (wu_own,), parts, wu, usem, wg.shape[1])

    @pl.when(j == 0)
    def _():
        pltpu.make_async_copy(y_in[0], dy.at[0], ysem.at[0]).start()
        down_w.start()
        for k in range(1, 4):
            pltpu.make_async_copy(y_in[k], dy.at[k], ysem.at[k]).start()
        gate_w.start()
        up_w.start()
        down_w.wait()

    pltpu.make_async_copy(y_in[0], dy.at[j], ysem.at[j]).wait()
    gh = contract(dy[j], wd[...], 1, 1)
    gg = (gh * fg_ref[...].astype(f32)).astype(bf16)
    gu = (gh * fu_ref[...].astype(f32)).astype(bf16)
    gg_ref[...] = gg
    gu_ref[...] = gu

    @pl.when(j == 0)
    def _():
        gate_w.wait()
        up_w.wait()

    grad = (contract(gg, wg[...], 1, 1) + contract(gu, wu[...], 1, 1)).astype(bf16)

    @pl.when(j < 2)
    def _():
        lo_ref[...] = grad

    @pl.when(j >= 2)
    def _():
        hi_ref[...] = grad


def ffn_back_call(s, dys, wd, d_parts, wg, wu, parts, fg, fu):
    b, d = dys[0].shape
    h = wg.shape[1]
    block = lambda wid: pl.BlockSpec((b, wid), lambda j, s: (j, 0))
    return pl.pallas_call(
        ffn_back_kernel,
        grid_spec=pltpu.PrefetchScalarGridSpec(
            num_scalar_prefetch=1,
            grid=(4,),
            in_specs=[ANY] * 23 + [block(h), block(h)],
            out_specs=[
                block(h),
                block(h),
                pl.BlockSpec((b, d), lambda j, s: (jnp.minimum(j, 1), 0)),
                pl.BlockSpec((b, d), lambda j, s: (jnp.maximum(j - 2, 0), 0)),
            ],
            scratch_shapes=[
                pltpu.VMEM((h, d), bf16),
                pltpu.VMEM((d, h), bf16),
                pltpu.VMEM((d, h), bf16),
                pltpu.VMEM((4, b, d), bf16),
                pltpu.SemaphoreType.DMA((4,)),
                pltpu.SemaphoreType.DMA((9,)),
                pltpu.SemaphoreType.DMA((9,)),
                pltpu.SemaphoreType.DMA((9,)),
            ],
        ),
        out_shape=[jax.ShapeDtypeStruct((4 * b, h), bf16)] * 2 + [jax.ShapeDtypeStruct((2 * b, d), bf16)] * 2,
        compiler_params=params(58),
        cost_estimate=cost(1 << 24),
        name="ffn_back",
    )(s, *dys, wd, *d_parts, wg, wu, *parts, fg, fu)


def ffn_out_kernel(s_ref, wd_own, *refs):
    wd_parts, (hid_ref, lo_ref, hi_ref, wd, dsem) = refs[:8], refs[8:]
    j = pl.program_id(0)
    down_w = Weight(s_ref, (wd_own,), wd_parts, wd, dsem)

    @pl.when(j == 0)
    def _():
        down_w.start()
        down_w.wait()

    part = jnp.dot(hid_ref[...], wd[...], preferred_element_type=f32).astype(bf16)

    @pl.when(j < 2)
    def _():
        lo_ref[...] = part

    @pl.when(j >= 2)
    def _():
        hi_ref[...] = part


def ffn_out_call(s, wd, d_parts, hidden):
    n, h = hidden.shape
    b, d = n // 4, wd.shape[1]
    return pl.pallas_call(
        ffn_out_kernel,
        grid_spec=pltpu.PrefetchScalarGridSpec(
            num_scalar_prefetch=1,
            grid=(4,),
            in_specs=[ANY] * 9 + [pl.BlockSpec((b, h), lambda j, s: (j, 0))],
            out_specs=[
                pl.BlockSpec((b, d), lambda j, s: (jnp.minimum(j, 1), 0)),
                pl.BlockSpec((b, d), lambda j, s: (jnp.maximum(j - 2, 0), 0)),
            ],
            scratch_shapes=[pltpu.VMEM((h, d), bf16), pltpu.SemaphoreType.DMA((9,))],
        ),
        out_shape=[jax.ShapeDtypeStruct((2 * b, d), bf16)] * 2,
        compiler_params=params(58),
        cost_estimate=cost(1 << 24),
        name="ffn_out",
    )(s, wd, *d_parts, hidden)


def grad_rows_kernel(s_ref, left_ref, a_ref, b_ref, sent_a, keep_a, sent_b, keep_b):
    j = pl.program_id(0)
    left = left_ref[...]
    first = contract(left, a_ref[...], 0, 0).astype(bf16)
    second = contract(left, b_ref[...], 0, 0).astype(bf16)

    @pl.when(j % 2 == 1)
    def _():
        sent_a[0] = first

    @pl.when(j % 2 == 0)
    def _():
        keep_a[0] = first

    @pl.when(j >= 2)
    def _():
        sent_b[0] = second

    @pl.when(j < 2)
    def _():
        keep_b[0] = second


def grad_rows_call(s, left, a, b, name):
    n, rows = left.shape
    cols = a.shape[1]
    maps = [
        lambda j, s: (j // 2, 0, 0),
        lambda j, s: (j // 2, 0, 0),
        lambda j, s: (jnp.maximum(j - 2, 0), 0, 0),
        lambda j, s: (jnp.minimum(j, 1), 0, 0),
    ]
    return pl.pallas_call(
        grad_rows_kernel,
        grid_spec=pltpu.PrefetchScalarGridSpec(
            num_scalar_prefetch=1,
            grid=(4,),
            in_specs=[pl.BlockSpec((n, rows // 4), lambda j, s: (0, s[2] ^ j)), fixed(n, cols), fixed(n, cols)],
            out_specs=[pl.BlockSpec((1, rows // 4, cols), m) for m in maps],
        ),
        out_shape=[jax.ShapeDtypeStruct((2, rows // 4, cols), bf16)] * 4,
        compiler_params=params(16),
        cost_estimate=cost(1 << 24),
        name=name,
    )(s, left, a, b)


def grad_cols_kernel(s_ref, left_ref, r0, r1, r2, r3, sent_a, keep_a, sent_b, keep_b, right, sems):
    k = pl.program_id(0)
    b = r0.shape[0]
    cols = left_ref.shape[0] // 4

    def copy(k, i):
        src = (r0, r1, r2, r3)[i].at[:, pl.ds(pl.multiple_of(k * cols, cols), cols)]
        return pltpu.make_async_copy(src, right.at[k, pl.ds(i * b, b), :], sems.at[k, i])

    @pl.when(k == 0)
    def _():
        for block in range(4):
            for i in range(4):
                copy(block, i).start()

    for i in range(4):
        copy(k, i).wait()
    grad = contract(left_ref[...], right[k], 0, 0)
    grad = grad.astype(bf16)
    rows = grad.shape[0] // 4
    for a in range(4):
        piece = grad[a * rows : (a + 1) * rows]
        j = s_ref[2] ^ a

        @pl.when((k < 2) & (j % 2 == 1))
        def _():
            sent_a[j // 2] = piece

        @pl.when((k < 2) & (j % 2 == 0))
        def _():
            keep_a[j // 2] = piece

        @pl.when((k >= 2) & (j >= 2))
        def _():
            sent_b[j % 2] = piece

        @pl.when((k >= 2) & (j < 2))
        def _():
            keep_b[j % 2] = piece


def grad_cols_call(s, left, rights, name):
    n, rows = left.shape
    b, cols = rights[0].shape
    first = pl.BlockSpec((2, rows // 4, cols // 4), lambda k, s: (0, 0, jnp.minimum(k, 1)))
    second = pl.BlockSpec((2, rows // 4, cols // 4), lambda k, s: (0, 0, jnp.maximum(k - 2, 0)))
    return pl.pallas_call(
        grad_cols_kernel,
        grid_spec=pltpu.PrefetchScalarGridSpec(
            num_scalar_prefetch=1,
            grid=(4,),
            in_specs=[fixed(n, rows)] + [ANY] * 4,
            out_specs=[first, first, second, second],
            scratch_shapes=[pltpu.VMEM((4, n, cols // 4), bf16), pltpu.SemaphoreType.DMA((4, 4))],
        ),
        out_shape=[jax.ShapeDtypeStruct((2, rows // 4, cols // 2), bf16)] * 4,
        compiler_params=params(14),
        cost_estimate=cost(1 << 24),
        name=name,
    )(s, left, *rights)


def widen_kernel(side, in_ref, *outs):
    first, second = in_ref[0, 0].astype(f32), in_ref[0, 1].astype(f32)
    if side:
        outs[0][...] = jnp.concatenate([first, second], 1)
    else:
        outs[0][...] = first
        outs[1][...] = second


def widen_call(whole, side, name):
    _, _, rows, cols = whole.shape
    block = (rows, 2 * cols) if side else (rows, cols)
    count = 1 if side else 2
    return pl.pallas_call(
        functools.partial(widen_kernel, side),
        grid=(8,),
        in_specs=[pl.BlockSpec((1, 2, rows, cols), lambda j: (j, 0, 0, 0))],
        out_specs=[pl.BlockSpec(block, lambda j: (j, 0))] * count,
        out_shape=[jax.ShapeDtypeStruct((8 * block[0], block[1]), f32)] * count,
        compiler_params=params(12),
        cost_estimate=cost(1 << 20),
        name=name,
    )(whole)


def place_kernel(write, s_ref, *refs):
    k = pl.program_id(0)
    for i in range(8):

        @pl.when(k == i)
        def _():
            write(refs[i], refs[8:])


def write_attention(piece, outs):
    query, key, value, out = outs
    r, s = query.shape[0], out.shape[0]
    query[...] = piece[0, :r].astype(f32)
    key[...] = piece[1, :r, :128].astype(f32)
    value[...] = piece[1, :r, 128:].astype(f32)
    sides = [piece[half, r + at * s : r + (at + 1) * s] for half in range(2) for at in range(2)]
    out[...] = jnp.concatenate(sides, 1).astype(f32)


def place_call(s, pieces, write, blocks, name):
    eighth = lambda k, s: (2 * (s[2] ^ (k % 4)) + (s[1] ^ (k // 4)), 0)
    return pl.pallas_call(
        functools.partial(place_kernel, write),
        grid_spec=pltpu.PrefetchScalarGridSpec(
            num_scalar_prefetch=1,
            grid=(8,),
            in_specs=[fixed(*pieces[0].shape)] * 8,
            out_specs=[pl.BlockSpec(block, eighth) for block in blocks],
        ),
        out_shape=[jax.ShapeDtypeStruct((8 * r, cols), f32) for r, cols in blocks],
        compiler_params=params(12),
        cost_estimate=cost(1 << 20),
        name=name,
    )(s, *pieces)


def grad_attention_kernel(s_ref, n1_ref, low_ref, att_ref, b0, b1, b2, b3, sent_a, keep_a, sent_b, keep_b, whole):
    j = pl.program_id(0)
    b = b0.shape[0]

    @pl.when(j == 0)
    def _():
        total = None
        for i, block in enumerate((b0, b1, b2, b3)):
            part = contract(att_ref[i * b : (i + 1) * b, :], block[...], 0, 0)
            total = part if total is None else total + part
        whole[...] = total.astype(bf16)

    qkv = contract(n1_ref[...], low_ref[...], 0, 0).astype(bf16)
    r = qkv.shape[0] // 2
    s = whole.shape[0] // 8
    k = qkv.shape[1] // 2
    out = whole[pl.ds(pl.multiple_of((s_ref[2] ^ j) * 2 * s, 2 * s), 2 * s), :]

    def joined(at):
        parts = []
        for core in range(2):
            some = out[core * s : (core + 1) * s]
            parts += [
                qkv[core * r : (core + 1) * r, at * k : (at + 1) * k],
                some[:, 2 * at * k : (2 * at + 1) * k],
                some[:, (2 * at + 1) * k : (2 * at + 2) * k],
            ]
        return jnp.concatenate(parts, 0)

    @pl.when(j % 2 == 1)
    def _():
        sent_a[0] = joined(0)

    @pl.when(j % 2 == 0)
    def _():
        keep_a[0] = joined(0)

    @pl.when(j >= 2)
    def _():
        sent_b[0] = joined(1)

    @pl.when(j < 2)
    def _():
        keep_b[0] = joined(1)


def grad_attention_call(s, n1, low, att, blocks):
    n, d = n1.shape
    b = n // 4
    half = (d // 4 + att.shape[1] // 2, 256)
    maps = [
        lambda j, s: (j // 2, 0, 0),
        lambda j, s: (j // 2, 0, 0),
        lambda j, s: (jnp.maximum(j - 2, 0), 0, 0),
        lambda j, s: (jnp.minimum(j, 1), 0, 0),
    ]
    return pl.pallas_call(
        grad_attention_kernel,
        grid_spec=pltpu.PrefetchScalarGridSpec(
            num_scalar_prefetch=1,
            grid=(4,),
            in_specs=[pl.BlockSpec((n, d // 4), lambda j, s: (0, s[2] ^ j)), fixed(n, low.shape[1]), fixed(n, att.shape[1])]
            + [fixed(b, d)] * 4,
            out_specs=[pl.BlockSpec((1,) + half, m) for m in maps],
            scratch_shapes=[pltpu.VMEM((att.shape[1], d), bf16)],
        ),
        out_shape=[jax.ShapeDtypeStruct((2,) + half, bf16)] * 4,
        compiler_params=params(18),
        cost_estimate=cost(1 << 24),
        name="grad_attention",
    )(s, n1, low, att, *blocks)


def permute(x, places, move):
    pairs = []
    for d in range(places):
        for t in range(T4):
            to = move(d, t)
            if to is not None:
                pairs.append((d * T4 + t, to[0] * T4 + to[1]))
    return lax.ppermute(x, AX, pairs)


def after(x, *events):
    return lax.optimization_barrier((x, events))[0]


def flip_core(d, t):
    return (d ^ 1, t)


def flip_z(d, t):
    return (d, t ^ 1)


def flip_far(d, t):
    return (d, t ^ 2)


def flip_e(bit):
    return lambda d, t: (d ^ (2 << bit), t)


def settle(d, t):
    return (d, t) if (d & 1) == (t >> 1) else (d ^ 1, t ^ 2)


def step(*values):
    return lax.optimization_barrier(values)


def eighth(w, c, e):
    rows = w.shape[0] // 8
    return lax.dynamic_slice_in_dim(w, (2 * e + c) * rows, rows, 0)


def around(piece, n):
    return [permute(piece, n, lambda d, t, j=j: (d ^ (2 * j), t)) for j in (1, 2, 3)]


def across(pieces, n):
    return [permute(piece, n, flip_core) for piece in pieces]


def first_sums(pieces, n):
    sent_a, keep_a, sent_b, keep_b = pieces
    got_a = permute(sent_a, n, flip_e(0))
    got_b = permute(sent_b, n, flip_e(1))
    return got_a, got_b


def first_add(pieces, got):
    got_a, got_b = got
    keep_a, keep_b = pieces[1], pieces[3]
    return keep_a[1] + got_a[1], keep_a[0] + got_a[0], keep_b[1] + got_b[1], keep_b[0] + got_b[0]


def second_sums(halves, n):
    return permute(halves[0], n, flip_e(1)), permute(halves[2], n, flip_e(0))


def second_add(halves, got, n):
    total = jnp.stack([halves[1] + got[0], halves[3] + got[1]])
    for extra in range(2, 20):
        if (2 << extra) < n:
            total = total + permute(total, n, flip_e(extra))
    return total


def cross_sent(total, c):
    half = total.shape[1] // 2
    return jnp.where(c == 0, total[:, half:], total[:, :half])


def cross_got(total, got, c):
    half = total.shape[1] // 2
    return jnp.where(c == 0, total[:, :half], got), jnp.where(c == 0, got, total[:, half:])


def neighbours(n):
    return None if n == 8 else [list(range(k, k + 8)) for k in range(0, n, 8)]


def whole_grad(mine, n):
    return lax.all_gather(mine, "dp", axis_index_groups=neighbours(n))


def vector_moves(n):
    bits = [1 << k for k in range(20) if 1 << k < n]
    return [flip_z] + [lambda d, t, bit=bit: (d ^ bit, t) for bit in bits] + [flip_far]


def local(
    block_input,
    doc_lengths,
    pad_mask,
    norm1_gain,
    w_query,
    w_key,
    w_value,
    query_gain,
    key_gain,
    w_out,
    norm2_gain,
    w_gate,
    w_up,
    w_down,
    cotangent,
):
    n = lax.axis_size("dp")
    d, t = lax.axis_index("dp"), lax.axis_index("tensor")
    c, p = d & 1, t >> 1
    e = (d >> 1) & 3
    shard = 2 * c + (t & 1)
    b = block_input.shape[0]
    seq_len = b * T4
    home = c == p
    wq = w_query.shape[1]
    wk = w_key.shape[1]
    width = block_input.shape[1]
    s = jnp.stack([shard, c, e]).astype(jnp.int32)

    marks = jnp.concatenate([doc_lengths, pad_mask], 1)
    mine_out = eighth(w_out, c, e)
    mine_qkv = jnp.concatenate([eighth(w, c, e) for w in (w_query, w_key, w_value)], 1)
    x_own = permute(block_input, n, settle)
    qkv_hop = permute(mine_qkv, n, flip_far)
    out_z = permute(mine_out, n, flip_z)
    marks = jnp.where(home, marks, permute(marks, n, flip_core))
    lengths_row, pad_row = marks[0, : doc_lengths.shape[1]], marks[0, doc_lengths.shape[1] :]
    mine_gate_up = jnp.concatenate([eighth(w, c, e) for w in (w_gate, w_up)], 1)
    mine_down = eighth(w_down, c, e)

    positions = jnp.arange(seq_len, dtype=jnp.int32)
    doc_starts, cos_half, sin_half = doc_tables(lengths_row, positions, HD)
    cos = jnp.concatenate([cos_half] * 4, 1)
    sin = jnp.concatenate([-sin_half, sin_half] * 2, 1)
    live = jnp.where(pad_row == 1, positions, -1)
    start_col = jnp.broadcast_to(doc_starts[:, None], (seq_len, 128))
    start_row = jnp.broadcast_to(doc_starts[None], (8, seq_len))
    live_col = jnp.broadcast_to(live[:, None], (seq_len, 128))
    live_row = jnp.broadcast_to(live[None], (8, seq_len))
    gains = jnp.concatenate([query_gain] * (wq // HD) + [key_gain] * (wk // HD))[None]
    qgain_pair = jnp.concatenate([query_gain] * 2)[None]
    kgain_pair = jnp.concatenate([key_gain] * 2)[None]

    x_own, cos, sin, start_col, start_row, live_col, live_row = step(
        x_own, cos, sin, start_col, start_row, live_col, live_row
    )
    qkv_hop, out_z, mine_gate_up, mine_down, late_dy = after([qkv_hop, out_z, mine_gate_up, mine_down, cotangent], x_own)
    x_over, x_near = permute(x_own, n, flip_z), permute(x_own, n, flip_core)
    two_out = jnp.stack([mine_out, out_z])
    out_far = permute(two_out, n, flip_far)
    qkv_around = around(qkv_hop, n)
    gate_up_hop = permute(mine_gate_up, n, flip_far)
    x_over, x_near, out_far, late_dy, *qkv_around = step(x_over, x_near, out_far, late_dy, *qkv_around)
    x_far = permute(x_over, n, flip_core)
    qkv_mine = [qkv_hop] + qkv_around
    qkv_other = across(qkv_mine, n)
    out_all = lax.all_gather(jnp.concatenate([two_out, out_far]), "dp", axis_index_groups=neighbours(n))
    x_blocks = [x_own, x_over, x_near, x_far]

    rows_one, pre, qk, values, w_qkv = qkv_call(
        s, x_blocks, (w_query, w_key, w_value), qkv_mine + qkv_other, norm1_gain[None], gains, cos, sin
    )
    attended, attended_f, lse = attend_call(s, qk, values, start_col, live_row)

    att_over, att_near = permute(attended, n, flip_z), permute(attended, n, flip_core)
    gate_up_hop = after(gate_up_hop, attended)
    gate_up_around = around(gate_up_hop, n)
    mine_down, late_dy = after([mine_down, late_dy], gate_up_hop)
    dy_own = permute(late_dy, n, settle)
    down_hop = permute(mine_down, n, flip_far)
    att_over, att_near, dy_own = step(att_over, att_near, dy_own)
    att_far = permute(att_over, n, flip_core)
    dy_over, dy_near = permute(dy_own, n, flip_z), permute(dy_own, n, flip_core)
    down_hop, *gate_up_around = step(*after([down_hop] + gate_up_around, att_far))
    gate_up_mine = [gate_up_hop] + gate_up_around
    gate_up_parts = gate_up_mine + across(gate_up_mine, n)
    down_around = around(down_hop, n)
    rows_two, hidden, by_gate, by_up, residual, w_out_own = ffn_call(
        s, x_blocks, [attended, att_over, att_near, att_far], out_all, w_gate, w_up, gate_up_parts,
        after(norm2_gain[None], dy_own),
    )
    hidden, dy_over, dy_near, *down_around = step(hidden, dy_over, dy_near, *down_around)
    down_mine = [down_hop] + down_around
    dy_far, *down_across = step(permute(dy_over, n, flip_core), *across(down_mine, n))
    down_parts = down_mine + down_across
    dy_blocks = [dy_own, dy_over, dy_near, dy_far]

    down = grad_cols_call(s, hidden, dy_blocks, "grad_down")
    down_got = first_sums(down, n)
    gate_grad, up_grad, low2, high2 = ffn_back_call(
        s, dy_blocks, w_down, down_parts, w_gate, w_up, gate_up_parts, after(by_gate, *down), by_up
    )
    low2, high2, *down_got = step(low2, high2, *down_got)
    (high_got,) = step(permute(high2, n, flip_core))
    low_half = low2 + high_got
    low_over = permute(low_half[b:], n, flip_z)
    gate_up = grad_rows_call(s, rows_two, after(gate_grad, low_half), up_grad, "grad_gate_up")
    gate_up_got = first_sums(gate_up, n)
    down = first_add(down, after(down_got, *gate_up))
    down_got = second_sums(down, n)
    grad_n2 = (low_half[:b] + after(low_over, *down)).astype(f32)
    inv = lax.rsqrt(jnp.mean(residual * residual, axis=-1, keepdims=True) + epsilon)
    scaled = norm2_gain * grad_n2
    grad_residual = (
        dy_own.astype(f32)
        + inv * scaled
        - residual * (inv * inv * inv) * jnp.mean(scaled * residual, axis=-1, keepdims=True)
    )
    grad_norm2 = jnp.sum(grad_n2 * residual * inv, axis=0)
    gb_own = grad_residual.astype(bf16)
    gb_over, gb_near = permute(gb_own, n, flip_z), permute(gb_own, n, flip_core)
    ffn_low, ffn_high = ffn_out_call(s, w_down, down_parts, after(hidden, gb_own))
    ffn_got = permute(ffn_high, n, flip_core)
    gb_over, gb_near = step(*after([gb_over, gb_near], ffn_low))
    ffn_got = after(ffn_got, gb_over)
    gb_far = permute(gb_over, n, flip_core)
    gate_up = first_add(gate_up, after(gate_up_got, gb_over))
    gate_up_got = second_sums(gate_up, n)
    down = second_add(down, after(down_got, gb_over, *gate_up), n)
    ffn_half = ffn_low + ffn_got
    gb_far, down_got = step(gb_far, permute(cross_sent(down, c), n, flip_core))
    down_kept, down_sent = cross_got(down, down_got, c)
    down_got = permute(down_sent, n, flip_far)
    ffn_over = permute(ffn_half[b:], n, flip_z)
    gb_blocks = [gb_own, gb_over, gb_near, gb_far]

    low, gain_terms, low1, high1 = attend_back_call(
        s, qk, after(values, ffn_half, down_sent), pre, qgain_pair, kgain_pair, cos, sin, start_row, live_col,
        attended_f, lse, w_out_own, w_qkv, gb_blocks,
    )
    low, low1, high1, down_got, ffn_over, *gate_up_got = step(low, low1, high1, down_got, ffn_over, *gate_up_got)
    down_mine = down_kept + down_got
    down_all = whole_grad(down_mine, n)
    gate_up = second_add(gate_up, after(gate_up_got, down_mine), n)
    high_got, gate_up_got = step(permute(high1, n, flip_core), permute(cross_sent(gate_up, c), n, flip_core))
    low_half = low1 + high_got
    low_over = permute(low_half[b:], n, flip_z)
    gate_up_kept, gate_up_sent = cross_got(gate_up, gate_up_got, c)
    gate_up_got = permute(gate_up_sent, n, flip_far)
    att = grad_attention_call(s, rows_one, after(low, low_half, gate_up_sent), attended, gb_blocks)
    att_got = first_sums(att, n)
    block_output = residual + (ffn_half[:b] + after(ffn_over, *att)).astype(f32)
    low_over, gate_up_got, *att_got = step(*after([low_over, gate_up_got, *att_got], block_output))
    gate_up_mine = gate_up_kept + gate_up_got
    gate_up_all = whole_grad(gate_up_mine, n)
    att = first_add(att, after(att_got, gate_up_mine))
    att_got = second_sums(att, n)
    grad_n1 = (low_half[:b] + after(low_over, *att)).astype(f32)
    x_f = x_own.astype(f32)
    inv = lax.rsqrt(jnp.mean(x_f * x_f, axis=-1, keepdims=True) + epsilon)
    scaled = norm1_gain * grad_n1
    input_grad = (
        grad_residual
        + inv * scaled
        - x_f * (inv * inv * inv) * jnp.mean(scaled * x_f, axis=-1, keepdims=True)
    )
    grad_norm1 = jnp.sum(grad_n1 * x_f * inv, axis=0)
    head_terms = gain_terms[:, :HD] + gain_terms[:, HD:]
    vec = jnp.concatenate([grad_norm1, grad_norm2, head_terms[0] + head_terms[1], head_terms[2]])[None]
    moves = vector_moves(n)
    vec_got = permute(vec, n, moves[0])
    att = second_add(att, after(att_got, input_grad, vec), n)
    att_got = permute(cross_sent(att, c), n, flip_core)
    att_got, vec_got = step(att_got, vec_got)
    att_kept, att_sent = cross_got(att, att_got, c)
    att_got = permute(att_sent, n, flip_far)
    vec = vec + vec_got
    vec_got = permute(vec, n, moves[1])
    att_got, vec_got = step(att_got, vec_got)
    att_mine = att_kept + att_got
    att_around = around(att_mine, n)
    late_output, late_grad = after([block_output, input_grad], att_mine)
    settled_output = permute(late_output.astype(bf16), n, settle)
    settled_grad = permute(late_grad.astype(bf16), n, settle)
    vec = vec + vec_got
    vec_got = permute(vec, n, moves[2])
    (grad_down,) = widen_call(after(down_all, vec), True, "widen_down")
    att_around, vec_got = after([att_around, vec_got], grad_down)
    att_across = across([att_mine] + att_around, n)
    vec = vec + vec_got
    vec_got = permute(vec, n, moves[3])
    settled_output, settled_grad, vec_got = after([settled_output, settled_grad, vec_got], *att_around)
    block_output = jnp.where(home, block_output, settled_output.astype(f32))
    input_grad = jnp.where(home, input_grad, settled_grad.astype(f32))
    vec = vec + vec_got
    vec_got = permute(vec, n, moves[4])
    grad_query, grad_key, grad_value, grad_out = place_call(
        s,
        [att_mine] + att_around + after(att_across, block_output, input_grad, vec),
        write_attention,
        [(width // 8, wq), (width // 8, wk), (width // 8, wk), (w_out.shape[0] // 8, width)],
        "place_attention",
    )
    vec = vec + after(vec_got, grad_query)
    for move in moves[5:]:
        vec = vec + permute(vec, n, move)
    grad_gate, grad_up = widen_call(after(gate_up_all, vec), False, "widen_gate_up")
    vec = vec[0]
    return (
        block_output,
        input_grad,
        vec[:width],
        grad_query,
        grad_key,
        grad_value,
        vec[2 * width : 2 * width + HD],
        vec[2 * width + HD :],
        grad_out,
        vec[width : 2 * width],
        grad_gate,
        grad_up,
        grad_down,
    )


def solution(mesh):
    placed = (
        P(("dp", "tensor"), None),
        P("dp", None),
        P("dp", None),
        P(),
        P(None, "tensor"),
        P(None, "tensor"),
        P(None, "tensor"),
        P(),
        P(),
        P("tensor", None),
        P(),
        P(None, "tensor"),
        P(None, "tensor"),
        P("tensor", None),
        P(("dp", "tensor"), None),
    )
    return jax.shard_map(
        local,
        mesh=mesh,
        in_specs=placed,
        out_specs=(
            P(("dp", "tensor"), None),
            P(("dp", "tensor"), None),
            P(),
            P(None, "tensor"),
            P(None, "tensor"),
            P(None, "tensor"),
            P(),
            P(),
            P("tensor", None),
            P(),
            P(None, "tensor"),
            P(None, "tensor"),
            P("tensor", None),
        ),
        check_vma=False,
    )
```

```python
import functools
import math

import jax
import jax.numpy as jnp
from jax import lax
from jax.experimental import pallas as pl
from jax.experimental.pallas import tpu as pltpu
from jax.sharding import PartitionSpec as P

HD = 64
AX = ("dp", "tensor")
T4 = 4
VMEM_MB = 1 << 20

epsilon = 1e-05
rope_base = 1000000.0
NEG = -1000000000.0
bf16 = jnp.bfloat16
f32 = jnp.float32


def doc_tables(lengths_row, positions, head_dim):
    doc_ends = jnp.cumsum(lengths_row)
    passed = positions[:, None] >= doc_ends[None, :]
    doc_starts = jnp.sum(jnp.where(passed, lengths_row[None, :], 0), axis=1)
    offsets = (positions - doc_starts).astype(f32)
    freqs = jnp.exp(
        jnp.arange(head_dim // 2, dtype=f32) * (-2.0 * math.log(rope_base) / head_dim)
    )
    angles = offsets[:, None] * freqs[None, :]
    return (doc_starts, jnp.cos(angles), jnp.sin(angles))


def contract(a, b, da, db):
    return lax.dot_general(a, b, (((da,), (db,)), ((), ())), preferred_element_type=f32)


def swap_halves(y):
    width = y.shape[1]
    lane = lax.broadcasted_iota(jnp.int32, y.shape, 1)
    return jnp.where(lane % HD < HD // 2, pltpu.roll(y, width - HD // 2, 1), pltpu.roll(y, HD // 2, 1))


def split_dot(left, right, da, db):
    high = left.astype(bf16)
    low = (left - high.astype(f32)).astype(bf16)
    return contract(high, right, da, db) + contract(low, right, da, db)


def head_mean(y):
    at = lax.broadcasted_iota(jnp.int32, (128, 128), 0) // HD
    to = lax.broadcasted_iota(jnp.int32, (128, 128), 1) // HD
    ones = jnp.where(at == to, 1.0 / HD, 0.0).astype(bf16)
    sides = [split_dot(y[:, k : k + 128], ones, 1, 0) for k in range(0, y.shape[1], 128)]
    return sides[0] if len(sides) == 1 else jnp.concatenate(sides, 1)


class Weight:
    def __init__(self, s_ref, own, parts, to, sems, start=0):
        self.core, self.e = s_ref[1], s_ref[2]
        self.own, self.parts, self.to, self.sems, self.start_col = own, parts, to, sems, start

    def copies(self):
        start = 0
        for i, w in enumerate(self.own):
            wide = w.shape[1]
            to = self.to if len(self.own) == 1 else self.to.at[:, pl.ds(start, wide)]
            yield 0, functools.partial(pltpu.make_async_copy, w, to, self.sems.at[8 + i])
            start += wide
        rows = self.to.shape[0] // 8
        for j in range(4):
            for other in range(2):
                at = pl.multiple_of((2 * (self.e ^ j) + 1 - other) * rows, rows)
                src = self.parts[4 * other + j]
                if src.shape[1] != self.to.shape[1]:
                    src = src.at[:, pl.ds(self.start_col, self.to.shape[1])]
                to = self.to.at[pl.ds(at, rows), :]
                yield 1, functools.partial(pltpu.make_async_copy, src, to, self.sems.at[2 * j + other])

    def each(self, act):
        for core in range(2):

            @pl.when(self.core == core)
            def _():
                for whose, copy in self.copies():
                    if whose == core:
                        act(copy())

    def start(self):
        self.each(lambda copy: copy.start())

    def wait(self):
        self.each(lambda copy: copy.wait())


ANY = pl.BlockSpec(memory_space=pl.ANY)


def fixed(*shape):
    return pl.BlockSpec(shape, lambda *_: (0,) * len(shape))


def cost(flops):
    return pl.CostEstimate(flops=flops, bytes_accessed=1 << 16, transcendentals=0)


def params(mib):
    return pltpu.CompilerParams(vmem_limit_bytes=mib * VMEM_MB)


def qkv_kernel(s_ref, *refs):
    pieces, own, parts, refs = refs[:4], refs[4:7], refs[7:15], refs[15:]
    g1_ref, gains_ref, cos_ref, sin_ref, n1_ref, pre_ref, qk_ref, v_ref, w_ref, xs, xsem, wsem = refs
    j = pl.program_id(0)
    weight = Weight(s_ref, own, parts, w_ref, wsem)

    @pl.when(j == 0)
    def _():
        for k in range(4):
            pltpu.make_async_copy(pieces[k], xs.at[k], xsem.at[k]).start()
        weight.start()

    pltpu.make_async_copy(pieces[0], xs.at[j], xsem.at[j]).wait()
    x = xs[j].astype(f32)
    inv = lax.rsqrt(jnp.mean(x * x, axis=-1, keepdims=True) + epsilon)
    n1 = (x * inv * g1_ref[...]).astype(bf16)
    n1_ref[...] = n1

    @pl.when(j == 0)
    def _():
        weight.wait()

    qkv = jnp.dot(n1, w_ref[...], preferred_element_type=f32)
    width = pre_ref.shape[1]
    pre = qkv[:, :width]
    pre_ref[...] = pre
    v_ref[...] = qkv[:, width:].astype(bf16)
    y = pre * lax.rsqrt(head_mean(pre * pre) + epsilon) * gains_ref[...]
    cos = jnp.concatenate([cos_ref[...]] * (width // 128), 1)
    sin = jnp.concatenate([sin_ref[...]] * (width // 128), 1)
    qk = (y * cos + swap_halves(y) * sin).astype(bf16)
    lane = lax.broadcasted_iota(jnp.int32, qk.shape, 1)
    qk_ref[...] = jnp.where(lane < width - 128, qk * 0.125, qk).astype(bf16)


def qkv_call(s, xs, w_own, w_parts, g1, gains, cos, sin):
    b, d = xs[0].shape
    wid = w_parts[0].shape[1]
    qkw = wid - 128
    natural = lambda j, s: (s[0] ^ j, 0)
    return pl.pallas_call(
        qkv_kernel,
        grid_spec=pltpu.PrefetchScalarGridSpec(
            num_scalar_prefetch=1,
            grid=(4,),
            in_specs=[ANY] * 15
            + [fixed(1, d), fixed(1, qkw), pl.BlockSpec((b, 128), natural), pl.BlockSpec((b, 128), natural)],
            out_specs=[
                pl.BlockSpec((b, d), lambda j, s: (j, 0)),
                pl.BlockSpec((b, qkw), natural),
                pl.BlockSpec((b, qkw), natural),
                pl.BlockSpec((b, 128), natural),
                fixed(d, wid),
            ],
            scratch_shapes=[
                pltpu.VMEM((4, b, d), bf16),
                pltpu.SemaphoreType.DMA((4,)),
                pltpu.SemaphoreType.DMA((11,)),
            ],
        ),
        out_shape=[
            jax.ShapeDtypeStruct((4 * b, d), bf16),
            jax.ShapeDtypeStruct((4 * b, qkw), f32),
            jax.ShapeDtypeStruct((4 * b, qkw), bf16),
            jax.ShapeDtypeStruct((4 * b, 128), bf16),
            jax.ShapeDtypeStruct((d, wid), bf16),
        ],
        compiler_params=params(58),
        cost_estimate=cost(1 << 24),
        name="qkv",
    )(s, *xs, *w_own, *w_parts, g1, gains, cos, sin)


def both_heads(pair):
    lane = lax.broadcasted_iota(jnp.int32, pair.shape, 1)
    zero = jnp.zeros_like(pair)
    return jnp.concatenate([jnp.where(lane < HD, pair, zero), jnp.where(lane < HD, zero, pair)], 0)


def pick_heads(both):
    r = both.shape[0] // 2
    lane = lax.broadcasted_iota(jnp.int32, (r, 128), 1)
    return jnp.where(lane < HD, both[:r], both[r:])


def twice(kv, g):
    lane = lax.broadcasted_iota(jnp.int32, kv.shape, 1)
    turned = pltpu.roll(kv.astype(f32), HD, 1).astype(kv.dtype)
    return jnp.where((lane < HD) == (g == 0), kv, turned)


def attend_kernel(s_ref, q_ref, k_ref, v_ref, start_ref, live_ref, att_ref, out_ref, lse_ref, bias):
    g = pl.program_id(0)
    n = k_ref.shape[0]
    b = n // 4

    @pl.when(g == 0)
    def _():
        for a in range(4):
            keys = (a + 1) * b
            start = start_ref[a * b : (a + 1) * b, :1]
            q_at = lax.broadcasted_iota(jnp.int32, (b, keys), 0) + a * b
            k_at = lax.broadcasted_iota(jnp.int32, (b, keys), 1)
            allowed = ((live_ref[:1, :keys] >= start) & (k_at <= q_at)) | (k_at == q_at)
            bias[a * b : (a + 1) * b, :keys] = jnp.where(allowed, 0.0, NEG)

    kd = twice(k_ref[...], g)
    vd = twice(v_ref[...], g)
    for a in range(4):
        keys = (a + 1) * b
        rows = slice(a * b, (a + 1) * b)
        qm = both_heads(q_ref[rows, :])
        scores = contract(qm, kd[:keys], 1, 1)
        extra = bias[rows, :keys]
        expo = jnp.exp(scores + jnp.concatenate([extra, extra], 0))
        total = jnp.sum(expo, axis=-1, keepdims=True)
        pair = pick_heads(contract(expo.astype(bf16), vd[:keys], 1, 0) / total)
        out_ref[rows, :] = pair
        att_ref[pl.ds(pl.multiple_of((s_ref[0] ^ a) * b, b), b), :] = pair.astype(bf16)
        lse_ref[0, a] = jnp.transpose(jnp.broadcast_to(jnp.log(total), (2 * b, 128)))[:1]


def attend_call(s, qk, v, start, live):
    n = qk.shape[0]
    b = n // 4
    lanes = lambda g, s: (0, g)
    return pl.pallas_call(
        attend_kernel,
        grid_spec=pltpu.PrefetchScalarGridSpec(
            num_scalar_prefetch=1,
            grid=(2,),
            in_specs=[
                pl.BlockSpec((n, 128), lanes),
                pl.BlockSpec((n, 128), lambda g, s: (0, 2)),
                fixed(n, 128),
                fixed(n, 128),
                fixed(8, n),
            ],
            out_specs=[
                pl.BlockSpec((n, 128), lanes),
                pl.BlockSpec((n, 128), lanes),
                pl.BlockSpec((1, 4, 1, 2 * b), lambda g, s: (g, 0, 0, 0)),
            ],
            scratch_shapes=[pltpu.VMEM((n, n), f32)],
        ),
        out_shape=[
            jax.ShapeDtypeStruct((n, 256), bf16),
            jax.ShapeDtypeStruct((n, 256), f32),
            jax.ShapeDtypeStruct((2, 4, 1, 2 * b), f32),
        ],
        compiler_params=params(14),
        cost_estimate=cost(1 << 24),
        name="attend",
    )(s, qk, qk, v, start, live)


def norm_back(grad, pre, gain, cos, sin):
    turned = grad * cos - swap_halves(grad) * sin
    inv = lax.rsqrt(head_mean(pre * pre) + epsilon)
    scaled = turned * gain
    dpre = inv * scaled - pre * (inv * inv * inv) * head_mean(scaled * pre)
    return dpre, jnp.sum(turned * pre * inv, axis=0, keepdims=True)


def attend_back_kernel(s_ref, q_ref, k_ref, v_ref, qpre_ref, kpre_ref, gains_ref, kgain_ref, cos_ref, sin_ref,
                       start_ref, live_ref, out_ref, lse_ref, wout_ref, w_ref, b0, b1, b2, b3,
                       low_ref, gain_ref, lo_ref, hi_ref, bias, dk, dv, dkall, dvall, dos, gb, sems):
    g = pl.program_id(0)
    n = k_ref.shape[0]
    b = n // 4
    pieces = (b0, b1, b2, b3)

    @pl.when(g == 0)
    def _():
        for k in range(4):
            pltpu.make_async_copy(pieces[k], gb.at[k], sems.at[k]).start()
        for a in range(4):
            keys = (a + 1) * b
            start = start_ref[:1, a * b : (a + 1) * b]
            k_at = lax.broadcasted_iota(jnp.int32, (keys, b), 0)
            q_at = lax.broadcasted_iota(jnp.int32, (keys, b), 1) + a * b
            allowed = ((live_ref[:keys, :1] >= start) & (k_at <= q_at)) | (k_at == q_at)
            bias[:keys, a * b : (a + 1) * b] = jnp.where(allowed, 0.0, NEG)
        for k in range(4):
            pltpu.make_async_copy(pieces[k], gb.at[k], sems.at[k]).wait()
            dos[k] = contract(gb[k], wout_ref[...], 1, 1).astype(bf16)

    kd = twice(k_ref[...], g)
    vd = twice(v_ref[...], g)
    gain_sum = jnp.zeros((1, 128), f32)
    ones = jnp.ones((16, 128), bf16)
    for a in (3, 2, 1, 0):
        keys = (a + 1) * b
        rows = slice(a * b, (a + 1) * b)
        home = s_ref[0] ^ a
        qm = both_heads(q_ref[rows, :])
        dout = jnp.where(g == 0, dos[home, :, :128], dos[home, :, 128:])
        dom = both_heads(dout)
        terms = both_heads(dout.astype(f32) * out_ref[rows, :])
        terms_high = terms.astype(bf16)
        terms_low = (terms - terms_high.astype(f32)).astype(bf16)
        delta = (contract(ones, terms_high, 1, 1) + contract(ones, terms_low, 1, 1))[:1]
        scores = contract(kd[:keys], qm, 1, 1)
        extra = bias[:keys, rows]
        probs = jnp.exp(scores + (jnp.concatenate([extra, extra], 1) - lse_ref[0, a]))
        dprobs = contract(vd[:keys], dom, 1, 1)
        dscores = (probs * (dprobs - delta)).astype(bf16)
        dv_add = contract(probs.astype(bf16), dom, 1, 0)
        dk_add = contract(dscores, qm, 1, 0)
        if a == 3:
            dv[...] = dv_add
            dk[...] = dk_add
        else:
            dv[:keys] += dv_add
            dk[:keys] += dk_add
        dq = pick_heads(contract(dscores, kd[:keys], 0, 0)) * 0.125
        dpre, gain_part = norm_back(dq, qpre_ref[rows, :], gains_ref[...], cos_ref[rows, :], sin_ref[rows, :])
        at = pl.ds(pl.multiple_of(home * b, b), b)
        low_ref[at, pl.ds(pl.multiple_of(g * 128, 128), 128)] = dpre.astype(bf16)
        gain_sum = gain_sum + gain_part
    gain_ref[pl.ds(g, 1), :] = gain_sum
    lane = lax.broadcasted_iota(jnp.int32, (n, 128), 1)
    dk_all = dk[...] + pltpu.roll(dk[...], HD, 1)
    dv_all = dv[...] + pltpu.roll(dv[...], HD, 1)

    @pl.when(g == 0)
    def _():
        dkall[...] = dk_all
        dvall[...] = dv_all

    @pl.when(g == 1)
    def _():
        grad_k = jnp.where(lane < HD, dkall[...], dk_all)
        grad_v = jnp.where(lane < HD, dvall[...], dv_all)
        dpre, gain_part = norm_back(grad_k, kpre_ref[...], kgain_ref[...], cos_ref[...], sin_ref[...])
        gain_ref[2:3, :] = gain_part
        for a in range(4):
            at = pl.ds(pl.multiple_of((s_ref[0] ^ a) * b, b), b)
            low_ref[at, 256:384] = dpre[a * b : (a + 1) * b].astype(bf16)
            low_ref[at, 384:512] = grad_v[a * b : (a + 1) * b].astype(bf16)
        hi_ref[...] = contract(low_ref[2 * b :, :], w_ref[...], 1, 1).astype(bf16)
        lo_ref[...] = contract(low_ref[: 2 * b, :], w_ref[...], 1, 1).astype(bf16)


def attend_back_call(s, qk, v, pre, qgain, kgain, cos, sin, start, live, out, lse, wout, w, blocks):
    n = v.shape[0]
    b = n // 4
    d = blocks[0].shape[1]
    lanes = pl.BlockSpec((n, 128), lambda g, s: (0, g))
    third = pl.BlockSpec((n, 128), lambda g, s: (0, 2))
    return pl.pallas_call(
        attend_back_kernel,
        grid_spec=pltpu.PrefetchScalarGridSpec(
            num_scalar_prefetch=1,
            grid=(2,),
            in_specs=[lanes, third, fixed(n, 128), lanes, third, fixed(1, 128), fixed(1, 128), fixed(n, 128),
                      fixed(n, 128), fixed(8, n), fixed(n, 128), lanes,
                      pl.BlockSpec((1, 4, 1, 2 * b), lambda g, s: (g, 0, 0, 0)),
                      fixed(256, d), fixed(d, 512)] + [ANY] * 4,
            out_specs=[fixed(n, 512), fixed(8, 128), fixed(2 * b, d), fixed(2 * b, d)],
            scratch_shapes=[pltpu.VMEM((n, n), f32)]
            + [pltpu.VMEM((n, 128), f32)] * 4
            + [pltpu.VMEM((4, b, 256), bf16), pltpu.VMEM((4, b, d), bf16), pltpu.SemaphoreType.DMA((4,))],
        ),
        out_shape=[
            jax.ShapeDtypeStruct((n, 512), bf16),
            jax.ShapeDtypeStruct((8, 128), f32),
            jax.ShapeDtypeStruct((2 * b, d), bf16),
            jax.ShapeDtypeStruct((2 * b, d), bf16),
        ],
        compiler_params=params(24),
        cost_estimate=cost(1 << 24),
        name="attend_back",
    )(s, qk, qk, v, pre, pre, qgain, kgain, cos, sin, start, live, out, lse, wout, w, *blocks)


def ffn_kernel(s_ref, *refs):
    x_in, a_in, o_in, refs = refs[:4], refs[4:8], refs[8], refs[9:]
    wg_own, wu_own, parts, refs = refs[0], refs[1], refs[2:10], refs[10:]
    gain_ref, n2_ref, hid_ref, fg_ref, fu_ref, res_ref, wout_ref, refs = *refs[:7], refs[7:]
    wg, wu, xs, att, wout, asem, xsem, osem, gsem, usem = refs
    j = pl.program_id(0)
    b = xs.shape[1]
    gate_w = Weight(s_ref, (wg_own,), parts, wg, gsem)
    up_w = Weight(s_ref, (wu_own,), parts, wu, usem, wg.shape[1])

    def out_copy(i):
        return pltpu.make_async_copy(o_in.at[:, i ^ (2 * s_ref[1])], wout.at[i], osem.at[i])

    def att_copy(k, i):
        return pltpu.make_async_copy(
            a_in[i].at[pl.ds((k ^ i) * b, b), :], att.at[k, :, pl.ds(i * b, b)], asem.at[k, i]
        )

    @pl.when(j == 0)
    def _():
        for k in range(4):
            pltpu.make_async_copy(x_in[k], xs.at[k], xsem.at[k]).start()
            for i in range(4):
                att_copy(k, i).start()
            if k == 0:
                for i in range(4):
                    out_copy(i).start()
                gate_w.start()
        up_w.start()
        for i in range(4):
            out_copy(i).wait()

    pltpu.make_async_copy(x_in[0], xs.at[j], xsem.at[j]).wait()
    for i in range(4):
        pltpu.make_async_copy(a_in[i].at[pl.ds(0, b), :], att.at[j, :, pl.ds(i * b, b)], asem.at[j, i]).wait()
    res = xs[j].astype(f32) + jnp.dot(att[j], wout[...].reshape(4 * b, -1), preferred_element_type=f32)

    @pl.when(j == 0)
    def _():
        res_ref[...] = res
        wout_ref[...] = wout[0].reshape(b, -1)
        gate_w.wait()
        up_w.wait()

    inv = lax.rsqrt(jnp.mean(res * res, axis=-1, keepdims=True) + epsilon)
    n2 = (res * inv * gain_ref[...]).astype(bf16)
    n2_ref[...] = n2
    gate = jnp.dot(n2, wg[...], preferred_element_type=f32)
    up = jnp.dot(n2, wu[...], preferred_element_type=f32)
    s = jax.nn.sigmoid(gate)
    silu = gate * s
    hid_ref[...] = (silu * up).astype(bf16)
    fg_ref[...] = (up * (s * (1.0 + gate * (1.0 - s)))).astype(bf16)
    fu_ref[...] = silu.astype(bf16)


def ffn_call(s, xs, atts, wout, wg, wu, parts, gain):
    b, d = xs[0].shape
    h = wg.shape[1]
    block = lambda wid: pl.BlockSpec((b, wid), lambda j, s: (j, 0))
    return pl.pallas_call(
        ffn_kernel,
        grid_spec=pltpu.PrefetchScalarGridSpec(
            num_scalar_prefetch=1,
            grid=(4,),
            in_specs=[ANY] * 19 + [fixed(1, d)],
            out_specs=[block(d), block(h), block(h), block(h), fixed(b, d), fixed(b, d)],
            scratch_shapes=[
                pltpu.VMEM((d, h), bf16),
                pltpu.VMEM((d, h), bf16),
                pltpu.VMEM((4, b, d), bf16),
                pltpu.VMEM((4, b, 4 * b), bf16),
                pltpu.VMEM((4,) + wout.shape[:1] + wout.shape[2:], bf16),
                pltpu.SemaphoreType.DMA((4, 4)),
                pltpu.SemaphoreType.DMA((4,)),
                pltpu.SemaphoreType.DMA((4,)),
                pltpu.SemaphoreType.DMA((9,)),
                pltpu.SemaphoreType.DMA((9,)),
            ],
        ),
        out_shape=[jax.ShapeDtypeStruct((4 * b, d), bf16)]
        + [jax.ShapeDtypeStruct((4 * b, h), bf16)] * 3
        + [jax.ShapeDtypeStruct((b, d), f32), jax.ShapeDtypeStruct((b, d), bf16)],
        compiler_params=params(58),
        cost_estimate=cost(1 << 24),
        name="ffn",
    )(s, *xs, *atts, wout, wg, wu, *parts, gain)


def ffn_back_kernel(s_ref, *refs):
    y_in, wd_own, wd_parts, refs = refs[:4], refs[4], refs[5:13], refs[13:]
    wg_own, wu_own, parts, refs = refs[0], refs[1], refs[2:10], refs[10:]
    fg_ref, fu_ref, gg_ref, gu_ref, lo_ref, hi_ref, wd, wg, wu, dy, ysem, dsem, gsem, usem = refs
    j = pl.program_id(0)
    down_w = Weight(s_ref, (wd_own,), wd_parts, wd, dsem)
    gate_w = Weight(s_ref, (wg_own,), parts, wg, gsem)
    up_w = Weight(s_ref, (wu_own,), parts, wu, usem, wg.shape[1])

    @pl.when(j == 0)
    def _():
        pltpu.make_async_copy(y_in[0], dy.at[0], ysem.at[0]).start()
        down_w.start()
        for k in range(1, 4):
            pltpu.make_async_copy(y_in[k], dy.at[k], ysem.at[k]).start()
        gate_w.start()
        up_w.start()
        down_w.wait()

    pltpu.make_async_copy(y_in[0], dy.at[j], ysem.at[j]).wait()
    gh = contract(dy[j], wd[...], 1, 1)
    gg = (gh * fg_ref[...].astype(f32)).astype(bf16)
    gu = (gh * fu_ref[...].astype(f32)).astype(bf16)
    gg_ref[...] = gg
    gu_ref[...] = gu

    @pl.when(j == 0)
    def _():
        gate_w.wait()
        up_w.wait()

    grad = (contract(gg, wg[...], 1, 1) + contract(gu, wu[...], 1, 1)).astype(bf16)

    @pl.when(j < 2)
    def _():
        lo_ref[...] = grad

    @pl.when(j >= 2)
    def _():
        hi_ref[...] = grad


def ffn_back_call(s, dys, wd, d_parts, wg, wu, parts, fg, fu):
    b, d = dys[0].shape
    h = wg.shape[1]
    block = lambda wid: pl.BlockSpec((b, wid), lambda j, s: (j, 0))
    return pl.pallas_call(
        ffn_back_kernel,
        grid_spec=pltpu.PrefetchScalarGridSpec(
            num_scalar_prefetch=1,
            grid=(4,),
            in_specs=[ANY] * 23 + [block(h), block(h)],
            out_specs=[
                block(h),
                block(h),
                pl.BlockSpec((b, d), lambda j, s: (jnp.minimum(j, 1), 0)),
                pl.BlockSpec((b, d), lambda j, s: (jnp.maximum(j - 2, 0), 0)),
            ],
            scratch_shapes=[
                pltpu.VMEM((h, d), bf16),
                pltpu.VMEM((d, h), bf16),
                pltpu.VMEM((d, h), bf16),
                pltpu.VMEM((4, b, d), bf16),
                pltpu.SemaphoreType.DMA((4,)),
                pltpu.SemaphoreType.DMA((9,)),
                pltpu.SemaphoreType.DMA((9,)),
                pltpu.SemaphoreType.DMA((9,)),
            ],
        ),
        out_shape=[jax.ShapeDtypeStruct((4 * b, h), bf16)] * 2 + [jax.ShapeDtypeStruct((2 * b, d), bf16)] * 2,
        compiler_params=params(58),
        cost_estimate=cost(1 << 24),
        name="ffn_back",
    )(s, *dys, wd, *d_parts, wg, wu, *parts, fg, fu)


def ffn_out_kernel(s_ref, wd_own, *refs):
    wd_parts, (hid_ref, lo_ref, hi_ref, wd, dsem) = refs[:8], refs[8:]
    j = pl.program_id(0)
    down_w = Weight(s_ref, (wd_own,), wd_parts, wd, dsem)

    @pl.when(j == 0)
    def _():
        down_w.start()
        down_w.wait()

    part = jnp.dot(hid_ref[...], wd[...], preferred_element_type=f32).astype(bf16)

    @pl.when(j < 2)
    def _():
        lo_ref[...] = part

    @pl.when(j >= 2)
    def _():
        hi_ref[...] = part


def ffn_out_call(s, wd, d_parts, hidden):
    n, h = hidden.shape
    b, d = n // 4, wd.shape[1]
    return pl.pallas_call(
        ffn_out_kernel,
        grid_spec=pltpu.PrefetchScalarGridSpec(
            num_scalar_prefetch=1,
            grid=(4,),
            in_specs=[ANY] * 9 + [pl.BlockSpec((b, h), lambda j, s: (j, 0))],
            out_specs=[
                pl.BlockSpec((b, d), lambda j, s: (jnp.minimum(j, 1), 0)),
                pl.BlockSpec((b, d), lambda j, s: (jnp.maximum(j - 2, 0), 0)),
            ],
            scratch_shapes=[pltpu.VMEM((h, d), bf16), pltpu.SemaphoreType.DMA((9,))],
        ),
        out_shape=[jax.ShapeDtypeStruct((2 * b, d), bf16)] * 2,
        compiler_params=params(58),
        cost_estimate=cost(1 << 24),
        name="ffn_out",
    )(s, wd, *d_parts, hidden)


def grad_rows_kernel(s_ref, left_ref, a_ref, b_ref, sent_a, keep_a, sent_b, keep_b):
    j = pl.program_id(0)
    left = left_ref[...]
    first = contract(left, a_ref[...], 0, 0).astype(bf16)
    second = contract(left, b_ref[...], 0, 0).astype(bf16)

    @pl.when(j % 2 == 1)
    def _():
        sent_a[0] = first

    @pl.when(j % 2 == 0)
    def _():
        keep_a[0] = first

    @pl.when(j >= 2)
    def _():
        sent_b[0] = second

    @pl.when(j < 2)
    def _():
        keep_b[0] = second


def grad_rows_call(s, left, a, b, name):
    n, rows = left.shape
    cols = a.shape[1]
    maps = [
        lambda j, s: (j // 2, 0, 0),
        lambda j, s: (j // 2, 0, 0),
        lambda j, s: (jnp.maximum(j - 2, 0), 0, 0),
        lambda j, s: (jnp.minimum(j, 1), 0, 0),
    ]
    return pl.pallas_call(
        grad_rows_kernel,
        grid_spec=pltpu.PrefetchScalarGridSpec(
            num_scalar_prefetch=1,
            grid=(4,),
            in_specs=[pl.BlockSpec((n, rows // 4), lambda j, s: (0, s[2] ^ j)), fixed(n, cols), fixed(n, cols)],
            out_specs=[pl.BlockSpec((1, rows // 4, cols), m) for m in maps],
        ),
        out_shape=[jax.ShapeDtypeStruct((2, rows // 4, cols), bf16)] * 4,
        compiler_params=params(16),
        cost_estimate=cost(1 << 24),
        name=name,
    )(s, left, a, b)


def grad_cols_kernel(s_ref, left_ref, r0, r1, r2, r3, sent_a, keep_a, sent_b, keep_b, right, sems):
    k = pl.program_id(0)
    b = r0.shape[0]
    cols = left_ref.shape[0] // 4

    def copy(k, i):
        src = (r0, r1, r2, r3)[i].at[:, pl.ds(pl.multiple_of(k * cols, cols), cols)]
        return pltpu.make_async_copy(src, right.at[k, pl.ds(i * b, b), :], sems.at[k, i])

    @pl.when(k == 0)
    def _():
        for block in range(4):
            for i in range(4):
                copy(block, i).start()

    for i in range(4):
        copy(k, i).wait()
    grad = contract(left_ref[...], right[k], 0, 0)
    grad = grad.astype(bf16)
    rows = grad.shape[0] // 4
    for a in range(4):
        piece = grad[a * rows : (a + 1) * rows]
        j = s_ref[2] ^ a

        @pl.when((k < 2) & (j % 2 == 1))
        def _():
            sent_a[j // 2] = piece

        @pl.when((k < 2) & (j % 2 == 0))
        def _():
            keep_a[j // 2] = piece

        @pl.when((k >= 2) & (j >= 2))
        def _():
            sent_b[j % 2] = piece

        @pl.when((k >= 2) & (j < 2))
        def _():
            keep_b[j % 2] = piece


def grad_cols_call(s, left, rights, name):
    n, rows = left.shape
    b, cols = rights[0].shape
    first = pl.BlockSpec((2, rows // 4, cols // 4), lambda k, s: (0, 0, jnp.minimum(k, 1)))
    second = pl.BlockSpec((2, rows // 4, cols // 4), lambda k, s: (0, 0, jnp.maximum(k - 2, 0)))
    return pl.pallas_call(
        grad_cols_kernel,
        grid_spec=pltpu.PrefetchScalarGridSpec(
            num_scalar_prefetch=1,
            grid=(4,),
            in_specs=[fixed(n, rows)] + [ANY] * 4,
            out_specs=[first, first, second, second],
            scratch_shapes=[pltpu.VMEM((4, n, cols // 4), bf16), pltpu.SemaphoreType.DMA((4, 4))],
        ),
        out_shape=[jax.ShapeDtypeStruct((2, rows // 4, cols // 2), bf16)] * 4,
        compiler_params=params(14),
        cost_estimate=cost(1 << 24),
        name=name,
    )(s, left, *rights)


def widen_kernel(side, in_ref, *outs):
    first, second = in_ref[0, 0].astype(f32), in_ref[0, 1].astype(f32)
    if side:
        outs[0][...] = jnp.concatenate([first, second], 1)
    else:
        outs[0][...] = first
        outs[1][...] = second


def widen_call(whole, side, name):
    _, _, rows, cols = whole.shape
    block = (rows, 2 * cols) if side else (rows, cols)
    count = 1 if side else 2
    return pl.pallas_call(
        functools.partial(widen_kernel, side),
        grid=(8,),
        in_specs=[pl.BlockSpec((1, 2, rows, cols), lambda j: (j, 0, 0, 0))],
        out_specs=[pl.BlockSpec(block, lambda j: (j, 0))] * count,
        out_shape=[jax.ShapeDtypeStruct((8 * block[0], block[1]), f32)] * count,
        compiler_params=params(12),
        cost_estimate=cost(1 << 20),
        name=name,
    )(whole)


def place_kernel(write, s_ref, *refs):
    k = pl.program_id(0)
    for i in range(8):

        @pl.when(k == i)
        def _():
            write(refs[i], refs[8:])


def write_attention(piece, outs):
    query, key, value, out = outs
    r, s = query.shape[0], out.shape[0]
    query[...] = piece[0, :r].astype(f32)
    key[...] = piece[1, :r, :128].astype(f32)
    value[...] = piece[1, :r, 128:].astype(f32)
    sides = [piece[half, r + at * s : r + (at + 1) * s] for half in range(2) for at in range(2)]
    out[...] = jnp.concatenate(sides, 1).astype(f32)


def place_call(s, pieces, write, blocks, name):
    eighth = lambda k, s: (2 * (s[2] ^ (k % 4)) + (s[1] ^ (k // 4)), 0)
    return pl.pallas_call(
        functools.partial(place_kernel, write),
        grid_spec=pltpu.PrefetchScalarGridSpec(
            num_scalar_prefetch=1,
            grid=(8,),
            in_specs=[fixed(*pieces[0].shape)] * 8,
            out_specs=[pl.BlockSpec(block, eighth) for block in blocks],
        ),
        out_shape=[jax.ShapeDtypeStruct((8 * r, cols), f32) for r, cols in blocks],
        compiler_params=params(12),
        cost_estimate=cost(1 << 20),
        name=name,
    )(s, *pieces)


def grad_attention_kernel(s_ref, n1_ref, low_ref, att_ref, b0, b1, b2, b3, sent_a, keep_a, sent_b, keep_b, whole):
    j = pl.program_id(0)
    b = b0.shape[0]

    @pl.when(j == 0)
    def _():
        total = None
        for i, block in enumerate((b0, b1, b2, b3)):
            part = contract(att_ref[i * b : (i + 1) * b, :], block[...], 0, 0)
            total = part if total is None else total + part
        whole[...] = total.astype(bf16)

    qkv = contract(n1_ref[...], low_ref[...], 0, 0).astype(bf16)
    r = qkv.shape[0] // 2
    s = whole.shape[0] // 8
    k = qkv.shape[1] // 2
    out = whole[pl.ds(pl.multiple_of((s_ref[2] ^ j) * 2 * s, 2 * s), 2 * s), :]

    def joined(at):
        parts = []
        for core in range(2):
            some = out[core * s : (core + 1) * s]
            parts += [
                qkv[core * r : (core + 1) * r, at * k : (at + 1) * k],
                some[:, 2 * at * k : (2 * at + 1) * k],
                some[:, (2 * at + 1) * k : (2 * at + 2) * k],
            ]
        return jnp.concatenate(parts, 0)

    @pl.when(j % 2 == 1)
    def _():
        sent_a[0] = joined(0)

    @pl.when(j % 2 == 0)
    def _():
        keep_a[0] = joined(0)

    @pl.when(j >= 2)
    def _():
        sent_b[0] = joined(1)

    @pl.when(j < 2)
    def _():
        keep_b[0] = joined(1)


def grad_attention_call(s, n1, low, att, blocks):
    n, d = n1.shape
    b = n // 4
    half = (d // 4 + att.shape[1] // 2, 256)
    maps = [
        lambda j, s: (j // 2, 0, 0),
        lambda j, s: (j // 2, 0, 0),
        lambda j, s: (jnp.maximum(j - 2, 0), 0, 0),
        lambda j, s: (jnp.minimum(j, 1), 0, 0),
    ]
    return pl.pallas_call(
        grad_attention_kernel,
        grid_spec=pltpu.PrefetchScalarGridSpec(
            num_scalar_prefetch=1,
            grid=(4,),
            in_specs=[pl.BlockSpec((n, d // 4), lambda j, s: (0, s[2] ^ j)), fixed(n, low.shape[1]), fixed(n, att.shape[1])]
            + [fixed(b, d)] * 4,
            out_specs=[pl.BlockSpec((1,) + half, m) for m in maps],
            scratch_shapes=[pltpu.VMEM((att.shape[1], d), bf16)],
        ),
        out_shape=[jax.ShapeDtypeStruct((2,) + half, bf16)] * 4,
        compiler_params=params(18),
        cost_estimate=cost(1 << 24),
        name="grad_attention",
    )(s, n1, low, att, *blocks)


def permute(x, places, move):
    pairs = []
    for d in range(places):
        for t in range(T4):
            to = move(d, t)
            if to is not None:
                pairs.append((d * T4 + t, to[0] * T4 + to[1]))
    return lax.ppermute(x, AX, pairs)


def after(x, *events):
    return lax.optimization_barrier((x, events))[0]


def flip_core(d, t):
    return (d ^ 1, t)


def flip_z(d, t):
    return (d, t ^ 1)


def flip_far(d, t):
    return (d, t ^ 2)


def flip_e(bit):
    return lambda d, t: (d ^ (2 << bit), t)


def settle(d, t):
    return (d, t) if (d & 1) == (t >> 1) else (d ^ 1, t ^ 2)


def step(*values):
    return lax.optimization_barrier(values)


def eighth(w, c, e):
    rows = w.shape[0] // 8
    return lax.dynamic_slice_in_dim(w, (2 * e + c) * rows, rows, 0)


def around(piece, n):
    return [permute(piece, n, lambda d, t, j=j: (d ^ (2 * j), t)) for j in (1, 2, 3)]


def across(pieces, n):
    return [permute(piece, n, flip_core) for piece in pieces]


def first_sums(pieces, n):
    sent_a, keep_a, sent_b, keep_b = pieces
    got_a = permute(sent_a, n, flip_e(0))
    got_b = permute(sent_b, n, flip_e(1))
    return got_a, got_b


def first_add(pieces, got):
    got_a, got_b = got
    keep_a, keep_b = pieces[1], pieces[3]
    return keep_a[1] + got_a[1], keep_a[0] + got_a[0], keep_b[1] + got_b[1], keep_b[0] + got_b[0]


def second_sums(halves, n):
    return permute(halves[0], n, flip_e(1)), permute(halves[2], n, flip_e(0))


def second_add(halves, got, n):
    total = jnp.stack([halves[1] + got[0], halves[3] + got[1]])
    for extra in range(2, 20):
        if (2 << extra) < n:
            total = total + permute(total, n, flip_e(extra))
    return total


def cross_sent(total, c):
    half = total.shape[1] // 2
    return jnp.where(c == 0, total[:, half:], total[:, :half])


def cross_got(total, got, c):
    half = total.shape[1] // 2
    return jnp.where(c == 0, total[:, :half], got), jnp.where(c == 0, got, total[:, half:])


def neighbours(n):
    return None if n == 8 else [list(range(k, k + 8)) for k in range(0, n, 8)]


def whole_grad(mine, n):
    return lax.all_gather(mine, "dp", axis_index_groups=neighbours(n))


def vector_moves(n):
    bits = [1 << k for k in range(20) if 1 << k < n]
    return [flip_z] + [lambda d, t, bit=bit: (d ^ bit, t) for bit in bits] + [flip_far]


def local(
    block_input,
    doc_lengths,
    pad_mask,
    norm1_gain,
    w_query,
    w_key,
    w_value,
    query_gain,
    key_gain,
    w_out,
    norm2_gain,
    w_gate,
    w_up,
    w_down,
    cotangent,
):
    n = lax.axis_size("dp")
    d, t = lax.axis_index("dp"), lax.axis_index("tensor")
    c, p = d & 1, t >> 1
    e = (d >> 1) & 3
    shard = 2 * c + (t & 1)
    b = block_input.shape[0]
    seq_len = b * T4
    home = c == p
    wq = w_query.shape[1]
    wk = w_key.shape[1]
    width = block_input.shape[1]
    s = jnp.stack([shard, c, e]).astype(jnp.int32)

    marks = jnp.concatenate([doc_lengths, pad_mask], 1)
    mine_out = eighth(w_out, c, e)
    mine_qkv = jnp.concatenate([eighth(w, c, e) for w in (w_query, w_key, w_value)], 1)
    x_own = permute(block_input, n, settle)
    qkv_hop = permute(mine_qkv, n, flip_far)
    out_z = permute(mine_out, n, flip_z)
    marks = jnp.where(home, marks, permute(marks, n, flip_core))
    lengths_row, pad_row = marks[0, : doc_lengths.shape[1]], marks[0, doc_lengths.shape[1] :]
    mine_gate_up = jnp.concatenate([eighth(w, c, e) for w in (w_gate, w_up)], 1)
    mine_down = eighth(w_down, c, e)

    positions = jnp.arange(seq_len, dtype=jnp.int32)
    doc_starts, cos_half, sin_half = doc_tables(lengths_row, positions, HD)
    cos = jnp.concatenate([cos_half] * 4, 1)
    sin = jnp.concatenate([-sin_half, sin_half] * 2, 1)
    live = jnp.where(pad_row == 1, positions, -1)
    start_col = jnp.broadcast_to(doc_starts[:, None], (seq_len, 128))
    start_row = jnp.broadcast_to(doc_starts[None], (8, seq_len))
    live_col = jnp.broadcast_to(live[:, None], (seq_len, 128))
    live_row = jnp.broadcast_to(live[None], (8, seq_len))
    gains = jnp.concatenate([query_gain] * (wq // HD) + [key_gain] * (wk // HD))[None]
    qgain_pair = jnp.concatenate([query_gain] * 2)[None]
    kgain_pair = jnp.concatenate([key_gain] * 2)[None]

    x_own, cos, sin, start_col, start_row, live_col, live_row = step(
        x_own, cos, sin, start_col, start_row, live_col, live_row
    )
    qkv_hop, out_z, mine_gate_up, mine_down, late_dy = after([qkv_hop, out_z, mine_gate_up, mine_down, cotangent], x_own)
    x_over, x_near = permute(x_own, n, flip_z), permute(x_own, n, flip_core)
    two_out = jnp.stack([mine_out, out_z])
    out_far = permute(two_out, n, flip_far)
    qkv_around = around(qkv_hop, n)
    gate_up_hop = permute(mine_gate_up, n, flip_far)
    x_over, x_near, out_far, late_dy, *qkv_around = step(x_over, x_near, out_far, late_dy, *qkv_around)
    x_far = permute(x_over, n, flip_core)
    qkv_mine = [qkv_hop] + qkv_around
    qkv_other = across(qkv_mine, n)
    out_all = lax.all_gather(jnp.concatenate([two_out, out_far]), "dp", axis_index_groups=neighbours(n))
    x_blocks = [x_own, x_over, x_near, x_far]

    rows_one, pre, qk, values, w_qkv = qkv_call(
        s, x_blocks, (w_query, w_key, w_value), qkv_mine + qkv_other, norm1_gain[None], gains, cos, sin
    )
    attended, attended_f, lse = attend_call(s, qk, values, start_col, live_row)

    att_over, att_near = permute(attended, n, flip_z), permute(attended, n, flip_core)
    gate_up_hop = after(gate_up_hop, attended)
    gate_up_around = around(gate_up_hop, n)
    mine_down, late_dy = after([mine_down, late_dy], gate_up_hop)
    dy_own = permute(late_dy, n, settle)
    down_hop = permute(mine_down, n, flip_far)
    att_over, att_near, dy_own, *gate_up_around = step(att_over, att_near, dy_own, *gate_up_around)
    att_far = permute(att_over, n, flip_core)
    dy_over, dy_near = permute(dy_own, n, flip_z), permute(dy_own, n, flip_core)
    down_hop = after(down_hop, att_far)
    gate_up_mine = [gate_up_hop] + gate_up_around
    gate_up_parts = gate_up_mine + across(gate_up_mine, n)
    down_around = around(down_hop, n)
    rows_two, hidden, by_gate, by_up, residual, w_out_own = ffn_call(
        s, x_blocks, [attended, att_over, att_near, att_far], out_all, w_gate, w_up, gate_up_parts,
        after(norm2_gain[None], dy_own),
    )
    hidden, dy_over, dy_near, *down_around = step(hidden, dy_over, dy_near, *down_around)
    down_mine = [down_hop] + down_around
    dy_far, *down_across = step(permute(dy_over, n, flip_core), *across(down_mine, n))
    down_parts = down_mine + down_across
    dy_blocks = [dy_own, dy_over, dy_near, dy_far]

    down = grad_cols_call(s, hidden, dy_blocks, "grad_down")
    down_got = first_sums(down, n)
    gate_grad, up_grad, low2, high2 = ffn_back_call(
        s, dy_blocks, w_down, down_parts, w_gate, w_up, gate_up_parts, after(by_gate, *down), by_up
    )
    low2, high2, *down_got = step(low2, high2, *down_got)
    (high_got,) = step(permute(high2, n, flip_core))
    low_half = low2 + high_got
    low_over = permute(low_half[b:], n, flip_z)
    gate_up = grad_rows_call(s, rows_two, after(gate_grad, low_half), up_grad, "grad_gate_up")
    gate_up_got = first_sums(gate_up, n)
    down = first_add(down, after(down_got, *gate_up))
    down_got = second_sums(down, n)
    grad_n2 = (low_half[:b] + after(low_over, *down)).astype(f32)
    inv = lax.rsqrt(jnp.mean(residual * residual, axis=-1, keepdims=True) + epsilon)
    scaled = norm2_gain * grad_n2
    grad_residual = (
        dy_own.astype(f32)
        + inv * scaled
        - residual * (inv * inv * inv) * jnp.mean(scaled * residual, axis=-1, keepdims=True)
    )
    grad_norm2 = jnp.sum(grad_n2 * residual * inv, axis=0)
    gb_own = grad_residual.astype(bf16)
    gb_over, gb_near = permute(gb_own, n, flip_z), permute(gb_own, n, flip_core)
    ffn_low, ffn_high = ffn_out_call(s, w_down, down_parts, after(hidden, gb_own))
    ffn_got = permute(ffn_high, n, flip_core)
    gb_over, gb_near = step(*after([gb_over, gb_near], ffn_low))
    ffn_got = after(ffn_got, gb_over)
    gb_far = permute(gb_over, n, flip_core)
    gate_up = first_add(gate_up, after(gate_up_got, gb_over))
    gate_up_got = second_sums(gate_up, n)
    down = second_add(down, after(down_got, gb_over, *gate_up), n)
    ffn_half = ffn_low + ffn_got
    gb_far, down_got = step(gb_far, permute(cross_sent(down, c), n, flip_core))
    down_kept, down_sent = cross_got(down, down_got, c)
    down_got = permute(down_sent, n, flip_far)
    ffn_over = permute(ffn_half[b:], n, flip_z)
    gb_blocks = [gb_own, gb_over, gb_near, gb_far]

    low, gain_terms, low1, high1 = attend_back_call(
        s, qk, after(values, ffn_half, down_sent), pre, qgain_pair, kgain_pair, cos, sin, start_row, live_col,
        attended_f, lse, w_out_own, w_qkv, gb_blocks,
    )
    low, low1, high1, down_got, ffn_over, *gate_up_got = step(low, low1, high1, down_got, ffn_over, *gate_up_got)
    down_mine = down_kept + down_got
    down_all = whole_grad(down_mine, n)
    gate_up = second_add(gate_up, after(gate_up_got, down_mine), n)
    high_got, gate_up_got = step(permute(high1, n, flip_core), permute(cross_sent(gate_up, c), n, flip_core))
    low_half = low1 + high_got
    low_over = permute(low_half[b:], n, flip_z)
    gate_up_kept, gate_up_sent = cross_got(gate_up, gate_up_got, c)
    gate_up_got = permute(gate_up_sent, n, flip_far)
    att = grad_attention_call(s, rows_one, after(low, low_half, gate_up_sent), attended, gb_blocks)
    att_got = first_sums(att, n)
    block_output = residual + (ffn_half[:b] + after(ffn_over, *att)).astype(f32)
    low_over, gate_up_got, *att_got = step(*after([low_over, gate_up_got, *att_got], block_output))
    gate_up_mine = gate_up_kept + gate_up_got
    gate_up_all = whole_grad(gate_up_mine, n)
    att = first_add(att, after(att_got, gate_up_mine))
    att_got = second_sums(att, n)
    grad_n1 = (low_half[:b] + after(low_over, *att)).astype(f32)
    x_f = x_own.astype(f32)
    inv = lax.rsqrt(jnp.mean(x_f * x_f, axis=-1, keepdims=True) + epsilon)
    scaled = norm1_gain * grad_n1
    input_grad = (
        grad_residual
        + inv * scaled
        - x_f * (inv * inv * inv) * jnp.mean(scaled * x_f, axis=-1, keepdims=True)
    )
    grad_norm1 = jnp.sum(grad_n1 * x_f * inv, axis=0)
    head_terms = gain_terms[:, :HD] + gain_terms[:, HD:]
    vec = jnp.concatenate([grad_norm1, grad_norm2, head_terms[0] + head_terms[1], head_terms[2]])[None]
    moves = vector_moves(n)
    att = second_add(att, after(att_got, input_grad, vec), n)
    (att_got,) = step(permute(cross_sent(att, c), n, flip_core))
    att_kept, att_sent = cross_got(att, att_got, c)
    att_got = permute(att_sent, n, flip_far)
    vec_got = permute(after(vec, att_sent), n, moves[0])
    late_output, late_grad = after([block_output, input_grad], att_sent)
    settled_output = permute(late_output.astype(bf16), n, settle)
    settled_grad = permute(late_grad.astype(bf16), n, settle)
    (grad_down,) = widen_call(after(down_all, att_sent), True, "widen_down")
    att_got, vec_got = step(*after([att_got, vec_got], grad_down))
    att_mine = att_kept + att_got
    att_around = around(att_mine, n)
    vec = vec + vec_got
    vec_got = permute(vec, n, moves[1])
    settled_output, settled_grad, vec_got = after([settled_output, settled_grad, vec_got], att_mine)
    block_output = jnp.where(home, block_output, settled_output.astype(f32))
    input_grad = jnp.where(home, input_grad, settled_grad.astype(f32))
    vec = vec + vec_got
    vec_got = permute(vec, n, moves[2])
    att_around, vec_got = after([att_around, vec_got], block_output, input_grad)
    att_across = across([att_mine] + att_around, n)
    vec = vec + vec_got
    vec_got = permute(vec, n, moves[3])
    grad_query, grad_key, grad_value, grad_out = place_call(
        s,
        [att_mine] + att_around + after(att_across, vec),
        write_attention,
        [(width // 8, wq), (width // 8, wk), (width // 8, wk), (w_out.shape[0] // 8, width)],
        "place_attention",
    )
    vec = vec + after(vec_got, grad_query)
    vec_got = permute(vec, n, moves[4])
    grad_gate, grad_up = widen_call(after(gate_up_all, vec), False, "widen_gate_up")
    vec = vec + after(vec_got, grad_gate)
    for move in moves[5:]:
        vec = vec + permute(vec, n, move)
    vec = vec[0]
    return (
        block_output,
        input_grad,
        vec[:width],
        grad_query,
        grad_key,
        grad_value,
        vec[2 * width : 2 * width + HD],
        vec[2 * width + HD :],
        grad_out,
        vec[width : 2 * width],
        grad_gate,
        grad_up,
        grad_down,
    )


def solution(mesh):
    placed = (
        P(("dp", "tensor"), None),
        P("dp", None),
        P("dp", None),
        P(),
        P(None, "tensor"),
        P(None, "tensor"),
        P(None, "tensor"),
        P(),
        P(),
        P("tensor", None),
        P(),
        P(None, "tensor"),
        P(None, "tensor"),
        P("tensor", None),
        P(("dp", "tensor"), None),
    )
    return jax.shard_map(
        local,
        mesh=mesh,
        in_specs=placed,
        out_specs=(
            P(("dp", "tensor"), None),
            P(("dp", "tensor"), None),
            P(),
            P(None, "tensor"),
            P(None, "tensor"),
            P(None, "tensor"),
            P(),
            P(),
            P("tensor", None),
            P(),
            P(None, "tensor"),
            P(None, "tensor"),
            P("tensor", None),
        ),
        check_vma=False,
    )
```

```python
import functools
import math

import jax
import jax.numpy as jnp
from jax import lax
from jax.experimental import pallas as pl
from jax.experimental.pallas import tpu as pltpu
from jax.sharding import PartitionSpec as P

HD = 64
AX = ("dp", "tensor")
T4 = 4
VMEM_MB = 1 << 20

epsilon = 1e-05
rope_base = 1000000.0
NEG = -1000000000.0
bf16 = jnp.bfloat16
f32 = jnp.float32


def doc_tables(lengths_row, positions, head_dim):
    doc_ends = jnp.cumsum(lengths_row)
    passed = positions[:, None] >= doc_ends[None, :]
    doc_starts = jnp.sum(jnp.where(passed, lengths_row[None, :], 0), axis=1)
    offsets = (positions - doc_starts).astype(f32)
    freqs = jnp.exp(
        jnp.arange(head_dim // 2, dtype=f32) * (-2.0 * math.log(rope_base) / head_dim)
    )
    angles = offsets[:, None] * freqs[None, :]
    return (doc_starts, jnp.cos(angles), jnp.sin(angles))


def contract(a, b, da, db):
    return lax.dot_general(a, b, (((da,), (db,)), ((), ())), preferred_element_type=f32)


def swap_halves(y):
    width = y.shape[1]
    lane = lax.broadcasted_iota(jnp.int32, y.shape, 1)
    return jnp.where(lane % HD < HD // 2, pltpu.roll(y, width - HD // 2, 1), pltpu.roll(y, HD // 2, 1))


def split_dot(left, right, da, db):
    high = left.astype(bf16)
    low = (left - high.astype(f32)).astype(bf16)
    return contract(high, right, da, db) + contract(low, right, da, db)


def head_mean(y):
    at = lax.broadcasted_iota(jnp.int32, (128, 128), 0) // HD
    to = lax.broadcasted_iota(jnp.int32, (128, 128), 1) // HD
    ones = jnp.where(at == to, 1.0 / HD, 0.0).astype(bf16)
    sides = [split_dot(y[:, k : k + 128], ones, 1, 0) for k in range(0, y.shape[1], 128)]
    return sides[0] if len(sides) == 1 else jnp.concatenate(sides, 1)


class Weight:
    def __init__(self, s_ref, own, parts, to, sems, start=0):
        self.core, self.e = s_ref[1], s_ref[2]
        self.own, self.parts, self.to, self.sems, self.start_col = own, parts, to, sems, start

    def copies(self):
        start = 0
        for i, w in enumerate(self.own):
            wide = w.shape[1]
            to = self.to if len(self.own) == 1 else self.to.at[:, pl.ds(start, wide)]
            yield 0, functools.partial(pltpu.make_async_copy, w, to, self.sems.at[8 + i])
            start += wide
        rows = self.to.shape[0] // 8
        for j in range(4):
            for other in range(2):
                at = pl.multiple_of((2 * (self.e ^ j) + 1 - other) * rows, rows)
                src = self.parts[4 * other + j]
                if src.shape[1] != self.to.shape[1]:
                    src = src.at[:, pl.ds(self.start_col, self.to.shape[1])]
                to = self.to.at[pl.ds(at, rows), :]
                yield 1, functools.partial(pltpu.make_async_copy, src, to, self.sems.at[2 * j + other])

    def each(self, act):
        for core in range(2):

            @pl.when(self.core == core)
            def _():
                for whose, copy in self.copies():
                    if whose == core:
                        act(copy())

    def start(self):
        self.each(lambda copy: copy.start())

    def wait(self):
        self.each(lambda copy: copy.wait())


ANY = pl.BlockSpec(memory_space=pl.ANY)


def fixed(*shape):
    return pl.BlockSpec(shape, lambda *_: (0,) * len(shape))


def cost(flops):
    return pl.CostEstimate(flops=flops, bytes_accessed=1 << 16, transcendentals=0)


def params(mib):
    return pltpu.CompilerParams(vmem_limit_bytes=mib * VMEM_MB)


def qkv_kernel(s_ref, *refs):
    pieces, own, parts, refs = refs[:4], refs[4:7], refs[7:15], refs[15:]
    g1_ref, gains_ref, cos_ref, sin_ref, n1_ref, pre_ref, qk_ref, v_ref, w_ref, xs, xsem, wsem = refs
    j = pl.program_id(0)
    weight = Weight(s_ref, own, parts, w_ref, wsem)

    @pl.when(j == 0)
    def _():
        for k in range(4):
            pltpu.make_async_copy(pieces[k], xs.at[k], xsem.at[k]).start()
        weight.start()

    pltpu.make_async_copy(pieces[0], xs.at[j], xsem.at[j]).wait()
    x = xs[j].astype(f32)
    inv = lax.rsqrt(jnp.mean(x * x, axis=-1, keepdims=True) + epsilon)
    n1 = (x * inv * g1_ref[...]).astype(bf16)
    n1_ref[...] = n1

    @pl.when(j == 0)
    def _():
        weight.wait()

    qkv = jnp.dot(n1, w_ref[...], preferred_element_type=f32)
    width = pre_ref.shape[1]
    pre = qkv[:, :width]
    pre_ref[...] = pre
    v_ref[...] = qkv[:, width:].astype(bf16)
    y = pre * lax.rsqrt(head_mean(pre * pre) + epsilon) * gains_ref[...]
    cos = jnp.concatenate([cos_ref[...]] * (width // 128), 1)
    sin = jnp.concatenate([sin_ref[...]] * (width // 128), 1)
    qk = (y * cos + swap_halves(y) * sin).astype(bf16)
    lane = lax.broadcasted_iota(jnp.int32, qk.shape, 1)
    qk_ref[...] = jnp.where(lane < width - 128, qk * 0.125, qk).astype(bf16)


def qkv_call(s, xs, w_own, w_parts, g1, gains, cos, sin):
    b, d = xs[0].shape
    wid = w_parts[0].shape[1]
    qkw = wid - 128
    natural = lambda j, s: (s[0] ^ j, 0)
    return pl.pallas_call(
        qkv_kernel,
        grid_spec=pltpu.PrefetchScalarGridSpec(
            num_scalar_prefetch=1,
            grid=(4,),
            in_specs=[ANY] * 15
            + [fixed(1, d), fixed(1, qkw), pl.BlockSpec((b, 128), natural), pl.BlockSpec((b, 128), natural)],
            out_specs=[
                pl.BlockSpec((b, d), lambda j, s: (j, 0)),
                pl.BlockSpec((b, qkw), natural),
                pl.BlockSpec((b, qkw), natural),
                pl.BlockSpec((b, 128), natural),
                fixed(d, wid),
            ],
            scratch_shapes=[
                pltpu.VMEM((4, b, d), bf16),
                pltpu.SemaphoreType.DMA((4,)),
                pltpu.SemaphoreType.DMA((11,)),
            ],
        ),
        out_shape=[
            jax.ShapeDtypeStruct((4 * b, d), bf16),
            jax.ShapeDtypeStruct((4 * b, qkw), f32),
            jax.ShapeDtypeStruct((4 * b, qkw), bf16),
            jax.ShapeDtypeStruct((4 * b, 128), bf16),
            jax.ShapeDtypeStruct((d, wid), bf16),
        ],
        compiler_params=params(58),
        cost_estimate=cost(1 << 24),
        name="qkv",
    )(s, *xs, *w_own, *w_parts, g1, gains, cos, sin)


def both_heads(pair):
    lane = lax.broadcasted_iota(jnp.int32, pair.shape, 1)
    zero = jnp.zeros_like(pair)
    return jnp.concatenate([jnp.where(lane < HD, pair, zero), jnp.where(lane < HD, zero, pair)], 0)


def pick_heads(both):
    r = both.shape[0] // 2
    lane = lax.broadcasted_iota(jnp.int32, (r, 128), 1)
    return jnp.where(lane < HD, both[:r], both[r:])


def twice(kv, g):
    lane = lax.broadcasted_iota(jnp.int32, kv.shape, 1)
    turned = pltpu.roll(kv.astype(f32), HD, 1).astype(kv.dtype)
    return jnp.where((lane < HD) == (g == 0), kv, turned)


def attend_kernel(s_ref, q_ref, k_ref, v_ref, start_ref, live_ref, att_ref, out_ref, lse_ref, bias):
    g = pl.program_id(0)
    n = k_ref.shape[0]
    b = n // 4

    @pl.when(g == 0)
    def _():
        for a in range(4):
            keys = (a + 1) * b
            start = start_ref[a * b : (a + 1) * b, :1]
            q_at = lax.broadcasted_iota(jnp.int32, (b, keys), 0) + a * b
            k_at = lax.broadcasted_iota(jnp.int32, (b, keys), 1)
            allowed = ((live_ref[:1, :keys] >= start) & (k_at <= q_at)) | (k_at == q_at)
            bias[a * b : (a + 1) * b, :keys] = jnp.where(allowed, 0.0, NEG)

    kd = twice(k_ref[...], g)
    vd = twice(v_ref[...], g)
    for a in range(4):
        keys = (a + 1) * b
        rows = slice(a * b, (a + 1) * b)
        qm = both_heads(q_ref[rows, :])
        scores = contract(qm, kd[:keys], 1, 1)
        extra = bias[rows, :keys]
        expo = jnp.exp(scores + jnp.concatenate([extra, extra], 0))
        total = jnp.sum(expo, axis=-1, keepdims=True)
        pair = pick_heads(contract(expo.astype(bf16), vd[:keys], 1, 0) / total)
        out_ref[rows, :] = pair
        att_ref[pl.ds(pl.multiple_of((s_ref[0] ^ a) * b, b), b), :] = pair.astype(bf16)
        lse_ref[0, a] = jnp.transpose(jnp.broadcast_to(jnp.log(total), (2 * b, 128)))[:1]


def attend_call(s, qk, v, start, live):
    n = qk.shape[0]
    b = n // 4
    lanes = lambda g, s: (0, g)
    return pl.pallas_call(
        attend_kernel,
        grid_spec=pltpu.PrefetchScalarGridSpec(
            num_scalar_prefetch=1,
            grid=(2,),
            in_specs=[
                pl.BlockSpec((n, 128), lanes),
                pl.BlockSpec((n, 128), lambda g, s: (0, 2)),
                fixed(n, 128),
                fixed(n, 128),
                fixed(8, n),
            ],
            out_specs=[
                pl.BlockSpec((n, 128), lanes),
                pl.BlockSpec((n, 128), lanes),
                pl.BlockSpec((1, 4, 1, 2 * b), lambda g, s: (g, 0, 0, 0)),
            ],
            scratch_shapes=[pltpu.VMEM((n, n), f32)],
        ),
        out_shape=[
            jax.ShapeDtypeStruct((n, 256), bf16),
            jax.ShapeDtypeStruct((n, 256), f32),
            jax.ShapeDtypeStruct((2, 4, 1, 2 * b), f32),
        ],
        compiler_params=params(14),
        cost_estimate=cost(1 << 24),
        name="attend",
    )(s, qk, qk, v, start, live)


def norm_back(grad, pre, gain, cos, sin):
    turned = grad * cos - swap_halves(grad) * sin
    inv = lax.rsqrt(head_mean(pre * pre) + epsilon)
    scaled = turned * gain
    dpre = inv * scaled - pre * (inv * inv * inv) * head_mean(scaled * pre)
    return dpre, jnp.sum(turned * pre * inv, axis=0, keepdims=True)


def attend_back_kernel(s_ref, q_ref, k_ref, v_ref, qpre_ref, kpre_ref, gains_ref, kgain_ref, cos_ref, sin_ref,
                       start_ref, live_ref, out_ref, lse_ref, wout_ref, w_ref, b0, b1, b2, b3,
                       low_ref, gain_ref, lo_ref, hi_ref, bias, dk, dv, dkall, dvall, dos, gb, sems):
    g = pl.program_id(0)
    n = k_ref.shape[0]
    b = n // 4
    pieces = (b0, b1, b2, b3)

    @pl.when(g == 0)
    def _():
        for k in range(4):
            pltpu.make_async_copy(pieces[k], gb.at[k], sems.at[k]).start()
        for a in range(4):
            keys = (a + 1) * b
            start = start_ref[:1, a * b : (a + 1) * b]
            k_at = lax.broadcasted_iota(jnp.int32, (keys, b), 0)
            q_at = lax.broadcasted_iota(jnp.int32, (keys, b), 1) + a * b
            allowed = ((live_ref[:keys, :1] >= start) & (k_at <= q_at)) | (k_at == q_at)
            bias[:keys, a * b : (a + 1) * b] = jnp.where(allowed, 0.0, NEG)
        for k in range(4):
            pltpu.make_async_copy(pieces[k], gb.at[k], sems.at[k]).wait()
            dos[k] = contract(gb[k], wout_ref[...], 1, 1).astype(bf16)

    kd = twice(k_ref[...], g)
    vd = twice(v_ref[...], g)
    gain_sum = jnp.zeros((1, 128), f32)
    ones = jnp.ones((16, 128), bf16)
    for a in (3, 2, 1, 0):
        keys = (a + 1) * b
        rows = slice(a * b, (a + 1) * b)
        home = s_ref[0] ^ a
        qm = both_heads(q_ref[rows, :])
        dout = jnp.where(g == 0, dos[home, :, :128], dos[home, :, 128:])
        dom = both_heads(dout)
        terms = both_heads(dout.astype(f32) * out_ref[rows, :])
        terms_high = terms.astype(bf16)
        terms_low = (terms - terms_high.astype(f32)).astype(bf16)
        delta = (contract(ones, terms_high, 1, 1) + contract(ones, terms_low, 1, 1))[:1]
        scores = contract(kd[:keys], qm, 1, 1)
        extra = bias[:keys, rows]
        probs = jnp.exp(scores + (jnp.concatenate([extra, extra], 1) - lse_ref[0, a]))
        dprobs = contract(vd[:keys], dom, 1, 1)
        dscores = (probs * (dprobs - delta)).astype(bf16)
        dv_add = contract(probs.astype(bf16), dom, 1, 0)
        dk_add = contract(dscores, qm, 1, 0)
        if a == 3:
            dv[...] = dv_add
            dk[...] = dk_add
        else:
            dv[:keys] += dv_add
            dk[:keys] += dk_add
        dq = pick_heads(contract(dscores, kd[:keys], 0, 0)) * 0.125
        dpre, gain_part = norm_back(dq, qpre_ref[rows, :], gains_ref[...], cos_ref[rows, :], sin_ref[rows, :])
        at = pl.ds(pl.multiple_of(home * b, b), b)
        low_ref[at, pl.ds(pl.multiple_of(g * 128, 128), 128)] = dpre.astype(bf16)
        gain_sum = gain_sum + gain_part
    gain_ref[pl.ds(g, 1), :] = gain_sum
    lane = lax.broadcasted_iota(jnp.int32, (n, 128), 1)
    dk_all = dk[...] + pltpu.roll(dk[...], HD, 1)
    dv_all = dv[...] + pltpu.roll(dv[...], HD, 1)

    @pl.when(g == 0)
    def _():
        dkall[...] = dk_all
        dvall[...] = dv_all

    @pl.when(g == 1)
    def _():
        grad_k = jnp.where(lane < HD, dkall[...], dk_all)
        grad_v = jnp.where(lane < HD, dvall[...], dv_all)
        dpre, gain_part = norm_back(grad_k, kpre_ref[...], kgain_ref[...], cos_ref[...], sin_ref[...])
        gain_ref[2:3, :] = gain_part
        for a in range(4):
            at = pl.ds(pl.multiple_of((s_ref[0] ^ a) * b, b), b)
            low_ref[at, 256:384] = dpre[a * b : (a + 1) * b].astype(bf16)
            low_ref[at, 384:512] = grad_v[a * b : (a + 1) * b].astype(bf16)
        hi_ref[...] = contract(low_ref[2 * b :, :], w_ref[...], 1, 1).astype(bf16)
        lo_ref[...] = contract(low_ref[: 2 * b, :], w_ref[...], 1, 1).astype(bf16)


def attend_back_call(s, qk, v, pre, qgain, kgain, cos, sin, start, live, out, lse, wout, w, blocks):
    n = v.shape[0]
    b = n // 4
    d = blocks[0].shape[1]
    lanes = pl.BlockSpec((n, 128), lambda g, s: (0, g))
    third = pl.BlockSpec((n, 128), lambda g, s: (0, 2))
    return pl.pallas_call(
        attend_back_kernel,
        grid_spec=pltpu.PrefetchScalarGridSpec(
            num_scalar_prefetch=1,
            grid=(2,),
            in_specs=[lanes, third, fixed(n, 128), lanes, third, fixed(1, 128), fixed(1, 128), fixed(n, 128),
                      fixed(n, 128), fixed(8, n), fixed(n, 128), lanes,
                      pl.BlockSpec((1, 4, 1, 2 * b), lambda g, s: (g, 0, 0, 0)),
                      fixed(256, d), fixed(d, 512)] + [ANY] * 4,
            out_specs=[fixed(n, 512), fixed(8, 128), fixed(2 * b, d), fixed(2 * b, d)],
            scratch_shapes=[pltpu.VMEM((n, n), f32)]
            + [pltpu.VMEM((n, 128), f32)] * 4
            + [pltpu.VMEM((4, b, 256), bf16), pltpu.VMEM((4, b, d), bf16), pltpu.SemaphoreType.DMA((4,))],
        ),
        out_shape=[
            jax.ShapeDtypeStruct((n, 512), bf16),
            jax.ShapeDtypeStruct((8, 128), f32),
            jax.ShapeDtypeStruct((2 * b, d), bf16),
            jax.ShapeDtypeStruct((2 * b, d), bf16),
        ],
        compiler_params=params(24),
        cost_estimate=cost(1 << 24),
        name="attend_back",
    )(s, qk, qk, v, pre, pre, qgain, kgain, cos, sin, start, live, out, lse, wout, w, *blocks)


def ffn_kernel(s_ref, *refs):
    x_in, a_in, o_in, refs = refs[:4], refs[4:8], refs[8], refs[9:]
    wg_own, wu_own, parts, refs = refs[0], refs[1], refs[2:10], refs[10:]
    gain_ref, n2_ref, hid_ref, fg_ref, fu_ref, res_ref, wout_ref, refs = *refs[:7], refs[7:]
    wg, wu, xs, att, wout, asem, xsem, osem, gsem, usem = refs
    j = pl.program_id(0)
    b = xs.shape[1]
    gate_w = Weight(s_ref, (wg_own,), parts, wg, gsem)
    up_w = Weight(s_ref, (wu_own,), parts, wu, usem, wg.shape[1])

    def out_copy(i):
        return pltpu.make_async_copy(o_in.at[:, i ^ (2 * s_ref[1])], wout.at[i], osem.at[i])

    def att_copy(k, i):
        return pltpu.make_async_copy(
            a_in[i].at[pl.ds((k ^ i) * b, b), :], att.at[k, :, pl.ds(i * b, b)], asem.at[k, i]
        )

    @pl.when(j == 0)
    def _():
        for k in range(4):
            pltpu.make_async_copy(x_in[k], xs.at[k], xsem.at[k]).start()
            for i in range(4):
                att_copy(k, i).start()
            if k == 0:
                for i in range(4):
                    out_copy(i).start()
                gate_w.start()
        up_w.start()
        for i in range(4):
            out_copy(i).wait()

    pltpu.make_async_copy(x_in[0], xs.at[j], xsem.at[j]).wait()
    for i in range(4):
        pltpu.make_async_copy(a_in[i].at[pl.ds(0, b), :], att.at[j, :, pl.ds(i * b, b)], asem.at[j, i]).wait()
    res = xs[j].astype(f32) + jnp.dot(att[j], wout[...].reshape(4 * b, -1), preferred_element_type=f32)

    @pl.when(j == 0)
    def _():
        res_ref[...] = res
        wout_ref[...] = wout[0].reshape(b, -1)
        gate_w.wait()
        up_w.wait()

    inv = lax.rsqrt(jnp.mean(res * res, axis=-1, keepdims=True) + epsilon)
    n2 = (res * inv * gain_ref[...]).astype(bf16)
    n2_ref[...] = n2
    gate = jnp.dot(n2, wg[...], preferred_element_type=f32)
    up = jnp.dot(n2, wu[...], preferred_element_type=f32)
    s = jax.nn.sigmoid(gate)
    silu = gate * s
    hid_ref[...] = (silu * up).astype(bf16)
    fg_ref[...] = (up * (s * (1.0 + gate * (1.0 - s)))).astype(bf16)
    fu_ref[...] = silu.astype(bf16)


def ffn_call(s, xs, atts, wout, wg, wu, parts, gain):
    b, d = xs[0].shape
    h = wg.shape[1]
    block = lambda wid: pl.BlockSpec((b, wid), lambda j, s: (j, 0))
    return pl.pallas_call(
        ffn_kernel,
        grid_spec=pltpu.PrefetchScalarGridSpec(
            num_scalar_prefetch=1,
            grid=(4,),
            in_specs=[ANY] * 19 + [fixed(1, d)],
            out_specs=[block(d), block(h), block(h), block(h), fixed(b, d), fixed(b, d)],
            scratch_shapes=[
                pltpu.VMEM((d, h), bf16),
                pltpu.VMEM((d, h), bf16),
                pltpu.VMEM((4, b, d), bf16),
                pltpu.VMEM((4, b, 4 * b), bf16),
                pltpu.VMEM((4,) + wout.shape[:1] + wout.shape[2:], bf16),
                pltpu.SemaphoreType.DMA((4, 4)),
                pltpu.SemaphoreType.DMA((4,)),
                pltpu.SemaphoreType.DMA((4,)),
                pltpu.SemaphoreType.DMA((9,)),
                pltpu.SemaphoreType.DMA((9,)),
            ],
        ),
        out_shape=[jax.ShapeDtypeStruct((4 * b, d), bf16)]
        + [jax.ShapeDtypeStruct((4 * b, h), bf16)] * 3
        + [jax.ShapeDtypeStruct((b, d), f32), jax.ShapeDtypeStruct((b, d), bf16)],
        compiler_params=params(58),
        cost_estimate=cost(1 << 24),
        name="ffn",
    )(s, *xs, *atts, wout, wg, wu, *parts, gain)


def ffn_back_kernel(s_ref, *refs):
    y_in, wd_own, wd_parts, refs = refs[:4], refs[4], refs[5:13], refs[13:]
    wg_own, wu_own, parts, refs = refs[0], refs[1], refs[2:10], refs[10:]
    fg_ref, fu_ref, gg_ref, gu_ref, lo_ref, hi_ref, wd, wg, wu, dy, ysem, dsem, gsem, usem = refs
    j = pl.program_id(0)
    down_w = Weight(s_ref, (wd_own,), wd_parts, wd, dsem)
    gate_w = Weight(s_ref, (wg_own,), parts, wg, gsem)
    up_w = Weight(s_ref, (wu_own,), parts, wu, usem, wg.shape[1])

    @pl.when(j == 0)
    def _():
        pltpu.make_async_copy(y_in[0], dy.at[0], ysem.at[0]).start()
        down_w.start()
        for k in range(1, 4):
            pltpu.make_async_copy(y_in[k], dy.at[k], ysem.at[k]).start()
        gate_w.start()
        up_w.start()
        down_w.wait()

    pltpu.make_async_copy(y_in[0], dy.at[j], ysem.at[j]).wait()
    gh = contract(dy[j], wd[...], 1, 1)
    gg = (gh * fg_ref[...].astype(f32)).astype(bf16)
    gu = (gh * fu_ref[...].astype(f32)).astype(bf16)
    gg_ref[...] = gg
    gu_ref[...] = gu

    @pl.when(j == 0)
    def _():
        gate_w.wait()
        up_w.wait()

    grad = (contract(gg, wg[...], 1, 1) + contract(gu, wu[...], 1, 1)).astype(bf16)

    @pl.when(j < 2)
    def _():
        lo_ref[...] = grad

    @pl.when(j >= 2)
    def _():
        hi_ref[...] = grad


def ffn_back_call(s, dys, wd, d_parts, wg, wu, parts, fg, fu):
    b, d = dys[0].shape
    h = wg.shape[1]
    block = lambda wid: pl.BlockSpec((b, wid), lambda j, s: (j, 0))
    return pl.pallas_call(
        ffn_back_kernel,
        grid_spec=pltpu.PrefetchScalarGridSpec(
            num_scalar_prefetch=1,
            grid=(4,),
            in_specs=[ANY] * 23 + [block(h), block(h)],
            out_specs=[
                block(h),
                block(h),
                pl.BlockSpec((b, d), lambda j, s: (jnp.minimum(j, 1), 0)),
                pl.BlockSpec((b, d), lambda j, s: (jnp.maximum(j - 2, 0), 0)),
            ],
            scratch_shapes=[
                pltpu.VMEM((h, d), bf16),
                pltpu.VMEM((d, h), bf16),
                pltpu.VMEM((d, h), bf16),
                pltpu.VMEM((4, b, d), bf16),
                pltpu.SemaphoreType.DMA((4,)),
                pltpu.SemaphoreType.DMA((9,)),
                pltpu.SemaphoreType.DMA((9,)),
                pltpu.SemaphoreType.DMA((9,)),
            ],
        ),
        out_shape=[jax.ShapeDtypeStruct((4 * b, h), bf16)] * 2 + [jax.ShapeDtypeStruct((2 * b, d), bf16)] * 2,
        compiler_params=params(58),
        cost_estimate=cost(1 << 24),
        name="ffn_back",
    )(s, *dys, wd, *d_parts, wg, wu, *parts, fg, fu)


def ffn_out_kernel(s_ref, wd_own, *refs):
    wd_parts, (hid_ref, lo_ref, hi_ref, wd, dsem) = refs[:8], refs[8:]
    j = pl.program_id(0)
    down_w = Weight(s_ref, (wd_own,), wd_parts, wd, dsem)

    @pl.when(j == 0)
    def _():
        down_w.start()
        down_w.wait()

    part = jnp.dot(hid_ref[...], wd[...], preferred_element_type=f32).astype(bf16)

    @pl.when(j < 2)
    def _():
        lo_ref[...] = part

    @pl.when(j >= 2)
    def _():
        hi_ref[...] = part


def ffn_out_call(s, wd, d_parts, hidden):
    n, h = hidden.shape
    b, d = n // 4, wd.shape[1]
    return pl.pallas_call(
        ffn_out_kernel,
        grid_spec=pltpu.PrefetchScalarGridSpec(
            num_scalar_prefetch=1,
            grid=(4,),
            in_specs=[ANY] * 9 + [pl.BlockSpec((b, h), lambda j, s: (j, 0))],
            out_specs=[
                pl.BlockSpec((b, d), lambda j, s: (jnp.minimum(j, 1), 0)),
                pl.BlockSpec((b, d), lambda j, s: (jnp.maximum(j - 2, 0), 0)),
            ],
            scratch_shapes=[pltpu.VMEM((h, d), bf16), pltpu.SemaphoreType.DMA((9,))],
        ),
        out_shape=[jax.ShapeDtypeStruct((2 * b, d), bf16)] * 2,
        compiler_params=params(58),
        cost_estimate=cost(1 << 24),
        name="ffn_out",
    )(s, wd, *d_parts, hidden)


def grad_rows_kernel(s_ref, left_ref, a_ref, b_ref, sent_a, keep_a, sent_b, keep_b):
    j = pl.program_id(0)
    left = left_ref[...]
    first = contract(left, a_ref[...], 0, 0).astype(bf16)
    second = contract(left, b_ref[...], 0, 0).astype(bf16)

    @pl.when(j % 2 == 1)
    def _():
        sent_a[0] = first

    @pl.when(j % 2 == 0)
    def _():
        keep_a[0] = first

    @pl.when(j >= 2)
    def _():
        sent_b[0] = second

    @pl.when(j < 2)
    def _():
        keep_b[0] = second


def grad_rows_call(s, left, a, b, name):
    n, rows = left.shape
    cols = a.shape[1]
    maps = [
        lambda j, s: (j // 2, 0, 0),
        lambda j, s: (j // 2, 0, 0),
        lambda j, s: (jnp.maximum(j - 2, 0), 0, 0),
        lambda j, s: (jnp.minimum(j, 1), 0, 0),
    ]
    return pl.pallas_call(
        grad_rows_kernel,
        grid_spec=pltpu.PrefetchScalarGridSpec(
            num_scalar_prefetch=1,
            grid=(4,),
            in_specs=[pl.BlockSpec((n, rows // 4), lambda j, s: (0, s[2] ^ j)), fixed(n, cols), fixed(n, cols)],
            out_specs=[pl.BlockSpec((1, rows // 4, cols), m) for m in maps],
        ),
        out_shape=[jax.ShapeDtypeStruct((2, rows // 4, cols), bf16)] * 4,
        compiler_params=params(16),
        cost_estimate=cost(1 << 24),
        name=name,
    )(s, left, a, b)


def grad_cols_kernel(s_ref, left_ref, r0, r1, r2, r3, sent_a, keep_a, sent_b, keep_b, right, sems):
    k = pl.program_id(0)
    b = r0.shape[0]
    cols = left_ref.shape[0] // 4

    def copy(k, i):
        src = (r0, r1, r2, r3)[i].at[:, pl.ds(pl.multiple_of(k * cols, cols), cols)]
        return pltpu.make_async_copy(src, right.at[k, pl.ds(i * b, b), :], sems.at[k, i])

    @pl.when(k == 0)
    def _():
        for block in range(4):
            for i in range(4):
                copy(block, i).start()

    for i in range(4):
        copy(k, i).wait()
    grad = contract(left_ref[...], right[k], 0, 0)
    grad = grad.astype(bf16)
    rows = grad.shape[0] // 4
    for a in range(4):
        piece = grad[a * rows : (a + 1) * rows]
        j = s_ref[2] ^ a

        @pl.when((k < 2) & (j % 2 == 1))
        def _():
            sent_a[j // 2] = piece

        @pl.when((k < 2) & (j % 2 == 0))
        def _():
            keep_a[j // 2] = piece

        @pl.when((k >= 2) & (j >= 2))
        def _():
            sent_b[j % 2] = piece

        @pl.when((k >= 2) & (j < 2))
        def _():
            keep_b[j % 2] = piece


def grad_cols_call(s, left, rights, name):
    n, rows = left.shape
    b, cols = rights[0].shape
    first = pl.BlockSpec((2, rows // 4, cols // 4), lambda k, s: (0, 0, jnp.minimum(k, 1)))
    second = pl.BlockSpec((2, rows // 4, cols // 4), lambda k, s: (0, 0, jnp.maximum(k - 2, 0)))
    return pl.pallas_call(
        grad_cols_kernel,
        grid_spec=pltpu.PrefetchScalarGridSpec(
            num_scalar_prefetch=1,
            grid=(4,),
            in_specs=[fixed(n, rows)] + [ANY] * 4,
            out_specs=[first, first, second, second],
            scratch_shapes=[pltpu.VMEM((4, n, cols // 4), bf16), pltpu.SemaphoreType.DMA((4, 4))],
        ),
        out_shape=[jax.ShapeDtypeStruct((2, rows // 4, cols // 2), bf16)] * 4,
        compiler_params=params(14),
        cost_estimate=cost(1 << 24),
        name=name,
    )(s, left, *rights)


def widen_kernel(side, in_ref, *outs):
    first, second = in_ref[0, 0].astype(f32), in_ref[0, 1].astype(f32)
    if side:
        outs[0][...] = jnp.concatenate([first, second], 1)
    else:
        outs[0][...] = first
        outs[1][...] = second


def widen_call(whole, side, name):
    _, _, rows, cols = whole.shape
    block = (rows, 2 * cols) if side else (rows, cols)
    count = 1 if side else 2
    return pl.pallas_call(
        functools.partial(widen_kernel, side),
        grid=(8,),
        in_specs=[pl.BlockSpec((1, 2, rows, cols), lambda j: (j, 0, 0, 0))],
        out_specs=[pl.BlockSpec(block, lambda j: (j, 0))] * count,
        out_shape=[jax.ShapeDtypeStruct((8 * block[0], block[1]), f32)] * count,
        compiler_params=params(12),
        cost_estimate=cost(1 << 20),
        name=name,
    )(whole)


def place_kernel(write, s_ref, *refs):
    k = pl.program_id(0)
    for i in range(8):

        @pl.when(k == i)
        def _():
            write(refs[i], refs[8:])


def write_attention(piece, outs):
    query, key, value, out = outs
    r, s = query.shape[0], out.shape[0]
    query[...] = piece[0, :r].astype(f32)
    key[...] = piece[1, :r, :128].astype(f32)
    value[...] = piece[1, :r, 128:].astype(f32)
    sides = [piece[half, r + at * s : r + (at + 1) * s] for half in range(2) for at in range(2)]
    out[...] = jnp.concatenate(sides, 1).astype(f32)


def place_call(s, pieces, write, blocks, name):
    eighth = lambda k, s: (2 * (s[2] ^ (k % 4)) + (s[1] ^ (k // 4)), 0)
    return pl.pallas_call(
        functools.partial(place_kernel, write),
        grid_spec=pltpu.PrefetchScalarGridSpec(
            num_scalar_prefetch=1,
            grid=(8,),
            in_specs=[fixed(*pieces[0].shape)] * 8,
            out_specs=[pl.BlockSpec(block, eighth) for block in blocks],
        ),
        out_shape=[jax.ShapeDtypeStruct((8 * r, cols), f32) for r, cols in blocks],
        compiler_params=params(12),
        cost_estimate=cost(1 << 20),
        name=name,
    )(s, *pieces)


def grad_attention_kernel(s_ref, n1_ref, low_ref, att_ref, b0, b1, b2, b3, sent_a, keep_a, sent_b, keep_b, whole):
    j = pl.program_id(0)
    b = b0.shape[0]

    @pl.when(j == 0)
    def _():
        total = None
        for i, block in enumerate((b0, b1, b2, b3)):
            part = contract(att_ref[i * b : (i + 1) * b, :], block[...], 0, 0)
            total = part if total is None else total + part
        whole[...] = total.astype(bf16)

    qkv = contract(n1_ref[...], low_ref[...], 0, 0).astype(bf16)
    r = qkv.shape[0] // 2
    s = whole.shape[0] // 8
    k = qkv.shape[1] // 2
    out = whole[pl.ds(pl.multiple_of((s_ref[2] ^ j) * 2 * s, 2 * s), 2 * s), :]

    def joined(at):
        parts = []
        for core in range(2):
            some = out[core * s : (core + 1) * s]
            parts += [
                qkv[core * r : (core + 1) * r, at * k : (at + 1) * k],
                some[:, 2 * at * k : (2 * at + 1) * k],
                some[:, (2 * at + 1) * k : (2 * at + 2) * k],
            ]
        return jnp.concatenate(parts, 0)

    @pl.when(j % 2 == 1)
    def _():
        sent_a[0] = joined(0)

    @pl.when(j % 2 == 0)
    def _():
        keep_a[0] = joined(0)

    @pl.when(j >= 2)
    def _():
        sent_b[0] = joined(1)

    @pl.when(j < 2)
    def _():
        keep_b[0] = joined(1)


def grad_attention_call(s, n1, low, att, blocks):
    n, d = n1.shape
    b = n // 4
    half = (d // 4 + att.shape[1] // 2, 256)
    maps = [
        lambda j, s: (j // 2, 0, 0),
        lambda j, s: (j // 2, 0, 0),
        lambda j, s: (jnp.maximum(j - 2, 0), 0, 0),
        lambda j, s: (jnp.minimum(j, 1), 0, 0),
    ]
    return pl.pallas_call(
        grad_attention_kernel,
        grid_spec=pltpu.PrefetchScalarGridSpec(
            num_scalar_prefetch=1,
            grid=(4,),
            in_specs=[pl.BlockSpec((n, d // 4), lambda j, s: (0, s[2] ^ j)), fixed(n, low.shape[1]), fixed(n, att.shape[1])]
            + [fixed(b, d)] * 4,
            out_specs=[pl.BlockSpec((1,) + half, m) for m in maps],
            scratch_shapes=[pltpu.VMEM((att.shape[1], d), bf16)],
        ),
        out_shape=[jax.ShapeDtypeStruct((2,) + half, bf16)] * 4,
        compiler_params=params(18),
        cost_estimate=cost(1 << 24),
        name="grad_attention",
    )(s, n1, low, att, *blocks)


def permute(x, places, move):
    pairs = []
    for d in range(places):
        for t in range(T4):
            to = move(d, t)
            if to is not None:
                pairs.append((d * T4 + t, to[0] * T4 + to[1]))
    return lax.ppermute(x, AX, pairs)


def after(x, *events):
    return lax.optimization_barrier((x, events))[0]


def flip_core(d, t):
    return (d ^ 1, t)


def flip_z(d, t):
    return (d, t ^ 1)


def flip_far(d, t):
    return (d, t ^ 2)


def flip_e(bit):
    return lambda d, t: (d ^ (2 << bit), t)


def settle(d, t):
    return (d, t) if (d & 1) == (t >> 1) else (d ^ 1, t ^ 2)


def step(*values):
    return lax.optimization_barrier(values)


def eighth(w, c, e):
    rows = w.shape[0] // 8
    return lax.dynamic_slice_in_dim(w, (2 * e + c) * rows, rows, 0)


def around(piece, n):
    return [permute(piece, n, lambda d, t, j=j: (d ^ (2 * j), t)) for j in (1, 2, 3)]


def across(pieces, n):
    return [permute(piece, n, flip_core) for piece in pieces]


def first_sums(pieces, n):
    sent_a, keep_a, sent_b, keep_b = pieces
    got_a = permute(sent_a, n, flip_e(0))
    got_b = permute(sent_b, n, flip_e(1))
    return got_a, got_b


def first_add(pieces, got):
    got_a, got_b = got
    keep_a, keep_b = pieces[1], pieces[3]
    return keep_a[1] + got_a[1], keep_a[0] + got_a[0], keep_b[1] + got_b[1], keep_b[0] + got_b[0]


def second_sums(halves, n):
    return permute(halves[0], n, flip_e(1)), permute(halves[2], n, flip_e(0))


def second_add(halves, got, n):
    total = jnp.stack([halves[1] + got[0], halves[3] + got[1]])
    for extra in range(2, 20):
        if (2 << extra) < n:
            total = total + permute(total, n, flip_e(extra))
    return total


def cross_sent(total, c):
    half = total.shape[1] // 2
    return jnp.where(c == 0, total[:, half:], total[:, :half])


def cross_got(total, got, c):
    half = total.shape[1] // 2
    return jnp.where(c == 0, total[:, :half], got), jnp.where(c == 0, got, total[:, half:])


def neighbours(n):
    return None if n == 8 else [list(range(k, k + 8)) for k in range(0, n, 8)]


def whole_grad(mine, n):
    return lax.all_gather(mine, "dp", axis_index_groups=neighbours(n))


def vector_moves(n):
    bits = [1 << k for k in range(20) if 1 << k < n]
    return [flip_z] + [lambda d, t, bit=bit: (d ^ bit, t) for bit in bits] + [flip_far]


def local(
    block_input,
    doc_lengths,
    pad_mask,
    norm1_gain,
    w_query,
    w_key,
    w_value,
    query_gain,
    key_gain,
    w_out,
    norm2_gain,
    w_gate,
    w_up,
    w_down,
    cotangent,
):
    n = lax.axis_size("dp")
    d, t = lax.axis_index("dp"), lax.axis_index("tensor")
    c, p = d & 1, t >> 1
    e = (d >> 1) & 3
    shard = 2 * c + (t & 1)
    b = block_input.shape[0]
    seq_len = b * T4
    home = c == p
    wq = w_query.shape[1]
    wk = w_key.shape[1]
    width = block_input.shape[1]
    s = jnp.stack([shard, c, e]).astype(jnp.int32)

    marks = jnp.concatenate([doc_lengths, pad_mask], 1)
    mine_out = eighth(w_out, c, e)
    mine_qkv = jnp.concatenate([eighth(w, c, e) for w in (w_query, w_key, w_value)], 1)
    x_own = permute(block_input, n, settle)
    qkv_hop = permute(mine_qkv, n, flip_far)
    out_z = permute(mine_out, n, flip_z)
    marks = jnp.where(home, marks, permute(marks, n, flip_core))
    lengths_row, pad_row = marks[0, : doc_lengths.shape[1]], marks[0, doc_lengths.shape[1] :]
    mine_gate_up = jnp.concatenate([eighth(w, c, e) for w in (w_gate, w_up)], 1)
    mine_down = eighth(w_down, c, e)

    positions = jnp.arange(seq_len, dtype=jnp.int32)
    doc_starts, cos_half, sin_half = doc_tables(lengths_row, positions, HD)
    cos = jnp.concatenate([cos_half] * 4, 1)
    sin = jnp.concatenate([-sin_half, sin_half] * 2, 1)
    live = jnp.where(pad_row == 1, positions, -1)
    start_col = jnp.broadcast_to(doc_starts[:, None], (seq_len, 128))
    start_row = jnp.broadcast_to(doc_starts[None], (8, seq_len))
    live_col = jnp.broadcast_to(live[:, None], (seq_len, 128))
    live_row = jnp.broadcast_to(live[None], (8, seq_len))
    gains = jnp.concatenate([query_gain] * (wq // HD) + [key_gain] * (wk // HD))[None]
    qgain_pair = jnp.concatenate([query_gain] * 2)[None]
    kgain_pair = jnp.concatenate([key_gain] * 2)[None]

    x_own, cos, sin, start_col, start_row, live_col, live_row = step(
        x_own, cos, sin, start_col, start_row, live_col, live_row
    )
    qkv_hop, out_z, mine_gate_up, mine_down, late_dy = after([qkv_hop, out_z, mine_gate_up, mine_down, cotangent], x_own)
    x_over, x_near = permute(x_own, n, flip_z), permute(x_own, n, flip_core)
    two_out = jnp.stack([mine_out, out_z])
    out_far = permute(two_out, n, flip_far)
    qkv_around = around(qkv_hop, n)
    gate_up_hop = permute(mine_gate_up, n, flip_far)
    x_over, x_near, out_far, late_dy, *qkv_around = step(x_over, x_near, out_far, late_dy, *qkv_around)
    x_far = permute(x_over, n, flip_core)
    qkv_mine = [qkv_hop] + qkv_around
    qkv_other = across(qkv_mine, n)
    out_all = lax.all_gather(jnp.concatenate([two_out, out_far]), "dp", axis_index_groups=neighbours(n))
    x_blocks = [x_own, x_over, x_near, x_far]

    rows_one, pre, qk, values, w_qkv = qkv_call(
        s, x_blocks, (w_query, w_key, w_value), qkv_mine + qkv_other, norm1_gain[None], gains, cos, sin
    )
    attended, attended_f, lse = attend_call(s, qk, values, start_col, live_row)

    att_over, att_near = permute(attended, n, flip_z), permute(attended, n, flip_core)
    gate_up_hop = after(gate_up_hop, attended)
    gate_up_around = around(gate_up_hop, n)
    mine_down, late_dy = after([mine_down, late_dy], gate_up_hop)
    dy_own = permute(late_dy, n, settle)
    down_hop = permute(mine_down, n, flip_far)
    att_over, att_near, dy_own, *gate_up_around = step(att_over, att_near, dy_own, *gate_up_around)
    att_far = permute(att_over, n, flip_core)
    dy_over, dy_near = permute(dy_own, n, flip_z), permute(dy_own, n, flip_core)
    down_hop = after(down_hop, att_far)
    gate_up_mine = [gate_up_hop] + gate_up_around
    gate_up_parts = gate_up_mine + across(gate_up_mine, n)
    down_around = around(down_hop, n)
    rows_two, hidden, by_gate, by_up, residual, w_out_own = ffn_call(
        s, x_blocks, [attended, att_over, att_near, att_far], out_all, w_gate, w_up, gate_up_parts,
        after(norm2_gain[None], dy_own),
    )
    hidden, dy_over, dy_near, *down_around = step(hidden, dy_over, dy_near, *down_around)
    down_mine = [down_hop] + down_around
    dy_far, *down_across = step(permute(dy_over, n, flip_core), *across(down_mine, n))
    down_parts = down_mine + down_across
    dy_blocks = [dy_own, dy_over, dy_near, dy_far]

    down = grad_cols_call(s, hidden, dy_blocks, "grad_down")
    down_got = first_sums(down, n)
    gate_grad, up_grad, low2, high2 = ffn_back_call(
        s, dy_blocks, w_down, down_parts, w_gate, w_up, gate_up_parts, after(by_gate, *down), by_up
    )
    low2, high2, *down_got = step(low2, high2, *down_got)
    (high_got,) = step(permute(high2, n, flip_core))
    low_half = low2 + high_got
    low_over = permute(low_half[b:], n, flip_z)
    gate_up = grad_rows_call(s, rows_two, after(gate_grad, low_half), up_grad, "grad_gate_up")
    gate_up_got = first_sums(gate_up, n)
    down = first_add(down, after(down_got, *gate_up))
    down_got = second_sums(down, n)
    grad_n2 = (low_half[:b] + after(low_over, *down)).astype(f32)
    inv = lax.rsqrt(jnp.mean(residual * residual, axis=-1, keepdims=True) + epsilon)
    scaled = norm2_gain * grad_n2
    grad_residual = (
        dy_own.astype(f32)
        + inv * scaled
        - residual * (inv * inv * inv) * jnp.mean(scaled * residual, axis=-1, keepdims=True)
    )
    grad_norm2 = jnp.sum(grad_n2 * residual * inv, axis=0)
    gb_own = grad_residual.astype(bf16)
    gb_over, gb_near = permute(gb_own, n, flip_z), permute(gb_own, n, flip_core)
    ffn_low, ffn_high = ffn_out_call(s, w_down, down_parts, after(hidden, gb_own))
    ffn_got = permute(ffn_high, n, flip_core)
    gb_over, gb_near = step(*after([gb_over, gb_near], ffn_low))
    ffn_got = after(ffn_got, gb_over)
    gb_far = permute(gb_over, n, flip_core)
    gate_up = first_add(gate_up, after(gate_up_got, gb_over))
    gate_up_got = second_sums(gate_up, n)
    down = second_add(down, after(down_got, gb_over, *gate_up), n)
    ffn_half = ffn_low + ffn_got
    gb_far, down_got = step(gb_far, permute(cross_sent(down, c), n, flip_core))
    down_kept, down_sent = cross_got(down, down_got, c)
    down_got = permute(down_sent, n, flip_far)
    ffn_over = permute(ffn_half[b:], n, flip_z)
    gb_blocks = [gb_own, gb_over, gb_near, gb_far]

    low, gain_terms, low1, high1 = attend_back_call(
        s, qk, after(values, ffn_half, down_sent), pre, qgain_pair, kgain_pair, cos, sin, start_row, live_col,
        attended_f, lse, w_out_own, w_qkv, gb_blocks,
    )
    low, low1, high1, down_got, ffn_over, *gate_up_got = step(low, low1, high1, down_got, ffn_over, *gate_up_got)
    down_mine = down_kept + down_got
    down_all = whole_grad(down_mine, n)
    gate_up = second_add(gate_up, after(gate_up_got, down_mine), n)
    high_got, gate_up_got = step(permute(high1, n, flip_core), permute(cross_sent(gate_up, c), n, flip_core))
    low_half = low1 + high_got
    low_over = permute(low_half[b:], n, flip_z)
    gate_up_kept, gate_up_sent = cross_got(gate_up, gate_up_got, c)
    gate_up_got = permute(gate_up_sent, n, flip_far)
    att = grad_attention_call(s, rows_one, after(low, low_half, gate_up_sent), attended, gb_blocks)
    att_got = first_sums(att, n)
    block_output = residual + (ffn_half[:b] + after(ffn_over, *att)).astype(f32)
    low_over, gate_up_got, *att_got = step(*after([low_over, gate_up_got, *att_got], block_output))
    gate_up_mine = gate_up_kept + gate_up_got
    gate_up_all = whole_grad(gate_up_mine, n)
    att = first_add(att, after(att_got, gate_up_mine))
    att_got = second_sums(att, n)
    grad_n1 = (low_half[:b] + after(low_over, *att)).astype(f32)
    x_f = x_own.astype(f32)
    inv = lax.rsqrt(jnp.mean(x_f * x_f, axis=-1, keepdims=True) + epsilon)
    scaled = norm1_gain * grad_n1
    input_grad = (
        grad_residual
        + inv * scaled
        - x_f * (inv * inv * inv) * jnp.mean(scaled * x_f, axis=-1, keepdims=True)
    )
    grad_norm1 = jnp.sum(grad_n1 * x_f * inv, axis=0)
    head_terms = gain_terms[:, :HD] + gain_terms[:, HD:]
    vec = jnp.concatenate([grad_norm1, grad_norm2, head_terms[0] + head_terms[1], head_terms[2]])[None]
    moves = vector_moves(n)
    att = second_add(att, after(att_got, input_grad, vec), n)
    (att_got,) = step(permute(cross_sent(att, c), n, flip_core))
    att_kept, att_sent = cross_got(att, att_got, c)
    att_got = permute(att_sent, n, flip_far)
    vec_got = permute(after(vec, att_sent), n, moves[0])
    (grad_down,) = widen_call(after(down_all, att_sent), True, "widen_down")
    att_got, vec_got = step(*after([att_got, vec_got], grad_down))
    att_mine = att_kept + att_got
    att_around = around(att_mine, n)
    late_output, late_grad = after([block_output, input_grad], att_mine)
    settled_output = permute(late_output.astype(bf16), n, settle)
    settled_grad = permute(late_grad.astype(bf16), n, settle)
    vec = vec + vec_got
    vec_got = permute(vec, n, moves[1])
    vec = vec + after(vec_got, att_mine)
    vec_got = permute(vec, n, moves[2])
    att_across = across([att_mine] + att_around, n)
    vec = vec + vec_got
    vec_got = permute(vec, n, moves[3])
    grad_query, grad_key, grad_value, grad_out = place_call(
        s,
        [att_mine] + att_around + after(att_across, vec),
        write_attention,
        [(width // 8, wq), (width // 8, wk), (width // 8, wk), (w_out.shape[0] // 8, width)],
        "place_attention",
    )
    settled_output, settled_grad, vec_got = after([settled_output, settled_grad, vec_got], grad_query)
    block_output = jnp.where(home, block_output, settled_output.astype(f32))
    input_grad = jnp.where(home, input_grad, settled_grad.astype(f32))
    vec = vec + vec_got
    vec_got = permute(vec, n, moves[4])
    grad_gate, grad_up = widen_call(after(gate_up_all, vec), False, "widen_gate_up")
    vec = vec + after(vec_got, grad_gate)
    for move in moves[5:]:
        vec = vec + permute(vec, n, move)
    vec = vec[0]
    return (
        block_output,
        input_grad,
        vec[:width],
        grad_query,
        grad_key,
        grad_value,
        vec[2 * width : 2 * width + HD],
        vec[2 * width + HD :],
        grad_out,
        vec[width : 2 * width],
        grad_gate,
        grad_up,
        grad_down,
    )


def solution(mesh):
    placed = (
        P(("dp", "tensor"), None),
        P("dp", None),
        P("dp", None),
        P(),
        P(None, "tensor"),
        P(None, "tensor"),
        P(None, "tensor"),
        P(),
        P(),
        P("tensor", None),
        P(),
        P(None, "tensor"),
        P(None, "tensor"),
        P("tensor", None),
        P(("dp", "tensor"), None),
    )
    return jax.shard_map(
        local,
        mesh=mesh,
        in_specs=placed,
        out_specs=(
            P(("dp", "tensor"), None),
            P(("dp", "tensor"), None),
            P(),
            P(None, "tensor"),
            P(None, "tensor"),
            P(None, "tensor"),
            P(),
            P(),
            P("tensor", None),
            P(),
            P(None, "tensor"),
            P(None, "tensor"),
            P("tensor", None),
        ),
        check_vma=False,
    )
```

```python
import functools
import math

import jax
import jax.numpy as jnp
from jax import lax
from jax.experimental import pallas as pl
from jax.experimental.pallas import tpu as pltpu
from jax.sharding import PartitionSpec as P

HD = 64
AX = ("dp", "tensor")
T4 = 4
VMEM_MB = 1 << 20

epsilon = 1e-05
rope_base = 1000000.0
NEG = -1000000000.0
bf16 = jnp.bfloat16
f32 = jnp.float32


def doc_tables(lengths_row, positions, head_dim):
    doc_ends = jnp.cumsum(lengths_row)
    passed = positions[:, None] >= doc_ends[None, :]
    doc_starts = jnp.sum(jnp.where(passed, lengths_row[None, :], 0), axis=1)
    offsets = (positions - doc_starts).astype(f32)
    freqs = jnp.exp(
        jnp.arange(head_dim // 2, dtype=f32) * (-2.0 * math.log(rope_base) / head_dim)
    )
    angles = offsets[:, None] * freqs[None, :]
    return (doc_starts, jnp.cos(angles), jnp.sin(angles))


def contract(a, b, da, db):
    return lax.dot_general(a, b, (((da,), (db,)), ((), ())), preferred_element_type=f32)


def swap_halves(y):
    width = y.shape[1]
    lane = lax.broadcasted_iota(jnp.int32, y.shape, 1)
    return jnp.where(lane % HD < HD // 2, pltpu.roll(y, width - HD // 2, 1), pltpu.roll(y, HD // 2, 1))


def split_dot(left, right, da, db):
    high = left.astype(bf16)
    low = (left - high.astype(f32)).astype(bf16)
    return contract(high, right, da, db) + contract(low, right, da, db)


def head_mean(y):
    at = lax.broadcasted_iota(jnp.int32, (128, 128), 0) // HD
    to = lax.broadcasted_iota(jnp.int32, (128, 128), 1) // HD
    ones = jnp.where(at == to, 1.0 / HD, 0.0).astype(bf16)
    sides = [split_dot(y[:, k : k + 128], ones, 1, 0) for k in range(0, y.shape[1], 128)]
    return sides[0] if len(sides) == 1 else jnp.concatenate(sides, 1)


class Weight:
    def __init__(self, s_ref, own, parts, to, sems, start=0):
        self.core, self.e = s_ref[1], s_ref[2]
        self.own, self.parts, self.to, self.sems, self.start_col = own, parts, to, sems, start

    def copies(self):
        start = 0
        for i, w in enumerate(self.own):
            wide = w.shape[1]
            to = self.to if len(self.own) == 1 else self.to.at[:, pl.ds(start, wide)]
            yield 0, functools.partial(pltpu.make_async_copy, w, to, self.sems.at[8 + i])
            start += wide
        rows = self.to.shape[0] // 8
        for j in range(4):
            for other in range(2):
                at = pl.multiple_of((2 * (self.e ^ j) + 1 - other) * rows, rows)
                src = self.parts[4 * other + j]
                if src.shape[1] != self.to.shape[1]:
                    src = src.at[:, pl.ds(self.start_col, self.to.shape[1])]
                to = self.to.at[pl.ds(at, rows), :]
                yield 1, functools.partial(pltpu.make_async_copy, src, to, self.sems.at[2 * j + other])

    def each(self, act):
        for core in range(2):

            @pl.when(self.core == core)
            def _():
                for whose, copy in self.copies():
                    if whose == core:
                        act(copy())

    def start(self):
        self.each(lambda copy: copy.start())

    def wait(self):
        self.each(lambda copy: copy.wait())


ANY = pl.BlockSpec(memory_space=pl.ANY)


def fixed(*shape):
    return pl.BlockSpec(shape, lambda *_: (0,) * len(shape))


def cost(flops):
    return pl.CostEstimate(flops=flops, bytes_accessed=1 << 16, transcendentals=0)


def params(mib):
    return pltpu.CompilerParams(vmem_limit_bytes=mib * VMEM_MB)


def qkv_kernel(s_ref, *refs):
    pieces, own, parts, refs = refs[:4], refs[4:7], refs[7:15], refs[15:]
    g1_ref, gains_ref, cos_ref, sin_ref, n1_ref, pre_ref, qk_ref, v_ref, w_ref, xs, xsem, wsem = refs
    j = pl.program_id(0)
    weight = Weight(s_ref, own, parts, w_ref, wsem)

    @pl.when(j == 0)
    def _():
        for k in range(4):
            pltpu.make_async_copy(pieces[k], xs.at[k], xsem.at[k]).start()
        weight.start()

    pltpu.make_async_copy(pieces[0], xs.at[j], xsem.at[j]).wait()
    x = xs[j].astype(f32)
    inv = lax.rsqrt(jnp.mean(x * x, axis=-1, keepdims=True) + epsilon)
    n1 = (x * inv * g1_ref[...]).astype(bf16)
    n1_ref[...] = n1

    @pl.when(j == 0)
    def _():
        weight.wait()

    qkv = jnp.dot(n1, w_ref[...], preferred_element_type=f32)
    width = pre_ref.shape[1]
    pre = qkv[:, :width]
    pre_ref[...] = pre
    v_ref[...] = qkv[:, width:].astype(bf16)
    y = pre * lax.rsqrt(head_mean(pre * pre) + epsilon) * gains_ref[...]
    cos = jnp.concatenate([cos_ref[...]] * (width // 128), 1)
    sin = jnp.concatenate([sin_ref[...]] * (width // 128), 1)
    qk = (y * cos + swap_halves(y) * sin).astype(bf16)
    lane = lax.broadcasted_iota(jnp.int32, qk.shape, 1)
    qk_ref[...] = jnp.where(lane < width - 128, qk * 0.125, qk).astype(bf16)


def qkv_call(s, xs, w_own, w_parts, g1, gains, cos, sin):
    b, d = xs[0].shape
    wid = w_parts[0].shape[1]
    qkw = wid - 128
    natural = lambda j, s: (s[0] ^ j, 0)
    return pl.pallas_call(
        qkv_kernel,
        grid_spec=pltpu.PrefetchScalarGridSpec(
            num_scalar_prefetch=1,
            grid=(4,),
            in_specs=[ANY] * 15
            + [fixed(1, d), fixed(1, qkw), pl.BlockSpec((b, 128), natural), pl.BlockSpec((b, 128), natural)],
            out_specs=[
                pl.BlockSpec((b, d), lambda j, s: (j, 0)),
                pl.BlockSpec((b, qkw), natural),
                pl.BlockSpec((b, qkw), natural),
                pl.BlockSpec((b, 128), natural),
                fixed(d, wid),
            ],
            scratch_shapes=[
                pltpu.VMEM((4, b, d), bf16),
                pltpu.SemaphoreType.DMA((4,)),
                pltpu.SemaphoreType.DMA((11,)),
            ],
        ),
        out_shape=[
            jax.ShapeDtypeStruct((4 * b, d), bf16),
            jax.ShapeDtypeStruct((4 * b, qkw), f32),
            jax.ShapeDtypeStruct((4 * b, qkw), bf16),
            jax.ShapeDtypeStruct((4 * b, 128), bf16),
            jax.ShapeDtypeStruct((d, wid), bf16),
        ],
        compiler_params=params(58),
        cost_estimate=cost(1 << 24),
        name="qkv",
    )(s, *xs, *w_own, *w_parts, g1, gains, cos, sin)


def both_heads(pair):
    lane = lax.broadcasted_iota(jnp.int32, pair.shape, 1)
    zero = jnp.zeros_like(pair)
    return jnp.concatenate([jnp.where(lane < HD, pair, zero), jnp.where(lane < HD, zero, pair)], 0)


def pick_heads(both):
    r = both.shape[0] // 2
    lane = lax.broadcasted_iota(jnp.int32, (r, 128), 1)
    return jnp.where(lane < HD, both[:r], both[r:])


def twice(kv, g):
    lane = lax.broadcasted_iota(jnp.int32, kv.shape, 1)
    turned = pltpu.roll(kv.astype(f32), HD, 1).astype(kv.dtype)
    return jnp.where((lane < HD) == (g == 0), kv, turned)


def attend_kernel(s_ref, q_ref, k_ref, v_ref, start_ref, live_ref, att_ref, out_ref, lse_ref, bias):
    g = pl.program_id(0)
    n = k_ref.shape[0]
    b = n // 4

    @pl.when(g == 0)
    def _():
        for a in range(4):
            keys = (a + 1) * b
            start = start_ref[a * b : (a + 1) * b, :1]
            q_at = lax.broadcasted_iota(jnp.int32, (b, keys), 0) + a * b
            k_at = lax.broadcasted_iota(jnp.int32, (b, keys), 1)
            allowed = ((live_ref[:1, :keys] >= start) & (k_at <= q_at)) | (k_at == q_at)
            bias[a * b : (a + 1) * b, :keys] = jnp.where(allowed, 0.0, NEG)

    kd = twice(k_ref[...], g)
    vd = twice(v_ref[...], g)
    for a in range(4):
        keys = (a + 1) * b
        rows = slice(a * b, (a + 1) * b)
        qm = both_heads(q_ref[rows, :])
        scores = contract(qm, kd[:keys], 1, 1)
        extra = bias[rows, :keys]
        expo = jnp.exp(scores + jnp.concatenate([extra, extra], 0))
        total = jnp.sum(expo, axis=-1, keepdims=True)
        pair = pick_heads(contract(expo.astype(bf16), vd[:keys], 1, 0) / total)
        out_ref[rows, :] = pair
        att_ref[pl.ds(pl.multiple_of((s_ref[0] ^ a) * b, b), b), :] = pair.astype(bf16)
        lse_ref[0, a] = jnp.transpose(jnp.broadcast_to(jnp.log(total), (2 * b, 128)))[:1]


def attend_call(s, qk, v, start, live):
    n = qk.shape[0]
    b = n // 4
    lanes = lambda g, s: (0, g)
    return pl.pallas_call(
        attend_kernel,
        grid_spec=pltpu.PrefetchScalarGridSpec(
            num_scalar_prefetch=1,
            grid=(2,),
            in_specs=[
                pl.BlockSpec((n, 128), lanes),
                pl.BlockSpec((n, 128), lambda g, s: (0, 2)),
                fixed(n, 128),
                fixed(n, 128),
                fixed(8, n),
            ],
            out_specs=[
                pl.BlockSpec((n, 128), lanes),
                pl.BlockSpec((n, 128), lanes),
                pl.BlockSpec((1, 4, 1, 2 * b), lambda g, s: (g, 0, 0, 0)),
            ],
            scratch_shapes=[pltpu.VMEM((n, n), f32)],
        ),
        out_shape=[
            jax.ShapeDtypeStruct((n, 256), bf16),
            jax.ShapeDtypeStruct((n, 256), f32),
            jax.ShapeDtypeStruct((2, 4, 1, 2 * b), f32),
        ],
        compiler_params=params(14),
        cost_estimate=cost(1 << 24),
        name="attend",
    )(s, qk, qk, v, start, live)


def norm_back(grad, pre, gain, cos, sin):
    turned = grad * cos - swap_halves(grad) * sin
    inv = lax.rsqrt(head_mean(pre * pre) + epsilon)
    scaled = turned * gain
    dpre = inv * scaled - pre * (inv * inv * inv) * head_mean(scaled * pre)
    return dpre, jnp.sum(turned * pre * inv, axis=0, keepdims=True)


def attend_back_kernel(s_ref, q_ref, k_ref, v_ref, qpre_ref, kpre_ref, gains_ref, kgain_ref, cos_ref, sin_ref,
                       start_ref, live_ref, out_ref, lse_ref, wout_ref, w_ref, b0, b1, b2, b3,
                       low_ref, gain_ref, lo_ref, hi_ref, bias, dk, dv, dkall, dvall, dos, gb, sems):
    g = pl.program_id(0)
    n = k_ref.shape[0]
    b = n // 4
    pieces = (b0, b1, b2, b3)

    @pl.when(g == 0)
    def _():
        for k in range(4):
            pltpu.make_async_copy(pieces[k], gb.at[k], sems.at[k]).start()
        for a in range(4):
            keys = (a + 1) * b
            start = start_ref[:1, a * b : (a + 1) * b]
            k_at = lax.broadcasted_iota(jnp.int32, (keys, b), 0)
            q_at = lax.broadcasted_iota(jnp.int32, (keys, b), 1) + a * b
            allowed = ((live_ref[:keys, :1] >= start) & (k_at <= q_at)) | (k_at == q_at)
            bias[:keys, a * b : (a + 1) * b] = jnp.where(allowed, 0.0, NEG)
        for k in range(4):
            pltpu.make_async_copy(pieces[k], gb.at[k], sems.at[k]).wait()
            dos[k] = contract(gb[k], wout_ref[...], 1, 1).astype(bf16)

    kd = twice(k_ref[...], g)
    vd = twice(v_ref[...], g)
    gain_sum = jnp.zeros((1, 128), f32)
    ones = jnp.ones((16, 128), bf16)
    for a in (3, 2, 1, 0):
        keys = (a + 1) * b
        rows = slice(a * b, (a + 1) * b)
        home = s_ref[0] ^ a
        qm = both_heads(q_ref[rows, :])
        dout = jnp.where(g == 0, dos[home, :, :128], dos[home, :, 128:])
        dom = both_heads(dout)
        terms = both_heads(dout.astype(f32) * out_ref[rows, :])
        terms_high = terms.astype(bf16)
        terms_low = (terms - terms_high.astype(f32)).astype(bf16)
        delta = (contract(ones, terms_high, 1, 1) + contract(ones, terms_low, 1, 1))[:1]
        scores = contract(kd[:keys], qm, 1, 1)
        extra = bias[:keys, rows]
        probs = jnp.exp(scores + (jnp.concatenate([extra, extra], 1) - lse_ref[0, a]))
        dprobs = contract(vd[:keys], dom, 1, 1)
        dscores = (probs * (dprobs - delta)).astype(bf16)
        dv_add = contract(probs.astype(bf16), dom, 1, 0)
        dk_add = contract(dscores, qm, 1, 0)
        if a == 3:
            dv[...] = dv_add
            dk[...] = dk_add
        else:
            dv[:keys] += dv_add
            dk[:keys] += dk_add
        dq = pick_heads(contract(dscores, kd[:keys], 0, 0)) * 0.125
        dpre, gain_part = norm_back(dq, qpre_ref[rows, :], gains_ref[...], cos_ref[rows, :], sin_ref[rows, :])
        at = pl.ds(pl.multiple_of(home * b, b), b)
        low_ref[at, pl.ds(pl.multiple_of(g * 128, 128), 128)] = dpre.astype(bf16)
        gain_sum = gain_sum + gain_part
    gain_ref[pl.ds(g, 1), :] = gain_sum
    lane = lax.broadcasted_iota(jnp.int32, (n, 128), 1)
    dk_all = dk[...] + pltpu.roll(dk[...], HD, 1)
    dv_all = dv[...] + pltpu.roll(dv[...], HD, 1)

    @pl.when(g == 0)
    def _():
        dkall[...] = dk_all
        dvall[...] = dv_all

    @pl.when(g == 1)
    def _():
        grad_k = jnp.where(lane < HD, dkall[...], dk_all)
        grad_v = jnp.where(lane < HD, dvall[...], dv_all)
        dpre, gain_part = norm_back(grad_k, kpre_ref[...], kgain_ref[...], cos_ref[...], sin_ref[...])
        gain_ref[2:3, :] = gain_part
        for a in range(4):
            at = pl.ds(pl.multiple_of((s_ref[0] ^ a) * b, b), b)
            low_ref[at, 256:384] = dpre[a * b : (a + 1) * b].astype(bf16)
            low_ref[at, 384:512] = grad_v[a * b : (a + 1) * b].astype(bf16)
        hi_ref[...] = contract(low_ref[2 * b :, :], w_ref[...], 1, 1).astype(bf16)
        lo_ref[...] = contract(low_ref[: 2 * b, :], w_ref[...], 1, 1).astype(bf16)


def attend_back_call(s, qk, v, pre, qgain, kgain, cos, sin, start, live, out, lse, wout, w, blocks):
    n = v.shape[0]
    b = n // 4
    d = blocks[0].shape[1]
    lanes = pl.BlockSpec((n, 128), lambda g, s: (0, g))
    third = pl.BlockSpec((n, 128), lambda g, s: (0, 2))
    return pl.pallas_call(
        attend_back_kernel,
        grid_spec=pltpu.PrefetchScalarGridSpec(
            num_scalar_prefetch=1,
            grid=(2,),
            in_specs=[lanes, third, fixed(n, 128), lanes, third, fixed(1, 128), fixed(1, 128), fixed(n, 128),
                      fixed(n, 128), fixed(8, n), fixed(n, 128), lanes,
                      pl.BlockSpec((1, 4, 1, 2 * b), lambda g, s: (g, 0, 0, 0)),
                      fixed(256, d), fixed(d, 512)] + [ANY] * 4,
            out_specs=[fixed(n, 512), fixed(8, 128), fixed(2 * b, d), fixed(2 * b, d)],
            scratch_shapes=[pltpu.VMEM((n, n), f32)]
            + [pltpu.VMEM((n, 128), f32)] * 4
            + [pltpu.VMEM((4, b, 256), bf16), pltpu.VMEM((4, b, d), bf16), pltpu.SemaphoreType.DMA((4,))],
        ),
        out_shape=[
            jax.ShapeDtypeStruct((n, 512), bf16),
            jax.ShapeDtypeStruct((8, 128), f32),
            jax.ShapeDtypeStruct((2 * b, d), bf16),
            jax.ShapeDtypeStruct((2 * b, d), bf16),
        ],
        compiler_params=params(24),
        cost_estimate=cost(1 << 24),
        name="attend_back",
    )(s, qk, qk, v, pre, pre, qgain, kgain, cos, sin, start, live, out, lse, wout, w, *blocks)


def ffn_kernel(s_ref, *refs):
    x_in, a_in, o_in, refs = refs[:4], refs[4:8], refs[8], refs[9:]
    wg_own, wu_own, parts, refs = refs[0], refs[1], refs[2:10], refs[10:]
    gain_ref, n2_ref, hid_ref, fg_ref, fu_ref, res_ref, wout_ref, refs = *refs[:7], refs[7:]
    wg, wu, xs, att, wout, asem, xsem, osem, gsem, usem = refs
    j = pl.program_id(0)
    b = xs.shape[1]
    gate_w = Weight(s_ref, (wg_own,), parts, wg, gsem)
    up_w = Weight(s_ref, (wu_own,), parts, wu, usem, wg.shape[1])

    def out_copy(i):
        return pltpu.make_async_copy(o_in.at[:, i ^ (2 * s_ref[1])], wout.at[i], osem.at[i])

    def att_copy(k, i):
        return pltpu.make_async_copy(
            a_in[i].at[pl.ds((k ^ i) * b, b), :], att.at[k, :, pl.ds(i * b, b)], asem.at[k, i]
        )

    @pl.when(j == 0)
    def _():
        for k in range(4):
            pltpu.make_async_copy(x_in[k], xs.at[k], xsem.at[k]).start()
            for i in range(4):
                att_copy(k, i).start()
            if k == 0:
                for i in range(4):
                    out_copy(i).start()
                gate_w.start()
        up_w.start()
        for i in range(4):
            out_copy(i).wait()

    pltpu.make_async_copy(x_in[0], xs.at[j], xsem.at[j]).wait()
    for i in range(4):
        pltpu.make_async_copy(a_in[i].at[pl.ds(0, b), :], att.at[j, :, pl.ds(i * b, b)], asem.at[j, i]).wait()
    res = xs[j].astype(f32) + jnp.dot(att[j], wout[...].reshape(4 * b, -1), preferred_element_type=f32)

    @pl.when(j == 0)
    def _():
        res_ref[...] = res
        wout_ref[...] = wout[0].reshape(b, -1)
        gate_w.wait()
        up_w.wait()

    inv = lax.rsqrt(jnp.mean(res * res, axis=-1, keepdims=True) + epsilon)
    n2 = (res * inv * gain_ref[...]).astype(bf16)
    n2_ref[...] = n2
    gate = jnp.dot(n2, wg[...], preferred_element_type=f32)
    up = jnp.dot(n2, wu[...], preferred_element_type=f32)
    s = jax.nn.sigmoid(gate)
    silu = gate * s
    hid_ref[...] = (silu * up).astype(bf16)
    fg_ref[...] = (up * (s * (1.0 + gate * (1.0 - s)))).astype(bf16)
    fu_ref[...] = silu.astype(bf16)


def ffn_call(s, xs, atts, wout, wg, wu, parts, gain):
    b, d = xs[0].shape
    h = wg.shape[1]
    block = lambda wid: pl.BlockSpec((b, wid), lambda j, s: (j, 0))
    return pl.pallas_call(
        ffn_kernel,
        grid_spec=pltpu.PrefetchScalarGridSpec(
            num_scalar_prefetch=1,
            grid=(4,),
            in_specs=[ANY] * 19 + [fixed(1, d)],
            out_specs=[block(d), block(h), block(h), block(h), fixed(b, d), fixed(b, d)],
            scratch_shapes=[
                pltpu.VMEM((d, h), bf16),
                pltpu.VMEM((d, h), bf16),
                pltpu.VMEM((4, b, d), bf16),
                pltpu.VMEM((4, b, 4 * b), bf16),
                pltpu.VMEM((4,) + wout.shape[:1] + wout.shape[2:], bf16),
                pltpu.SemaphoreType.DMA((4, 4)),
                pltpu.SemaphoreType.DMA((4,)),
                pltpu.SemaphoreType.DMA((4,)),
                pltpu.SemaphoreType.DMA((9,)),
                pltpu.SemaphoreType.DMA((9,)),
            ],
        ),
        out_shape=[jax.ShapeDtypeStruct((4 * b, d), bf16)]
        + [jax.ShapeDtypeStruct((4 * b, h), bf16)] * 3
        + [jax.ShapeDtypeStruct((b, d), f32), jax.ShapeDtypeStruct((b, d), bf16)],
        compiler_params=params(58),
        cost_estimate=cost(1 << 24),
        name="ffn",
    )(s, *xs, *atts, wout, wg, wu, *parts, gain)


def ffn_back_kernel(s_ref, *refs):
    y_in, wd_own, wd_parts, refs = refs[:4], refs[4], refs[5:13], refs[13:]
    wg_own, wu_own, parts, refs = refs[0], refs[1], refs[2:10], refs[10:]
    fg_ref, fu_ref, gg_ref, gu_ref, lo_ref, hi_ref, wd, wg, wu, dy, ysem, dsem, gsem, usem = refs
    j = pl.program_id(0)
    down_w = Weight(s_ref, (wd_own,), wd_parts, wd, dsem)
    gate_w = Weight(s_ref, (wg_own,), parts, wg, gsem)
    up_w = Weight(s_ref, (wu_own,), parts, wu, usem, wg.shape[1])

    @pl.when(j == 0)
    def _():
        pltpu.make_async_copy(y_in[0], dy.at[0], ysem.at[0]).start()
        down_w.start()
        for k in range(1, 4):
            pltpu.make_async_copy(y_in[k], dy.at[k], ysem.at[k]).start()
        gate_w.start()
        up_w.start()
        down_w.wait()

    pltpu.make_async_copy(y_in[0], dy.at[j], ysem.at[j]).wait()
    gh = contract(dy[j], wd[...], 1, 1)
    gg = (gh * fg_ref[...].astype(f32)).astype(bf16)
    gu = (gh * fu_ref[...].astype(f32)).astype(bf16)
    gg_ref[...] = gg
    gu_ref[...] = gu

    @pl.when(j == 0)
    def _():
        gate_w.wait()
        up_w.wait()

    grad = (contract(gg, wg[...], 1, 1) + contract(gu, wu[...], 1, 1)).astype(bf16)

    @pl.when(j < 2)
    def _():
        lo_ref[...] = grad

    @pl.when(j >= 2)
    def _():
        hi_ref[...] = grad


def ffn_back_call(s, dys, wd, d_parts, wg, wu, parts, fg, fu):
    b, d = dys[0].shape
    h = wg.shape[1]
    block = lambda wid: pl.BlockSpec((b, wid), lambda j, s: (j, 0))
    return pl.pallas_call(
        ffn_back_kernel,
        grid_spec=pltpu.PrefetchScalarGridSpec(
            num_scalar_prefetch=1,
            grid=(4,),
            in_specs=[ANY] * 23 + [block(h), block(h)],
            out_specs=[
                block(h),
                block(h),
                pl.BlockSpec((b, d), lambda j, s: (jnp.minimum(j, 1), 0)),
                pl.BlockSpec((b, d), lambda j, s: (jnp.maximum(j - 2, 0), 0)),
            ],
            scratch_shapes=[
                pltpu.VMEM((h, d), bf16),
                pltpu.VMEM((d, h), bf16),
                pltpu.VMEM((d, h), bf16),
                pltpu.VMEM((4, b, d), bf16),
                pltpu.SemaphoreType.DMA((4,)),
                pltpu.SemaphoreType.DMA((9,)),
                pltpu.SemaphoreType.DMA((9,)),
                pltpu.SemaphoreType.DMA((9,)),
            ],
        ),
        out_shape=[jax.ShapeDtypeStruct((4 * b, h), bf16)] * 2 + [jax.ShapeDtypeStruct((2 * b, d), bf16)] * 2,
        compiler_params=params(58),
        cost_estimate=cost(1 << 24),
        name="ffn_back",
    )(s, *dys, wd, *d_parts, wg, wu, *parts, fg, fu)


def ffn_out_kernel(s_ref, wd_own, *refs):
    wd_parts, (hid_ref, lo_ref, hi_ref, wd, dsem) = refs[:8], refs[8:]
    j = pl.program_id(0)
    down_w = Weight(s_ref, (wd_own,), wd_parts, wd, dsem)

    @pl.when(j == 0)
    def _():
        down_w.start()
        down_w.wait()

    part = jnp.dot(hid_ref[...], wd[...], preferred_element_type=f32).astype(bf16)

    @pl.when(j < 2)
    def _():
        lo_ref[...] = part

    @pl.when(j >= 2)
    def _():
        hi_ref[...] = part


def ffn_out_call(s, wd, d_parts, hidden):
    n, h = hidden.shape
    b, d = n // 4, wd.shape[1]
    return pl.pallas_call(
        ffn_out_kernel,
        grid_spec=pltpu.PrefetchScalarGridSpec(
            num_scalar_prefetch=1,
            grid=(4,),
            in_specs=[ANY] * 9 + [pl.BlockSpec((b, h), lambda j, s: (j, 0))],
            out_specs=[
                pl.BlockSpec((b, d), lambda j, s: (jnp.minimum(j, 1), 0)),
                pl.BlockSpec((b, d), lambda j, s: (jnp.maximum(j - 2, 0), 0)),
            ],
            scratch_shapes=[pltpu.VMEM((h, d), bf16), pltpu.SemaphoreType.DMA((9,))],
        ),
        out_shape=[jax.ShapeDtypeStruct((2 * b, d), bf16)] * 2,
        compiler_params=params(58),
        cost_estimate=cost(1 << 24),
        name="ffn_out",
    )(s, wd, *d_parts, hidden)


def grad_rows_kernel(s_ref, left_ref, a_ref, b_ref, sent_a, keep_a, sent_b, keep_b):
    j = pl.program_id(0)
    left = left_ref[...]
    first = contract(left, a_ref[...], 0, 0).astype(bf16)
    second = contract(left, b_ref[...], 0, 0).astype(bf16)

    @pl.when(j % 2 == 1)
    def _():
        sent_a[0] = first

    @pl.when(j % 2 == 0)
    def _():
        keep_a[0] = first

    @pl.when(j >= 2)
    def _():
        sent_b[0] = second

    @pl.when(j < 2)
    def _():
        keep_b[0] = second


def grad_rows_call(s, left, a, b, name):
    n, rows = left.shape
    cols = a.shape[1]
    maps = [
        lambda j, s: (j // 2, 0, 0),
        lambda j, s: (j // 2, 0, 0),
        lambda j, s: (jnp.maximum(j - 2, 0), 0, 0),
        lambda j, s: (jnp.minimum(j, 1), 0, 0),
    ]
    return pl.pallas_call(
        grad_rows_kernel,
        grid_spec=pltpu.PrefetchScalarGridSpec(
            num_scalar_prefetch=1,
            grid=(4,),
            in_specs=[pl.BlockSpec((n, rows // 4), lambda j, s: (0, s[2] ^ j)), fixed(n, cols), fixed(n, cols)],
            out_specs=[pl.BlockSpec((1, rows // 4, cols), m) for m in maps],
        ),
        out_shape=[jax.ShapeDtypeStruct((2, rows // 4, cols), bf16)] * 4,
        compiler_params=params(16),
        cost_estimate=cost(1 << 24),
        name=name,
    )(s, left, a, b)


def grad_cols_kernel(s_ref, left_ref, r0, r1, r2, r3, sent_a, keep_a, sent_b, keep_b, right, sems):
    k = pl.program_id(0)
    b = r0.shape[0]
    cols = left_ref.shape[0] // 4

    def copy(k, i):
        src = (r0, r1, r2, r3)[i].at[:, pl.ds(pl.multiple_of(k * cols, cols), cols)]
        return pltpu.make_async_copy(src, right.at[k, pl.ds(i * b, b), :], sems.at[k, i])

    @pl.when(k == 0)
    def _():
        for block in range(4):
            for i in range(4):
                copy(block, i).start()

    for i in range(4):
        copy(k, i).wait()
    grad = contract(left_ref[...], right[k], 0, 0)
    grad = grad.astype(bf16)
    rows = grad.shape[0] // 4
    for a in range(4):
        piece = grad[a * rows : (a + 1) * rows]
        j = s_ref[2] ^ a

        @pl.when((k < 2) & (j % 2 == 1))
        def _():
            sent_a[j // 2] = piece

        @pl.when((k < 2) & (j % 2 == 0))
        def _():
            keep_a[j // 2] = piece

        @pl.when((k >= 2) & (j >= 2))
        def _():
            sent_b[j % 2] = piece

        @pl.when((k >= 2) & (j < 2))
        def _():
            keep_b[j % 2] = piece


def grad_cols_call(s, left, rights, name):
    n, rows = left.shape
    b, cols = rights[0].shape
    first = pl.BlockSpec((2, rows // 4, cols // 4), lambda k, s: (0, 0, jnp.minimum(k, 1)))
    second = pl.BlockSpec((2, rows // 4, cols // 4), lambda k, s: (0, 0, jnp.maximum(k - 2, 0)))
    return pl.pallas_call(
        grad_cols_kernel,
        grid_spec=pltpu.PrefetchScalarGridSpec(
            num_scalar_prefetch=1,
            grid=(4,),
            in_specs=[fixed(n, rows)] + [ANY] * 4,
            out_specs=[first, first, second, second],
            scratch_shapes=[pltpu.VMEM((4, n, cols // 4), bf16), pltpu.SemaphoreType.DMA((4, 4))],
        ),
        out_shape=[jax.ShapeDtypeStruct((2, rows // 4, cols // 2), bf16)] * 4,
        compiler_params=params(14),
        cost_estimate=cost(1 << 24),
        name=name,
    )(s, left, *rights)


def widen_kernel(side, in_ref, *outs):
    first, second = in_ref[0, 0].astype(f32), in_ref[0, 1].astype(f32)
    if side:
        outs[0][...] = jnp.concatenate([first, second], 1)
    else:
        outs[0][...] = first
        outs[1][...] = second


def widen_call(whole, side, name):
    _, _, rows, cols = whole.shape
    block = (rows, 2 * cols) if side else (rows, cols)
    count = 1 if side else 2
    return pl.pallas_call(
        functools.partial(widen_kernel, side),
        grid=(8,),
        in_specs=[pl.BlockSpec((1, 2, rows, cols), lambda j: (j, 0, 0, 0))],
        out_specs=[pl.BlockSpec(block, lambda j: (j, 0))] * count,
        out_shape=[jax.ShapeDtypeStruct((8 * block[0], block[1]), f32)] * count,
        compiler_params=params(12),
        cost_estimate=cost(1 << 20),
        name=name,
    )(whole)


def place_kernel(write, s_ref, *refs):
    k = pl.program_id(0)
    for i in range(8):

        @pl.when(k == i)
        def _():
            write(refs[i], refs[8:])


def write_attention(piece, outs):
    query, key, value, out = outs
    r, s = query.shape[0], out.shape[0]
    query[...] = piece[0, :r].astype(f32)
    key[...] = piece[1, :r, :128].astype(f32)
    value[...] = piece[1, :r, 128:].astype(f32)
    sides = [piece[half, r + at * s : r + (at + 1) * s] for half in range(2) for at in range(2)]
    out[...] = jnp.concatenate(sides, 1).astype(f32)


def place_call(s, pieces, write, blocks, name):
    eighth = lambda k, s: (2 * (s[2] ^ (k % 4)) + (s[1] ^ (k // 4)), 0)
    return pl.pallas_call(
        functools.partial(place_kernel, write),
        grid_spec=pltpu.PrefetchScalarGridSpec(
            num_scalar_prefetch=1,
            grid=(8,),
            in_specs=[fixed(*pieces[0].shape)] * 8,
            out_specs=[pl.BlockSpec(block, eighth) for block in blocks],
        ),
        out_shape=[jax.ShapeDtypeStruct((8 * r, cols), f32) for r, cols in blocks],
        compiler_params=params(12),
        cost_estimate=cost(1 << 20),
        name=name,
    )(s, *pieces)


def grad_attention_kernel(s_ref, n1_ref, low_ref, att_ref, b0, b1, b2, b3, sent_a, keep_a, sent_b, keep_b, whole):
    j = pl.program_id(0)
    b = b0.shape[0]

    @pl.when(j == 0)
    def _():
        total = None
        for i, block in enumerate((b0, b1, b2, b3)):
            part = contract(att_ref[i * b : (i + 1) * b, :], block[...], 0, 0)
            total = part if total is None else total + part
        whole[...] = total.astype(bf16)

    qkv = contract(n1_ref[...], low_ref[...], 0, 0).astype(bf16)
    r = qkv.shape[0] // 2
    s = whole.shape[0] // 8
    k = qkv.shape[1] // 2
    out = whole[pl.ds(pl.multiple_of((s_ref[2] ^ j) * 2 * s, 2 * s), 2 * s), :]

    def joined(at):
        parts = []
        for core in range(2):
            some = out[core * s : (core + 1) * s]
            parts += [
                qkv[core * r : (core + 1) * r, at * k : (at + 1) * k],
                some[:, 2 * at * k : (2 * at + 1) * k],
                some[:, (2 * at + 1) * k : (2 * at + 2) * k],
            ]
        return jnp.concatenate(parts, 0)

    @pl.when(j % 2 == 1)
    def _():
        sent_a[0] = joined(0)

    @pl.when(j % 2 == 0)
    def _():
        keep_a[0] = joined(0)

    @pl.when(j >= 2)
    def _():
        sent_b[0] = joined(1)

    @pl.when(j < 2)
    def _():
        keep_b[0] = joined(1)


def grad_attention_call(s, n1, low, att, blocks):
    n, d = n1.shape
    b = n // 4
    half = (d // 4 + att.shape[1] // 2, 256)
    maps = [
        lambda j, s: (j // 2, 0, 0),
        lambda j, s: (j // 2, 0, 0),
        lambda j, s: (jnp.maximum(j - 2, 0), 0, 0),
        lambda j, s: (jnp.minimum(j, 1), 0, 0),
    ]
    return pl.pallas_call(
        grad_attention_kernel,
        grid_spec=pltpu.PrefetchScalarGridSpec(
            num_scalar_prefetch=1,
            grid=(4,),
            in_specs=[pl.BlockSpec((n, d // 4), lambda j, s: (0, s[2] ^ j)), fixed(n, low.shape[1]), fixed(n, att.shape[1])]
            + [fixed(b, d)] * 4,
            out_specs=[pl.BlockSpec((1,) + half, m) for m in maps],
            scratch_shapes=[pltpu.VMEM((att.shape[1], d), bf16)],
        ),
        out_shape=[jax.ShapeDtypeStruct((2,) + half, bf16)] * 4,
        compiler_params=params(18),
        cost_estimate=cost(1 << 24),
        name="grad_attention",
    )(s, n1, low, att, *blocks)


def permute(x, places, move):
    pairs = []
    for d in range(places):
        for t in range(T4):
            to = move(d, t)
            if to is not None:
                pairs.append((d * T4 + t, to[0] * T4 + to[1]))
    return lax.ppermute(x, AX, pairs)


def after(x, *events):
    return lax.optimization_barrier((x, events))[0]


def flip_core(d, t):
    return (d ^ 1, t)


def flip_z(d, t):
    return (d, t ^ 1)


def flip_far(d, t):
    return (d, t ^ 2)


def flip_e(bit):
    return lambda d, t: (d ^ (2 << bit), t)


def settle(d, t):
    return (d, t) if (d & 1) == (t >> 1) else (d ^ 1, t ^ 2)


def step(*values):
    return lax.optimization_barrier(values)


def eighth(w, c, e):
    rows = w.shape[0] // 8
    return lax.dynamic_slice_in_dim(w, (2 * e + c) * rows, rows, 0)


def around(piece, n):
    return [permute(piece, n, lambda d, t, j=j: (d ^ (2 * j), t)) for j in (1, 2, 3)]


def across(pieces, n):
    return [permute(piece, n, flip_core) for piece in pieces]


def first_sums(pieces, n):
    sent_a, keep_a, sent_b, keep_b = pieces
    got_a = permute(sent_a, n, flip_e(0))
    got_b = permute(sent_b, n, flip_e(1))
    return got_a, got_b


def first_add(pieces, got):
    got_a, got_b = got
    keep_a, keep_b = pieces[1], pieces[3]
    return keep_a[1] + got_a[1], keep_a[0] + got_a[0], keep_b[1] + got_b[1], keep_b[0] + got_b[0]


def second_sums(halves, n):
    return permute(halves[0], n, flip_e(1)), permute(halves[2], n, flip_e(0))


def second_add(halves, got, n):
    total = jnp.stack([halves[1] + got[0], halves[3] + got[1]])
    for extra in range(2, 20):
        if (2 << extra) < n:
            total = total + permute(total, n, flip_e(extra))
    return total


def cross_sent(total, c):
    half = total.shape[1] // 2
    return jnp.where(c == 0, total[:, half:], total[:, :half])


def cross_got(total, got, c):
    half = total.shape[1] // 2
    return jnp.where(c == 0, total[:, :half], got), jnp.where(c == 0, got, total[:, half:])


def neighbours(n):
    return None if n == 8 else [list(range(k, k + 8)) for k in range(0, n, 8)]


def whole_grad(mine, n):
    return lax.all_gather(mine, "dp", axis_index_groups=neighbours(n))


def vector_moves(n):
    bits = [1 << k for k in range(20) if 1 << k < n]
    return [flip_z] + [lambda d, t, bit=bit: (d ^ bit, t) for bit in bits] + [flip_far]


def local(
    block_input,
    doc_lengths,
    pad_mask,
    norm1_gain,
    w_query,
    w_key,
    w_value,
    query_gain,
    key_gain,
    w_out,
    norm2_gain,
    w_gate,
    w_up,
    w_down,
    cotangent,
):
    n = lax.axis_size("dp")
    d, t = lax.axis_index("dp"), lax.axis_index("tensor")
    c, p = d & 1, t >> 1
    e = (d >> 1) & 3
    shard = 2 * c + (t & 1)
    b = block_input.shape[0]
    seq_len = b * T4
    home = c == p
    wq = w_query.shape[1]
    wk = w_key.shape[1]
    width = block_input.shape[1]
    s = jnp.stack([shard, c, e]).astype(jnp.int32)

    marks = jnp.concatenate([doc_lengths, pad_mask], 1)
    mine_out = eighth(w_out, c, e)
    mine_qkv = jnp.concatenate([eighth(w, c, e) for w in (w_query, w_key, w_value)], 1)
    x_own = permute(block_input, n, settle)
    qkv_hop = permute(mine_qkv, n, flip_far)
    out_z = permute(mine_out, n, flip_z)
    marks = jnp.where(home, marks, permute(marks, n, flip_core))
    lengths_row, pad_row = marks[0, : doc_lengths.shape[1]], marks[0, doc_lengths.shape[1] :]
    mine_gate_up = jnp.concatenate([eighth(w, c, e) for w in (w_gate, w_up)], 1)
    mine_down = eighth(w_down, c, e)

    positions = jnp.arange(seq_len, dtype=jnp.int32)
    doc_starts, cos_half, sin_half = doc_tables(lengths_row, positions, HD)
    cos = jnp.concatenate([cos_half] * 4, 1)
    sin = jnp.concatenate([-sin_half, sin_half] * 2, 1)
    live = jnp.where(pad_row == 1, positions, -1)
    start_col = jnp.broadcast_to(doc_starts[:, None], (seq_len, 128))
    start_row = jnp.broadcast_to(doc_starts[None], (8, seq_len))
    live_col = jnp.broadcast_to(live[:, None], (seq_len, 128))
    live_row = jnp.broadcast_to(live[None], (8, seq_len))
    gains = jnp.concatenate([query_gain] * (wq // HD) + [key_gain] * (wk // HD))[None]
    qgain_pair = jnp.concatenate([query_gain] * 2)[None]
    kgain_pair = jnp.concatenate([key_gain] * 2)[None]

    x_own, cos, sin, start_col, start_row, live_col, live_row = step(
        x_own, cos, sin, start_col, start_row, live_col, live_row
    )
    qkv_hop, out_z, mine_gate_up, mine_down, late_dy = after([qkv_hop, out_z, mine_gate_up, mine_down, cotangent], x_own)
    x_over, x_near = permute(x_own, n, flip_z), permute(x_own, n, flip_core)
    two_out = jnp.stack([mine_out, out_z])
    out_far = permute(two_out, n, flip_far)
    qkv_around = around(qkv_hop, n)
    gate_up_hop = permute(mine_gate_up, n, flip_far)
    x_over, x_near, out_far, late_dy, *qkv_around = step(x_over, x_near, out_far, late_dy, *qkv_around)
    x_far = permute(x_over, n, flip_core)
    qkv_mine = [qkv_hop] + qkv_around
    qkv_other = across(qkv_mine, n)
    out_all = lax.all_gather(jnp.concatenate([two_out, out_far]), "dp", axis_index_groups=neighbours(n))
    x_blocks = [x_own, x_over, x_near, x_far]

    rows_one, pre, qk, values, w_qkv = qkv_call(
        s, x_blocks, (w_query, w_key, w_value), qkv_mine + qkv_other, norm1_gain[None], gains, cos, sin
    )
    attended, attended_f, lse = attend_call(s, qk, values, start_col, live_row)

    att_over, att_near = permute(attended, n, flip_z), permute(attended, n, flip_core)
    gate_up_hop = after(gate_up_hop, attended)
    gate_up_around = around(gate_up_hop, n)
    mine_down, late_dy = after([mine_down, late_dy], gate_up_hop)
    dy_own = permute(late_dy, n, settle)
    down_hop = permute(mine_down, n, flip_far)
    att_over, att_near, dy_own, *gate_up_around = step(att_over, att_near, dy_own, *gate_up_around)
    att_far = permute(att_over, n, flip_core)
    dy_over, dy_near = permute(dy_own, n, flip_z), permute(dy_own, n, flip_core)
    down_hop = after(down_hop, att_far)
    gate_up_mine = [gate_up_hop] + gate_up_around
    gate_up_parts = gate_up_mine + across(gate_up_mine, n)
    down_around = around(down_hop, n)
    rows_two, hidden, by_gate, by_up, residual, w_out_own = ffn_call(
        s, x_blocks, [attended, att_over, att_near, att_far], out_all, w_gate, w_up, gate_up_parts,
        after(norm2_gain[None], dy_own),
    )
    hidden, dy_over, dy_near, *down_around = step(hidden, dy_over, dy_near, *down_around)
    down_mine = [down_hop] + down_around
    dy_far, *down_across = step(permute(dy_over, n, flip_core), *across(down_mine, n))
    down_parts = down_mine + down_across
    dy_blocks = [dy_own, dy_over, dy_near, dy_far]

    down = grad_cols_call(s, hidden, dy_blocks, "grad_down")
    down_got = first_sums(down, n)
    gate_grad, up_grad, low2, high2 = ffn_back_call(
        s, dy_blocks, w_down, down_parts, w_gate, w_up, gate_up_parts, after(by_gate, *down), by_up
    )
    low2, high2, *down_got = step(low2, high2, *down_got)
    (high_got,) = step(permute(high2, n, flip_core))
    low_half = low2 + high_got
    low_over = permute(low_half[b:], n, flip_z)
    gate_up = grad_rows_call(s, rows_two, after(gate_grad, low_half), up_grad, "grad_gate_up")
    gate_up_got = first_sums(gate_up, n)
    down = first_add(down, after(down_got, *gate_up))
    down_got = second_sums(down, n)
    grad_n2 = (low_half[:b] + after(low_over, *down)).astype(f32)
    inv = lax.rsqrt(jnp.mean(residual * residual, axis=-1, keepdims=True) + epsilon)
    scaled = norm2_gain * grad_n2
    grad_residual = (
        dy_own.astype(f32)
        + inv * scaled
        - residual * (inv * inv * inv) * jnp.mean(scaled * residual, axis=-1, keepdims=True)
    )
    grad_norm2 = jnp.sum(grad_n2 * residual * inv, axis=0)
    gb_own = grad_residual.astype(bf16)
    gb_over, gb_near = permute(gb_own, n, flip_z), permute(gb_own, n, flip_core)
    ffn_low, ffn_high = ffn_out_call(s, w_down, down_parts, after(hidden, gb_own))
    ffn_got = permute(ffn_high, n, flip_core)
    gb_over, gb_near = step(*after([gb_over, gb_near], ffn_low))
    ffn_got = after(ffn_got, gb_over)
    gb_far = permute(gb_over, n, flip_core)
    gate_up = first_add(gate_up, after(gate_up_got, gb_over))
    gate_up_got = second_sums(gate_up, n)
    down = second_add(down, after(down_got, gb_over, *gate_up), n)
    ffn_half = ffn_low + ffn_got
    gb_far, down_got = step(gb_far, permute(cross_sent(down, c), n, flip_core))
    down_kept, down_sent = cross_got(down, down_got, c)
    down_got = permute(down_sent, n, flip_far)
    ffn_over = permute(ffn_half[b:], n, flip_z)
    gb_blocks = [gb_own, gb_over, gb_near, gb_far]

    low, gain_terms, low1, high1 = attend_back_call(
        s, qk, after(values, ffn_half, down_sent), pre, qgain_pair, kgain_pair, cos, sin, start_row, live_col,
        attended_f, lse, w_out_own, w_qkv, gb_blocks,
    )
    low, low1, high1, down_got, ffn_over, *gate_up_got = step(low, low1, high1, down_got, ffn_over, *gate_up_got)
    down_mine = down_kept + down_got
    down_all = whole_grad(down_mine, n)
    gate_up = second_add(gate_up, after(gate_up_got, down_mine), n)
    high_got, gate_up_got = step(permute(high1, n, flip_core), permute(cross_sent(gate_up, c), n, flip_core))
    low_half = low1 + high_got
    low_over = permute(low_half[b:], n, flip_z)
    gate_up_kept, gate_up_sent = cross_got(gate_up, gate_up_got, c)
    gate_up_got = permute(gate_up_sent, n, flip_far)
    att = grad_attention_call(s, rows_one, after(low, low_half, gate_up_sent), attended, gb_blocks)
    att_got = first_sums(att, n)
    block_output = residual + (ffn_half[:b] + after(ffn_over, *att)).astype(f32)
    low_over, gate_up_got, *att_got = step(*after([low_over, gate_up_got, *att_got], block_output))
    gate_up_mine = gate_up_kept + gate_up_got
    gate_up_all = whole_grad(gate_up_mine, n)
    att = first_add(att, after(att_got, gate_up_mine))
    att_got = second_sums(att, n)
    grad_n1 = (low_half[:b] + after(low_over, *att)).astype(f32)
    x_f = x_own.astype(f32)
    inv = lax.rsqrt(jnp.mean(x_f * x_f, axis=-1, keepdims=True) + epsilon)
    scaled = norm1_gain * grad_n1
    input_grad = (
        grad_residual
        + inv * scaled
        - x_f * (inv * inv * inv) * jnp.mean(scaled * x_f, axis=-1, keepdims=True)
    )
    grad_norm1 = jnp.sum(grad_n1 * x_f * inv, axis=0)
    head_terms = gain_terms[:, :HD] + gain_terms[:, HD:]
    vec = jnp.concatenate([grad_norm1, grad_norm2, head_terms[0] + head_terms[1], head_terms[2]])[None]
    moves = vector_moves(n)
    vec_got = permute(vec, n, moves[0])
    att = second_add(att, after(att_got, input_grad, vec), n)
    (att_got,) = step(permute(cross_sent(att, c), n, flip_core))
    att_kept, att_sent = cross_got(att, att_got, c)
    att_got = permute(att_sent, n, flip_far)
    vec = vec + after(vec_got, att_sent)
    vec_got = permute(vec, n, moves[1])
    (grad_down,) = widen_call(after(down_all, att_sent), True, "widen_down")
    att_got, vec_got = step(*after([att_got, vec_got], grad_down))
    att_mine = att_kept + att_got
    att_around = around(att_mine, n)
    late_output, late_grad = after([block_output, input_grad], att_mine)
    settled_output = permute(late_output.astype(bf16), n, settle)
    settled_grad = permute(late_grad.astype(bf16), n, settle)
    vec = vec + vec_got
    vec_got = permute(vec, n, moves[2])
    vec_got, *att_around = step(vec_got, *att_around)
    att_across = across([att_mine] + att_around, n)
    vec = vec + vec_got
    vec_got = permute(vec, n, moves[3])
    grad_query, grad_key, grad_value, grad_out = place_call(
        s,
        [att_mine] + att_around + after(att_across, vec),
        write_attention,
        [(width // 8, wq), (width // 8, wk), (width // 8, wk), (w_out.shape[0] // 8, width)],
        "place_attention",
    )
    settled_output, settled_grad, vec_got = after([settled_output, settled_grad, vec_got], grad_query)
    block_output = jnp.where(home, block_output, settled_output.astype(f32))
    input_grad = jnp.where(home, input_grad, settled_grad.astype(f32))
    vec = vec + vec_got
    vec_got = permute(vec, n, moves[4])
    grad_gate, grad_up = widen_call(after(gate_up_all, vec), False, "widen_gate_up")
    vec = vec + after(vec_got, grad_gate)
    for move in moves[5:]:
        vec = vec + permute(vec, n, move)
    vec = vec[0]
    return (
        block_output,
        input_grad,
        vec[:width],
        grad_query,
        grad_key,
        grad_value,
        vec[2 * width : 2 * width + HD],
        vec[2 * width + HD :],
        grad_out,
        vec[width : 2 * width],
        grad_gate,
        grad_up,
        grad_down,
    )


def solution(mesh):
    placed = (
        P(("dp", "tensor"), None),
        P("dp", None),
        P("dp", None),
        P(),
        P(None, "tensor"),
        P(None, "tensor"),
        P(None, "tensor"),
        P(),
        P(),
        P("tensor", None),
        P(),
        P(None, "tensor"),
        P(None, "tensor"),
        P("tensor", None),
        P(("dp", "tensor"), None),
    )
    return jax.shard_map(
        local,
        mesh=mesh,
        in_specs=placed,
        out_specs=(
            P(("dp", "tensor"), None),
            P(("dp", "tensor"), None),
            P(),
            P(None, "tensor"),
            P(None, "tensor"),
            P(None, "tensor"),
            P(),
            P(),
            P("tensor", None),
            P(),
            P(None, "tensor"),
            P(None, "tensor"),
            P("tensor", None),
        ),
        check_vma=False,
    )
```
